32 devices in a mesh: dp: 8 (over z, x), head: 4 (over y, core).
Axes of the slice: x: 2, y: 2, z: 4, core: 2. Of those that a mesh axis runs over, the one named last changes fastest.
Arguments:
- frames: bfloat16 [16384, 1024], P(('dp', 'head')), may hold values from -6 to 6
- ffn_inner: bfloat16 [2, 1024, 4096], P(None, ('dp', 'head')), may hold values from -0.1875 to 0.1875
- ffn_outer: bfloat16 [2, 4096, 1024], P(None, ('dp', 'head')), may hold values from -0.09375 to 0.09375
- attn_qkv: bfloat16 [1024, 3072], P(('dp', 'head')), may hold values from -0.1875 to 0.1875
- attn_proj: bfloat16 [1024, 1024], P(('dp', 'head')), may hold values from -0.75 to 0.75
- conv_expand: bfloat16 [1024, 2048], P(('dp', 'head')), may hold values from -0.1875 to 0.1875
- conv_depth: bfloat16 [32, 1024], P(None, ('dp', 'head')), may hold values from -1 to 1
- conv_proj: bfloat16 [1024, 1024], P(('dp', 'head')), may hold values from -0.1875 to 0.1875
- norm_gains: bfloat16 [6, 1024], P(None, ('dp', 'head')), may hold values from 0.099609375 to 1.8984375
- head_proj: bfloat16 [1024, 8192], P('dp', 'head'), may hold values from -0.1875 to 0.1875
- lengths: int32 [32], P(('dp', 'head')), may hold values from 256 to 512, as said below
- mask_starts: int32 [32, 20], P(('dp', 'head')), may hold values from 0 to 512, as said below
- target_codes: int32 [16384], P(('dp', 'head')), may hold values from 0 to 8191
- out_grad: bfloat16 [16384, 1024], P(('dp', 'head')), may hold values from -6 to 6
Outputs:
- activations: bfloat16 [16384, 1024], P(('dp', 'head'))
- loss: float32 [], replicated
- input_grad: float32 [16384, 1024], P(('dp', 'head'))
- ffn_inner_grad: float32 [2, 1024, 4096], P(None, ('dp', 'head'))
- ffn_outer_grad: float32 [2, 4096, 1024], P(None, ('dp', 'head'))
- attn_qkv_grad: float32 [1024, 3072], P(('dp', 'head'))
- attn_proj_grad: float32 [1024, 1024], P(('dp', 'head'))
- conv_expand_grad: float32 [1024, 2048], P(('dp', 'head'))
- conv_depth_grad: float32 [32, 1024], P(None, ('dp', 'head'))
- conv_proj_grad: float32 [1024, 1024], P(('dp', 'head'))
- norm_gains_grad: float32 [6, 1024], P(None, ('dp', 'head'))
- head_proj_grad: float32 [1024, 8192], P('dp', 'head')
The draws below stay inside these ranges and needn't reach their ends.
Inputs may be any that keep to these rules, and one draw needn't show every extreme that they name: `lengths`: each utterance has at least half of its 512 frames valid; in every draw some device has all of its utterances fully valid. `mask_starts`: span place i of an utterance starts between i * (25) and (i + 1) * 25 - 10, or holds 512 when unused, so spans never intersect. At most 200 frames of one device are masked, and in every draw some device has exactly 200.
All inputs are finite; a program needn't handle non-finite values.
Results may differ from the reference program's by a relative error of at most 0.017.
Values may be sent and summed in bfloat16 or wider, within the bound.
No kernel may reach another device: no remote copies, remote signals or barrier semaphores. Data moves between devices by JAX's collectives and lax.ppermute only.
A program may use at most 448 MiB of HBM per device.

```python
import jax
import jax.numpy as jnp
from jax import lax

D = 1024
FF = 4096
H = 8
HD = 128
KERNEL = 32
VOCAB = 8192
SEQ = 512
SPAN = 10
NSPAN = 20
UTT_DEV = 1
UTTS = 32
TOKENS = 16384


def full_block(key):
    picked = jax.random.randint(jax.random.fold_in(key, 11), (), 0, UTTS // UTT_DEV)
    return jnp.arange(UTTS) // UTT_DEV == picked


def draw_lengths(key, part):
    drawn_lengths = jax.random.randint(jax.random.fold_in(key, 12), (UTTS,), SEQ // 2, SEQ + 1)
    return jnp.where(full_block(key), SEQ, drawn_lengths).astype(jnp.int32)


def draw_mask_starts(key, part):
    spacing = SEQ // NSPAN
    device_count = UTTS // UTT_DEV
    device_of = jnp.arange(UTTS, dtype=jnp.int32) // UTT_DEV
    rising = NSPAN * (device_count - 1) + 2 * NSPAN * device_of
    span_cap = (rising + 3 * (device_count - 1) - 1) // (3 * (device_count - 1))
    span_cap = jnp.clip(span_cap, 1, NSPAN)
    span_floor = span_cap // 2
    uniform_pick = jax.random.randint(jax.random.fold_in(key, 13), (UTTS,), 0, 1 << 20)
    counts = span_floor + uniform_pick % (span_cap - span_floor + 1)
    counts = jnp.where(full_block(key), NSPAN, counts)
    offsets = jax.random.randint(jax.random.fold_in(key, 14), (UTTS, NSPAN), 0, spacing - SPAN + 1)
    starts = jnp.arange(NSPAN)[None, :] * spacing + offsets
    scores = jax.random.randint(jax.random.fold_in(key, 15), (UTTS, NSPAN), 0, 1 << 20) * NSPAN + jnp.arange(NSPAN)[None, :]
    span_ranks = jnp.argsort(jnp.argsort(scores, axis=1, stable=True), axis=1, stable=True)
    return jnp.where(span_ranks < counts[:, None], starts, SEQ).astype(jnp.int32)


def set_ends(values, key, smallest, high):
    longest = values.shape.index(max(values.shape))
    spots = []
    for shift in (0, 1):
        where = [jax.random.randint(jax.random.fold_in(key, axis), (), 0, length) for axis, length in enumerate(values.shape)]
        where[longest] = (where[longest] + shift) % values.shape[longest]
        spots.append(tuple(where))
    return values.at[spots[0]].set(smallest).at[spots[1]].set(high)


def level_of(stream_key, extent, split, least, high):
    factor_of = 1.0
    for position, blocks in split:
        heights = jax.random.uniform(jax.random.fold_in(jax.random.fold_in(stream_key, 6), position), (blocks,), jnp.float32, least / len(split), high / len(split))
        factor_of = factor_of * jnp.repeat(jnp.exp(heights), extent[position] // blocks).reshape((-1,) + (1,) * (len(extent) - 1 - position))
    return factor_of


def bell_draw(own_key, dims, spread, bound, cuts=(), held_as=jnp.bfloat16):
    gain = level_of(own_key, dims, cuts, -0.22, 0.18) if cuts else 1.0
    entries = jax.random.normal(own_key, dims, jnp.float32) * spread * gain
    return jnp.minimum(jnp.maximum(entries, -bound), bound).astype(held_as)


def setup_inputs(seed: int = 0) -> dict:
    keys = jax.random.split(jax.random.key(seed), 15)
    frames = bell_draw(keys[0], (TOKENS, D), 1.0, 6.0, ((0, 32),))
    ffn_inner = bell_draw(keys[1], (2, D, FF), D ** -0.5, 0.1875, ((1, 32),))
    ffn_outer = bell_draw(keys[2], (2, FF, D), FF ** -0.5, 0.09375, ((1, 32),))
    attn_qkv = bell_draw(keys[3], (D, 3 * D), D ** -0.5, 0.1875, ((0, 32),))
    attn_proj = bell_draw(keys[4], (D, D), (D // 16) ** -0.5, 0.75, ((0, 32),))
    conv_expand = bell_draw(keys[5], (D, 2 * D), D ** -0.5, 0.1875, ((0, 32),))
    conv_depth = bell_draw(keys[6], (KERNEL, D), KERNEL ** -0.5, 1.0, ((1, 32),))
    conv_proj = bell_draw(keys[7], (D, D), D ** -0.5, 0.1875, ((0, 32),))
    norm_gains = jnp.clip(1.0 + 0.18 * jax.random.normal(keys[8], (6, D), jnp.float32), 0.099609375, 1.8984375).astype(jnp.bfloat16)
    head_proj = bell_draw(keys[9], (D, VOCAB), D ** -0.5, 0.1875, ((0, 8), (1, 4)))
    lengths = draw_lengths(jax.random.fold_in(keys[14], 71), 0)
    mask_starts = draw_mask_starts(jax.random.fold_in(keys[14], 71), 0)
    target_codes = set_ends(jax.random.randint(keys[12], (TOKENS,), 0, VOCAB), jax.random.fold_in(keys[12], 1), 0, VOCAB - 1).astype(jnp.int32)
    out_grad = bell_draw(keys[13], (TOKENS, D), 1.0, 6.0, ((0, 32),))
    return dict(frames=frames, ffn_inner=ffn_inner, ffn_outer=ffn_outer, attn_qkv=attn_qkv, attn_proj=attn_proj, conv_expand=conv_expand, conv_depth=conv_depth, conv_proj=conv_proj, norm_gains=norm_gains, head_proj=head_proj, lengths=lengths, mask_starts=mask_starts, target_codes=target_codes, out_grad=out_grad)


eps = 1e-05
group_utts = 8

@jax.custom_vjp
def low(v):
    return lax.optimization_barrier(v.astype(jnp.bfloat16)).astype(jnp.float32)

@jax.custom_vjp
def low_back(v):
    return v

def low_keep(v):
    return (low(v), None)

def low_pass(kept, grad):
    return (grad,)

def back_keep(v):
    return (v, None)

def back_low(kept, grad):
    return (low(grad),)
low.defvjp(low_keep, low_pass)
low_back.defvjp(back_keep, back_low)

def matmul(operand, weight):
    return jnp.dot(operand, weight, precision=lax.Precision.HIGHEST)

def layer_norm(values, gain_row):
    center = values - lax.optimization_barrier(jnp.mean(values, axis=-1, keepdims=True))
    variance = lax.optimization_barrier(jnp.mean(center * center, axis=-1, keepdims=True))
    return center * lax.rsqrt(variance + eps) * gain_row

def rotate(values, cosine, sine_table):
    half_width = values.shape[-1] // 2
    lead_part = values[..., :half_width]
    tail_part = values[..., half_width:]
    return jnp.concatenate([lead_part * cosine - tail_part * sine_table, tail_part * cosine + lead_part * sine_table], axis=-1)

def depthwise(values, tap_weights):
    kernel = tap_weights.shape[0]
    length = values.shape[1]
    padded = jnp.pad(values, ((0, 0), (kernel // 2, kernel - 1 - kernel // 2), (0, 0)))
    result = padded[:, 0:length] * tap_weights[0]
    for tap_at in range(1, kernel):
        result = result + padded[:, tap_at:tap_at + length] * tap_weights[tap_at]
    return result

def feed_forward(values, inner_weight, outer_weight, gain_row):
    normed = layer_norm(values, gain_row)
    hidden = low_back(matmul(low(normed), inner_weight))
    return low_back(matmul(low(jax.nn.silu(hidden)), outer_weight))

def attention(values, mix_weight, proj_weight, gain_row, key_ok, cosine, sine_table):
    normed = layer_norm(values, gain_row)
    mixed = low_back(matmul(low(normed), mix_weight))
    count_utts = key_ok.shape[0]
    mixed = mixed.reshape(count_utts, SEQ, 3, H, HD)
    queries = low(rotate(mixed[:, :, 0], cosine, sine_table))
    key_rows = low(rotate(mixed[:, :, 1], cosine, sine_table))
    value_rows = low(mixed[:, :, 2])
    scores = jnp.einsum('bqhd,bkhd->bhqk', queries, key_rows, precision=lax.Precision.HIGHEST) * HD ** (-0.5)
    scores = low_back(scores)
    scores = jnp.where(key_ok[:, None, None, :], scores, -1e+30)
    attn_probs = jax.nn.softmax(scores, axis=-1)
    attended = low_back(jnp.einsum('bhqk,bkhd->bqhd', low(attn_probs), value_rows, precision=lax.Precision.HIGHEST))
    return low_back(matmul(low(attended.reshape(count_utts * SEQ, D)), proj_weight))

def reference(frames, ffn_inner, ffn_outer, attn_qkv, attn_proj, conv_expand, conv_depth, conv_proj, norm_gains, head_proj, lengths, mask_starts, target_codes, out_grad):
    positions = jnp.arange(SEQ, dtype=jnp.int32)
    valid_mat = positions[None, :] < lengths[:, None]
    span_hits = (positions[None, None, :] >= mask_starts[:, :, None]) & (positions[None, None, :] < mask_starts[:, :, None] + SPAN)
    masked_mat = jnp.any(span_hits, axis=1) & valid_mat
    frequency = 10000.0 ** (-(jnp.arange(HD // 2, dtype=jnp.float32) * 2.0) / HD)
    angles = positions.astype(jnp.float32)[:, None] * frequency[None, :]
    cosine = jnp.cos(angles)[:, None, :]
    sine_table = jnp.sin(angles)[:, None, :]
    groups = UTTS // group_utts
    group_rows = group_utts * SEQ
    valid_rows = valid_mat.reshape(groups, group_rows).astype(jnp.float32)
    key_valid = valid_mat.reshape(groups, group_utts, SEQ)
    masked_rows = masked_mat.reshape(groups, group_rows).astype(jnp.float32)
    code_rows = target_codes.reshape(groups, group_rows)
    frame_count = jnp.sum(valid_mat.astype(jnp.float32))

    def forward(inputs, inner_weight, outer_weight, mix_weight, proj_weight, expand_weight, depth_weight, conv_weight, gain_rows, head_weight):

        def first_part(batch_items):
            rows_in, row_ok, key_ok = batch_items
            after_first = rows_in + 0.5 * feed_forward(rows_in, inner_weight[0], outer_weight[0], gain_rows[0])
            after_attention = after_first + attention(after_first, mix_weight, proj_weight, gain_rows[1], key_ok, cosine, sine_table)
            normed = layer_norm(after_attention, gain_rows[2])
            expanded = low_back(matmul(low(normed), expand_weight))
            gated_rows = expanded[:, :D] * jax.nn.sigmoid(expanded[:, D:]) * row_ok[:, None]
            conv_out = depthwise(gated_rows.reshape(group_utts, SEQ, D), depth_weight).reshape(group_rows, D)
            return (after_attention, conv_out)
        attn_all, conv_all = lax.map(jax.checkpoint(first_part), (inputs.reshape(groups, group_rows, D), valid_rows, key_valid))
        weighted = conv_all * valid_rows[:, :, None]
        channel_mean = lax.optimization_barrier(jnp.sum(weighted, axis=(0, 1))) / frame_count
        variance = lax.optimization_barrier(jnp.sum(weighted * conv_all, axis=(0, 1))) / frame_count - channel_mean * channel_mean
        inverse = lax.rsqrt(variance + eps)

        def second_part(batch_items):
            after_attention, conv_out, mask_rows, code_list = batch_items
            normed_bn = (conv_out - channel_mean) * inverse * gain_rows[3]
            after_conv = after_attention + low_back(matmul(low(jax.nn.silu(normed_bn)), conv_weight))
            after_second = after_conv + 0.5 * feed_forward(after_conv, inner_weight[1], outer_weight[1], gain_rows[4])
            result = low(layer_norm(after_second, gain_rows[5]))
            logits = low_back(matmul(result, head_weight))
            picked = jnp.take_along_axis(logits, code_list[:, None], axis=1)[:, 0]
            return (result, jnp.sum((jax.nn.logsumexp(logits, axis=1) - picked) * mask_rows))
        results, losses = lax.map(jax.checkpoint(second_part), (attn_all, conv_all, masked_rows, code_rows))
        return (results.reshape(TOKENS, D), jnp.sum(losses))
    floats = [array.astype(jnp.float32) for array in (frames, ffn_inner, ffn_outer, attn_qkv, attn_proj, conv_expand, conv_depth, conv_proj, norm_gains, head_proj)]
    primal, pullback = jax.vjp(forward, *floats)
    grads = pullback((out_grad.astype(jnp.float32), jnp.ones_like(primal[1])))
    loss = primal[1] / jnp.float32(UTTS * NSPAN * SPAN)
    return (primal[0].astype(jnp.bfloat16), loss, grads[0], grads[1], grads[2], grads[3], grads[4], grads[5], grads[6], grads[7], grads[8], grads[9])
```

```python
import functools

import jax
import jax.numpy as jnp
from jax import lax
from jax.sharding import PartitionSpec as P

D = 1024
H = 8
HD = 128
VOCAB = 8192
SEQ = 512
SPAN = 10
NSPAN = 20
UTT_DEV = 1


eps = 1e-05


def layer_norm(values, gain_row):
    center = values - jnp.mean(values, axis=-1, keepdims=True)
    variance = jnp.mean(center * center, axis=-1, keepdims=True)
    return center * lax.rsqrt(variance + eps) * gain_row


def rotate(values, cosine, sine_table):
    half_width = values.shape[-1] // 2
    lead_part = values[..., :half_width]
    tail_part = values[..., half_width:]
    return jnp.concatenate(
        [lead_part * cosine - tail_part * sine_table, tail_part * cosine + lead_part * sine_table],
        axis=-1,
    )


def rotate_back(grads, cosine, sine_table):
    half_width = grads.shape[-1] // 2
    lead_part = grads[..., :half_width]
    tail_part = grads[..., half_width:]
    return jnp.concatenate(
        [lead_part * cosine + tail_part * sine_table, tail_part * cosine - lead_part * sine_table],
        axis=-1,
    )


def depthwise(values, tap_weights):
    kernel = tap_weights.shape[0]
    length = values.shape[1]
    padded = jnp.pad(values, ((0, 0), (kernel // 2, kernel - 1 - kernel // 2), (0, 0)))
    result = padded[:, 0:length] * tap_weights[0]
    for tap_at in range(1, kernel):
        result = result + padded[:, tap_at : tap_at + length] * tap_weights[tap_at]
    return result


def lowered(values):
    return values.astype(jnp.bfloat16)


def matmul(operand, weight):
    return jnp.dot(operand, weight, preferred_element_type=jnp.float32)


def matmul_tn(operand, weight):
    return lax.dot_general(
        operand, weight, (((0,), (0,)), ((), ())), preferred_element_type=jnp.float32
    )


def matmul_nt(operand, weight):
    return lax.dot_general(
        operand, weight, (((1,), (1,)), ((), ())), preferred_element_type=jnp.float32
    )


def norm_back(values, gain_row, grads):
    unused, pullback = jax.vjp(layer_norm, values, gain_row)
    return pullback(grads)


def silu_back(values, grads):
    return jax.vjp(jax.nn.silu, values)[1](grads)[0]


AXES = ("dp", "head")


class Cube:
    def __init__(self, sizes):
        self.sizes = sizes
        self.bits = []
        for axis in AXES:
            bit = sizes[axis] // 2
            while bit:
                self.bits.append((axis, bit))
                bit //= 2

    def orders(self):
        whole = list(range(len(self.bits)))
        dp_count = sum(axis == "dp" for axis, bit in self.bits)
        if self.sizes == {"dp": 8, "head": 4}:
            return [0, 1, 2, 3, 4], [0, 1, 3, 2, 4], [2, 0, 1]
        return whole, whole, whole[:dp_count]

    def mine(self, at):
        axis, bit = self.bits[at]
        return (lax.axis_index(axis) // bit) % 2

    def swap(self, values, at):
        axis, bit = self.bits[at]
        return lax.ppermute(values, axis, [(i, i ^ bit) for i in range(self.sizes[axis])])

    def gather(self, shard, order):
        held = []
        values = shard
        for at in order:
            place = sum(other < at for other in held)
            got = self.swap(values, at)
            mine = self.mine(at)
            first = jnp.where(mine == 0, values, got)
            second = jnp.where(mine == 0, got, values)
            values = jnp.stack([first, second], axis=place)
            held.append(at)
        return values

    def scatter(self, values, order, final=jnp.float32):
        held = sorted(order)
        for step, at in enumerate(order[::-1]):
            place = held.index(at)
            mine = self.mine(at)
            send = lax.dynamic_index_in_dim(values, 1 - mine, place, keepdims=False)
            keep = lax.dynamic_index_in_dim(values, mine, place, keepdims=False)
            got = self.swap(send, at)
            total = keep.astype(jnp.float32) + got.astype(jnp.float32)
            values = total.astype(final if step == len(order) - 1 else values.dtype)
            held.remove(at)
        return values

    def total(self, values, only=None):
        for at in range(len(self.bits)):
            if only is None or self.bits[at][0] == only:
                values = values + self.swap(values, at)
        return values


def rows_of(values, count):
    return values.reshape(count, values.shape[-1])


def shards(
    sizes,
    frames,
    ffn_inner,
    ffn_outer,
    attn_qkv,
    attn_proj,
    conv_expand,
    conv_depth,
    conv_proj,
    norm_gains,
    head_proj,
    lengths,
    mask_starts,
    target_codes,
    out_grad,
):
    cube = Cube(sizes)
    order_a, order_b, order_dp = cube.orders()
    devices = sizes["dp"] * sizes["head"]
    ff = ffn_inner.shape[2]

    def gathered(shard):
        half = shard.shape[1] // 2
        return (
            rows_of(cube.gather(shard[:, :half], order_a), shard.shape[0] * devices),
            rows_of(cube.gather(shard[:, half:], order_b), shard.shape[0] * devices),
        )

    def scattered(left, right):
        bits = (2,) * len(cube.bits)
        rows = left.shape[0] // devices
        return jnp.concatenate(
            [
                cube.scatter(left.reshape(bits + (rows, -1)), order_a),
                cube.scatter(right.reshape(bits + (rows, -1)), order_b),
            ],
            axis=1,
        )

    vectors = jnp.concatenate([norm_gains, conv_depth], axis=0)
    vectors = cube.gather(vectors, order_a)
    vectors = jnp.moveaxis(vectors.reshape((devices,) + vectors.shape[-2:]), 0, 1).reshape(-1, D)
    vectors = vectors.astype(jnp.float32)
    gain_f, depth_f = vectors[:6], vectors[6:]
    inner_a0, inner_b0 = gathered(ffn_inner[0])
    outer_a0, outer_b0 = gathered(ffn_outer[0])
    mix_a, mix_b = gathered(attn_qkv)
    mid = jnp.concatenate([attn_proj, conv_expand, conv_proj], axis=1)
    mid_a, mid_b = gathered(mid)
    inner_a1, inner_b1 = gathered(ffn_inner[1])
    head_cols = cube.gather(head_proj, order_dp).reshape(D, -1)
    outer_a1, outer_b1 = gathered(ffn_outer[1])
    proj_weight, lead_weight = mid_a[:, :D], mid_a[:, D:]
    gate_weight, conv_weight = mid_b[:, :D], mid_b[:, D:]

    row_total = UTT_DEV * SEQ
    positions = jnp.arange(SEQ, dtype=jnp.int32)
    valid_mat = positions[None, :] < lengths[:, None]
    valid_rows = valid_mat.reshape(row_total).astype(jnp.float32)
    frequency = 10000.0 ** (-(jnp.arange(HD // 2, dtype=jnp.float32) * 2.0) / HD)
    angles = positions.astype(jnp.float32)[:, None] * frequency[None, :]
    cosine = jnp.cos(angles)[:, None, :]
    sine_table = jnp.sin(angles)[:, None, :]
    score_scale = HD ** (-0.5)

    slots = UTT_DEV * NSPAN * SPAN
    slot_at = (mask_starts[:, :, None] + jnp.arange(SPAN, dtype=jnp.int32)).reshape(UTT_DEV, -1)
    slot_ok = slot_at < lengths[:, None]
    chosen = (slot_at + SEQ * jnp.arange(UTT_DEV, dtype=jnp.int32)[:, None]).reshape(slots)
    slot_live = slot_ok.reshape(slots)
    pick = (
        (chosen[:, None] == jnp.arange(row_total, dtype=jnp.int32)[None, :]) & slot_live[:, None]
    )
    picked_codes = jnp.sum(jnp.where(pick, target_codes[None, :], 0), axis=1)
    picked_codes = jnp.where(slot_live, picked_codes, -1)
    pick_lo = pick.astype(jnp.bfloat16)
    head_order = [at for at in range(len(cube.bits)) if cube.bits[at][0] == "head"]
    group = sizes["head"]
    vocab_cols = head_proj.shape[1]
    group_codes = cube.gather(picked_codes, head_order).reshape(group * slots)
    group_live = (group_codes >= 0).astype(jnp.float32)
    local_codes = group_codes - lax.axis_index("head") * vocab_cols

    inputs = frames.astype(jnp.float32)
    norm_first = lowered(layer_norm(inputs, gain_f[0]))
    pre_first = [matmul(norm_first, inner_a0), matmul(norm_first, inner_b0)]
    act_first = jnp.concatenate([lowered(jax.nn.silu(part)) for part in pre_first], axis=1)
    after_first = inputs + 0.5 * jnp.concatenate(
        [matmul(act_first, outer_a0), matmul(act_first, outer_b0)], axis=1
    )
    norm_attn = lowered(layer_norm(after_first, gain_f[1]))
    mixed = jnp.concatenate([matmul(norm_attn, mix_a), matmul(norm_attn, mix_b)], axis=1)
    mixed = mixed.reshape(UTT_DEV, SEQ, 3, H, HD)
    queries = lowered(rotate(mixed[:, :, 0], cosine, sine_table))
    key_rows = lowered(rotate(mixed[:, :, 1], cosine, sine_table))
    value_rows = lowered(mixed[:, :, 2])

    def scores_of(query_one, key_one, key_ok):
        scores = (
            jnp.einsum("qhd,khd->hqk", query_one, key_one, preferred_element_type=jnp.float32)
            * score_scale
        )
        return jnp.where(key_ok[None, None, :], scores, -1e30)

    def attend_one(query_one, key_one, value_one, key_ok):
        scores = scores_of(query_one, key_one, key_ok)
        row_top = jnp.max(scores, axis=-1, keepdims=True)
        weights = jnp.exp(scores - row_top)
        totals = jnp.sum(weights, axis=-1, keepdims=True)
        attn_probs = weights / totals
        attended = jnp.einsum(
            "hqk,khd->qhd", lowered(attn_probs), value_one, preferred_element_type=jnp.float32
        )
        return (attended, row_top[..., 0] + jnp.log(totals[..., 0]))

    attended, log_totals = attend_one(queries[0], key_rows[0], value_rows[0], valid_mat[0])
    attended_lo = lowered(attended.reshape(row_total, D))
    after_attention = after_first + matmul(attended_lo, proj_weight)
    norm_conv = lowered(layer_norm(after_attention, gain_f[2]))
    lead = matmul(norm_conv, lead_weight)
    gate = matmul(norm_conv, gate_weight)

    def gate_rows(lead_rows, gate_in):
        return lead_rows * jax.nn.sigmoid(gate_in) * valid_rows[:, None]

    def conv_rows(gated_rows, tap_weights):
        return depthwise(gated_rows.reshape(UTT_DEV, SEQ, D), tap_weights).reshape(row_total, D)

    gated_rows = gate_rows(lead, gate)
    conv_out = conv_rows(gated_rows, depth_f)
    weighted = conv_out * valid_rows[:, None]
    sums = cube.total(
        jnp.stack(
            [
                jnp.sum(weighted, axis=0),
                jnp.sum(weighted * conv_out, axis=0),
                jnp.broadcast_to(jnp.sum(valid_rows), (D,)),
            ]
        )
    )
    frame_count = sums[2, 0]
    channel_mean = sums[0] / frame_count
    variance = sums[1] / frame_count - channel_mean * channel_mean
    inverse = lax.rsqrt(variance + eps)
    normalized = (conv_out - channel_mean) * inverse
    normed_bn = normalized * gain_f[3]
    swish_lo = lowered(jax.nn.silu(normed_bn))
    after_conv = after_attention + matmul(swish_lo, conv_weight)
    norm_second = lowered(layer_norm(after_conv, gain_f[4]))
    pre_second = [matmul(norm_second, inner_a1), matmul(norm_second, inner_b1)]
    act_second = jnp.concatenate([lowered(jax.nn.silu(part)) for part in pre_second], axis=1)
    after_second = after_conv + 0.5 * jnp.concatenate(
        [matmul(act_second, outer_a1), matmul(act_second, outer_b1)], axis=1
    )
    output_lo = lowered(layer_norm(after_second, gain_f[5]))

    picked_rows = lowered(matmul(pick_lo, output_lo))
    group_rows = cube.gather(picked_rows, head_order).reshape(group * slots, D)
    logits = matmul(group_rows, head_cols)
    row_top = jnp.max(logits, axis=1)
    row_sum = jnp.sum(jnp.exp(logits - row_top[:, None]), axis=1)
    onehot = jnp.arange(vocab_cols, dtype=jnp.int32)[None, :] == local_codes[:, None]
    target_logit = jnp.sum(jnp.where(onehot, logits, 0.0), axis=1)
    stats = cube.gather(jnp.stack([row_top, row_sum, target_logit]), head_order)
    stats = stats.reshape(group, 3, group * slots)
    whole_top = jnp.max(stats[:, 0], axis=0)
    whole_sum = jnp.sum(stats[:, 1] * jnp.exp(stats[:, 0] - whole_top), axis=0)
    log_norm = whole_top + jnp.log(whole_sum)
    ce_group = jnp.sum((log_norm - jnp.sum(stats[:, 2], axis=0)) * group_live)
    grad_logits = lowered(
        (jnp.exp(logits - log_norm[:, None]) - onehot.astype(jnp.float32)) * group_live[:, None]
    )
    head_bits = (2,) * len(order_dp)
    head_grad = cube.scatter(
        lowered(matmul_tn(group_rows, grad_logits)).reshape(
            head_bits + (head_proj.shape[0], vocab_cols)
        ),
        order_dp,
    )
    row_grads = lowered(matmul_nt(grad_logits, head_cols))
    row_grads = cube.scatter(
        row_grads.reshape((2,) * len(head_order) + (slots, D)), head_order, jnp.bfloat16
    )
    grad_output = out_grad.astype(jnp.float32) + matmul_tn(pick_lo, row_grads)

    def feed_back_parts(grad_in, normed_lo, pre_act, act_lo, inner_parts, outer_parts):
        grad_out_lo = lowered(0.5 * grad_in)
        half = D // 2
        outer_grads = [
            lowered(matmul_tn(act_lo, grad_out_lo[:, :half])),
            lowered(matmul_tn(act_lo, grad_out_lo[:, half:])),
        ]
        outer_grad = scattered(*outer_grads)
        grad_act = matmul_nt(grad_out_lo, jnp.concatenate(outer_parts, axis=1))
        grad_pre = [
            lowered(silu_back(pre_act[0], grad_act[:, : ff // 2])),
            lowered(silu_back(pre_act[1], grad_act[:, ff // 2 :])),
        ]
        inner_grad = scattered(
            lowered(matmul_tn(normed_lo, grad_pre[0])), lowered(matmul_tn(normed_lo, grad_pre[1]))
        )
        below = matmul_nt(grad_pre[0], inner_parts[0]) + matmul_nt(grad_pre[1], inner_parts[1])
        return (below, inner_grad, outer_grad)

    grad_second, gain_grad_final = norm_back(after_second, gain_f[5], grad_output)
    below_second, inner_second, outer_second = feed_back_parts(
        grad_second,
        norm_second,
        pre_second,
        act_second,
        (inner_a1, inner_b1),
        (outer_a1, outer_b1),
    )
    norm_part, gain_grad_second = norm_back(after_conv, gain_f[4], below_second)
    grad_conv_res = grad_second + norm_part
    conv_res_lo = lowered(grad_conv_res)
    grad_bn = silu_back(normed_bn, matmul_nt(conv_res_lo, conv_weight))
    gain_grad_bn = jnp.sum(grad_bn * normalized, axis=0)
    grad_normalized = grad_bn * gain_f[3]
    back_sums = cube.total(
        jnp.stack(
            [
                jnp.sum(grad_normalized, axis=0),
                jnp.sum(grad_normalized * normalized, axis=0),
                jnp.broadcast_to(ce_group / group, (D,)),
            ]
        )
    )
    conv_proj_grad = lowered(matmul_tn(swish_lo, conv_res_lo))
    sum_plain, sum_scaled = back_sums[0], back_sums[1]
    loss = back_sums[2, 0] / jnp.float32(devices * UTT_DEV * NSPAN * SPAN)
    grad_variance = -0.5 * inverse * inverse * sum_scaled
    grad_mean = -inverse * sum_plain - 2.0 * channel_mean * grad_variance
    grad_conv_out = (
        grad_normalized * inverse
        + (grad_mean + 2.0 * grad_variance * conv_out) * valid_rows[:, None] / frame_count
    )
    grad_gated, depth_grad = jax.vjp(conv_rows, gated_rows, depth_f)[1](grad_conv_out)
    grad_lead, grad_gate = jax.vjp(gate_rows, lead, gate)[1](grad_gated)
    grad_lead, grad_gate = lowered(grad_lead), lowered(grad_gate)
    norm_part, gain_grad_conv = norm_back(
        after_attention,
        gain_f[2],
        matmul_nt(grad_lead, lead_weight) + matmul_nt(grad_gate, gate_weight),
    )
    grad_attn_res = grad_conv_res + norm_part
    attn_res_lo = lowered(grad_attn_res)
    mid_grad = scattered(
        lowered(
            jnp.concatenate(
                [matmul_tn(attended_lo, attn_res_lo), matmul_tn(norm_conv, grad_lead)], axis=1
            )
        ),
        lowered(
            jnp.concatenate([matmul_tn(norm_conv, grad_gate), matmul_tn(swish_lo, conv_res_lo)], axis=1)
        ),
    )
    grad_attended = lowered(matmul_nt(attn_res_lo, proj_weight)).reshape(UTT_DEV, SEQ, H, HD)

    def attend_back(query_one, key_one, value_one, key_ok, log_total, grad_one):
        attn_probs = jnp.exp(scores_of(query_one, key_one, key_ok) - log_total[:, :, None])
        grad_value = jnp.einsum(
            "hqk,qhd->khd", lowered(attn_probs), grad_one, preferred_element_type=jnp.float32
        )
        grad_probs = jnp.einsum(
            "qhd,khd->hqk", grad_one, value_one, preferred_element_type=jnp.float32
        )
        grad_scores = lowered(
            attn_probs * (grad_probs - jnp.sum(attn_probs * grad_probs, axis=-1, keepdims=True))
        )
        grad_query = (
            jnp.einsum("hqk,khd->qhd", grad_scores, key_one, preferred_element_type=jnp.float32)
            * score_scale
        )
        grad_key = (
            jnp.einsum("hqk,qhd->khd", grad_scores, query_one, preferred_element_type=jnp.float32)
            * score_scale
        )
        return (grad_query, grad_key, grad_value)

    grad_query, grad_key, grad_value = attend_back(
        queries[0], key_rows[0], value_rows[0], valid_mat[0], log_totals, grad_attended[0]
    )
    grad_mixed = jnp.concatenate(
        [
            lowered(rotate_back(grad_query, cosine[:, :, :], sine_table)).reshape(row_total, D),
            lowered(rotate_back(grad_key, cosine, sine_table)).reshape(row_total, D),
            lowered(grad_value).reshape(row_total, D),
        ],
        axis=1,
    )
    mix_half = 3 * D // 2
    mix_grad = scattered(
        lowered(matmul_tn(norm_attn, grad_mixed[:, :mix_half])),
        lowered(matmul_tn(norm_attn, grad_mixed[:, mix_half:])),
    )
    norm_part, gain_grad_attn = norm_back(
        after_first,
        gain_f[1],
        matmul_nt(grad_mixed[:, :mix_half], mix_a) + matmul_nt(grad_mixed[:, mix_half:], mix_b),
    )
    grad_first_res = grad_attn_res + norm_part
    below_first, inner_first, outer_first = feed_back_parts(
        grad_first_res, norm_first, pre_first, act_first, (inner_a0, inner_b0), (outer_a0, outer_b0)
    )
    norm_part, gain_grad_first = norm_back(inputs, gain_f[0], below_first)
    input_grad = grad_first_res + norm_part
    vector_grad = jnp.concatenate(
        [
            jnp.stack(
                [
                    gain_grad_first,
                    gain_grad_attn,
                    gain_grad_conv,
                    gain_grad_bn,
                    gain_grad_second,
                    gain_grad_final,
                ],
                axis=0,
            ),
            depth_grad,
        ],
        axis=0,
    )
    vector_grad = jnp.moveaxis(vector_grad.reshape(vector_grad.shape[0], devices, -1), 1, 0)
    vector_grad = cube.scatter(
        vector_grad.reshape((2,) * len(cube.bits) + vector_grad.shape[1:]), order_a
    )
    return (
        output_lo,
        loss,
        input_grad,
        jnp.stack([inner_first, inner_second], axis=0),
        jnp.stack([outer_first, outer_second], axis=0),
        mix_grad,
        mid_grad[:, :D],
        mid_grad[:, D : 3 * D],
        vector_grad[6:],
        mid_grad[:, 3 * D :],
        vector_grad[:6],
        head_grad,
    )


def solution(mesh):
    placed = (
        P(("dp", "head"), None),
        P(None, ("dp", "head"), None),
        P(None, ("dp", "head"), None),
        P(("dp", "head"), None),
        P(("dp", "head"), None),
        P(("dp", "head"), None),
        P(None, ("dp", "head")),
        P(("dp", "head"), None),
        P(None, ("dp", "head")),
        P("dp", "head"),
        P(("dp", "head")),
        P(("dp", "head"), None),
        P(("dp", "head")),
        P(("dp", "head"), None),
    )
    sizes = {axis: mesh.shape[axis] for axis in AXES}
    return jax.shard_map(
        functools.partial(shards, sizes),
        mesh=mesh,
        in_specs=placed,
        out_specs=(
            P(("dp", "head"), None),
            P(),
            P(("dp", "head"), None),
            P(None, ("dp", "head"), None),
            P(None, ("dp", "head"), None),
            P(("dp", "head"), None),
            P(("dp", "head"), None),
            P(("dp", "head"), None),
            P(None, ("dp", "head")),
            P(("dp", "head"), None),
            P(None, ("dp", "head")),
            P("dp", "head"),
        ),
        check_vma=False,
    )
```

```python
import functools

import jax
import jax.numpy as jnp
from jax import lax
from jax.experimental import pallas as pl
from jax.experimental.pallas import tpu as pltpu
from jax.sharding import PartitionSpec as P

D = 1024
H = 8
HD = 128
VOCAB = 8192
SEQ = 512
SPAN = 10
NSPAN = 20
UTT_DEV = 1


eps = 1e-05


def layer_norm(values, gain_row):
    center = values - jnp.mean(values, axis=-1, keepdims=True)
    variance = jnp.mean(center * center, axis=-1, keepdims=True)
    return center * lax.rsqrt(variance + eps) * gain_row


def rotate(values, cosine, sine_table):
    half_width = values.shape[-1] // 2
    lead_part = values[..., :half_width]
    tail_part = values[..., half_width:]
    return jnp.concatenate(
        [lead_part * cosine - tail_part * sine_table, tail_part * cosine + lead_part * sine_table],
        axis=-1,
    )


def rotate_back(grads, cosine, sine_table):
    half_width = grads.shape[-1] // 2
    lead_part = grads[..., :half_width]
    tail_part = grads[..., half_width:]
    return jnp.concatenate(
        [lead_part * cosine + tail_part * sine_table, tail_part * cosine - lead_part * sine_table],
        axis=-1,
    )


def depthwise(values, tap_weights):
    kernel = tap_weights.shape[0]
    length = values.shape[1]
    padded = jnp.pad(values, ((0, 0), (kernel // 2, kernel - 1 - kernel // 2), (0, 0)))
    result = padded[:, 0:length] * tap_weights[0]
    for tap_at in range(1, kernel):
        result = result + padded[:, tap_at : tap_at + length] * tap_weights[tap_at]
    return result


def lowered(values):
    return values.astype(jnp.bfloat16)


def matmul(operand, weight):
    return jnp.dot(operand, weight, preferred_element_type=jnp.float32)


def matmul_tn(operand, weight):
    return lax.dot_general(
        operand, weight, (((0,), (0,)), ((), ())), preferred_element_type=jnp.float32
    )


def matmul_nt(operand, weight):
    return lax.dot_general(
        operand, weight, (((1,), (1,)), ((), ())), preferred_element_type=jnp.float32
    )


def norm_back(values, gain_row, grads):
    unused, pullback = jax.vjp(layer_norm, values, gain_row)
    return pullback(grads)


def silu_back(values, grads):
    return jax.vjp(jax.nn.silu, values)[1](grads)[0]


AXES = ("dp", "head")
ANY = pl.BlockSpec(memory_space=pl.ANY)
VMEM = pl.BlockSpec(memory_space=pltpu.VMEM)
Z1, Z0, X, Y, C = range(5)


def place_copies(refs, out, sem, wheres):
    copies = []
    for at, (ref, where) in enumerate(zip(refs, wheres)):
        copies.append(pltpu.make_async_copy(ref, out.at[where], sem.at[at]))
        copies[-1].start()
    for copy in copies:
        copy.wait()


def weave_z_kernel(own, far, near, both, out, sem):
    z = lax.axis_index("dp") // 2
    high, low = z // 2, z % 2
    wheres = []
    for flip_high, flip_low in ((0, 0), (1, 0), (0, 1), (1, 1)):
        wheres.append((high + flip_high) % 2 * 2 + (low + flip_low) % 2)
    place_copies((own, far, near, both), out, sem, wheres)


def weave_z(parts):
    return pl.pallas_call(
        weave_z_kernel,
        out_shape=jax.ShapeDtypeStruct((4,) + parts[0].shape, parts[0].dtype),
        in_specs=[ANY] * 4,
        out_specs=VMEM,
        scratch_shapes=[pltpu.SemaphoreType.DMA((4,))],
        compiler_params=pltpu.CompilerParams(vmem_limit_bytes=16 << 20),
    )(*parts)


def weave_kernel(*refs):
    bufs, out, sem = refs[:-2], refs[-2], refs[-1]
    x, y, c = lax.axis_index("dp") % 2, lax.axis_index("head") // 2, lax.axis_index("head") % 2
    half = bufs[0].shape[-1]
    wheres = []
    for side in range(2):
        for flip_c in range(2):
            for flip_first, flip_second in ((0, 0), (1, 0), (0, 1), (1, 1)):
                flip_x, flip_y = ((flip_first, flip_second), (flip_second, flip_first))[side]
                wheres.append(
                    (
                        slice(None),
                        (x + flip_x) % 2,
                        (y + flip_y) % 2,
                        (c + flip_c) % 2,
                        slice(None),
                        pl.ds(side * half, half),
                    )
                )
    place_copies(bufs, out, sem, wheres)


def weave(bufs):
    _, rows, half = bufs[0].shape
    whole = pl.pallas_call(
        weave_kernel,
        out_shape=jax.ShapeDtypeStruct((4, 2, 2, 2, rows, 2 * half), bufs[0].dtype),
        in_specs=[ANY] * 16,
        out_specs=VMEM,
        scratch_shapes=[pltpu.SemaphoreType.DMA((16,))],
        compiler_params=pltpu.CompilerParams(vmem_limit_bytes=16 << 20),
    )(*bufs)
    return whole.reshape(32 * rows, 2 * half)


class Cube:
    def __init__(self, sizes):
        self.sizes = sizes
        self.tuned = sizes == {"dp": 8, "head": 4}
        self.bits = []
        for axis in AXES:
            bit = sizes[axis] // 2
            while bit:
                self.bits.append((axis, bit))
                bit //= 2

    def mine(self, at):
        axis, bit = self.bits[at]
        return (lax.axis_index(axis) // bit) % 2

    def swap(self, values, at):
        axis, bit = self.bits[at]
        return lax.ppermute(values, axis, [(i, i ^ bit) for i in range(self.sizes[axis])])

    def gather(self, shard, order):
        held = []
        values = shard
        for at in order:
            place = sum(other < at for other in held)
            values = self.join(values, self.swap(values, at), at, place)
            held.append(at)
        return values

    def join(self, values, got, at, place):
        mine = self.mine(at)
        first = jnp.where(mine == 0, values, got)
        second = jnp.where(mine == 0, got, values)
        return jnp.stack([first, second], axis=place)

    def total(self, values):
        for at in range(len(self.bits)):
            values = values + self.swap(values, at)
        return values


def weave_head_kernel(*refs):
    bufs, out, sem = refs[:-2], refs[-2], refs[-1]
    place = lax.axis_index("dp")
    width = bufs[0].shape[-1]
    wheres = []
    for at in range(len(bufs)):
        flip_x, flip_far, flip_near = at % 2, at // 2 % 2, at // 4 % 2
        high = (place // 4 + flip_far) % 2
        low = (place // 2 + flip_near) % 2
        wheres.append(
            (
                high * 4 + low * 2 + (place + flip_x) % 2,
                slice(None),
                pl.ds(at // 8 * width, width),
            )
        )
    place_copies(bufs, out, sem, wheres)


def weave_head(bufs):
    rows, width = bufs[0].shape
    columns = len(bufs) // 8 * width
    whole = pl.pallas_call(
        weave_head_kernel,
        out_shape=jax.ShapeDtypeStruct((8, rows, columns), bufs[0].dtype),
        in_specs=[ANY] * len(bufs),
        out_specs=VMEM,
        scratch_shapes=[pltpu.SemaphoreType.DMA((len(bufs),))],
        compiler_params=pltpu.CompilerParams(vmem_limit_bytes=16 << 20),
    )(*bufs)
    return whole.reshape(8 * rows, columns)


class HeadGathering:
    def __init__(self, cube, shard):
        self.cube = cube
        self.state = [shard]

    def step(self, phase):
        if not self.cube.tuned:
            if phase == "x":
                self.state = [lax.all_gather(self.state[0], "dp", axis=0, tiled=True)]
            return
        at = {"x": X, "far": Z1, "near": Z0}[phase]
        self.state = self.state + [self.cube.swap(part, at) for part in self.state]


class Gathering:
    def __init__(self, cube, shard):
        self.cube = cube
        half = shard.shape[1] // 2
        self.state = [shard[:, :half], shard[:, half:]] if cube.tuned else [shard]

    def step(self, phase):
        cube, state = self.cube, self.state
        if not cube.tuned:
            if phase == "z":
                self.state = [lax.all_gather(state[0], AXES, axis=0, tiled=True)]
            return
        if phase == "z":
            parts = []
            for own in state:
                far, near = cube.swap(own, Z1), cube.swap(own, Z0)
                parts += [own, far, near, cube.swap(far, Z0)]
            self.state = parts
        if phase == "m":
            left, right = weave_z(state[:4]), weave_z(state[4:])
            self.state = [left, cube.swap(left, X), right, cube.swap(right, Y)]
        if phase == "n":
            a, b, c, d = state
            self.state = [
                a, b, cube.swap(a, Y), cube.swap(b, Y), c, d, cube.swap(c, X), cube.swap(d, X)
            ]
        if phase == "c":
            other = [cube.swap(part, C) for part in state]
            self.state = [weave(state[:4] + other[:4] + state[4:] + other[4:])]

    @property
    def whole(self):
        return self.state[0]


def pick_of(values, index, place):
    return lax.dynamic_index_in_dim(values, index, place, keepdims=False)


class Summing:
    def __init__(self, cube, values, order):
        self.cube, self.order = cube, list(order)
        self.held = sorted(order)
        self.keep, self.got, self.last = values, None, None

    @property
    def state(self):
        return [part for part in (self.keep, self.got) if part is not None]

    @state.setter
    def state(self, parts):
        self.keep = parts[0]
        if len(parts) > 1:
            self.got = parts[1]

    def part(self, at, want_mine):
        keep, got = self.keep, self.got
        if self.last is not None:
            keep = pick_of(keep, self.cube.mine(self.last[0]), self.last[1])
        if at is not None:
            mine, place = self.cube.mine(at), self.held.index(at)
            index = mine if want_mine else 1 - mine
            keep = pick_of(keep, index, place)
            got = None if got is None else pick_of(got, index, place)
        if got is None:
            return keep
        return keep.astype(jnp.float32) + got.astype(jnp.float32)

    def step(self):
        at = self.order.pop(0)
        kind = self.keep.dtype
        place = self.held.index(at)
        send = self.part(at, False).astype(kind)
        if self.got is None:
            self.last = (at, place)
        else:
            self.keep = self.part(at, True).astype(kind)
            self.last = None
        self.got = self.cube.swap(send, at)
        self.held.remove(at)

    def result(self):
        return self.part(None, True)


class Scattering:
    def __init__(self, cube, left, right, rows):
        self.cube = cube
        if not cube.tuned:
            self.parts = []
            self.whole = jnp.concatenate([left, right], axis=1)
            return
        bits = (2,) * len(cube.bits)
        self.parts = [
            Summing(cube, left.reshape(bits + (rows, -1)), (C, Y, X, Z0, Z1)),
            Summing(cube, right.reshape(bits + (rows, -1)), (C, X, Y, Z0, Z1)),
        ]

    @property
    def state(self):
        if not self.cube.tuned:
            return [self.whole]
        return [self.parts[0].state, self.parts[1].state]

    @state.setter
    def state(self, values):
        if not self.cube.tuned:
            self.whole = values[0]
        else:
            self.parts[0].state, self.parts[1].state = values

    def step(self, count=1):
        if self.cube.tuned:
            for _ in range(count):
                for part in self.parts:
                    part.step()

    def result(self):
        if not self.cube.tuned:
            return lax.psum_scatter(self.whole, AXES, scatter_dimension=0, tiled=True).astype(
                jnp.float32
            )
        return jnp.concatenate([part.result() for part in self.parts], axis=1)


class HeadScattering:
    def __init__(self, cube, values, rows):
        self.cube = cube
        if not cube.tuned:
            self.whole = values
            return
        half = values.shape[1] // 2
        self.parts = [
            Summing(cube, values[:, :half].reshape(2, 2, 2, rows, half), (X, Z0, Z1)),
            Summing(cube, values[:, half:].reshape(2, 2, 2, rows, half), (Z0, Z1, X)),
        ]

    state = Scattering.state
    step = Scattering.step

    def result(self):
        if not self.cube.tuned:
            return lax.psum_scatter(self.whole, "dp", scatter_dimension=0, tiled=True).astype(
                jnp.float32
            )
        return jnp.concatenate([part.result() for part in self.parts], axis=1)


def fence(flows, *values):
    states, values = lax.optimization_barrier(([flow.state for flow in flows], values))
    for flow, state in zip(flows, states):
        flow.state = state
    return values[0] if len(values) == 1 else values


def rows_of(values, count):
    return values.reshape(count, values.shape[-1])


def shards(
    sizes,
    frames,
    ffn_inner,
    ffn_outer,
    attn_qkv,
    attn_proj,
    conv_expand,
    conv_depth,
    conv_proj,
    norm_gains,
    head_proj,
    lengths,
    mask_starts,
    target_codes,
    out_grad,
):
    cube = Cube(sizes)
    devices = sizes["dp"] * sizes["head"]
    ff = ffn_inner.shape[2]
    all_bits = list(range(len(cube.bits)))

    mid = jnp.concatenate([attn_proj, conv_expand, conv_proj], axis=1)
    pieces = [
        Gathering(cube, shard)
        for shard in (
            ffn_inner[0],
            ffn_outer[0],
            attn_qkv,
            mid,
            ffn_inner[1],
            ffn_outer[1],
        )
    ]
    head_half = head_proj.shape[1] // 2
    heads = [
        HeadGathering(cube, head_proj[:, :head_half]),
        HeadGathering(cube, head_proj[:, head_half:]),
    ]

    row_total = UTT_DEV * SEQ
    positions = jnp.arange(SEQ, dtype=jnp.int32)
    valid_mat = positions[None, :] < lengths[:, None]
    valid_rows = valid_mat.reshape(row_total).astype(jnp.float32)
    frequency = 10000.0 ** (-(jnp.arange(HD // 2, dtype=jnp.float32) * 2.0) / HD)
    angles = positions.astype(jnp.float32)[:, None] * frequency[None, :]
    cosine = jnp.cos(angles)[:, None, :]
    sine_table = jnp.sin(angles)[:, None, :]
    score_scale = HD ** (-0.5)

    slots = UTT_DEV * NSPAN * SPAN
    slot_at = (mask_starts[:, :, None] + jnp.arange(SPAN, dtype=jnp.int32)).reshape(UTT_DEV, -1)
    slot_ok = slot_at < lengths[:, None]
    chosen = (slot_at + SEQ * jnp.arange(UTT_DEV, dtype=jnp.int32)[:, None]).reshape(slots)
    slot_live = slot_ok.reshape(slots)
    pick = (
        (chosen[:, None] == jnp.arange(row_total, dtype=jnp.int32)[None, :]) & slot_live[:, None]
    )
    picked_codes = jnp.sum(jnp.where(pick, target_codes[None, :], 0), axis=1)
    picked_codes = jnp.where(slot_live, picked_codes, -1)
    pick_lo = pick.astype(jnp.bfloat16)
    head_order = [at for at in range(len(cube.bits)) if cube.bits[at][0] == "head"]
    group = sizes["head"]
    vocab_cols = head_proj.shape[1]

    vectors = cube.gather(jnp.concatenate([norm_gains, conv_depth], axis=0), all_bits)
    vectors = jnp.moveaxis(vectors.reshape((devices,) + vectors.shape[-2:]), 0, 1).reshape(-1, D)
    group_codes = cube.gather(picked_codes, head_order).reshape(group * slots)
    pieces[0].step("z")
    heads[0].step("x")
    heads[1].step("x")
    vectors, group_codes = fence([pieces[0], *heads], vectors, group_codes)
    gain_f, depth_f = vectors[:6].astype(jnp.float32), vectors[6:].astype(jnp.float32)
    group_live = (group_codes >= 0).astype(jnp.float32)
    local_codes = group_codes - lax.axis_index("head") * vocab_cols


    pieces[0].step("m")
    pieces[1].step("z")
    inputs = frames.astype(jnp.float32)
    norm_first = lowered(layer_norm(inputs, gain_f[0]))
    norm_first = fence(pieces[:2], norm_first)

    pieces[0].step("n")
    pieces[1].step("m")
    pieces[2].step("z")
    norm_first = fence(pieces[:3], norm_first)

    pieces[0].step("c")
    pieces[1].step("n")
    pieces[2].step("m")
    pieces[3].step("z")
    inner_0 = pieces[0].whole
    pre_first = matmul(norm_first, inner_0)
    act_first = lowered(jax.nn.silu(pre_first))
    pre_first, act_first = fence(pieces[:4], pre_first, act_first)

    pieces[1].step("c")
    pieces[2].step("n")
    pieces[3].step("m")
    pieces[4].step("z")
    outer_0 = pieces[1].whole
    after_first = inputs + 0.5 * matmul(act_first, outer_0)
    norm_attn = lowered(layer_norm(after_first, gain_f[1]))
    after_first, norm_attn = fence(pieces[1:5], after_first, norm_attn)

    pieces[2].step("c")
    pieces[3].step("n")
    pieces[4].step("m")
    pieces[5].step("z")
    heads[0].step("far")
    mix_weight = pieces[2].whole
    mixed = matmul(norm_attn, mix_weight)
    mixed = mixed.reshape(UTT_DEV, SEQ, 3, H, HD)
    queries = lowered(rotate(mixed[:, :, 0], cosine, sine_table))
    key_rows = lowered(rotate(mixed[:, :, 1], cosine, sine_table))
    value_rows = lowered(mixed[:, :, 2])

    def scores_of(query_one, key_one, key_ok):
        scores = (
            jnp.einsum("qhd,khd->hqk", query_one, key_one, preferred_element_type=jnp.float32)
            * score_scale
        )
        return jnp.where(key_ok[None, None, :], scores, -1e30)

    def attend_one(query_one, key_one, value_one, key_ok):
        scores = scores_of(query_one, key_one, key_ok)
        row_top = jnp.max(scores, axis=-1, keepdims=True)
        weights = jnp.exp(scores - row_top)
        totals = jnp.sum(weights, axis=-1, keepdims=True)
        attn_probs = weights / totals
        attended = jnp.einsum(
            "hqk,khd->qhd", lowered(attn_probs), value_one, preferred_element_type=jnp.float32
        )
        return (attended, row_top[..., 0] + jnp.log(totals[..., 0]))

    attended, log_totals = attend_one(queries[0], key_rows[0], value_rows[0], valid_mat[0])
    attended_lo = lowered(attended.reshape(row_total, D))
    attended_lo, queries, key_rows, value_rows, log_totals = fence(
        [*pieces[2:6], heads[0]], attended_lo, queries, key_rows, value_rows, log_totals
    )

    pieces[3].step("c")
    pieces[4].step("n")
    pieces[5].step("m")
    heads[0].step("near")
    heads[1].step("far")
    mid_weight = pieces[3].whole
    proj_weight, conv_weight = mid_weight[:, :D], mid_weight[:, 3 * D :]
    expand_weight = mid_weight[:, D : 3 * D]
    after_attention = after_first + matmul(attended_lo, proj_weight)
    norm_conv = lowered(layer_norm(after_attention, gain_f[2]))
    expanded = matmul(norm_conv, expand_weight)

    def gate_rows(expanded_rows):
        return expanded_rows[:, :D] * jax.nn.sigmoid(expanded_rows[:, D:]) * valid_rows[:, None]

    def conv_rows(gated_rows, tap_weights):
        return depthwise(gated_rows.reshape(UTT_DEV, SEQ, D), tap_weights).reshape(row_total, D)

    gated_rows = gate_rows(expanded)
    conv_out = conv_rows(gated_rows, depth_f)
    weighted = conv_out * valid_rows[:, None]
    sums = cube.total(
        jnp.stack(
            [
                jnp.sum(weighted, axis=0),
                jnp.sum(weighted * conv_out, axis=0),
                jnp.broadcast_to(jnp.sum(valid_rows), (D,)),
            ]
        )
    )
    sums, conv_out, after_attention, expanded, norm_conv = fence(
        [*pieces[3:6], *heads], sums, conv_out, after_attention, expanded, norm_conv
    )

    pieces[4].step("c")
    pieces[5].step("n")
    heads[1].step("near")
    inner_1 = pieces[4].whole
    frame_count = sums[2, 0]
    channel_mean = sums[0] / frame_count
    variance = sums[1] / frame_count - channel_mean * channel_mean
    inverse = lax.rsqrt(variance + eps)
    normalized = (conv_out - channel_mean) * inverse
    normed_bn = normalized * gain_f[3]
    swish_lo = lowered(jax.nn.silu(normed_bn))
    after_conv = after_attention + matmul(swish_lo, conv_weight)
    norm_second = lowered(layer_norm(after_conv, gain_f[4]))
    pre_second = matmul(norm_second, inner_1)
    act_second = lowered(jax.nn.silu(pre_second))
    after_conv, norm_second, pre_second, act_second, swish_lo = fence(
        [*pieces[4:6], *heads], after_conv, norm_second, pre_second, act_second, swish_lo
    )

    pieces[5].step("c")
    outer_1 = pieces[5].whole
    if cube.tuned:
        head_cols = weave_head(heads[0].state + heads[1].state)
    else:
        head_cols = jnp.concatenate(heads[0].state + heads[1].state, axis=1)
    after_second = after_conv + 0.5 * matmul(act_second, outer_1)
    output_lo = lowered(layer_norm(after_second, gain_f[5]))

    picked_rows = lowered(matmul(pick_lo, output_lo))
    group_rows = cube.gather(picked_rows, head_order).reshape(group * slots, D)
    logits = matmul(group_rows, head_cols)
    row_top = jnp.max(logits, axis=1)
    row_sum = jnp.sum(jnp.exp(logits - row_top[:, None]), axis=1)
    onehot = jnp.arange(vocab_cols, dtype=jnp.int32)[None, :] == local_codes[:, None]
    target_logit = jnp.sum(jnp.where(onehot, logits, 0.0), axis=1)
    stats = cube.gather(jnp.stack([row_top, row_sum, target_logit]), head_order)
    stats = stats.reshape(group, 3, group * slots)
    whole_top = jnp.max(stats[:, 0], axis=0)
    whole_sum = jnp.sum(stats[:, 1] * jnp.exp(stats[:, 0] - whole_top), axis=0)
    log_norm = whole_top + jnp.log(whole_sum)
    ce_group = jnp.sum((log_norm - jnp.sum(stats[:, 2], axis=0)) * group_live)
    grad_logits = lowered(
        (jnp.exp(logits - log_norm[:, None]) - onehot.astype(jnp.float32)) * group_live[:, None]
    )
    head_grad = lowered(matmul_tn(group_rows, grad_logits))
    head_flow = HeadScattering(cube, head_grad, head_proj.shape[0])
    row_grads = lowered(matmul_nt(grad_logits, head_cols))
    row_sum = Summing(cube, row_grads.reshape((2,) * len(head_order) + (slots, D)), head_order[::-1])
    head_flow.step()
    for _ in head_order:
        row_sum.step()
    row_grads = lowered(row_sum.result())
    grad_output = out_grad.astype(jnp.float32) + matmul_tn(pick_lo, row_grads)

    def outer_back(grad_in, act_lo):
        grad_out_lo = lowered(0.5 * grad_in)
        half = D // 2
        left = lowered(matmul_tn(act_lo, grad_out_lo[:, :half]))
        right = lowered(matmul_tn(act_lo, grad_out_lo[:, half:]))
        return grad_out_lo, Scattering(cube, left, right, ffn_outer.shape[1])

    def inner_back(grad_out_lo, normed_lo, pre_act, inner_weight, outer_weight):
        grad_pre = lowered(silu_back(pre_act, matmul_nt(grad_out_lo, outer_weight)))
        half = ff // 2
        left = lowered(matmul_tn(normed_lo, grad_pre[:, :half]))
        right = lowered(matmul_tn(normed_lo, grad_pre[:, half:]))
        below = matmul_nt(grad_pre, inner_weight)
        return below, Scattering(cube, left, right, ffn_inner.shape[1])

    grad_second, gain_grad_final = norm_back(after_second, gain_f[5], grad_output)
    grad_out_lo, outer_flow_1 = outer_back(grad_second, act_second)
    grad_second, grad_out_lo = fence([head_flow, outer_flow_1], grad_second, grad_out_lo)

    head_flow.step()
    outer_flow_1.step(2)
    below_second, inner_flow_1 = inner_back(grad_out_lo, norm_second, pre_second, inner_1, outer_1)
    below_second = fence([head_flow, outer_flow_1, inner_flow_1], below_second)

    head_flow.step()
    outer_flow_1.step()
    inner_flow_1.step(2)
    norm_part, gain_grad_second = norm_back(after_conv, gain_f[4], below_second)
    grad_conv_res = grad_second + norm_part
    conv_res_lo = lowered(grad_conv_res)
    grad_bn = silu_back(normed_bn, matmul_nt(conv_res_lo, conv_weight))
    gain_grad_bn = jnp.sum(grad_bn * normalized, axis=0)
    grad_normalized = grad_bn * gain_f[3]
    back_sums = cube.total(
        jnp.stack(
            [
                jnp.sum(grad_normalized, axis=0),
                jnp.sum(grad_normalized * normalized, axis=0),
                jnp.broadcast_to(ce_group / group, (D,)),
            ]
        )
    )
    conv_proj_grad = lowered(matmul_tn(swish_lo, conv_res_lo))
    back_sums, grad_normalized, grad_conv_res, conv_proj_grad = fence(
        [head_flow, outer_flow_1, inner_flow_1],
        back_sums,
        grad_normalized,
        grad_conv_res,
        conv_proj_grad,
    )

    outer_flow_1.step(2)
    inner_flow_1.step()
    sum_plain, sum_scaled = back_sums[0], back_sums[1]
    loss = back_sums[2, 0] / jnp.float32(devices * UTT_DEV * NSPAN * SPAN)
    grad_variance = -0.5 * inverse * inverse * sum_scaled
    grad_mean = -inverse * sum_plain - 2.0 * channel_mean * grad_variance
    grad_conv_out = (
        grad_normalized * inverse
        + (grad_mean + 2.0 * grad_variance * conv_out) * valid_rows[:, None] / frame_count
    )
    grad_gated, depth_grad = jax.vjp(conv_rows, gated_rows, depth_f)[1](grad_conv_out)
    grad_expanded = lowered(jax.vjp(gate_rows, expanded)[1](grad_gated)[0])
    expand_grad = lowered(matmul_tn(norm_conv, grad_expanded))
    norm_part, gain_grad_conv = norm_back(
        after_attention, gain_f[2], matmul_nt(grad_expanded, expand_weight)
    )
    grad_attn_res = grad_conv_res + norm_part
    attn_res_lo = lowered(grad_attn_res)
    proj_grad = lowered(matmul_tn(attended_lo, attn_res_lo))
    mid_flow = Scattering(
        cube,
        jnp.concatenate([proj_grad, expand_grad[:, :D]], axis=1),
        jnp.concatenate([expand_grad[:, D:], conv_proj_grad], axis=1),
        attn_proj.shape[0],
    )
    grad_attn_res, attn_res_lo = fence(
        [outer_flow_1, inner_flow_1, mid_flow], grad_attn_res, attn_res_lo
    )

    inner_flow_1.step(2)
    mid_flow.step(2)
    grad_attended = lowered(matmul_nt(attn_res_lo, proj_weight)).reshape(UTT_DEV, SEQ, H, HD)

    def attend_back(query_one, key_one, value_one, key_ok, log_total, grad_one):
        attn_probs = jnp.exp(scores_of(query_one, key_one, key_ok) - log_total[:, :, None])
        grad_value = jnp.einsum(
            "hqk,qhd->khd", lowered(attn_probs), grad_one, preferred_element_type=jnp.float32
        )
        grad_probs = jnp.einsum(
            "qhd,khd->hqk", grad_one, value_one, preferred_element_type=jnp.float32
        )
        grad_scores = lowered(
            attn_probs * (grad_probs - jnp.sum(attn_probs * grad_probs, axis=-1, keepdims=True))
        )
        grad_query = (
            jnp.einsum("hqk,khd->qhd", grad_scores, key_one, preferred_element_type=jnp.float32)
            * score_scale
        )
        grad_key = (
            jnp.einsum("hqk,qhd->khd", grad_scores, query_one, preferred_element_type=jnp.float32)
            * score_scale
        )
        return (grad_query, grad_key, grad_value)

    grad_query, grad_key, grad_value = attend_back(
        queries[0], key_rows[0], value_rows[0], valid_mat[0], log_totals, grad_attended[0]
    )
    grad_mixed = jnp.concatenate(
        [
            lowered(rotate_back(grad_query, cosine[:, :, :], sine_table)).reshape(row_total, D),
            lowered(rotate_back(grad_key, cosine, sine_table)).reshape(row_total, D),
            lowered(grad_value).reshape(row_total, D),
        ],
        axis=1,
    )
    grad_mixed = fence([inner_flow_1, mid_flow], grad_mixed)

    mid_flow.step()
    mix_half = 3 * D // 2
    mix_flow = Scattering(
        cube,
        lowered(matmul_tn(norm_attn, grad_mixed[:, :mix_half])),
        lowered(matmul_tn(norm_attn, grad_mixed[:, mix_half:])),
        attn_qkv.shape[0],
    )
    norm_part, gain_grad_attn = norm_back(after_first, gain_f[1], matmul_nt(grad_mixed, mix_weight))
    grad_first_res = grad_attn_res + norm_part
    grad_out_lo, outer_flow_0 = outer_back(grad_first_res, act_first)
    grad_first_res, grad_out_lo = fence(
        [mid_flow, mix_flow, outer_flow_0], grad_first_res, grad_out_lo
    )

    mid_flow.step(2)
    mix_flow.step(2)
    outer_flow_0.step(2)
    below_first, inner_flow_0 = inner_back(grad_out_lo, norm_first, pre_first, inner_0, outer_0)
    norm_part, gain_grad_first = norm_back(inputs, gain_f[0], below_first)
    input_grad = grad_first_res + norm_part
    vector_grad = jnp.concatenate(
        [
            jnp.stack(
                [
                    gain_grad_first,
                    gain_grad_attn,
                    gain_grad_conv,
                    gain_grad_bn,
                    gain_grad_second,
                    gain_grad_final,
                ],
                axis=0,
            ),
            depth_grad,
        ],
        axis=0,
    )
    vector_grad = jnp.moveaxis(vector_grad.reshape(vector_grad.shape[0], devices, -1), 1, 0)
    vector_flow = Summing(
        cube, vector_grad.reshape((2,) * len(cube.bits) + vector_grad.shape[1:]), all_bits[::-1]
    )
    input_grad = fence([mid_flow, mix_flow, outer_flow_0, inner_flow_0, vector_flow], input_grad)

    mix_flow.step()
    outer_flow_0.step()
    inner_flow_0.step(2)
    for _ in all_bits:
        vector_flow.step()
    fence([mix_flow, outer_flow_0, inner_flow_0, vector_flow], loss)

    mix_flow.step(2)
    outer_flow_0.step(2)
    inner_flow_0.step()
    fence([mix_flow, outer_flow_0, inner_flow_0], loss)

    inner_flow_0.step(2)
    mid_grad = mid_flow.result()
    vector_grad = vector_flow.result()
    return (
        output_lo,
        loss,
        input_grad,
        jnp.stack([inner_flow_0.result(), inner_flow_1.result()], axis=0),
        jnp.stack([outer_flow_0.result(), outer_flow_1.result()], axis=0),
        mix_flow.result(),
        mid_grad[:, :D],
        mid_grad[:, D : 3 * D],
        vector_grad[6:],
        mid_grad[:, 3 * D :],
        vector_grad[:6],
        head_flow.result(),
    )


def solution(mesh):
    placed = (
        P(("dp", "head"), None),
        P(None, ("dp", "head"), None),
        P(None, ("dp", "head"), None),
        P(("dp", "head"), None),
        P(("dp", "head"), None),
        P(("dp", "head"), None),
        P(None, ("dp", "head")),
        P(("dp", "head"), None),
        P(None, ("dp", "head")),
        P("dp", "head"),
        P(("dp", "head")),
        P(("dp", "head"), None),
        P(("dp", "head")),
        P(("dp", "head"), None),
    )
    sizes = {axis: mesh.shape[axis] for axis in AXES}
    return jax.shard_map(
        functools.partial(shards, sizes),
        mesh=mesh,
        in_specs=placed,
        out_specs=(
            P(("dp", "head"), None),
            P(),
            P(("dp", "head"), None),
            P(None, ("dp", "head"), None),
            P(None, ("dp", "head"), None),
            P(("dp", "head"), None),
            P(("dp", "head"), None),
            P(("dp", "head"), None),
            P(None, ("dp", "head")),
            P(("dp", "head"), None),
            P(None, ("dp", "head")),
            P("dp", "head"),
        ),
        check_vma=False,
    )
```

```python
import functools
import math

import jax
import jax.numpy as jnp
from jax import lax
from jax.experimental import pallas as pl
from jax.experimental.pallas import tpu as pltpu
from jax.sharding import PartitionSpec as P

D = 1024
H = 8
HD = 128
VOCAB = 8192
SEQ = 512
SPAN = 10
NSPAN = 20
UTT_DEV = 1


eps = 1e-05


def layer_norm(values, gain_row):
    center = values - jnp.mean(values, axis=-1, keepdims=True)
    variance = jnp.mean(center * center, axis=-1, keepdims=True)
    return center * lax.rsqrt(variance + eps) * gain_row


def rotate(values, cosine, sine_table):
    half_width = values.shape[-1] // 2
    lead_part = values[..., :half_width]
    tail_part = values[..., half_width:]
    return jnp.concatenate(
        [lead_part * cosine - tail_part * sine_table, tail_part * cosine + lead_part * sine_table],
        axis=-1,
    )


def rotate_back(grads, cosine, sine_table):
    half_width = grads.shape[-1] // 2
    lead_part = grads[..., :half_width]
    tail_part = grads[..., half_width:]
    return jnp.concatenate(
        [lead_part * cosine + tail_part * sine_table, tail_part * cosine - lead_part * sine_table],
        axis=-1,
    )


def lowered(values):
    return values.astype(jnp.bfloat16)


def matmul(operand, weight):
    return jnp.dot(operand, weight, preferred_element_type=jnp.float32)


def matmul_tn(operand, weight):
    return lax.dot_general(
        operand, weight, (((0,), (0,)), ((), ())), preferred_element_type=jnp.float32
    )


def matmul_nt(operand, weight):
    return lax.dot_general(
        operand, weight, (((1,), (1,)), ((), ())), preferred_element_type=jnp.float32
    )


def norm_back(values, gain_row, grads):
    unused, pullback = jax.vjp(layer_norm, values, gain_row)
    return pullback(grads)


def silu_back(values, grads):
    return jax.vjp(jax.nn.silu, values)[1](grads)[0]


AXES = ("dp", "head")
ANY = pl.BlockSpec(memory_space=pl.ANY)
VMEM = pl.BlockSpec(memory_space=pltpu.VMEM)
Z1, Z0, X, Y, C = range(5)


def local_copies(plan, inputs, outputs):
    count = len(inputs)

    def kernel(*refs):
        sources, targets, sem = refs[:count], refs[count:-1], refs[-1]
        dp, head = lax.axis_index("dp"), lax.axis_index("head")
        where = (dp // 4, dp // 2 % 2, dp % 2, head // 2, head % 2)
        copies = []
        for at, (source, target) in enumerate(plan(where, sources, targets)):
            copies.append(pltpu.make_async_copy(source, target, sem.at[at]))
            copies[-1].start()
        for copy in copies:
            copy.wait()

    size = sum(math.prod(shape) for shape in outputs) * inputs[0].dtype.itemsize
    results = pl.pallas_call(
        kernel,
        out_shape=[jax.ShapeDtypeStruct(shape, inputs[0].dtype) for shape in outputs],
        in_specs=[ANY] * count,
        out_specs=[VMEM] * len(outputs),
        scratch_shapes=[pltpu.SemaphoreType.DMA((16,))],
        cost_estimate=pl.CostEstimate(flops=0, bytes_accessed=2 * size, transcendentals=0),
        compiler_params=pltpu.CompilerParams(vmem_limit_bytes=16 << 20),
    )(*inputs)
    return list(results)


def flip(bit, by):
    return (bit + by) % 2


class Cube:
    def __init__(self, sizes):
        self.sizes = sizes
        self.tuned = sizes == {"dp": 8, "head": 4}
        self.bits = []
        for axis in AXES:
            bit = sizes[axis] // 2
            while bit:
                self.bits.append((axis, bit))
                bit //= 2

    def mine(self, at):
        axis, bit = self.bits[at]
        return (lax.axis_index(axis) // bit) % 2

    def swap(self, values, at):
        axis, bit = self.bits[at]
        return lax.ppermute(values, axis, [(i, i ^ bit) for i in range(self.sizes[axis])])

    def gather(self, shard, order):
        held = []
        values = shard
        for at in order:
            place = sum(other < at for other in held)
            values = self.join(values, self.swap(values, at), at, place)
            held.append(at)
        return values

    def join(self, values, got, at, place):
        mine = self.mine(at)
        first = jnp.where(mine == 0, values, got)
        second = jnp.where(mine == 0, got, values)
        return jnp.stack([first, second], axis=place)

    def total(self, values):
        for at in range(len(self.bits)):
            values = values + self.swap(values, at)
        return values


class HeadGathering:
    def __init__(self, cube, shard):
        self.cube = cube
        self.state = [shard]

    def step(self, phase):
        if not self.cube.tuned:
            if phase == "x":
                self.state = [lax.all_gather(self.state[0], "dp", axis=0, tiled=True)]
            return
        if phase == "x":
            (own,) = self.state
            self.state = [own, self.cube.swap(own, X)]
        if phase == "far":
            own, got = self.state

            def plan(where, sources, targets):
                for by in range(2):
                    yield sources[by], targets[0].at[flip(where[X], by)]

            (pair,) = local_copies(plan, self.state, [(2,) + own.shape])
            self.state = [pair, self.cube.swap(pair, Z1)]
        if phase == "near":
            pair, got = self.state

            def plan(where, sources, targets):
                for by in range(2):
                    yield sources[by], targets[0].at[flip(where[Z1], by)]

            (four,) = local_copies(plan, self.state, [(2,) + pair.shape])
            self.state = [four, self.cube.swap(four, Z0)]


def joined_heads(cube, heads):
    if not cube.tuned:
        return jnp.concatenate([part.state[0] for part in heads], axis=1)
    parts = [part for flow in heads for part in flow.state]
    _, _, rows, half = parts[0].shape

    def plan(where, sources, targets):
        for at in range(4):
            columns = pl.ds(at // 2 * half, half)
            yield sources[at], targets[0].at[:, flip(where[Z0], at % 2), :, :, columns]

    (whole,) = local_copies(plan, parts, [(2, 2, 2, rows, 2 * half)])
    return whole.reshape(8 * rows, 2 * half)


class Gathering:
    def __init__(self, cube, shard):
        self.cube = cube
        self.rows, self.columns = shard.shape
        self.state = [shard]

    def step(self, phase):
        cube, state, rows = self.cube, self.state, self.rows
        half = self.columns // 2
        if not cube.tuned:
            if phase == "z":
                self.state = [lax.all_gather(state[0], AXES, axis=0, tiled=True)]
            return
        if phase == "z":
            (own,) = state

            def plan(where, sources, targets):
                for by in range(2):
                    yield sources[by], targets[0].at[flip(where[Z1], by)]

            (pair,) = local_copies(plan, [own, cube.swap(own, Z1)], [(2,) + own.shape])
            self.state = [pair, cube.swap(pair, Z0)]
        if phase == "m":

            def plan(where, sources, targets):
                for by in range(2):
                    for side in range(2):
                        columns = pl.ds(side * half, half)
                        yield (
                            sources[by].at[:, :, columns],
                            targets[side].at[:, flip(where[Z0], by)],
                        )

            left, right = local_copies(plan, state, [(2, 2, rows, half)] * 2)
            self.state = [left, cube.swap(left, X), right, cube.swap(right, Y)]
        if phase == "n":

            def plan(where, sources, targets):
                for by in range(2):
                    yield sources[by], targets[0].at[:, :, flip(where[X], by)]
                    yield sources[2 + by], targets[1].at[:, :, flip(where[Y], by)]

            left, right = local_copies(plan, state, [(2, 2, 2, rows, half)] * 2)
            self.state = [left, cube.swap(left, Y), right, cube.swap(right, X)]
        if phase == "c":

            def plan(where, sources, targets):
                for by in range(2):
                    yield (
                        sources[by],
                        targets[0].at[:, :, :, flip(where[Y], by), :, pl.ds(0, half)],
                    )
                    yield (
                        sources[2 + by],
                        targets[0].at[:, :, flip(where[X], by), :, :, pl.ds(half, half)],
                    )

            (most,) = local_copies(plan, state, [(2, 2, 2, 2, rows, self.columns)])

            def plan_whole(where, sources, targets):
                for by in range(2):
                    yield sources[by], targets[0].at[:, :, :, :, flip(where[C], by)]

            (whole,) = local_copies(
                plan_whole, [most, cube.swap(most, C)], [(2, 2, 2, 2, 2, rows, self.columns)]
            )
            self.state = [whole.reshape(32 * rows, self.columns)]

    @property
    def whole(self):
        return self.state[0]


def pick_of(values, index, place):
    return lax.dynamic_index_in_dim(values, index, place, keepdims=False)


class Summing:
    def __init__(self, cube, values, order):
        self.cube, self.order = cube, list(order)
        self.held = sorted(order)
        self.keep, self.got, self.last = values, None, None

    @property
    def state(self):
        return [part for part in (self.keep, self.got) if part is not None]

    @state.setter
    def state(self, parts):
        self.keep = parts[0]
        if len(parts) > 1:
            self.got = parts[1]

    def part(self, at, want_mine):
        keep, got = self.keep, self.got
        if self.last is not None:
            keep = pick_of(keep, self.cube.mine(self.last[0]), self.last[1])
        if at is not None:
            mine, place = self.cube.mine(at), self.held.index(at)
            index = mine if want_mine else 1 - mine
            keep = pick_of(keep, index, place)
            got = None if got is None else pick_of(got, index, place)
        if got is None:
            return keep
        return keep.astype(jnp.float32) + got.astype(jnp.float32)

    def step(self):
        at = self.order.pop(0)
        kind = self.keep.dtype
        place = self.held.index(at)
        send = self.part(at, False).astype(kind)
        if self.got is None:
            self.last = (at, place)
        else:
            self.keep = self.part(at, True).astype(kind)
            self.last = None
        self.got = self.cube.swap(send, at)
        self.held.remove(at)

    def result(self):
        return self.part(None, True)


class Scattering:
    def __init__(self, cube, values, rows):
        self.cube = cube
        self.phase = 0
        self.state = [values.reshape((2,) * len(cube.bits) + (rows, -1)) if cube.tuned else values]

    def both(self, keep, got, at, place, columns=slice(None)):
        halves = []
        for index in (1 - self.cube.mine(at), self.cube.mine(at)):
            first = pick_of(keep[..., columns], index, place).astype(jnp.float32)
            second = pick_of(got[..., columns], index, place).astype(jnp.float32)
            halves.append((first + second).astype(keep.dtype))
        return halves

    def step(self, count=1):
        cube = self.cube
        for _ in range(count if cube.tuned else 0):
            if self.phase == 0:
                (values,) = self.state
                send = pick_of(values, 1 - cube.mine(C), 4)
                self.state = [values, cube.swap(send, C)]
            if self.phase == 1:
                values, got = self.state
                keep = pick_of(values, cube.mine(C), 4)
                half = keep.shape[-1] // 2
                send_a, keep_a = self.both(keep, got, Y, 3, slice(0, half))
                send_b, keep_b = self.both(keep, got, X, 2, slice(half, None))
                self.state = [keep_a, cube.swap(send_a, Y), keep_b, cube.swap(send_b, X)]
            if self.phase == 2:
                keep_a, got_a, keep_b, got_b = self.state
                send_a, keep_a = self.both(keep_a, got_a, X, 2)
                send_b, keep_b = self.both(keep_b, got_b, Y, 2)
                self.state = [keep_a, cube.swap(send_a, X), keep_b, cube.swap(send_b, Y)]
            if self.phase == 3:
                keep_a, got_a, keep_b, got_b = self.state
                keep = jnp.concatenate([keep_a, keep_b], axis=-1)
                got = jnp.concatenate([got_a, got_b], axis=-1)
                send, keep = self.both(keep, got, Z0, 1)
                self.state = [keep, cube.swap(send, Z0)]
            if self.phase == 4:
                send, keep = self.both(*self.state, Z1, 0)
                self.state = [keep, cube.swap(send, Z1)]
            self.phase += 1

    def result(self):
        if not self.cube.tuned:
            return lax.psum_scatter(self.state[0], AXES, scatter_dimension=0, tiled=True).astype(
                jnp.float32
            )
        keep, got = self.state
        return keep.astype(jnp.float32) + got.astype(jnp.float32)


class HeadScattering:
    def __init__(self, cube, values, rows):
        self.cube = cube
        if not cube.tuned:
            self.whole = values
            return
        half = values.shape[1] // 2
        self.parts = [
            Summing(cube, values[:, :half].reshape(2, 2, 2, rows, half), (X, Z0, Z1)),
            Summing(cube, values[:, half:].reshape(2, 2, 2, rows, half), (Z0, Z1, X)),
        ]

    @property
    def state(self):
        return [part.state for part in self.parts] if self.cube.tuned else [self.whole]

    @state.setter
    def state(self, values):
        if not self.cube.tuned:
            self.whole = values[0]
            return
        for part, state in zip(self.parts, values):
            part.state = state

    def step(self):
        if self.cube.tuned:
            for part in self.parts:
                part.step()

    def result(self):
        if not self.cube.tuned:
            return lax.psum_scatter(self.whole, "dp", scatter_dimension=0, tiled=True).astype(
                jnp.float32
            )
        return jnp.concatenate([part.result() for part in self.parts], axis=1)


def shifted(pad_ref, shift_ref, rows):
    for r in range(8):
        shift_ref[r] = pad_ref[r : r + rows, :]


def conv_forward_kernel(lead_ref, gate_ref, valid_ref, taps_ref, conv_ref, sums_ref, pad, shift):
    length, width = lead_ref.shape
    edge = jnp.zeros((16, width), jnp.float32)
    valid = valid_ref[...]
    pad[0:16, :] = edge
    pad[16 : 16 + length, :] = lead_ref[...] * jax.nn.sigmoid(gate_ref[...]) * valid
    pad[16 + length : 40 + length, :] = jnp.zeros((24, width), jnp.float32)
    shifted(pad, shift, length + 32)
    chunk = 64
    taps = [taps_ref[j : j + 1, :] for j in range(32)]

    def step(at, totals):
        start = pl.multiple_of(at * chunk, chunk)
        total = jnp.zeros((chunk, width), jnp.float32)
        for j in range(32):
            total += shift[j % 8, pl.ds(start + j // 8 * 8, chunk), :] * taps[j]
        conv_ref[pl.ds(start, chunk), :] = total
        weighted = total * valid_ref[pl.ds(start, chunk), :]
        plain, squares = totals
        return (
            plain + jnp.sum(weighted, axis=0, keepdims=True),
            squares + jnp.sum(weighted * total, axis=0, keepdims=True),
        )

    zero = jnp.zeros((1, width), jnp.float32)
    plain, squares = lax.fori_loop(0, length // chunk, step, (zero, zero))
    sums_ref[0:1, :] = plain
    sums_ref[1:2, :] = squares
    sums_ref[2:8, :] = jnp.zeros((6, width), jnp.float32)


def conv_forward(expanded, valid, taps):
    rows = expanded.shape[0]
    width = 128
    count = D // width
    return pl.pallas_call(
        conv_forward_kernel,
        grid=(count,),
        in_specs=[
            pl.BlockSpec((rows, width), lambda i: (0, i)),
            pl.BlockSpec((rows, width), lambda i: (0, i + count)),
            pl.BlockSpec((rows, 1), lambda i: (0, 0)),
            pl.BlockSpec((32, width), lambda i: (0, i)),
        ],
        out_specs=[
            pl.BlockSpec((rows, width), lambda i: (0, i)),
            pl.BlockSpec((8, width), lambda i: (0, i)),
        ],
        out_shape=[
            jax.ShapeDtypeStruct((rows, D), jnp.float32),
            jax.ShapeDtypeStruct((8, D), jnp.float32),
        ],
        scratch_shapes=[
            pltpu.VMEM((rows + 40, width), jnp.float32),
            pltpu.VMEM((8, rows + 32, width), jnp.float32),
        ],
        cost_estimate=pl.CostEstimate(
            flops=80 * rows * D, bytes_accessed=16 * rows * D, transcendentals=rows * D
        ),
        compiler_params=pltpu.CompilerParams(vmem_limit_bytes=16 << 20),
    )(expanded, expanded, valid, taps)


def conv_backward_kernel(
    lead_ref,
    gate_ref,
    valid_ref,
    taps_ref,
    conv_ref,
    grad_ref,
    vectors_ref,
    out_lead_ref,
    out_gate_ref,
    taps_grad_ref,
    pad,
    shift,
    tap_sums,
):
    length, width = lead_ref.shape
    inverse, plain, scaled = vectors_ref[0:1, :], vectors_ref[1:2, :], vectors_ref[2:3, :]
    pad[0:16, :] = jnp.zeros((16, width), jnp.float32)
    pad[16 : 16 + length, :] = (
        grad_ref[...] * inverse + (plain + scaled * conv_ref[...]) * valid_ref[...]
    )
    pad[16 + length : 40 + length, :] = jnp.zeros((24, width), jnp.float32)
    shifted(pad, shift, length + 32)
    tap_sums[...] = jnp.zeros(tap_sums.shape, jnp.float32)
    chunk = 64
    taps = [taps_ref[j : j + 1, :] for j in range(32)]

    def step(at, carry):
        start = pl.multiple_of(at * chunk, chunk)
        here = pl.ds(start, chunk)
        lead, valid = lead_ref[here, :], valid_ref[here, :]
        gate = jax.nn.sigmoid(gate_ref[here, :])
        gated = lead * gate * valid
        total = jnp.zeros((chunk, width), jnp.float32)
        for j in range(32):
            off = 32 - j
            part = shift[off % 8, pl.ds(start + off // 8 * 8, chunk), :]
            total += part * taps[j]
            tap_sums[j] += jnp.sum((part * gated).reshape(chunk // 8, 8, width), axis=0)
        grad = total * valid
        out_lead_ref[here, :] = (grad * gate).astype(jnp.bfloat16)
        out_gate_ref[here, :] = (grad * lead * gate * (1.0 - gate)).astype(jnp.bfloat16)
        return carry

    lax.fori_loop(0, length // chunk, step, 0)
    taps_grad_ref[...] = jnp.sum(tap_sums[...], axis=1)


def conv_backward(expanded, valid, taps, conv_out, grads, vectors):
    rows = expanded.shape[0]
    width = 128
    count = D // width
    block = pl.BlockSpec((rows, width), lambda i: (0, i))
    return pl.pallas_call(
        conv_backward_kernel,
        grid=(count,),
        in_specs=[
            block,
            pl.BlockSpec((rows, width), lambda i: (0, i + count)),
            pl.BlockSpec((rows, 1), lambda i: (0, 0)),
            pl.BlockSpec((32, width), lambda i: (0, i)),
            block,
            block,
            pl.BlockSpec((8, width), lambda i: (0, i)),
        ],
        out_specs=[block, block, pl.BlockSpec((32, width), lambda i: (0, i))],
        out_shape=[
            jax.ShapeDtypeStruct((rows, D), jnp.bfloat16),
            jax.ShapeDtypeStruct((rows, D), jnp.bfloat16),
            jax.ShapeDtypeStruct((32, D), jnp.float32),
        ],
        scratch_shapes=[
            pltpu.VMEM((rows + 40, width), jnp.float32),
            pltpu.VMEM((8, rows + 32, width), jnp.float32),
            pltpu.VMEM((32, 8, width), jnp.float32),
        ],
        cost_estimate=pl.CostEstimate(
            flops=160 * rows * D, bytes_accessed=20 * rows * D, transcendentals=rows * D
        ),
        compiler_params=pltpu.CompilerParams(vmem_limit_bytes=16 << 20),
    )(expanded, expanded, valid, taps, conv_out, grads, vectors)


def fence(flows, *values):
    states, values = lax.optimization_barrier(([flow.state for flow in flows], values))
    for flow, state in zip(flows, states):
        flow.state = state
    return values[0] if len(values) == 1 else values


def rows_of(values, count):
    return values.reshape(count, values.shape[-1])


def shards(
    sizes,
    frames,
    ffn_inner,
    ffn_outer,
    attn_qkv,
    attn_proj,
    conv_expand,
    conv_depth,
    conv_proj,
    norm_gains,
    head_proj,
    lengths,
    mask_starts,
    target_codes,
    out_grad,
):
    cube = Cube(sizes)
    devices = sizes["dp"] * sizes["head"]
    ff = ffn_inner.shape[2]
    all_bits = list(range(len(cube.bits)))

    mid = jnp.concatenate([attn_proj, conv_expand, conv_proj], axis=1)
    pieces = [
        Gathering(cube, shard)
        for shard in (
            ffn_inner[0],
            ffn_outer[0],
            attn_qkv,
            mid,
            ffn_inner[1],
            ffn_outer[1],
        )
    ]
    head_half = head_proj.shape[1] // 2
    heads = [
        HeadGathering(cube, head_proj[:, :head_half]),
        HeadGathering(cube, head_proj[:, head_half:]),
    ]

    row_total = UTT_DEV * SEQ
    positions = jnp.arange(SEQ, dtype=jnp.int32)
    valid_mat = positions[None, :] < lengths[:, None]
    valid_rows = valid_mat.reshape(row_total).astype(jnp.float32)
    frequency = 10000.0 ** (-(jnp.arange(HD // 2, dtype=jnp.float32) * 2.0) / HD)
    angles = positions.astype(jnp.float32)[:, None] * frequency[None, :]
    cosine = jnp.cos(angles)[:, None, :]
    sine_table = jnp.sin(angles)[:, None, :]
    score_scale = HD ** (-0.5)

    slots = UTT_DEV * NSPAN * SPAN
    slot_at = (mask_starts[:, :, None] + jnp.arange(SPAN, dtype=jnp.int32)).reshape(UTT_DEV, -1)
    slot_ok = slot_at < lengths[:, None]
    chosen = (slot_at + SEQ * jnp.arange(UTT_DEV, dtype=jnp.int32)[:, None]).reshape(slots)
    slot_live = slot_ok.reshape(slots)
    pick = (
        (chosen[:, None] == jnp.arange(row_total, dtype=jnp.int32)[None, :]) & slot_live[:, None]
    )
    picked_codes = jnp.sum(jnp.where(pick, target_codes[None, :], 0), axis=1)
    picked_codes = jnp.where(slot_live, picked_codes, -1)
    pick_lo = pick.astype(jnp.bfloat16)
    head_order = [at for at in range(len(cube.bits)) if cube.bits[at][0] == "head"]
    group = sizes["head"]
    vocab_cols = head_proj.shape[1]

    loss_scale = jnp.float32(devices * UTT_DEV * NSPAN * SPAN)
    vectors = cube.gather(jnp.concatenate([norm_gains, conv_depth], axis=0), all_bits)
    vectors = jnp.moveaxis(vectors.reshape((devices,) + vectors.shape[-2:]), 0, 1).reshape(-1, D)
    group_codes = cube.gather(picked_codes, head_order).reshape(group * slots)
    pieces[0].step("z")
    heads[0].step("x")
    heads[1].step("x")
    fence([pieces[0], *heads], loss_scale)
    pieces[0].step("m")
    pieces[1].step("z")
    inputs = frames.astype(jnp.float32)
    fence(pieces[:2], loss_scale)

    pieces[0].step("n")
    pieces[1].step("m")
    pieces[2].step("z")
    vectors, group_codes = fence(pieces[:3], vectors, group_codes)
    gain_f, depth_f = vectors[:6].astype(jnp.float32), vectors[6:].astype(jnp.float32)
    norm_first = lowered(layer_norm(inputs, gain_f[0]))
    group_live = (group_codes >= 0).astype(jnp.float32)
    local_codes = group_codes - lax.axis_index("head") * vocab_cols

    pieces[0].step("c")
    pieces[1].step("n")
    pieces[2].step("m")
    pieces[3].step("z")
    inner_0 = pieces[0].whole
    pre_first = matmul(norm_first, inner_0)
    act_first = lowered(jax.nn.silu(pre_first))
    pre_first, act_first = fence(pieces[:4], pre_first, act_first)

    pieces[1].step("c")
    pieces[2].step("n")
    pieces[3].step("m")
    pieces[4].step("z")
    outer_0 = pieces[1].whole
    after_first = inputs + 0.5 * matmul(act_first, outer_0)
    norm_attn = lowered(layer_norm(after_first, gain_f[1]))
    after_first, norm_attn = fence(pieces[1:5], after_first, norm_attn)

    pieces[2].step("c")
    pieces[3].step("n")
    pieces[4].step("m")
    pieces[5].step("z")
    heads[0].step("far")
    mix_weight = pieces[2].whole
    mixed = matmul(norm_attn, mix_weight)
    mixed = mixed.reshape(UTT_DEV, SEQ, 3, H, HD)
    queries = lowered(rotate(mixed[:, :, 0], cosine, sine_table))
    key_rows = lowered(rotate(mixed[:, :, 1], cosine, sine_table))
    value_rows = lowered(mixed[:, :, 2])

    def scores_of(query_one, key_one, key_ok):
        scores = (
            jnp.einsum("qhd,khd->hqk", query_one, key_one, preferred_element_type=jnp.float32)
            * score_scale
        )
        return jnp.where(key_ok[None, None, :], scores, -1e30)

    def attend_one(query_one, key_one, value_one, key_ok):
        scores = scores_of(query_one, key_one, key_ok)
        row_top = jnp.max(scores, axis=-1, keepdims=True)
        weights = jnp.exp(scores - row_top)
        totals = jnp.sum(weights, axis=-1, keepdims=True)
        attn_probs = weights / totals
        attended = jnp.einsum(
            "hqk,khd->qhd", lowered(attn_probs), value_one, preferred_element_type=jnp.float32
        )
        return (attended, row_top[..., 0] + jnp.log(totals[..., 0]))

    attended, log_totals = attend_one(queries[0], key_rows[0], value_rows[0], valid_mat[0])
    attended_lo = lowered(attended.reshape(row_total, D))
    attended_lo, queries, key_rows, value_rows, log_totals = fence(
        [*pieces[2:6], heads[0]], attended_lo, queries, key_rows, value_rows, log_totals
    )

    pieces[3].step("c")
    pieces[4].step("n")
    pieces[5].step("m")
    heads[0].step("near")
    heads[1].step("far")
    mid_weight = pieces[3].whole
    proj_weight, conv_weight = mid_weight[:, :D], mid_weight[:, 3 * D :]
    expand_weight = mid_weight[:, D : 3 * D]
    after_attention = after_first + matmul(attended_lo, proj_weight)
    norm_conv = lowered(layer_norm(after_attention, gain_f[2]))
    expanded = matmul(norm_conv, expand_weight)

    conv_out, conv_sums = conv_forward(expanded, valid_rows[:, None], depth_f)
    valid_total = jnp.broadcast_to(jnp.sum(valid_rows), (1, D))
    sums = cube.total(jnp.concatenate([conv_sums[:2], valid_total], axis=0))
    sums, conv_out, after_attention, expanded, norm_conv = fence(
        [*pieces[3:6], *heads], sums, conv_out, after_attention, expanded, norm_conv
    )

    pieces[4].step("c")
    pieces[5].step("n")
    heads[1].step("near")
    inner_1 = pieces[4].whole
    frame_count = sums[2, 0]
    channel_mean = sums[0] / frame_count
    variance = sums[1] / frame_count - channel_mean * channel_mean
    inverse = lax.rsqrt(variance + eps)
    normalized = (conv_out - channel_mean) * inverse
    normed_bn = normalized * gain_f[3]
    swish_lo = lowered(jax.nn.silu(normed_bn))
    after_conv = after_attention + matmul(swish_lo, conv_weight)
    norm_second = lowered(layer_norm(after_conv, gain_f[4]))
    pre_second = matmul(norm_second, inner_1)
    act_second = lowered(jax.nn.silu(pre_second))
    after_conv, norm_second, pre_second, act_second, swish_lo = fence(
        [*pieces[4:6], *heads], after_conv, norm_second, pre_second, act_second, swish_lo
    )

    pieces[5].step("c")
    outer_1 = pieces[5].whole
    head_cols = joined_heads(cube, heads)
    after_second = after_conv + 0.5 * matmul(act_second, outer_1)
    output_lo = lowered(layer_norm(after_second, gain_f[5]))

    picked_rows = lowered(matmul(pick_lo, output_lo))
    group_rows = cube.gather(picked_rows, head_order).reshape(group * slots, D)
    logits = matmul(group_rows, head_cols)
    row_top = jnp.max(logits, axis=1)
    row_sum = jnp.sum(jnp.exp(logits - row_top[:, None]), axis=1)
    onehot = jnp.arange(vocab_cols, dtype=jnp.int32)[None, :] == local_codes[:, None]
    target_logit = jnp.sum(jnp.where(onehot, logits, 0.0), axis=1)
    stats = cube.gather(jnp.stack([row_top, row_sum, target_logit]), head_order)
    stats = stats.reshape(group, 3, group * slots)
    whole_top = jnp.max(stats[:, 0], axis=0)
    whole_sum = jnp.sum(stats[:, 1] * jnp.exp(stats[:, 0] - whole_top), axis=0)
    log_norm = whole_top + jnp.log(whole_sum)
    ce_group = jnp.sum((log_norm - jnp.sum(stats[:, 2], axis=0)) * group_live)
    grad_logits = lowered(
        (jnp.exp(logits - log_norm[:, None]) - onehot.astype(jnp.float32)) * group_live[:, None]
    )
    head_grad = lowered(matmul_tn(group_rows, grad_logits))
    head_flow = HeadScattering(cube, head_grad, head_proj.shape[0])
    row_grads = lowered(matmul_nt(grad_logits, head_cols))
    row_sum = Summing(cube, row_grads.reshape((2,) * len(head_order) + (slots, D)), head_order[::-1])
    head_flow.step()
    for _ in head_order:
        row_sum.step()
    row_grads = lowered(row_sum.result())
    grad_output = out_grad.astype(jnp.float32) + matmul_tn(pick_lo, row_grads)

    def outer_back(grad_in, act_lo):
        grad_out_lo = lowered(0.5 * grad_in)
        weight_grad = lowered(matmul_tn(act_lo, grad_out_lo))
        return grad_out_lo, Scattering(cube, weight_grad, ffn_outer.shape[1])

    def inner_back(grad_out_lo, normed_lo, pre_act, inner_weight, outer_weight):
        grad_pre = lowered(silu_back(pre_act, matmul_nt(grad_out_lo, outer_weight)))
        weight_grad = lowered(matmul_tn(normed_lo, grad_pre))
        below = matmul_nt(grad_pre, inner_weight)
        return below, Scattering(cube, weight_grad, ffn_inner.shape[1])

    grad_second, gain_grad_final = norm_back(after_second, gain_f[5], grad_output)
    grad_out_lo, outer_flow_1 = outer_back(grad_second, act_second)
    grad_second, grad_out_lo = fence([head_flow, outer_flow_1], grad_second, grad_out_lo)

    head_flow.step()
    outer_flow_1.step(2)
    below_second, inner_flow_1 = inner_back(grad_out_lo, norm_second, pre_second, inner_1, outer_1)
    below_second = fence([head_flow, outer_flow_1, inner_flow_1], below_second)

    head_flow.step()
    outer_flow_1.step()
    inner_flow_1.step(2)
    norm_part, gain_grad_second = norm_back(after_conv, gain_f[4], below_second)
    grad_conv_res = grad_second + norm_part
    conv_res_lo = lowered(grad_conv_res)
    grad_bn = silu_back(normed_bn, matmul_nt(conv_res_lo, conv_weight))
    gain_grad_bn = jnp.sum(grad_bn * normalized, axis=0)
    grad_normalized = grad_bn * gain_f[3]
    back_sums = cube.total(
        jnp.stack(
            [
                jnp.sum(grad_normalized, axis=0),
                jnp.sum(grad_normalized * normalized, axis=0),
                jnp.broadcast_to(ce_group / group, (D,)),
            ]
        )
    )
    conv_proj_grad = lowered(matmul_tn(swish_lo, conv_res_lo))
    back_sums, grad_normalized, grad_conv_res, conv_proj_grad = fence(
        [head_flow, outer_flow_1, inner_flow_1],
        back_sums,
        grad_normalized,
        grad_conv_res,
        conv_proj_grad,
    )

    outer_flow_1.step(2)
    inner_flow_1.step()
    sum_plain, sum_scaled = back_sums[0], back_sums[1]
    loss = back_sums[2, 0] / loss_scale
    grad_variance = -0.5 * inverse * inverse * sum_scaled
    grad_mean = -inverse * sum_plain - 2.0 * channel_mean * grad_variance
    back_vectors = jnp.stack(
        [inverse, grad_mean / frame_count, 2.0 * grad_variance / frame_count]
        + [jnp.zeros_like(inverse)] * 5
    )
    grad_lead, grad_gate, depth_grad = conv_backward(
        expanded, valid_rows[:, None], depth_f, conv_out, grad_normalized, back_vectors
    )
    grad_expanded = jnp.concatenate([grad_lead, grad_gate], axis=1)
    norm_part, gain_grad_conv = norm_back(
        after_attention, gain_f[2], matmul_nt(grad_expanded, expand_weight)
    )
    grad_attn_res = grad_conv_res + norm_part
    attn_res_lo = lowered(grad_attn_res)
    mid_flow = Scattering(
        cube,
        jnp.concatenate(
            [
                lowered(matmul_tn(attended_lo, attn_res_lo)),
                lowered(matmul_tn(norm_conv, grad_expanded)),
                conv_proj_grad,
            ],
            axis=1,
        ),
        attn_proj.shape[0],
    )
    grad_attn_res, attn_res_lo = fence(
        [outer_flow_1, inner_flow_1, mid_flow], grad_attn_res, attn_res_lo
    )

    inner_flow_1.step(2)
    mid_flow.step(2)
    grad_attended = lowered(matmul_nt(attn_res_lo, proj_weight)).reshape(UTT_DEV, SEQ, H, HD)

    def attend_back(query_one, key_one, value_one, key_ok, log_total, grad_one):
        attn_probs = jnp.exp(scores_of(query_one, key_one, key_ok) - log_total[:, :, None])
        grad_value = jnp.einsum(
            "hqk,qhd->khd", lowered(attn_probs), grad_one, preferred_element_type=jnp.float32
        )
        grad_probs = jnp.einsum(
            "qhd,khd->hqk", grad_one, value_one, preferred_element_type=jnp.float32
        )
        grad_scores = lowered(
            attn_probs * (grad_probs - jnp.sum(attn_probs * grad_probs, axis=-1, keepdims=True))
        )
        grad_query = (
            jnp.einsum("hqk,khd->qhd", grad_scores, key_one, preferred_element_type=jnp.float32)
            * score_scale
        )
        grad_key = (
            jnp.einsum("hqk,qhd->khd", grad_scores, query_one, preferred_element_type=jnp.float32)
            * score_scale
        )
        return (grad_query, grad_key, grad_value)

    grad_query, grad_key, grad_value = attend_back(
        queries[0], key_rows[0], value_rows[0], valid_mat[0], log_totals, grad_attended[0]
    )
    grad_mixed = jnp.concatenate(
        [
            lowered(rotate_back(grad_query, cosine[:, :, :], sine_table)).reshape(row_total, D),
            lowered(rotate_back(grad_key, cosine, sine_table)).reshape(row_total, D),
            lowered(grad_value).reshape(row_total, D),
        ],
        axis=1,
    )
    grad_mixed = fence([inner_flow_1, mid_flow], grad_mixed)

    mid_flow.step()
    mix_flow = Scattering(cube, lowered(matmul_tn(norm_attn, grad_mixed)), attn_qkv.shape[0])
    norm_part, gain_grad_attn = norm_back(after_first, gain_f[1], matmul_nt(grad_mixed, mix_weight))
    grad_first_res = grad_attn_res + norm_part
    grad_out_lo, outer_flow_0 = outer_back(grad_first_res, act_first)
    grad_first_res, grad_out_lo = fence(
        [mid_flow, mix_flow, outer_flow_0], grad_first_res, grad_out_lo
    )

    mid_flow.step(2)
    mix_flow.step(2)
    outer_flow_0.step(2)
    below_first, inner_flow_0 = inner_back(grad_out_lo, norm_first, pre_first, inner_0, outer_0)
    norm_part, gain_grad_first = norm_back(inputs, gain_f[0], below_first)
    input_grad = grad_first_res + norm_part
    vector_grad = jnp.concatenate(
        [
            jnp.stack(
                [
                    gain_grad_first,
                    gain_grad_attn,
                    gain_grad_conv,
                    gain_grad_bn,
                    gain_grad_second,
                    gain_grad_final,
                ],
                axis=0,
            ),
            depth_grad,
        ],
        axis=0,
    )
    vector_grad = jnp.moveaxis(vector_grad.reshape(vector_grad.shape[0], devices, -1), 1, 0)
    vector_flow = Summing(
        cube, vector_grad.reshape((2,) * len(cube.bits) + vector_grad.shape[1:]), all_bits[::-1]
    )
    input_grad = fence([mid_flow, mix_flow, outer_flow_0, inner_flow_0, vector_flow], input_grad)

    mix_flow.step()
    outer_flow_0.step()
    inner_flow_0.step(2)
    for _ in all_bits:
        vector_flow.step()
    fence([mix_flow, outer_flow_0, inner_flow_0, vector_flow], loss)

    mix_flow.step(2)
    outer_flow_0.step(2)
    inner_flow_0.step()
    fence([mix_flow, outer_flow_0, inner_flow_0], loss)

    inner_flow_0.step(2)
    mid_grad = mid_flow.result()
    vector_grad = vector_flow.result()
    return (
        output_lo,
        loss,
        input_grad,
        jnp.stack([inner_flow_0.result(), inner_flow_1.result()], axis=0),
        jnp.stack([outer_flow_0.result(), outer_flow_1.result()], axis=0),
        mix_flow.result(),
        mid_grad[:, :D],
        mid_grad[:, D : 3 * D],
        vector_grad[6:],
        mid_grad[:, 3 * D :],
        vector_grad[:6],
        head_flow.result(),
    )


def solution(mesh):
    placed = (
        P(("dp", "head"), None),
        P(None, ("dp", "head"), None),
        P(None, ("dp", "head"), None),
        P(("dp", "head"), None),
        P(("dp", "head"), None),
        P(("dp", "head"), None),
        P(None, ("dp", "head")),
        P(("dp", "head"), None),
        P(None, ("dp", "head")),
        P("dp", "head"),
        P(("dp", "head")),
        P(("dp", "head"), None),
        P(("dp", "head")),
        P(("dp", "head"), None),
    )
    sizes = {axis: mesh.shape[axis] for axis in AXES}
    return jax.shard_map(
        functools.partial(shards, sizes),
        mesh=mesh,
        in_specs=placed,
        out_specs=(
            P(("dp", "head"), None),
            P(),
            P(("dp", "head"), None),
            P(None, ("dp", "head"), None),
            P(None, ("dp", "head"), None),
            P(("dp", "head"), None),
            P(("dp", "head"), None),
            P(("dp", "head"), None),
            P(None, ("dp", "head")),
            P(("dp", "head"), None),
            P(None, ("dp", "head")),
            P("dp", "head"),
        ),
        check_vma=False,
    )
```

```python
import functools
import math

import jax
import jax.numpy as jnp
from jax import lax
from jax.experimental import pallas as pl
from jax.experimental.pallas import tpu as pltpu
from jax.sharding import PartitionSpec as P

D = 1024
H = 8
HD = 128
VOCAB = 8192
SEQ = 512
SPAN = 10
NSPAN = 20
UTT_DEV = 1


eps = 1e-05


def layer_norm(values, gain_row):
    center = values - jnp.mean(values, axis=-1, keepdims=True)
    variance = jnp.mean(center * center, axis=-1, keepdims=True)
    return center * lax.rsqrt(variance + eps) * gain_row


def rotate(values, cosine, sine_table):
    half_width = values.shape[-1] // 2
    lead_part = values[..., :half_width]
    tail_part = values[..., half_width:]
    return jnp.concatenate(
        [lead_part * cosine - tail_part * sine_table, tail_part * cosine + lead_part * sine_table],
        axis=-1,
    )


def rotate_back(grads, cosine, sine_table):
    half_width = grads.shape[-1] // 2
    lead_part = grads[..., :half_width]
    tail_part = grads[..., half_width:]
    return jnp.concatenate(
        [lead_part * cosine + tail_part * sine_table, tail_part * cosine - lead_part * sine_table],
        axis=-1,
    )


def lowered(values):
    return values.astype(jnp.bfloat16)


def matmul(operand, weight):
    return jnp.dot(operand, weight, preferred_element_type=jnp.float32)


def matmul_tn(operand, weight):
    return lax.dot_general(
        operand, weight, (((0,), (0,)), ((), ())), preferred_element_type=jnp.float32
    )


def matmul_nt(operand, weight):
    return lax.dot_general(
        operand, weight, (((1,), (1,)), ((), ())), preferred_element_type=jnp.float32
    )


def norm_back(values, gain_row, grads):
    unused, pullback = jax.vjp(layer_norm, values, gain_row)
    return pullback(grads)


def silu_back(values, grads):
    return jax.vjp(jax.nn.silu, values)[1](grads)[0]


AXES = ("dp", "head")
ANY = pl.BlockSpec(memory_space=pl.ANY)
VMEM = pl.BlockSpec(memory_space=pltpu.VMEM)
Z1, Z0, X, Y, C = range(5)


def local_copies(plan, inputs, outputs, after=()):
    count = len(inputs)

    def kernel(*refs):
        sources, targets, sem = refs[:count], refs[count + len(after) : -1], refs[-1]
        dp, head = lax.axis_index("dp"), lax.axis_index("head")
        where = (dp // 4, dp // 2 % 2, dp % 2, head // 2, head % 2)
        copies = []
        for at, (source, target) in enumerate(plan(where, sources, targets)):
            copies.append(pltpu.make_async_copy(source, target, sem.at[at]))
            copies[-1].start()
        for copy in copies:
            copy.wait()

    size = sum(math.prod(shape) for shape in outputs) * inputs[0].dtype.itemsize
    results = pl.pallas_call(
        kernel,
        out_shape=[jax.ShapeDtypeStruct(shape, inputs[0].dtype) for shape in outputs],
        in_specs=[ANY] * (count + len(after)),
        out_specs=[VMEM] * len(outputs),
        scratch_shapes=[pltpu.SemaphoreType.DMA((16,))],
        cost_estimate=pl.CostEstimate(flops=0, bytes_accessed=2 * size, transcendentals=0),
        compiler_params=pltpu.CompilerParams(vmem_limit_bytes=size + (1 << 20)),
    )(*inputs, *after)
    return list(results)


def flip(bit, by):
    return (bit + by) % 2


class Cube:
    def __init__(self, sizes):
        self.sizes = sizes
        self.tuned = sizes == {"dp": 8, "head": 4}
        self.bits = []
        for axis in AXES:
            bit = sizes[axis] // 2
            while bit:
                self.bits.append((axis, bit))
                bit //= 2

    def mine(self, at):
        axis, bit = self.bits[at]
        return (lax.axis_index(axis) // bit) % 2

    def swap(self, values, at):
        axis, bit = self.bits[at]
        return lax.ppermute(values, axis, [(i, i ^ bit) for i in range(self.sizes[axis])])

    def gather(self, shard, order):
        held = []
        values = shard
        for at in order:
            place = sum(other < at for other in held)
            values = self.join(values, self.swap(values, at), at, place)
            held.append(at)
        return values

    def join(self, values, got, at, place):
        mine = self.mine(at)
        first = jnp.where(mine == 0, values, got)
        second = jnp.where(mine == 0, got, values)
        return jnp.stack([first, second], axis=place)

    def total(self, values):
        for at in range(len(self.bits)):
            values = values + self.swap(values, at)
        return values


class VectorGathering:
    def __init__(self, cube, shard, order):
        self.cube, self.order, self.held = cube, list(order), []
        self.state = [shard]

    def step(self, count=1):
        for _ in range(min(count, len(self.order))):
            at = self.order.pop(0)
            place = sum(other < at for other in self.held)
            (values,) = self.state
            self.state = [self.cube.join(values, self.cube.swap(values, at), at, place)]
            self.held.append(at)


class HeadGathering:
    def __init__(self, cube, shard):
        self.cube = cube
        self.state = [shard]

    def step(self, phase):
        if not self.cube.tuned:
            if phase == "x":
                self.state = [lax.all_gather(self.state[0], "dp", axis=0, tiled=True)]
            return
        if phase == "x":
            (own,) = self.state
            self.state = [own, self.cube.swap(own, X)]
        if phase == "far":
            own, got = self.state

            def plan(where, sources, targets):
                for by in range(2):
                    yield sources[by], targets[0].at[flip(where[X], by)]

            (pair,) = local_copies(plan, self.state, [(2,) + own.shape])
            self.state = [pair, self.cube.swap(pair, Z1)]
        if phase == "near":
            pair, got = self.state

            def plan(where, sources, targets):
                for by in range(2):
                    yield sources[by], targets[0].at[flip(where[Z1], by)]

            (four,) = local_copies(plan, self.state, [(2,) + pair.shape])
            self.state = [four, self.cube.swap(four, Z0)]


def joined_heads(cube, heads):
    if not cube.tuned:
        return jnp.concatenate([part.state[0] for part in heads], axis=1)
    parts = [part for flow in heads for part in flow.state]
    _, _, rows, half = parts[0].shape

    def plan(where, sources, targets):
        for at in range(4):
            columns = pl.ds(at // 2 * half, half)
            yield sources[at], targets[0].at[:, flip(where[Z0], at % 2), :, :, columns]

    (whole,) = local_copies(plan, parts, [(2, 2, 2, rows, 2 * half)])
    return whole.reshape(8 * rows, 2 * half)


def pick_of(values, index, place):
    return lax.dynamic_index_in_dim(values, index, place, keepdims=False)


class Summing:
    def __init__(self, cube, values, order):
        self.cube, self.order = cube, list(order)
        self.held = sorted(order)
        self.keep, self.got, self.last = values, None, None

    @property
    def state(self):
        return [part for part in (self.keep, self.got) if part is not None]

    @state.setter
    def state(self, parts):
        self.keep = parts[0]
        if len(parts) > 1:
            self.got = parts[1]

    def part(self, at, want_mine):
        keep, got = self.keep, self.got
        if self.last is not None:
            keep = pick_of(keep, self.cube.mine(self.last[0]), self.last[1])
        if at is not None:
            mine, place = self.cube.mine(at), self.held.index(at)
            index = mine if want_mine else 1 - mine
            keep = pick_of(keep, index, place)
            got = None if got is None else pick_of(got, index, place)
        if got is None:
            return keep
        return keep.astype(jnp.float32) + got.astype(jnp.float32)

    def step(self):
        at = self.order.pop(0)
        kind = self.keep.dtype
        place = self.held.index(at)
        send = self.part(at, False).astype(kind)
        if self.got is None:
            self.last = (at, place)
        else:
            self.keep = self.part(at, True).astype(kind)
            self.last = None
        self.got = self.cube.swap(send, at)
        self.held.remove(at)

    def result(self):
        return self.part(None, True)


class Gather:
    def __init__(self, cube, pieces):
        self.cube = cube
        self.pieces = pieces
        self.wholes = [None] * len(pieces)
        if cube.tuned:
            self.shards = [uniform_shard(kind, arrays) for kind, arrays in pieces]
        self.state = {}

    def stage(self, t):
        cube, old, new = self.cube, self.state, {}
        count = len(self.pieces)
        live = lambda at: 0 <= at < count
        if not cube.tuned:
            if live(t - 1):
                self.wholes[t - 1] = [
                    lax.all_gather(array, AXES, axis=0, tiled=True)
                    for array in self.pieces[t - 1][1]
                ]
            return
        half = COLUMNS // 2
        slots = 2 * live(t) + live(t + 1)
        old_slots = 2 * live(t - 1) + live(t)
        inputs, shapes, jobs = [], [], []

        def give(name):
            inputs.append(old[name])
            return len(inputs) - 1

        def make(shape):
            shapes.append(shape)
            return len(shapes) - 1

        pair = None
        if live(t + 2):
            parts, pair = (give("z1s"), give("z1g")), make((2, ROWS, COLUMNS))
            jobs.append(lambda w, s, o, parts=parts, pair=pair: [
                (s[parts[by]], o[pair].at[flip(w[Z1], by)]) for by in range(2)
            ])
        if slots:
            x_out, y_out = (make((2, 2, slots, ROWS, half)) for _ in range(2))
        if live(t):
            xs, xg, ys, yg = (give(name) for name in ("xs", "xg", "ys", "yg"))
            jobs.append(lambda w, s, o: [
                pair_of
                for by in range(2)
                for pair_of in (
                    (s[(xs, xg)[by]].at[:, :, old_slots - 1], o[y_out].at[:, :, flip(w[X], by)]),
                    (s[(ys, yg)[by]].at[:, :, old_slots - 1], o[x_out].at[:, :, flip(w[Y], by)]),
                )
            ])
        if live(t + 1):
            zs, zg = give("z0s"), give("z0g")
            jobs.append(lambda w, s, o: [
                (
                    s[(zs, zg)[by]].at[:, :, pl.ds(side * half, half)],
                    o[(x_out, y_out)[side]].at[:, flip(w[Z0], by), slots - 1],
                )
                for by in range(2)
                for side in range(2)
            ])
        if jobs:
            made = local_copies(
                lambda w, s, o: [each for job in jobs for each in job(w, s, o)], inputs, shapes
            )
            if slots:
                new["xs"], new["ys"] = made[x_out], made[y_out]
                new["xg"], new["yg"] = cube.swap(made[x_out], X), cube.swap(made[y_out], Y)
            if pair is not None:
                new["z0s"], new["z0g"] = made[pair], cube.swap(made[pair], Z0)
        if live(t + 3):
            new["z1s"] = self.shards[t + 3]
            new["z1g"] = cube.swap(self.shards[t + 3], Z1)
        if live(t - 1):

            def plan(w, s, o):
                for by in range(2):
                    yield (
                        s[by].at[:, :, pl.ds(0, 2)],
                        o[0].at[:, :, :, flip(w[Y], by), :, pl.ds(0, half)],
                    )
                    yield (
                        s[2 + by].at[:, :, pl.ds(0, 2)],
                        o[0].at[:, :, flip(w[X], by), :, :, pl.ds(half, half)],
                    )

            (most,) = local_copies(
                plan,
                [old[name] for name in ("ys", "yg", "xs", "xg")],
                [(2, 2, 2, 2, ROWS, COLUMNS)],
                [new[name] for name in ("xs", "z0s") if name in new][:1],
            )
            got = cube.swap(most, C)
            kind, arrays = self.pieces[t - 1]

            def plan_whole(w, s, o):
                for by in range(2):
                    for at, rows, columns in tiles_of(kind, arrays):
                        yield (
                            s[by].at[:, :, :, :, :, columns],
                            o[at].at[:, :, :, :, flip(w[C], by), rows],
                        )

            made = local_copies(
                plan_whole, [most, got], [(2, 2, 2, 2, 2) + array.shape for array in arrays]
            )
            self.wholes[t - 1] = [
                whole.reshape(-1, array.shape[1]) for whole, array in zip(made, arrays)
            ]
        self.state = new


ROWS, COLUMNS = 32, 4096


def uniform_shard(kind, arrays):
    if kind == "tall":
        return jnp.concatenate([arrays[0][at : at + ROWS] for at in range(0, 4 * ROWS, ROWS)], axis=1)
    spare = COLUMNS - sum(array.shape[1] for array in arrays)
    extra = [arrays[0][:, :spare]] if spare else []
    return jnp.concatenate(arrays + extra, axis=1) if len(arrays) > 1 else arrays[0]


def tiles_of(kind, arrays):
    if kind == "tall":
        width = arrays[0].shape[1]
        for at in range(4):
            yield 0, pl.ds(at * ROWS, ROWS), pl.ds(at * width, width)
    else:
        start = 0
        for at, array in enumerate(arrays):
            yield at, pl.ds(0, ROWS), pl.ds(start, array.shape[1])
            start += array.shape[1]


def added(out, out_at, first, first_at, second, second_at):
    total = first[first_at].astype(jnp.float32) + second[second_at].astype(jnp.float32)
    out[out_at] = total.astype(out.dtype)


class Scatter:
    def __init__(self, cube):
        self.cube = cube
        self.state = {}
        self.results = []

    def stage(self, piece=None):
        cube, old, new = self.cube, self.state, {}
        if not cube.tuned:
            if piece is not None:
                self.results.append(
                    [
                        lax.psum_scatter(grad, AXES, scatter_dimension=0, tiled=True).astype(
                            jnp.float32
                        )
                        for grad in piece[2]
                    ]
                )
            return
        half = COLUMNS // 2
        inputs, shapes, jobs = [], [], []

        def give(name):
            inputs.append(old[name])
            return len(inputs) - 1

        def make(sent, *shape):
            shapes.append((sent, shape))
            return len(shapes) - 1

        left, right = slice(0, half), slice(half, COLUMNS)
        has_n, has_m = "ck" in old, "ak" in old
        slots = 2 * has_n + has_m
        if slots:
            x_out, y_out = (make(1, 2, 2, slots, ROWS, half) for _ in range(2))
        corners = [(a, b) for a in range(2) for b in range(2)]
        if has_n:
            ck, cg = give("ck"), give("cg")
            a_out, b_out = (make(0, 2, 2, 2, ROWS, half) for _ in range(2))

            def job_n(w, s, o, sent):
                y, x = flip(w[Y], sent), flip(w[X], sent)
                for a, b in corners:
                    for k in range(2):
                        from_a = (a, b, k, y, slice(None), left)
                        from_b = (a, b, x, k, slice(None), right)
                        out_a, out_b = o[y_out if sent else a_out], o[x_out if sent else b_out]
                        added(out_a, (a, b, k), s[ck], from_a, s[cg], from_a)
                        added(out_b, (a, b, k), s[ck], from_b, s[cg], from_b)

            jobs.append(job_n)
        if has_m:
            ak, bk, xg, yg = (give(name) for name in ("ak", "bk", "xg", "yg"))
            a4_out, b4_out = (make(0, 2, 2, ROWS, half) for _ in range(2))

            def job_m(w, s, o, sent):
                y, x = flip(w[Y], sent), flip(w[X], sent)
                for a, b in corners:
                    place = (a, b, slots - 1) if sent else (a, b)
                    added(o[x_out if sent else a4_out], place, s[ak], (a, b, x), s[yg], (a, b, x))
                    added(o[y_out if sent else b4_out], place, s[bk], (a, b, y), s[xg], (a, b, y))

            jobs.append(job_m)
        if "a4k" in old:
            a4k, b4k = give("a4k"), give("b4k")
            x4g, y4g = (xg, yg) if has_m else (give("xg"), give("yg"))
            last = old["xg"].shape[2] - 1
            z_out, zk_out = (make(sent, 2, ROWS, COLUMNS) for sent in (1, 0))

            def job_z(w, s, o, sent):
                z = flip(w[Z0], sent)
                out = o[z_out if sent else zk_out]
                for a in range(2):
                    added(out, (a, slice(None), left), s[a4k], (a, z), s[x4g], (a, z, last))
                    added(out, (a, slice(None), right), s[b4k], (a, z), s[y4g], (a, z, last))

            jobs.append(job_z)
        if "zk" in old:
            zk, zg = give("zk"), give("zg")
            f_out, fk_out = (make(sent, ROWS, COLUMNS) for sent in (1, 0))

            def job_f(w, s, o, sent):
                z = flip(w[Z1], sent)
                added(o[f_out if sent else fk_out], slice(None), s[zk], z, s[zg], z)

            jobs.append(job_f)
        if "fk" in old:
            kind, arrays = self.queue.pop(0)
            total = old["fk"].astype(jnp.float32) + old["fg"].astype(jnp.float32)
            self.results.append(split_shard(kind, arrays, total))
        made = {}
        for sent in (1, 0) if jobs else ():
            chosen = [at for at, (side, shape) in enumerate(shapes) if side == sent]
            after = [made[x_out if slots else z_out if "a4k" in old else f_out]] if made else []

            def kernel(*refs):
                dp, head = lax.axis_index("dp"), lax.axis_index("head")
                where = (dp // 4, dp // 2 % 2, dp % 2, head // 2, head % 2)
                outs = dict(zip(chosen, refs[len(inputs) + len(after) :]))
                for job in jobs:
                    job(where, refs[: len(inputs)], outs, sent)

            size = sum(math.prod(shapes[at][1]) for at in chosen)
            results = pl.pallas_call(
                kernel,
                out_shape=[jax.ShapeDtypeStruct(shapes[at][1], jnp.bfloat16) for at in chosen],
                in_specs=[VMEM] * len(inputs) + [ANY] * len(after),
                out_specs=[VMEM] * len(chosen),
                cost_estimate=pl.CostEstimate(
                    flops=size, bytes_accessed=6 * size, transcendentals=0
                ),
                compiler_params=pltpu.CompilerParams(
                    vmem_limit_bytes=2 * size + 2 * sum(each.size for each in inputs) + (1 << 20)
                ),
            )(*inputs, *after)
            made.update(zip(chosen, results))
        if jobs:
            if slots:
                new["xg"], new["yg"] = cube.swap(made[x_out], X), cube.swap(made[y_out], Y)
            if has_n:
                new["ak"], new["bk"] = made[a_out], made[b_out]
            if has_m:
                new["a4k"], new["b4k"] = made[a4_out], made[b4_out]
            if "a4k" in old:
                new["zk"], new["zg"] = made[zk_out], cube.swap(made[z_out], Z0)
            if "zk" in old:
                new["fk"], new["fg"] = made[fk_out], cube.swap(made[f_out], Z1)
        if piece is not None:
            kind, arrays, grads = piece
            self.queue = getattr(self, "queue", []) + [(kind, arrays)]
            bits = [
                grad.reshape((2, 2, 2, 2, 2) + array.shape) for grad, array in zip(grads, arrays)
            ]

            def plan(w, s, o):
                for sent in range(2):
                    for at, rows, columns in tiles_of(kind, arrays):
                        yield (
                            s[at].at[:, :, :, :, flip(w[C], sent), rows],
                            o[sent].at[:, :, :, :, :, columns],
                        )
                    spare = COLUMNS - sum(array.size for array in arrays) // ROWS
                    if spare:
                        yield (
                            s[0].at[:, :, :, :, flip(w[C], sent), :, pl.ds(0, spare)],
                            o[sent].at[:, :, :, :, :, pl.ds(COLUMNS - spare, spare)],
                        )

            keep, send = local_copies(
                plan, bits, [(2, 2, 2, 2, ROWS, COLUMNS)] * 2, [made[x_out]] if slots else []
            )
            new["ck"], new["cg"] = keep, cube.swap(send, C)
        self.state = new


def split_shard(kind, arrays, total):
    if kind == "tall":
        width = arrays[0].shape[1]
        return [jnp.concatenate([total[:, at * width : (at + 1) * width] for at in range(4)], axis=0)]
    parts, start = [], 0
    for array in arrays:
        parts.append(total[:, start : start + array.shape[1]])
        start += array.shape[1]
    return parts


class HeadScattering:
    def __init__(self, cube, values, rows):
        self.cube = cube
        if not cube.tuned:
            self.whole = values
            return
        half = values.shape[1] // 2
        self.parts = [
            Summing(cube, values[:, :half].reshape(2, 2, 2, rows, half), (X, Z0, Z1)),
            Summing(cube, values[:, half:].reshape(2, 2, 2, rows, half), (Z0, Z1, X)),
        ]

    @property
    def state(self):
        return [part.state for part in self.parts] if self.cube.tuned else [self.whole]

    @state.setter
    def state(self, values):
        if not self.cube.tuned:
            self.whole = values[0]
            return
        for part, state in zip(self.parts, values):
            part.state = state

    def step(self):
        if self.cube.tuned:
            for part in self.parts:
                part.step()

    def result(self):
        if not self.cube.tuned:
            return lax.psum_scatter(self.whole, "dp", scatter_dimension=0, tiled=True).astype(
                jnp.float32
            )
        return jnp.concatenate([part.result() for part in self.parts], axis=1)


def shifted(pad_ref, shift_ref, rows):
    for r in range(8):
        shift_ref[r] = pad_ref[r : r + rows, :]


def conv_forward_kernel(lead_ref, gate_ref, valid_ref, taps_ref, conv_ref, sums_ref, pad, shift):
    length, width = lead_ref.shape
    edge = jnp.zeros((16, width), jnp.float32)
    valid = valid_ref[...]
    pad[0:16, :] = edge
    pad[16 : 16 + length, :] = lead_ref[...] * jax.nn.sigmoid(gate_ref[...]) * valid
    pad[16 + length : 40 + length, :] = jnp.zeros((24, width), jnp.float32)
    shifted(pad, shift, length + 32)
    chunk = 64
    taps = [taps_ref[j : j + 1, :] for j in range(32)]

    def step(at, totals):
        start = pl.multiple_of(at * chunk, chunk)
        total = jnp.zeros((chunk, width), jnp.float32)
        for j in range(32):
            total += shift[j % 8, pl.ds(start + j // 8 * 8, chunk), :] * taps[j]
        conv_ref[pl.ds(start, chunk), :] = total
        weighted = total * valid_ref[pl.ds(start, chunk), :]
        plain, squares = totals
        return (
            plain + jnp.sum(weighted, axis=0, keepdims=True),
            squares + jnp.sum(weighted * total, axis=0, keepdims=True),
        )

    zero = jnp.zeros((1, width), jnp.float32)
    plain, squares = lax.fori_loop(0, length // chunk, step, (zero, zero))
    sums_ref[0:1, :] = plain
    sums_ref[1:2, :] = squares
    sums_ref[2:8, :] = jnp.zeros((6, width), jnp.float32)


def conv_forward(expanded, valid, taps):
    rows = expanded.shape[0]
    width = 128
    count = D // width
    return pl.pallas_call(
        conv_forward_kernel,
        grid=(count,),
        in_specs=[
            pl.BlockSpec((rows, width), lambda i: (0, i)),
            pl.BlockSpec((rows, width), lambda i: (0, i + count)),
            pl.BlockSpec((rows, 1), lambda i: (0, 0)),
            pl.BlockSpec((32, width), lambda i: (0, i)),
        ],
        out_specs=[
            pl.BlockSpec((rows, width), lambda i: (0, i)),
            pl.BlockSpec((8, width), lambda i: (0, i)),
        ],
        out_shape=[
            jax.ShapeDtypeStruct((rows, D), jnp.float32),
            jax.ShapeDtypeStruct((8, D), jnp.float32),
        ],
        scratch_shapes=[
            pltpu.VMEM((rows + 40, width), jnp.float32),
            pltpu.VMEM((8, rows + 32, width), jnp.float32),
        ],
        cost_estimate=pl.CostEstimate(
            flops=80 * rows * D, bytes_accessed=16 * rows * D, transcendentals=rows * D
        ),
        compiler_params=pltpu.CompilerParams(vmem_limit_bytes=8 << 20),
    )(expanded, expanded, valid, taps)


def conv_backward_kernel(
    lead_ref,
    gate_ref,
    valid_ref,
    taps_ref,
    conv_ref,
    grad_ref,
    vectors_ref,
    out_lead_ref,
    out_gate_ref,
    taps_grad_ref,
    pad,
    shift,
    tap_sums,
):
    length, width = lead_ref.shape
    inverse, plain, scaled = vectors_ref[0:1, :], vectors_ref[1:2, :], vectors_ref[2:3, :]
    pad[0:16, :] = jnp.zeros((16, width), jnp.float32)
    pad[16 : 16 + length, :] = (
        grad_ref[...] * inverse + (plain + scaled * conv_ref[...]) * valid_ref[...]
    )
    pad[16 + length : 40 + length, :] = jnp.zeros((24, width), jnp.float32)
    shifted(pad, shift, length + 32)
    tap_sums[...] = jnp.zeros(tap_sums.shape, jnp.float32)
    chunk = 64
    taps = [taps_ref[j : j + 1, :] for j in range(32)]

    def step(at, carry):
        start = pl.multiple_of(at * chunk, chunk)
        here = pl.ds(start, chunk)
        lead, valid = lead_ref[here, :], valid_ref[here, :]
        gate = jax.nn.sigmoid(gate_ref[here, :])
        gated = lead * gate * valid
        total = jnp.zeros((chunk, width), jnp.float32)
        for j in range(32):
            off = 32 - j
            part = shift[off % 8, pl.ds(start + off // 8 * 8, chunk), :]
            total += part * taps[j]
            tap_sums[j] += jnp.sum((part * gated).reshape(chunk // 8, 8, width), axis=0)
        grad = total * valid
        out_lead_ref[here, :] = (grad * gate).astype(jnp.bfloat16)
        out_gate_ref[here, :] = (grad * lead * gate * (1.0 - gate)).astype(jnp.bfloat16)
        return carry

    lax.fori_loop(0, length // chunk, step, 0)
    taps_grad_ref[...] = jnp.sum(tap_sums[...], axis=1)


def conv_backward(expanded, valid, taps, conv_out, grads, vectors):
    rows = expanded.shape[0]
    width = 128
    count = D // width
    block = pl.BlockSpec((rows, width), lambda i: (0, i))
    return pl.pallas_call(
        conv_backward_kernel,
        grid=(count,),
        in_specs=[
            block,
            pl.BlockSpec((rows, width), lambda i: (0, i + count)),
            pl.BlockSpec((rows, 1), lambda i: (0, 0)),
            pl.BlockSpec((32, width), lambda i: (0, i)),
            block,
            block,
            pl.BlockSpec((8, width), lambda i: (0, i)),
        ],
        out_specs=[block, block, pl.BlockSpec((32, width), lambda i: (0, i))],
        out_shape=[
            jax.ShapeDtypeStruct((rows, D), jnp.bfloat16),
            jax.ShapeDtypeStruct((rows, D), jnp.bfloat16),
            jax.ShapeDtypeStruct((32, D), jnp.float32),
        ],
        scratch_shapes=[
            pltpu.VMEM((rows + 40, width), jnp.float32),
            pltpu.VMEM((8, rows + 32, width), jnp.float32),
            pltpu.VMEM((32, 8, width), jnp.float32),
        ],
        cost_estimate=pl.CostEstimate(
            flops=160 * rows * D, bytes_accessed=20 * rows * D, transcendentals=rows * D
        ),
        compiler_params=pltpu.CompilerParams(vmem_limit_bytes=8 << 20),
    )(expanded, expanded, valid, taps, conv_out, grads, vectors)


def fence(flows, *values):
    states, values = lax.optimization_barrier(([flow.state for flow in flows], values))
    for flow, state in zip(flows, states):
        flow.state = state
    return values[0] if len(values) == 1 else values


def rows_of(values, count):
    return values.reshape(count, values.shape[-1])


def shards(
    sizes,
    frames,
    ffn_inner,
    ffn_outer,
    attn_qkv,
    attn_proj,
    conv_expand,
    conv_depth,
    conv_proj,
    norm_gains,
    head_proj,
    lengths,
    mask_starts,
    target_codes,
    out_grad,
):
    cube = Cube(sizes)
    devices = sizes["dp"] * sizes["head"]
    ff = ffn_inner.shape[2]
    all_bits = list(range(len(cube.bits)))

    rows_in = Gather(
        cube,
        [
            ("wide", [ffn_inner[0]]),
            ("tall", [ffn_outer[0]]),
            ("wide", [attn_qkv, attn_proj]),
            ("wide", [conv_expand, conv_proj]),
            ("wide", [ffn_inner[1]]),
            ("tall", [ffn_outer[1]]),
        ],
    )
    head_half = head_proj.shape[1] // 2
    heads = [
        HeadGathering(cube, head_proj[:, :head_half]),
        HeadGathering(cube, head_proj[:, head_half:]),
    ]

    row_total = UTT_DEV * SEQ
    positions = jnp.arange(SEQ, dtype=jnp.int32)
    valid_mat = positions[None, :] < lengths[:, None]
    valid_rows = valid_mat.reshape(row_total).astype(jnp.float32)
    frequency = 10000.0 ** (-(jnp.arange(HD // 2, dtype=jnp.float32) * 2.0) / HD)
    angles = positions.astype(jnp.float32)[:, None] * frequency[None, :]
    cosine = jnp.cos(angles)[:, None, :]
    sine_table = jnp.sin(angles)[:, None, :]
    score_scale = HD ** (-0.5)

    slots = UTT_DEV * NSPAN * SPAN
    slot_at = (mask_starts[:, :, None] + jnp.arange(SPAN, dtype=jnp.int32)).reshape(UTT_DEV, -1)
    slot_ok = slot_at < lengths[:, None]
    chosen = (slot_at + SEQ * jnp.arange(UTT_DEV, dtype=jnp.int32)[:, None]).reshape(slots)
    slot_live = slot_ok.reshape(slots)
    pick = (
        (chosen[:, None] == jnp.arange(row_total, dtype=jnp.int32)[None, :]) & slot_live[:, None]
    )
    picked_codes = jnp.sum(jnp.where(pick, target_codes[None, :], 0), axis=1)
    picked_codes = jnp.where(slot_live, picked_codes, -1)
    pick_lo = pick.astype(jnp.bfloat16)
    head_order = [at for at in range(len(cube.bits)) if cube.bits[at][0] == "head"]
    group = sizes["head"]
    vocab_cols = head_proj.shape[1]

    loss_scale = jnp.float32(devices * UTT_DEV * NSPAN * SPAN)
    hops = [C, Z1, Z0, X, Y] if cube.tuned else all_bits
    vector_in = VectorGathering(cube, jnp.concatenate([norm_gains, conv_depth], axis=0), hops)
    vector_in.step(2)
    group_codes = cube.gather(picked_codes, head_order).reshape(group * slots)
    rows_in.stage(-3)
    heads[0].step("x")
    heads[1].step("x")
    group_codes = fence([rows_in, vector_in, *heads], group_codes)

    rows_in.stage(-2)
    vector_in.step()
    fence([rows_in, vector_in], loss_scale)

    rows_in.stage(-1)
    vector_in.step()
    inputs = frames.astype(jnp.float32)
    fence([rows_in, vector_in], loss_scale)

    rows_in.stage(0)
    vector_in.step(len(hops))
    fence([rows_in, vector_in], loss_scale)
    (vectors,) = vector_in.state
    vectors = jnp.moveaxis(vectors.reshape((devices,) + vectors.shape[-2:]), 0, 1).reshape(-1, D)
    gain_f, depth_f = vectors[:6].astype(jnp.float32), vectors[6:].astype(jnp.float32)
    norm_first = lowered(layer_norm(inputs, gain_f[0]))
    group_live = (group_codes >= 0).astype(jnp.float32)
    local_codes = group_codes - lax.axis_index("head") * vocab_cols

    rows_in.stage(1)
    (inner_0,) = rows_in.wholes[0]
    pre_first = matmul(norm_first, inner_0)
    act_first = lowered(jax.nn.silu(pre_first))
    pre_first, act_first = fence([rows_in], pre_first, act_first)

    rows_in.stage(2)
    (outer_0,) = rows_in.wholes[1]
    after_first = inputs + 0.5 * matmul(act_first, outer_0)
    norm_attn = lowered(layer_norm(after_first, gain_f[1]))
    after_first, norm_attn = fence([rows_in], after_first, norm_attn)

    rows_in.stage(3)
    heads[0].step("far")
    mix_weight, proj_weight = rows_in.wholes[2]
    mixed = matmul(norm_attn, mix_weight)
    mixed = mixed.reshape(UTT_DEV, SEQ, 3, H, HD)
    queries = lowered(rotate(mixed[:, :, 0], cosine, sine_table))
    key_rows = lowered(rotate(mixed[:, :, 1], cosine, sine_table))
    value_rows = lowered(mixed[:, :, 2])

    def scores_of(query_one, key_one, key_ok):
        scores = (
            jnp.einsum("qhd,khd->hqk", query_one, key_one, preferred_element_type=jnp.float32)
            * score_scale
        )
        return jnp.where(key_ok[None, None, :], scores, -1e30)

    def attend_one(query_one, key_one, value_one, key_ok):
        scores = scores_of(query_one, key_one, key_ok)
        row_top = jnp.max(scores, axis=-1, keepdims=True)
        weights = jnp.exp(scores - row_top)
        totals = jnp.sum(weights, axis=-1, keepdims=True)
        attn_probs = weights / totals
        attended = jnp.einsum(
            "hqk,khd->qhd", lowered(attn_probs), value_one, preferred_element_type=jnp.float32
        )
        return (attended, row_top[..., 0] + jnp.log(totals[..., 0]))

    attended, log_totals = attend_one(queries[0], key_rows[0], value_rows[0], valid_mat[0])
    attended_lo = lowered(attended.reshape(row_total, D))
    after_attention = after_first + matmul(attended_lo, proj_weight)
    norm_conv = lowered(layer_norm(after_attention, gain_f[2]))
    after_attention, norm_conv, attended_lo, queries, key_rows, value_rows, log_totals = fence(
        [rows_in, heads[0]],
        after_attention,
        norm_conv,
        attended_lo,
        queries,
        key_rows,
        value_rows,
        log_totals,
    )

    rows_in.stage(4)
    heads[0].step("near")
    heads[1].step("far")
    expand_weight, conv_weight = rows_in.wholes[3]
    expanded = matmul(norm_conv, expand_weight)
    conv_out, conv_sums = conv_forward(expanded, valid_rows[:, None], depth_f)
    valid_total = jnp.broadcast_to(jnp.sum(valid_rows), (1, D))
    sums = cube.total(jnp.concatenate([conv_sums[:2], valid_total], axis=0))
    sums, conv_out, after_attention, expanded, norm_conv = fence(
        [rows_in, *heads], sums, conv_out, after_attention, expanded, norm_conv
    )

    rows_in.stage(5)
    heads[1].step("near")
    (inner_1,) = rows_in.wholes[4]
    frame_count = sums[2, 0]
    channel_mean = sums[0] / frame_count
    variance = sums[1] / frame_count - channel_mean * channel_mean
    inverse = lax.rsqrt(variance + eps)
    normalized = (conv_out - channel_mean) * inverse
    normed_bn = normalized * gain_f[3]
    swish_lo = lowered(jax.nn.silu(normed_bn))
    after_conv = after_attention + matmul(swish_lo, conv_weight)
    norm_second = lowered(layer_norm(after_conv, gain_f[4]))
    pre_second = matmul(norm_second, inner_1)
    act_second = lowered(jax.nn.silu(pre_second))
    after_conv, norm_second, pre_second, act_second, swish_lo = fence(
        [rows_in, *heads], after_conv, norm_second, pre_second, act_second, swish_lo
    )

    rows_in.stage(6)
    (outer_1,) = rows_in.wholes[5]
    head_cols = joined_heads(cube, heads)
    after_second = after_conv + 0.5 * matmul(act_second, outer_1)
    output_lo = lowered(layer_norm(after_second, gain_f[5]))

    picked_rows = lowered(matmul(pick_lo, output_lo))
    group_rows = cube.gather(picked_rows, head_order).reshape(group * slots, D)
    logits = matmul(group_rows, head_cols)
    row_top = jnp.max(logits, axis=1)
    row_sum = jnp.sum(jnp.exp(logits - row_top[:, None]), axis=1)
    onehot = jnp.arange(vocab_cols, dtype=jnp.int32)[None, :] == local_codes[:, None]
    target_logit = jnp.sum(jnp.where(onehot, logits, 0.0), axis=1)
    stats = cube.gather(jnp.stack([row_top, row_sum, target_logit]), head_order)
    stats = stats.reshape(group, 3, group * slots)
    whole_top = jnp.max(stats[:, 0], axis=0)
    whole_sum = jnp.sum(stats[:, 1] * jnp.exp(stats[:, 0] - whole_top), axis=0)
    log_norm = whole_top + jnp.log(whole_sum)
    ce_group = jnp.sum((log_norm - jnp.sum(stats[:, 2], axis=0)) * group_live)
    grad_logits = lowered(
        (jnp.exp(logits - log_norm[:, None]) - onehot.astype(jnp.float32)) * group_live[:, None]
    )
    head_grad = lowered(matmul_tn(group_rows, grad_logits))
    head_flow = HeadScattering(cube, head_grad, head_proj.shape[0])
    row_grads = lowered(matmul_nt(grad_logits, head_cols))
    row_sum = Summing(cube, row_grads.reshape((2,) * len(head_order) + (slots, D)), head_order[::-1])
    head_flow.step()
    for _ in head_order:
        row_sum.step()
    row_grads = lowered(row_sum.result())
    grad_output = out_grad.astype(jnp.float32) + matmul_tn(pick_lo, row_grads)

    def outer_back(grad_in, act_lo):
        grad_out_lo = lowered(0.5 * grad_in)
        weight_grad = lowered(matmul_tn(act_lo, grad_out_lo))
        return grad_out_lo, ("tall", [ffn_outer[0]], [weight_grad])

    def inner_back(grad_out_lo, normed_lo, pre_act, inner_weight, outer_weight):
        grad_pre = lowered(silu_back(pre_act, matmul_nt(grad_out_lo, outer_weight)))
        weight_grad = lowered(matmul_tn(normed_lo, grad_pre))
        below = matmul_nt(grad_pre, inner_weight)
        return below, ("wide", [ffn_inner[0]], [weight_grad])

    rows_out = Scatter(cube)
    grad_second, gain_grad_final = norm_back(after_second, gain_f[5], grad_output)
    grad_out_lo, piece = outer_back(grad_second, act_second)
    grad_second, grad_out_lo, piece[2][0] = fence(
        [head_flow], grad_second, grad_out_lo, piece[2][0]
    )

    head_flow.step()
    rows_out.stage(piece)
    below_second, piece = inner_back(grad_out_lo, norm_second, pre_second, inner_1, outer_1)
    below_second, piece[2][0] = fence([head_flow, rows_out], below_second, piece[2][0])

    norm_part, gain_grad_second = norm_back(after_conv, gain_f[4], below_second)
    grad_conv_res = grad_second + norm_part
    conv_res_lo = lowered(grad_conv_res)
    grad_bn = silu_back(normed_bn, matmul_nt(conv_res_lo, conv_weight))
    gain_grad_bn = jnp.sum(grad_bn * normalized, axis=0)
    grad_normalized = grad_bn * gain_f[3]
    back_sums = cube.total(
        jnp.stack(
            [
                jnp.sum(grad_normalized, axis=0),
                jnp.sum(grad_normalized * normalized, axis=0),
                jnp.broadcast_to(ce_group / group, (D,)),
            ]
        )
    )
    conv_proj_grad = lowered(matmul_tn(swish_lo, conv_res_lo))
    back_sums, grad_normalized, grad_conv_res, conv_proj_grad = fence(
        [],
        back_sums,
        grad_normalized,
        grad_conv_res,
        conv_proj_grad,
    )

    head_flow.step()
    rows_out.stage(piece)
    sum_plain, sum_scaled = back_sums[0], back_sums[1]
    loss = back_sums[2, 0] / loss_scale
    grad_variance = -0.5 * inverse * inverse * sum_scaled
    grad_mean = -inverse * sum_plain - 2.0 * channel_mean * grad_variance
    back_vectors = jnp.stack(
        [inverse, grad_mean / frame_count, 2.0 * grad_variance / frame_count]
        + [jnp.zeros_like(inverse)] * 5
    )
    grad_lead, grad_gate, depth_grad = conv_backward(
        expanded, valid_rows[:, None], depth_f, conv_out, grad_normalized, back_vectors
    )
    grad_expanded = jnp.concatenate([grad_lead, grad_gate], axis=1)
    expand_grad = lowered(matmul_tn(norm_conv, grad_expanded))
    grad_expanded, expand_grad = fence([rows_out, head_flow], grad_expanded, expand_grad)

    rows_out.stage(("wide", [conv_expand, conv_proj], [expand_grad, conv_proj_grad]))
    norm_part, gain_grad_conv = norm_back(
        after_attention, gain_f[2], matmul_nt(grad_expanded, expand_weight)
    )
    grad_attn_res = grad_conv_res + norm_part
    attn_res_lo = lowered(grad_attn_res)
    proj_grad = lowered(matmul_tn(attended_lo, attn_res_lo))
    grad_attended = lowered(matmul_nt(attn_res_lo, proj_weight)).reshape(UTT_DEV, SEQ, H, HD)

    def attend_back(query_one, key_one, value_one, key_ok, log_total, grad_one):
        attn_probs = jnp.exp(scores_of(query_one, key_one, key_ok) - log_total[:, :, None])
        grad_value = jnp.einsum(
            "hqk,qhd->khd", lowered(attn_probs), grad_one, preferred_element_type=jnp.float32
        )
        grad_probs = jnp.einsum(
            "qhd,khd->hqk", grad_one, value_one, preferred_element_type=jnp.float32
        )
        grad_scores = lowered(
            attn_probs * (grad_probs - jnp.sum(attn_probs * grad_probs, axis=-1, keepdims=True))
        )
        grad_query = (
            jnp.einsum("hqk,khd->qhd", grad_scores, key_one, preferred_element_type=jnp.float32)
            * score_scale
        )
        grad_key = (
            jnp.einsum("hqk,qhd->khd", grad_scores, query_one, preferred_element_type=jnp.float32)
            * score_scale
        )
        return (grad_query, grad_key, grad_value)

    grad_query, grad_key, grad_value = attend_back(
        queries[0], key_rows[0], value_rows[0], valid_mat[0], log_totals, grad_attended[0]
    )
    grad_mixed = jnp.concatenate(
        [
            lowered(rotate_back(grad_query, cosine[:, :, :], sine_table)).reshape(row_total, D),
            lowered(rotate_back(grad_key, cosine, sine_table)).reshape(row_total, D),
            lowered(grad_value).reshape(row_total, D),
        ],
        axis=1,
    )
    grad_mixed, proj_grad, grad_attn_res = fence([rows_out], grad_mixed, proj_grad, grad_attn_res)

    rows_out.stage()
    mix_grad = lowered(matmul_tn(norm_attn, grad_mixed))
    norm_part, gain_grad_attn = norm_back(after_first, gain_f[1], matmul_nt(grad_mixed, mix_weight))
    grad_first_res = grad_attn_res + norm_part
    grad_first_res, mix_grad = fence([rows_out], grad_first_res, mix_grad)

    rows_out.stage(("wide", [attn_qkv, attn_proj], [mix_grad, proj_grad]))
    grad_out_lo, piece = outer_back(grad_first_res, act_first)
    grad_out_lo, piece[2][0] = fence([rows_out], grad_out_lo, piece[2][0])

    rows_out.stage(piece)
    below_first, piece = inner_back(grad_out_lo, norm_first, pre_first, inner_0, outer_0)
    below_first, piece[2][0] = fence([rows_out], below_first, piece[2][0])

    rows_out.stage(piece)
    norm_part, gain_grad_first = norm_back(inputs, gain_f[0], below_first)
    input_grad = grad_first_res + norm_part
    vector_grad = jnp.concatenate(
        [
            jnp.stack(
                [
                    gain_grad_first,
                    gain_grad_attn,
                    gain_grad_conv,
                    gain_grad_bn,
                    gain_grad_second,
                    gain_grad_final,
                ],
                axis=0,
            ),
            depth_grad,
        ],
        axis=0,
    )
    vector_grad = jnp.moveaxis(vector_grad.reshape(vector_grad.shape[0], devices, -1), 1, 0)
    vector_flow = Summing(
        cube, vector_grad.reshape((2,) * len(cube.bits) + vector_grad.shape[1:]), hops
    )
    vector_flow.step()
    vector_flow.step()
    input_grad = fence([rows_out, vector_flow], input_grad)

    for _ in range(4):
        rows_out.stage()
        if vector_flow.order:
            vector_flow.step()
        fence([rows_out, vector_flow], loss)
    for _ in vector_flow.order[:]:
        vector_flow.step()
    vector_grad = vector_flow.result()
    rows_out.stage()
    (
        (outer_grad_1,),
        (inner_grad_1,),
        (expand_grad, conv_proj_grad),
        (mix_grad, proj_grad),
        (outer_grad_0,),
        (inner_grad_0,),
    ) = rows_out.results
    return (
        output_lo,
        loss,
        input_grad,
        jnp.stack([inner_grad_0, inner_grad_1], axis=0),
        jnp.stack([outer_grad_0, outer_grad_1], axis=0),
        mix_grad,
        proj_grad,
        expand_grad,
        vector_grad[6:],
        conv_proj_grad,
        vector_grad[:6],
        head_flow.result(),
    )


def solution(mesh):
    placed = (
        P(("dp", "head"), None),
        P(None, ("dp", "head"), None),
        P(None, ("dp", "head"), None),
        P(("dp", "head"), None),
        P(("dp", "head"), None),
        P(("dp", "head"), None),
        P(None, ("dp", "head")),
        P(("dp", "head"), None),
        P(None, ("dp", "head")),
        P("dp", "head"),
        P(("dp", "head")),
        P(("dp", "head"), None),
        P(("dp", "head")),
        P(("dp", "head"), None),
    )
    sizes = {axis: mesh.shape[axis] for axis in AXES}
    return jax.shard_map(
        functools.partial(shards, sizes),
        mesh=mesh,
        in_specs=placed,
        out_specs=(
            P(("dp", "head"), None),
            P(),
            P(("dp", "head"), None),
            P(None, ("dp", "head"), None),
            P(None, ("dp", "head"), None),
            P(("dp", "head"), None),
            P(("dp", "head"), None),
            P(("dp", "head"), None),
            P(None, ("dp", "head")),
            P(("dp", "head"), None),
            P(None, ("dp", "head")),
            P("dp", "head"),
        ),
        check_vma=False,
    )
```

```python
import functools
import math

import jax
import jax.numpy as jnp
from jax import lax
from jax.experimental import pallas as pl
from jax.experimental.pallas import tpu as pltpu
from jax.sharding import PartitionSpec as P

D = 1024
H = 8
HD = 128
VOCAB = 8192
SEQ = 512
SPAN = 10
NSPAN = 20
UTT_DEV = 1


eps = 1e-05


def layer_norm(values, gain_row):
    center = values - jnp.mean(values, axis=-1, keepdims=True)
    variance = jnp.mean(center * center, axis=-1, keepdims=True)
    return center * lax.rsqrt(variance + eps) * gain_row


def lowered(values):
    return values.astype(jnp.bfloat16)


def matmul(operand, weight):
    return jnp.dot(operand, weight, preferred_element_type=jnp.float32)


def matmul_tn(operand, weight):
    return lax.dot_general(
        operand, weight, (((0,), (0,)), ((), ())), preferred_element_type=jnp.float32
    )


def matmul_nt(operand, weight):
    return lax.dot_general(
        operand, weight, (((1,), (1,)), ((), ())), preferred_element_type=jnp.float32
    )


def norm_back(values, gain_row, grads):
    unused, pullback = jax.vjp(layer_norm, values, gain_row)
    return pullback(grads)


def silu_back(values, grads):
    return jax.vjp(jax.nn.silu, values)[1](grads)[0]


AXES = ("dp", "head")
ANY = pl.BlockSpec(memory_space=pl.ANY)
VMEM = pl.BlockSpec(memory_space=pltpu.VMEM)
Z1, Z0, X, Y, C = range(5)


def local_copies(plan, inputs, outputs, after=()):
    count = len(inputs)

    def kernel(*refs):
        sources, targets, sem = refs[:count], refs[count + len(after) : -1], refs[-1]
        dp, head = lax.axis_index("dp"), lax.axis_index("head")
        where = (dp // 4, dp // 2 % 2, dp % 2, head // 2, head % 2)
        copies = []
        for at, (source, target) in enumerate(plan(where, sources, targets)):
            copies.append(pltpu.make_async_copy(source, target, sem.at[at]))
            copies[-1].start()
        for copy in copies:
            copy.wait()

    size = sum(math.prod(shape) for shape in outputs) * inputs[0].dtype.itemsize
    results = pl.pallas_call(
        kernel,
        out_shape=[jax.ShapeDtypeStruct(shape, inputs[0].dtype) for shape in outputs],
        in_specs=[ANY] * (count + len(after)),
        out_specs=[VMEM] * len(outputs),
        scratch_shapes=[pltpu.SemaphoreType.DMA((16,))],
        cost_estimate=pl.CostEstimate(flops=0, bytes_accessed=2 * size, transcendentals=0),
        compiler_params=pltpu.CompilerParams(vmem_limit_bytes=size + (1 << 20)),
    )(*inputs, *after)
    return list(results)


def flip(bit, by):
    return (bit + by) % 2


class Cube:
    def __init__(self, sizes):
        self.sizes = sizes
        self.tuned = sizes == {"dp": 8, "head": 4}
        self.bits = []
        for axis in AXES:
            bit = sizes[axis] // 2
            while bit:
                self.bits.append((axis, bit))
                bit //= 2

    def mine(self, at):
        axis, bit = self.bits[at]
        return (lax.axis_index(axis) // bit) % 2

    def swap(self, values, at):
        axis, bit = self.bits[at]
        return lax.ppermute(values, axis, [(i, i ^ bit) for i in range(self.sizes[axis])])

    def gather(self, shard, order):
        held = []
        values = shard
        for at in order:
            place = sum(other < at for other in held)
            values = self.join(values, self.swap(values, at), at, place)
            held.append(at)
        return values

    def join(self, values, got, at, place):
        if self.tuned and values.dtype != jnp.int32:
            shape = values.shape[:place] + (2,) + values.shape[place:]

            def plan(where, sources, targets):
                for by in range(2):
                    index = (slice(None),) * place + (flip(where[at], by),)
                    yield sources[by], targets[0].at[index]

            return local_copies(plan, [values, got], [shape])[0]
        mine = self.mine(at)
        first = jnp.where(mine == 0, values, got)
        second = jnp.where(mine == 0, got, values)
        return jnp.stack([first, second], axis=place)

    def place(self):
        dp, head = lax.axis_index("dp"), lax.axis_index("head")
        parts = jnp.array([4, 2, 1, 0, 0]), jnp.array([0, 0, 0, 2, 1])
        either = jnp.where(parts[0] > 0, dp & parts[0], head & parts[1])
        return (either > 0).astype(jnp.int32)

    def total(self, values):
        for at in range(len(self.bits)):
            values = values + self.swap(values, at)
        return values


TAPS = 32


def joined_vectors(parts):
    devices, rows, width = parts.shape

    def kernel(parts_ref, out_ref):
        pieces = [parts_ref[at].astype(jnp.float32) for at in range(devices)]
        out_ref[...] = jnp.concatenate(pieces, axis=1)

    return pl.pallas_call(
        kernel,
        out_shape=jax.ShapeDtypeStruct((rows, devices * width), jnp.float32),
        compiler_params=pltpu.CompilerParams(vmem_limit_bytes=16 << 20),
    )(parts)


def parted_vectors(arrays, devices):
    rows = sum(array.shape[0] for array in arrays)
    width = D // devices

    def kernel(*refs):
        start = 0
        for ref in refs[:-1]:
            count = ref.shape[0]
            values = ref[...]
            for at in range(devices):
                refs[-1][at, start : start + count, :] = values[:, at * width : (at + 1) * width]
            start += count

    return pl.pallas_call(
        kernel,
        out_shape=jax.ShapeDtypeStruct((devices, rows, width), jnp.float32),
        compiler_params=pltpu.CompilerParams(vmem_limit_bytes=16 << 20),
    )(*arrays)


class VectorGathering:
    def __init__(self, cube, shard, order):
        self.cube, self.order, self.held = cube, list(order), []
        self.state = [shard]

    def step(self, count=1):
        for _ in range(min(count, len(self.order))):
            at = self.order.pop(0)
            place = sum(other < at for other in self.held)
            (values,) = self.state
            self.state = [self.cube.join(values, self.cube.swap(values, at), at, place)]
            self.held.append(at)


class HeadGathering:
    def __init__(self, cube, shard):
        self.cube = cube
        self.state = [shard]

    def step(self, phase):
        if not self.cube.tuned:
            if phase == "x":
                self.state = [lax.all_gather(self.state[0], "dp", axis=0, tiled=True)]
            return
        if phase == "x":
            (own,) = self.state
            self.state = [own, self.cube.swap(own, X)]
        if phase == "far":
            own, got = self.state

            def plan(where, sources, targets):
                for by in range(2):
                    yield sources[by], targets[0].at[flip(where[X], by)]

            (pair,) = local_copies(plan, self.state, [(2,) + own.shape])
            self.state = [pair, self.cube.swap(pair, Z1)]
        if phase == "near":
            pair, got = self.state

            def plan(where, sources, targets):
                for by in range(2):
                    yield sources[by], targets[0].at[flip(where[Z1], by)]

            (four,) = local_copies(plan, self.state, [(2,) + pair.shape])
            self.state = [four, self.cube.swap(four, Z0)]


def joined_heads(cube, heads):
    if not cube.tuned:
        return jnp.concatenate([part.state[0] for part in heads], axis=1)
    parts = [part for flow in heads for part in flow.state]
    _, _, rows, half = parts[0].shape

    def plan(where, sources, targets):
        for at in range(4):
            columns = pl.ds(at // 2 * half, half)
            yield sources[at], targets[0].at[:, flip(where[Z0], at % 2), :, :, columns]

    (whole,) = local_copies(plan, parts, [(2, 2, 2, rows, 2 * half)])
    return whole.reshape(8 * rows, 2 * half)


def pick_of(values, index, place):
    return lax.dynamic_index_in_dim(values, index, place, keepdims=False)


def halves_kernel(at, place, *refs):
    dp, head = lax.axis_index("dp"), lax.axis_index("head")
    mine = (dp // 4, dp // 2 % 2, dp % 2, head // 2, head % 2)[at]
    keep, got, send_ref, keep_ref = refs
    for out, by in ((send_ref, 1), (keep_ref, 0)):
        index = (slice(None),) * place + (flip(mine, by),)
        total = keep[index].astype(jnp.float32) + got[index].astype(jnp.float32)
        out[...] = total.astype(out.dtype)


class Summing:
    def __init__(self, cube, values, order):
        self.cube, self.order = cube, list(order)
        self.held = sorted(order)
        self.state = [values]

    def step(self):
        cube, at = self.cube, self.order.pop(0)
        place = self.held.index(at)
        self.held.remove(at)
        left = self.state[0].shape[:place] + self.state[0].shape[place + 1 :]
        if not cube.tuned:
            values = sum(part.astype(jnp.float32) for part in self.state)
            values = values.astype(self.state[0].dtype)
            send = pick_of(values, 1 - cube.mine(at), place)
            keep = pick_of(values, cube.mine(at), place)
        elif len(self.state) == 1:

            def plan(where, sources, targets):
                for by in range(2):
                    index = (slice(None),) * place + (flip(where[at], 1 - by),)
                    yield sources[0].at[index], targets[by]

            send, keep = local_copies(plan, self.state, [left, left])
        else:
            size = math.prod(left) * self.state[0].dtype.itemsize
            send, keep = pl.pallas_call(
                functools.partial(halves_kernel, at, place),
                out_shape=[jax.ShapeDtypeStruct(left, self.state[0].dtype)] * 2,
                in_specs=[VMEM] * 2,
                out_specs=[VMEM] * 2,
                compiler_params=pltpu.CompilerParams(vmem_limit_bytes=6 * size + (4 << 20)),
            )(*self.state)
        self.state = [keep, cube.swap(send, at)]

    def result(self):
        return sum(part.astype(jnp.float32) for part in self.state)


class Gather:
    def __init__(self, cube, pieces):
        self.cube = cube
        self.pieces = pieces
        self.wholes = [None] * len(pieces)
        if cube.tuned:
            self.shards = [uniform_shard(kind, arrays) for kind, arrays in pieces]
        self.state = {}

    def stage(self, t):
        cube, old, new = self.cube, self.state, {}
        count = len(self.pieces)
        live = lambda at: 0 <= at < count
        if not cube.tuned:
            if live(t - 1):
                self.wholes[t - 1] = [
                    lax.all_gather(array, AXES, axis=0, tiled=True)
                    for array in self.pieces[t - 1][1]
                ]
            return
        half = COLUMNS // 2
        slots = 2 * live(t) + live(t + 1)
        old_slots = 2 * live(t - 1) + live(t)
        inputs, shapes, jobs = [], [], []

        def give(name):
            inputs.append(old[name])
            return len(inputs) - 1

        def make(shape):
            shapes.append(shape)
            return len(shapes) - 1

        pair = None
        if live(t + 2):
            parts, pair = (give("z1s"), give("z1g")), make((2, ROWS, COLUMNS))
            jobs.append(lambda w, s, o, parts=parts, pair=pair: [
                (s[parts[by]], o[pair].at[flip(w[Z1], by)]) for by in range(2)
            ])
        if slots:
            x_out, y_out = (make((2, 2, slots, ROWS, half)) for _ in range(2))
        if live(t):
            xs, xg, ys, yg = (give(name) for name in ("xs", "xg", "ys", "yg"))
            jobs.append(lambda w, s, o: [
                pair_of
                for by in range(2)
                for pair_of in (
                    (s[(xs, xg)[by]].at[:, :, old_slots - 1], o[y_out].at[:, :, flip(w[X], by)]),
                    (s[(ys, yg)[by]].at[:, :, old_slots - 1], o[x_out].at[:, :, flip(w[Y], by)]),
                )
            ])
        if live(t + 1):
            zs, zg = give("z0s"), give("z0g")
            jobs.append(lambda w, s, o: [
                (
                    s[(zs, zg)[by]].at[:, :, pl.ds(side * half, half)],
                    o[(x_out, y_out)[side]].at[:, flip(w[Z0], by), slots - 1],
                )
                for by in range(2)
                for side in range(2)
            ])
        if jobs:
            made = local_copies(
                lambda w, s, o: [each for job in jobs for each in job(w, s, o)], inputs, shapes
            )
            if slots:
                new["xs"], new["ys"] = made[x_out], made[y_out]
                new["xg"], new["yg"] = cube.swap(made[x_out], X), cube.swap(made[y_out], Y)
            if pair is not None:
                new["z0s"], new["z0g"] = made[pair], cube.swap(made[pair], Z0)
        if live(t + 3):
            new["z1s"] = self.shards[t + 3]
            new["z1g"] = cube.swap(self.shards[t + 3], Z1)
        if live(t - 1):

            def plan(w, s, o):
                for by in range(2):
                    yield (
                        s[by].at[:, :, pl.ds(0, 2)],
                        o[0].at[:, :, :, flip(w[Y], by), :, pl.ds(0, half)],
                    )
                    yield (
                        s[2 + by].at[:, :, pl.ds(0, 2)],
                        o[0].at[:, :, flip(w[X], by), :, :, pl.ds(half, half)],
                    )

            (most,) = local_copies(
                plan,
                [old[name] for name in ("ys", "yg", "xs", "xg")],
                [(2, 2, 2, 2, ROWS, COLUMNS)],
                [new[name] for name in ("xs", "z0s") if name in new][:1],
            )
            got = cube.swap(most, C)
            kind, arrays = self.pieces[t - 1]

            def plan_whole(w, s, o):
                for by in range(2):
                    for at, rows, columns in tiles_of(kind, arrays):
                        yield (
                            s[by].at[:, :, :, :, :, columns],
                            o[at].at[:, :, :, :, flip(w[C], by), rows],
                        )

            made = local_copies(
                plan_whole, [most, got], [(2, 2, 2, 2, 2) + array.shape for array in arrays]
            )
            self.wholes[t - 1] = [
                whole.reshape(-1, array.shape[1]) for whole, array in zip(made, arrays)
            ]
        self.state = new


ROWS, COLUMNS = 32, 4096


def uniform_shard(kind, arrays):
    if kind == "tall":
        return jnp.concatenate([arrays[0][at : at + ROWS] for at in range(0, 4 * ROWS, ROWS)], axis=1)
    spare = COLUMNS - sum(array.shape[1] for array in arrays)
    extra = [arrays[0][:, :spare]] if spare else []
    return jnp.concatenate(arrays + extra, axis=1) if len(arrays) > 1 else arrays[0]


def tiles_of(kind, arrays):
    if kind == "tall":
        width = arrays[0].shape[1]
        for at in range(4):
            yield 0, pl.ds(at * ROWS, ROWS), pl.ds(at * width, width)
    else:
        start = 0
        for at, array in enumerate(arrays):
            yield at, pl.ds(0, ROWS), pl.ds(start, array.shape[1])
            start += array.shape[1]


def added(out, out_at, first, first_at, second, second_at):
    total = first[first_at].astype(jnp.float32) + second[second_at].astype(jnp.float32)
    out[out_at] = total.astype(out.dtype)


class Scatter:
    def __init__(self, cube):
        self.cube = cube
        self.state = {}
        self.results = []
        self.queue = []

    def sums(self, sent, after):
        old = self.state
        half = COLUMNS // 2
        inputs, in_specs, names, shapes, out_specs, jobs = [], [], [], [], [], []
        mine = lambda w, at: (w[at] + sent) % 2

        def take(name, block, index):
            inputs.append(old[name])
            in_specs.append(pl.BlockSpec(block, index))
            return len(inputs) - 1

        def make(name, shape, block, index):
            names.append(name)
            shapes.append(jax.ShapeDtypeStruct(shape, jnp.bfloat16))
            out_specs.append(pl.BlockSpec(block, index))
            return len(names) - 1

        has_n, has_m = "ck" in old, "ak" in old
        slots = 2 * has_n + has_m
        corner = (None, None)
        if sent and slots:
            sent_shape = (2, 2, slots, ROWS, half)
            x_out = make("x", sent_shape, corner + sent_shape[2:], lambda a, b, w: (a, b, 0, 0, 0))
            y_out = make("y", sent_shape, corner + sent_shape[2:], lambda a, b, w: (a, b, 0, 0, 0))
        if has_n:
            left_block, right_block = corner + (2, None, ROWS, half), corner + (None, 2, ROWS, half)
            left_index = lambda a, b, w: (a, b, 0, mine(w, Y), 0, 0)
            right_index = lambda a, b, w: (a, b, mine(w, X), 0, 0, 1)
            lefts = [take(name, left_block, left_index) for name in ("ck", "cg")]
            rights = [take(name, right_block, right_index) for name in ("ck", "cg")]
            if not sent:
                kept = (2, 2, 2, ROWS, half)
                y_out = make("ak", kept, corner + kept[2:], lambda a, b, w: (a, b, 0, 0, 0))
                x_out = make("bk", kept, corner + kept[2:], lambda a, b, w: (a, b, 0, 0, 0))

            def job_n(s, o, y_out=y_out, x_out=x_out):
                for k in range(2):
                    added(o[y_out], k, s[lefts[0]], k, s[lefts[1]], k)
                    added(o[x_out], k, s[rights[0]], k, s[rights[1]], k)

            jobs.append(job_n)
        if has_m:
            block = corner + (None, ROWS, half)
            x_index = lambda a, b, w: (a, b, mine(w, X), 0, 0)
            y_index = lambda a, b, w: (a, b, mine(w, Y), 0, 0)
            lefts_m = take("ak", block, x_index), take("yg", block, x_index)
            rights_m = take("bk", block, y_index), take("xg", block, y_index)
            place = slots - 1 if sent else slice(None)
            if not sent:
                kept = (2, 2, ROWS, half)
                a_out = make("a4k", kept, corner + kept[2:], lambda a, b, w: (a, b, 0, 0))
                b_out = make("b4k", kept, corner + kept[2:], lambda a, b, w: (a, b, 0, 0))
            else:
                a_out, b_out = x_out, y_out

            def job_m(s, o):
                every = slice(None)
                added(o[a_out], place, s[lefts_m[0]], every, s[lefts_m[1]], every)
                added(o[b_out], place, s[rights_m[0]], every, s[rights_m[1]], every)

            jobs.append(job_m)
        if "a4k" in old:
            last = old["xg"].shape[2] - 1
            block = (None, None, ROWS, half)
            index = lambda a, b, w: (a, mine(w, Z0), 0, 0)
            got_block = (None, None, None, ROWS, half)
            got_index = lambda a, b, w: (a, mine(w, Z0), last, 0, 0)
            lefts_z = take("a4k", block, index), take("xg", got_block, got_index)
            rights_z = take("b4k", block, index), take("yg", got_block, got_index)
            z_out = make(
                "z" if sent else "zk",
                (2, ROWS, COLUMNS),
                (None, ROWS, COLUMNS),
                lambda a, b, w: (a, 0, 0),
            )

            def job_z(s, o):
                @pl.when(pl.program_id(1) == 0)
                def _():
                    every = slice(None)
                    left = (every, slice(0, half))
                    right = (every, slice(half, COLUMNS))
                    added(o[z_out], left, s[lefts_z[0]], every, s[lefts_z[1]], every)
                    added(o[z_out], right, s[rights_z[0]], every, s[rights_z[1]], every)

            jobs.append(job_z)
        if "zk" in old:
            block, index = (None, ROWS, COLUMNS), lambda a, b, w: (mine(w, Z1), 0, 0)
            pair = take("zk", block, index), take("zg", block, index)
            f_out = make(
                "f" if sent else "fk", (ROWS, COLUMNS), (ROWS, COLUMNS), lambda a, b, w: (0, 0)
            )

            def job_f(s, o):
                @pl.when((pl.program_id(0) == 0) & (pl.program_id(1) == 0))
                def _():
                    every = slice(None)
                    added(o[f_out], every, s[pair[0]], every, s[pair[1]], every)

            jobs.append(job_f)
        if not jobs:
            return {}

        def kernel(where, *refs):
            sources, targets = refs[: len(inputs)], refs[len(inputs) + len(after) :]
            for job in jobs:
                job(sources, targets)

        size = sum(math.prod(shape.shape) for shape in shapes)
        made = pl.pallas_call(
            kernel,
            grid_spec=pltpu.PrefetchScalarGridSpec(
                num_scalar_prefetch=1,
                grid=(2, 2),
                in_specs=in_specs + [ANY] * len(after),
                out_specs=out_specs,
            ),
            out_shape=shapes,
            cost_estimate=pl.CostEstimate(flops=size, bytes_accessed=6 * size, transcendentals=0),
            compiler_params=pltpu.CompilerParams(vmem_limit_bytes=9 << 20),
        )(self.cube.where, *inputs, *after)
        return dict(zip(names, made))

    def stage(self, piece=None):
        cube, old, new = self.cube, self.state, {}
        if not cube.tuned:
            if piece is not None:
                self.results.append(
                    [
                        lax.psum_scatter(grad, AXES, scatter_dimension=0, tiled=True).astype(
                            jnp.float32
                        )
                        for grad in piece[2]
                    ]
                )
            return
        sends = self.sums(1, [])
        for name, at, got in (("x", X, "xg"), ("y", Y, "yg"), ("z", Z0, "zg"), ("f", Z1, "fg")):
            if name in sends:
                new[got] = cube.swap(sends[name], at)
        first = list(sends.values())[:1]
        new.update(self.sums(0, first))
        if "fk" in old:
            kind, arrays = self.queue.pop(0)
            total = old["fk"].astype(jnp.float32) + old["fg"].astype(jnp.float32)
            self.results.append(split_shard(kind, arrays, total))
        if piece is not None:
            kind, arrays, grads = piece
            self.queue.append((kind, arrays))
            bits = [
                grad.reshape((2, 2, 2, 2, 2) + array.shape) for grad, array in zip(grads, arrays)
            ]

            def plan(w, s, o):
                for sent in range(2):
                    for at, rows, columns in tiles_of(kind, arrays):
                        yield (
                            s[at].at[:, :, :, :, flip(w[C], sent), rows],
                            o[sent].at[:, :, :, :, :, columns],
                        )
                    spare = COLUMNS - sum(array.size for array in arrays) // ROWS
                    if spare:
                        yield (
                            s[0].at[:, :, :, :, flip(w[C], sent), :, pl.ds(0, spare)],
                            o[sent].at[:, :, :, :, :, pl.ds(COLUMNS - spare, spare)],
                        )

            keep, send = local_copies(plan, bits, [(2, 2, 2, 2, ROWS, COLUMNS)] * 2, first)
            new["ck"], new["cg"] = keep, cube.swap(send, C)
        self.state = new


def split_shard(kind, arrays, total):
    if kind == "tall":
        width = arrays[0].shape[1]
        return [jnp.concatenate([total[:, at * width : (at + 1) * width] for at in range(4)], axis=0)]
    parts, start = [], 0
    for array in arrays:
        parts.append(total[:, start : start + array.shape[1]])
        start += array.shape[1]
    return parts


class HeadScattering:
    def __init__(self, cube, values, rows):
        self.cube = cube
        if not cube.tuned:
            self.whole = values
            return
        half = values.shape[1] // 2
        self.parts = [
            Summing(cube, values[:, :half].reshape(2, 2, 2, rows, half), (X, Z0, Z1)),
            Summing(cube, values[:, half:].reshape(2, 2, 2, rows, half), (Z0, Z1, X)),
        ]

    @property
    def state(self):
        return [part.state for part in self.parts] if self.cube.tuned else [self.whole]

    @state.setter
    def state(self, values):
        if not self.cube.tuned:
            self.whole = values[0]
            return
        for part, state in zip(self.parts, values):
            part.state = state

    def step(self):
        if self.cube.tuned:
            for part in self.parts:
                part.step()

    def result(self):
        if not self.cube.tuned:
            return lax.psum_scatter(self.whole, "dp", scatter_dimension=0, tiled=True).astype(
                jnp.float32
            )
        return jnp.concatenate([part.result() for part in self.parts], axis=1)


def shifted(pad_ref, shift_ref, rows):
    for r in range(8):
        shift_ref[r] = pad_ref[r : r + rows, :]


def conv_forward_kernel(lead_ref, gate_ref, valid_ref, taps_ref, conv_ref, sums_ref, pad, shift):
    length, width = lead_ref.shape
    edge = jnp.zeros((16, width), jnp.float32)
    valid = valid_ref[...]
    pad[0:16, :] = edge
    pad[16 : 16 + length, :] = lead_ref[...] * jax.nn.sigmoid(gate_ref[...]) * valid
    pad[16 + length : 40 + length, :] = jnp.zeros((24, width), jnp.float32)
    shifted(pad, shift, length + 32)
    chunk = 64
    taps = [taps_ref[j : j + 1, :] for j in range(32)]

    def step(at, totals):
        start = pl.multiple_of(at * chunk, chunk)
        total = jnp.zeros((chunk, width), jnp.float32)
        for j in range(32):
            total += shift[j % 8, pl.ds(start + j // 8 * 8, chunk), :] * taps[j]
        conv_ref[pl.ds(start, chunk), :] = total
        weighted = total * valid_ref[pl.ds(start, chunk), :]
        plain, squares = totals
        return (
            plain + jnp.sum(weighted, axis=0, keepdims=True),
            squares + jnp.sum(weighted * total, axis=0, keepdims=True),
        )

    zero = jnp.zeros((1, width), jnp.float32)
    plain, squares = lax.fori_loop(0, length // chunk, step, (zero, zero))
    sums_ref[0:1, :] = plain
    sums_ref[1:2, :] = squares
    sums_ref[2:3, :] = jnp.broadcast_to(jnp.sum(valid, axis=0, keepdims=True), (1, width))
    sums_ref[3:8, :] = jnp.zeros((5, width), jnp.float32)


def conv_forward(expanded, valid, taps):
    rows = expanded.shape[0]
    width = 128
    count = D // width
    return pl.pallas_call(
        conv_forward_kernel,
        grid=(count,),
        in_specs=[
            pl.BlockSpec((rows, width), lambda i: (0, i)),
            pl.BlockSpec((rows, width), lambda i: (0, i + count)),
            pl.BlockSpec((rows, 1), lambda i: (0, 0)),
            pl.BlockSpec((TAPS + 16, width), lambda i: (0, i)),
        ],
        out_specs=[
            pl.BlockSpec((rows, width), lambda i: (0, i)),
            pl.BlockSpec((8, width), lambda i: (0, i)),
        ],
        out_shape=[
            jax.ShapeDtypeStruct((rows, D), jnp.float32),
            jax.ShapeDtypeStruct((8, D), jnp.float32),
        ],
        scratch_shapes=[
            pltpu.VMEM((rows + 40, width), jnp.float32),
            pltpu.VMEM((8, rows + 32, width), jnp.float32),
        ],
        cost_estimate=pl.CostEstimate(
            flops=80 * rows * D, bytes_accessed=16 * rows * D, transcendentals=rows * D
        ),
        compiler_params=pltpu.CompilerParams(vmem_limit_bytes=8 << 20),
    )(expanded, expanded, valid, taps)


def conv_backward_kernel(
    lead_ref,
    gate_ref,
    valid_ref,
    taps_ref,
    conv_ref,
    grad_ref,
    sums_ref,
    back_sums_ref,
    out_lead_ref,
    out_gate_ref,
    taps_grad_ref,
    pad,
    shift,
    tap_sums,
):
    length, width = lead_ref.shape
    count = sums_ref[2:3, :]
    mean = sums_ref[0:1, :] / count
    inverse = lax.rsqrt(sums_ref[1:2, :] / count - mean * mean + eps)
    variance_grad = -0.5 * inverse * inverse * back_sums_ref[1:2, :]
    plain = (-inverse * back_sums_ref[0:1, :] - 2.0 * mean * variance_grad) / count
    scaled = 2.0 * variance_grad / count
    pad[0:16, :] = jnp.zeros((16, width), jnp.float32)
    pad[16 : 16 + length, :] = (
        grad_ref[...] * inverse + (plain + scaled * conv_ref[...]) * valid_ref[...]
    )
    pad[16 + length : 40 + length, :] = jnp.zeros((24, width), jnp.float32)
    shifted(pad, shift, length + 32)
    tap_sums[...] = jnp.zeros(tap_sums.shape, jnp.float32)
    chunk = 64
    taps = [taps_ref[j : j + 1, :] for j in range(32)]

    def step(at, carry):
        start = pl.multiple_of(at * chunk, chunk)
        here = pl.ds(start, chunk)
        lead, valid = lead_ref[here, :], valid_ref[here, :]
        gate = jax.nn.sigmoid(gate_ref[here, :])
        gated = lead * gate * valid
        total = jnp.zeros((chunk, width), jnp.float32)
        for j in range(32):
            off = 32 - j
            part = shift[off % 8, pl.ds(start + off // 8 * 8, chunk), :]
            total += part * taps[j]
            tap_sums[j] += jnp.sum((part * gated).reshape(chunk // 8, 8, width), axis=0)
        grad = total * valid
        out_lead_ref[here, :] = (grad * gate).astype(jnp.bfloat16)
        out_gate_ref[here, :] = (grad * lead * gate * (1.0 - gate)).astype(jnp.bfloat16)
        return carry

    lax.fori_loop(0, length // chunk, step, 0)
    taps_grad_ref[...] = jnp.sum(tap_sums[...], axis=1)


def conv_backward(expanded, valid, taps, conv_out, grads, sums, back_sums):
    rows = expanded.shape[0]
    width = 128
    count = D // width
    block = pl.BlockSpec((rows, width), lambda i: (0, i))
    return pl.pallas_call(
        conv_backward_kernel,
        grid=(count,),
        in_specs=[
            block,
            pl.BlockSpec((rows, width), lambda i: (0, i + count)),
            pl.BlockSpec((rows, 1), lambda i: (0, 0)),
            pl.BlockSpec((TAPS + 16, width), lambda i: (0, i)),
            block,
            block,
            pl.BlockSpec((8, width), lambda i: (0, i)),
            pl.BlockSpec((8, width), lambda i: (0, i)),
        ],
        out_specs=[block, block, pl.BlockSpec((TAPS, width), lambda i: (0, i))],
        out_shape=[
            jax.ShapeDtypeStruct((rows, D), jnp.bfloat16),
            jax.ShapeDtypeStruct((rows, D), jnp.bfloat16),
            jax.ShapeDtypeStruct((32, D), jnp.float32),
        ],
        scratch_shapes=[
            pltpu.VMEM((rows + 40, width), jnp.float32),
            pltpu.VMEM((8, rows + 32, width), jnp.float32),
            pltpu.VMEM((32, 8, width), jnp.float32),
        ],
        cost_estimate=pl.CostEstimate(
            flops=160 * rows * D, bytes_accessed=20 * rows * D, transcendentals=rows * D
        ),
        compiler_params=pltpu.CompilerParams(vmem_limit_bytes=8 << 20),
    )(expanded, expanded, valid, taps, conv_out, grads, sums, back_sums)


def nt_dot(left, right):
    return lax.dot_general(left, right, (((1,), (1,)), ((), ())), preferred_element_type=jnp.float32)


def act_back_kernel(grad_ref, weight_ref, pre_ref, out_ref):
    pre = pre_ref[...].astype(jnp.float32)
    gate = jax.nn.sigmoid(pre)
    slope = gate * (1.0 + pre * (1.0 - gate))
    out_ref[...] = (nt_dot(grad_ref[...], weight_ref[...]) * slope).astype(jnp.bfloat16)


def act_back(grad_lo, weight, pre):
    rows, inner = grad_lo.shape
    total = weight.shape[0]
    width = min(512, total)
    return pl.pallas_call(
        act_back_kernel,
        grid=(total // width,),
        in_specs=[
            pl.BlockSpec((rows, inner), lambda i: (0, 0)),
            pl.BlockSpec((width, inner), lambda i: (i, 0)),
            pl.BlockSpec((rows, width), lambda i: (0, i)),
        ],
        out_specs=pl.BlockSpec((rows, width), lambda i: (0, i)),
        out_shape=jax.ShapeDtypeStruct((rows, total), jnp.bfloat16),
        cost_estimate=pl.CostEstimate(
            flops=2 * rows * inner * total,
            bytes_accessed=2 * total * (inner + 2 * rows),
            transcendentals=rows * total,
        ),
        compiler_params=pltpu.CompilerParams(vmem_limit_bytes=10 << 20),
    )(grad_lo, weight, pre)


def norm_back_kernel(
    row, grad_ref, weight_ref, values_ref, vectors_ref, above_ref, out_ref, gain_out, total
):
    step = pl.program_id(0)

    @pl.when(step == 0)
    def _():
        total[...] = jnp.zeros(total.shape, jnp.float32)

    total[...] += nt_dot(grad_ref[...], weight_ref[...])

    @pl.when(step == pl.num_programs(0) - 1)
    def _():
        rows = 128
        gain = vectors_ref[TAPS + row : TAPS + row + 1, :]

        def part(at, gain_total):
            here = pl.ds(pl.multiple_of(at * rows, rows), rows)
            values, grads = values_ref[here, :], total[here, :]
            center = values - jnp.mean(values, axis=-1, keepdims=True)
            scale = lax.rsqrt(jnp.mean(center * center, axis=-1, keepdims=True) + eps)
            normed = center * scale
            scaled = grads * gain
            mean = jnp.mean(scaled, axis=-1, keepdims=True)
            along = jnp.mean(scaled * normed, axis=-1, keepdims=True)
            out_ref[here, :] = above_ref[here, :] + (scaled - mean - normed * along) * scale
            return gain_total + jnp.sum(grads * normed, axis=0, keepdims=True)

        gain_out[...] = lax.fori_loop(
            0, total.shape[0] // rows, part, jnp.zeros(gain_out.shape, jnp.float32)
        )


def product_norm_back(grad_lo, weight, values, vectors, row, above):
    rows, inner = grad_lo.shape
    width = 512
    whole, vector = VMEM, VMEM
    return pl.pallas_call(
        functools.partial(norm_back_kernel, row),
        grid=(inner // width,),
        in_specs=[
            pl.BlockSpec((rows, width), lambda i: (0, i)),
            pl.BlockSpec((D, width), lambda i: (0, i)),
            whole,
            vector,
            whole,
        ],
        out_specs=[whole, vector],
        out_shape=[
            jax.ShapeDtypeStruct((rows, D), jnp.float32),
            jax.ShapeDtypeStruct((1, D), jnp.float32),
        ],
        scratch_shapes=[pltpu.VMEM((rows, D), jnp.float32)],
        cost_estimate=pl.CostEstimate(
            flops=2 * rows * inner * D,
            bytes_accessed=2 * inner * (D + rows) + 12 * rows * D,
            transcendentals=0,
        ),
        compiler_params=pltpu.CompilerParams(vmem_limit_bytes=14 << 20),
    )(grad_lo, weight, values, vectors, above)


def turned(values, cosine, sine):
    half = HD // 2
    lead, tail = values[:, :half], values[:, half:]
    return jnp.concatenate([lead * cosine - tail * sine, tail * cosine + lead * sine], axis=1)


def attend_kernel(
    query_ref, key_ref, value_ref, cosine_ref, sine_ref, bias_ref, out_ref, query_out, key_out, value_out, log_out
):
    cosine, sine = cosine_ref[...], sine_ref[...]
    query = turned(query_ref[...], cosine, sine).astype(jnp.bfloat16)
    key = turned(key_ref[...], cosine, sine).astype(jnp.bfloat16)
    value = value_ref[...].astype(jnp.bfloat16)
    query_out[...], key_out[...], value_out[...] = query, key, value
    scores = jnp.where(bias_ref[...] > 0, nt_dot(query, key) * HD**-0.5, -1e30)
    top = jnp.max(scores, axis=-1, keepdims=True)
    weights = jnp.exp(scores - top)
    total = jnp.sum(weights, axis=-1, keepdims=True)
    probs = (weights * (1.0 / total)).astype(jnp.bfloat16)
    out_ref[...] = jnp.dot(probs, value, preferred_element_type=jnp.float32).astype(jnp.bfloat16)
    log_out[...] = jnp.broadcast_to(top + jnp.log(total), log_out.shape)


def attend(mixed, cosine, sine, valid):
    rows = mixed.shape[0]
    head = lambda shift: pl.BlockSpec((rows, HD), lambda i: (0, i + shift))
    fixed = lambda *shape: pl.BlockSpec(shape, lambda i: (0, 0))
    return pl.pallas_call(
        attend_kernel,
        grid=(H,),
        in_specs=[
            head(0),
            head(H),
            head(2 * H),
            fixed(rows, HD // 2),
            fixed(rows, HD // 2),
            fixed(1, rows),
        ],
        out_specs=[head(0)] * 5,
        out_shape=[jax.ShapeDtypeStruct((rows, D), jnp.bfloat16)] * 4
        + [jax.ShapeDtypeStruct((rows, D), jnp.float32)],
        cost_estimate=pl.CostEstimate(
            flops=4 * rows * rows * D,
            bytes_accessed=28 * rows * D,
            transcendentals=rows * rows * H,
        ),
        compiler_params=pltpu.CompilerParams(vmem_limit_bytes=12 << 20),
    )(mixed, mixed, mixed, cosine, sine, valid)


def attend_back_kernel(
    query_ref, key_ref, value_ref, log_ref, grad_ref, cosine_ref, sine_ref, bias_ref, query_out, key_out, value_out
):
    query, key, value, grad = query_ref[...], key_ref[...], value_ref[...], grad_ref[...]
    cosine, sine = cosine_ref[...], -sine_ref[...]
    scores = jnp.where(bias_ref[...] > 0, nt_dot(query, key) * HD**-0.5, -1e30)
    probs = jnp.exp(scores - log_ref[:, :1])
    grad_probs = nt_dot(grad, value)
    along = jnp.sum(probs * grad_probs, axis=-1, keepdims=True)
    grad_scores = (probs * (grad_probs - along)).astype(jnp.bfloat16)
    value_out[...] = matmul_tn(probs.astype(jnp.bfloat16), grad).astype(jnp.bfloat16)
    query_grad = matmul(grad_scores, key) * HD**-0.5
    key_grad = matmul_tn(grad_scores, query) * HD**-0.5
    query_out[...] = turned(query_grad, cosine, sine).astype(jnp.bfloat16)
    key_out[...] = turned(key_grad, cosine, sine).astype(jnp.bfloat16)


def attend_back(query, key, value, logs, grads, cosine, sine, valid):
    rows = query.shape[0]
    head = pl.BlockSpec((rows, HD), lambda i: (0, i))
    fixed = lambda *shape: pl.BlockSpec(shape, lambda i: (0, 0))
    return pl.pallas_call(
        attend_back_kernel,
        grid=(H,),
        in_specs=[head] * 5
        + [fixed(rows, HD // 2), fixed(rows, HD // 2), fixed(1, rows)],
        out_specs=[head] * 3,
        out_shape=[jax.ShapeDtypeStruct((rows, D), jnp.bfloat16)] * 3,
        cost_estimate=pl.CostEstimate(
            flops=10 * rows * rows * D,
            bytes_accessed=18 * rows * D,
            transcendentals=rows * rows * H,
        ),
        compiler_params=pltpu.CompilerParams(vmem_limit_bytes=12 << 20),
    )(query, key, value, logs, grads, cosine, sine, valid)


def fence(flows, *values):
    states, values = lax.optimization_barrier(([flow.state for flow in flows], values))
    for flow, state in zip(flows, states):
        flow.state = state
    return values[0] if len(values) == 1 else values


def rows_of(values, count):
    return values.reshape(count, values.shape[-1])


def shards(
    sizes,
    frames,
    ffn_inner,
    ffn_outer,
    attn_qkv,
    attn_proj,
    conv_expand,
    conv_depth,
    conv_proj,
    norm_gains,
    head_proj,
    lengths,
    mask_starts,
    target_codes,
    out_grad,
):
    cube = Cube(sizes)
    cube.where = lax.optimization_barrier(cube.place()) if cube.tuned else None
    devices = sizes["dp"] * sizes["head"]
    ff = ffn_inner.shape[2]
    all_bits = list(range(len(cube.bits)))

    rows_in = Gather(
        cube,
        [
            ("wide", [ffn_inner[0]]),
            ("tall", [ffn_outer[0]]),
            ("wide", [attn_qkv, attn_proj]),
            ("wide", [conv_expand, conv_proj]),
            ("wide", [ffn_inner[1]]),
            ("tall", [ffn_outer[1]]),
        ],
    )
    head_half = head_proj.shape[1] // 2
    heads = [
        HeadGathering(cube, head_proj[:, :head_half]),
        HeadGathering(cube, head_proj[:, head_half:]),
    ]

    row_total = UTT_DEV * SEQ
    positions = jnp.arange(SEQ, dtype=jnp.int32)
    valid_mat = positions[None, :] < lengths[:, None]
    valid_rows = valid_mat.reshape(row_total).astype(jnp.float32)
    frequency = 10000.0 ** (-(jnp.arange(HD // 2, dtype=jnp.float32) * 2.0) / HD)
    angles = positions.astype(jnp.float32)[:, None] * frequency[None, :]
    cosine, sine_table = jnp.cos(angles), jnp.sin(angles)

    slots = UTT_DEV * NSPAN * SPAN
    slot_at = (mask_starts[:, :, None] + jnp.arange(SPAN, dtype=jnp.int32)).reshape(UTT_DEV, -1)
    slot_ok = slot_at < lengths[:, None]
    chosen = (slot_at + SEQ * jnp.arange(UTT_DEV, dtype=jnp.int32)[:, None]).reshape(slots)
    slot_live = slot_ok.reshape(slots)
    pick = (
        (chosen[:, None] == jnp.arange(row_total, dtype=jnp.int32)[None, :]) & slot_live[:, None]
    )
    picked_codes = jnp.sum(jnp.where(pick, target_codes[None, :], 0), axis=1)
    picked_codes = jnp.where(slot_live, picked_codes, -1)
    pick_lo = pick.astype(jnp.bfloat16)
    head_order = [at for at in range(len(cube.bits)) if cube.bits[at][0] == "head"]
    group = sizes["head"]
    vocab_cols = head_proj.shape[1]

    loss_scale = jnp.float32(devices * UTT_DEV * NSPAN * SPAN)
    hops = [C, Z1, Z0, X, Y] if cube.tuned else all_bits
    vector_in = VectorGathering(cube, jnp.concatenate([conv_depth, norm_gains, jnp.zeros_like(conv_depth[:10])], axis=0), hops)
    vector_in.step(2)
    group_codes = cube.gather(picked_codes, head_order).reshape(group * slots)
    rows_in.stage(-3)
    heads[0].step("x")
    heads[1].step("x")
    group_codes = fence([rows_in, vector_in, *heads], group_codes)

    rows_in.stage(-2)
    vector_in.step()
    fence([rows_in, vector_in], loss_scale)

    rows_in.stage(-1)
    vector_in.step()
    inputs = frames.astype(jnp.float32)
    fence([rows_in, vector_in], loss_scale)

    rows_in.stage(0)
    vector_in.step(len(hops))
    fence([rows_in, vector_in], loss_scale)
    (vectors,) = vector_in.state
    vectors = fence([], joined_vectors(vectors.reshape((devices,) + vectors.shape[-2:])))
    gain_f = vectors[TAPS : TAPS + 6]
    norm_first = lowered(layer_norm(inputs, gain_f[0]))
    group_live = (group_codes >= 0).astype(jnp.float32)
    local_codes = group_codes - lax.axis_index("head") * vocab_cols

    rows_in.stage(1)
    (inner_0,) = rows_in.wholes[0]
    pre_first = matmul(norm_first, inner_0)
    act_first = lowered(jax.nn.silu(pre_first))
    pre_first = lowered(pre_first)
    pre_first, act_first = fence([rows_in], pre_first, act_first)

    rows_in.stage(2)
    (outer_0,) = rows_in.wholes[1]
    after_first = inputs + 0.5 * matmul(act_first, outer_0)
    norm_attn = lowered(layer_norm(after_first, gain_f[1]))
    after_first, norm_attn = fence([rows_in], after_first, norm_attn)

    rows_in.stage(3)
    heads[0].step("far")
    mix_weight, proj_weight = rows_in.wholes[2]
    mixed = matmul(norm_attn, mix_weight)
    attended_lo, queries, key_rows, value_rows, log_totals = attend(
        mixed, cosine, sine_table, valid_rows[None, :]
    )
    after_attention = after_first + matmul(attended_lo, proj_weight)
    norm_conv = lowered(layer_norm(after_attention, gain_f[2]))
    after_attention, norm_conv, attended_lo, queries, key_rows, value_rows, log_totals = fence(
        [rows_in, heads[0]],
        after_attention,
        norm_conv,
        attended_lo,
        queries,
        key_rows,
        value_rows,
        log_totals,
    )

    rows_in.stage(4)
    heads[0].step("near")
    heads[1].step("far")
    expand_weight, conv_weight = rows_in.wholes[3]
    expanded = matmul(norm_conv, expand_weight)
    conv_out, conv_sums = conv_forward(expanded, valid_rows[:, None], vectors)
    sums = cube.total(conv_sums)
    sums, conv_out, after_attention, expanded, norm_conv = fence(
        [rows_in, *heads], sums, conv_out, after_attention, expanded, norm_conv
    )

    rows_in.stage(5)
    heads[1].step("near")
    (inner_1,) = rows_in.wholes[4]
    frame_count = sums[2, 0]
    channel_mean = sums[0] / frame_count
    variance = sums[1] / frame_count - channel_mean * channel_mean
    inverse = lax.rsqrt(variance + eps)
    normalized = (conv_out - channel_mean) * inverse
    normed_bn = normalized * gain_f[3]
    swish_lo = lowered(jax.nn.silu(normed_bn))
    after_conv = after_attention + matmul(swish_lo, conv_weight)
    norm_second = lowered(layer_norm(after_conv, gain_f[4]))
    pre_second = matmul(norm_second, inner_1)
    act_second = lowered(jax.nn.silu(pre_second))
    pre_second = lowered(pre_second)
    after_conv, norm_second, pre_second, act_second, swish_lo = fence(
        [rows_in, *heads], after_conv, norm_second, pre_second, act_second, swish_lo
    )

    rows_in.stage(6)
    (outer_1,) = rows_in.wholes[5]
    head_cols = joined_heads(cube, heads)
    after_second = after_conv + 0.5 * matmul(act_second, outer_1)
    output_lo = lowered(layer_norm(after_second, gain_f[5]))

    picked_rows = lowered(matmul(pick_lo, output_lo))
    group_rows = cube.gather(picked_rows, head_order).reshape(group * slots, D)
    logits = matmul(group_rows, head_cols)
    row_top = jnp.max(logits, axis=1)
    row_sum = jnp.sum(jnp.exp(logits - row_top[:, None]), axis=1)
    onehot = jnp.arange(vocab_cols, dtype=jnp.int32)[None, :] == local_codes[:, None]
    target_logit = jnp.sum(jnp.where(onehot, logits, 0.0), axis=1)
    stats = cube.gather(jnp.stack([row_top, row_sum, target_logit]), head_order)
    stats = stats.reshape(group, 3, group * slots)
    whole_top = jnp.max(stats[:, 0], axis=0)
    whole_sum = jnp.sum(stats[:, 1] * jnp.exp(stats[:, 0] - whole_top), axis=0)
    log_norm = whole_top + jnp.log(whole_sum)
    ce_group = jnp.sum((log_norm - jnp.sum(stats[:, 2], axis=0)) * group_live)
    grad_logits = lowered(
        (jnp.exp(logits - log_norm[:, None]) - onehot.astype(jnp.float32)) * group_live[:, None]
    )
    head_grad = lowered(matmul_tn(group_rows, grad_logits))
    head_flow = HeadScattering(cube, head_grad, head_proj.shape[0])
    row_grads = lowered(matmul_nt(grad_logits, head_cols))
    row_sum = Summing(cube, row_grads.reshape((2,) * len(head_order) + (slots, D)), head_order[::-1])
    head_flow.step()
    for _ in head_order:
        row_sum.step()
    row_grads = lowered(row_sum.result())
    grad_output = out_grad.astype(jnp.float32) + matmul_tn(pick_lo, row_grads)

    def outer_back(grad_in, act_lo):
        grad_out_lo = lowered(0.5 * grad_in)
        weight_grad = lowered(matmul_tn(act_lo, grad_out_lo))
        return grad_out_lo, ("tall", [ffn_outer[0]], [weight_grad])

    def inner_back(grad_out_lo, normed_lo, pre_act, outer_weight):
        grad_pre = act_back(grad_out_lo, outer_weight, pre_act)
        weight_grad = lowered(matmul_tn(normed_lo, grad_pre))
        return grad_pre, ("wide", [ffn_inner[0]], [weight_grad])

    rows_out = Scatter(cube)
    grad_second, gain_grad_final = norm_back(after_second, gain_f[5], grad_output)
    grad_out_lo, piece = outer_back(grad_second, act_second)
    grad_second, grad_out_lo, piece[2][0] = fence(
        [head_flow], grad_second, grad_out_lo, piece[2][0]
    )

    head_flow.step()
    rows_out.stage(piece)
    grad_pre, piece = inner_back(grad_out_lo, norm_second, pre_second, outer_1)
    grad_conv_res, gain_grad_second = product_norm_back(
        grad_pre, inner_1, after_conv, vectors, 4, grad_second
    )
    grad_conv_res, piece[2][0] = fence([head_flow, rows_out], grad_conv_res, piece[2][0])

    conv_res_lo = lowered(grad_conv_res)
    grad_bn = silu_back(normed_bn, matmul_nt(conv_res_lo, conv_weight))
    gain_grad_bn = jnp.sum(grad_bn * normalized, axis=0)
    grad_normalized = grad_bn * gain_f[3]
    back_sums = cube.total(
        jnp.stack(
            [
                jnp.sum(grad_normalized, axis=0),
                jnp.sum(grad_normalized * normalized, axis=0),
                jnp.broadcast_to(ce_group / group, (D,)),
            ]
            + [jnp.zeros((D,), jnp.float32)] * 5
        )
    )
    conv_proj_grad = lowered(matmul_tn(swish_lo, conv_res_lo))
    back_sums, grad_normalized, grad_conv_res, conv_proj_grad = fence(
        [],
        back_sums,
        grad_normalized,
        grad_conv_res,
        conv_proj_grad,
    )

    head_flow.step()
    rows_out.stage(piece)
    loss = back_sums[2, 0] / loss_scale
    grad_lead, grad_gate, depth_grad = conv_backward(
        expanded, valid_rows[:, None], vectors, conv_out, grad_normalized, sums, back_sums
    )
    grad_expanded = jnp.concatenate([grad_lead, grad_gate], axis=1)
    expand_grad = lowered(matmul_tn(norm_conv, grad_expanded))
    grad_expanded, expand_grad = fence([rows_out, head_flow], grad_expanded, expand_grad)

    rows_out.stage(("wide", [conv_expand, conv_proj], [expand_grad, conv_proj_grad]))
    grad_attn_res, gain_grad_conv = product_norm_back(
        grad_expanded, expand_weight, after_attention, vectors, 2, grad_conv_res
    )
    attn_res_lo = lowered(grad_attn_res)
    proj_grad = lowered(matmul_tn(attended_lo, attn_res_lo))
    grad_attended = lowered(matmul_nt(attn_res_lo, proj_weight))
    grad_mixed = jnp.concatenate(
        attend_back(
            queries,
            key_rows,
            value_rows,
            log_totals,
            grad_attended,
            cosine,
            sine_table,
            valid_rows[None, :],
        ),
        axis=1,
    )
    grad_mixed, proj_grad, grad_attn_res = fence([rows_out], grad_mixed, proj_grad, grad_attn_res)

    rows_out.stage()
    mix_grad = lowered(matmul_tn(norm_attn, grad_mixed))
    grad_first_res, gain_grad_attn = product_norm_back(
        grad_mixed, mix_weight, after_first, vectors, 1, grad_attn_res
    )
    grad_first_res, mix_grad = fence([rows_out], grad_first_res, mix_grad)

    rows_out.stage(("wide", [attn_qkv, attn_proj], [mix_grad, proj_grad]))
    grad_out_lo, piece = outer_back(grad_first_res, act_first)
    grad_out_lo, piece[2][0] = fence([rows_out], grad_out_lo, piece[2][0])

    rows_out.stage(piece)
    grad_pre, piece = inner_back(grad_out_lo, norm_first, pre_first, outer_0)
    grad_pre, piece[2][0] = fence([rows_out], grad_pre, piece[2][0])

    rows_out.stage(piece)
    input_grad, gain_grad_first = product_norm_back(
        grad_pre, inner_0, inputs, vectors, 0, grad_first_res
    )
    vector_grad = parted_vectors(
        [
            depth_grad,
            gain_grad_first,
            gain_grad_attn,
            gain_grad_conv,
            gain_grad_bn.reshape(1, D),
            gain_grad_second,
            gain_grad_final.reshape(1, D),
        ],
        devices,
    )
    vector_flow = Summing(
        cube, vector_grad.reshape((2,) * len(cube.bits) + vector_grad.shape[1:]), hops
    )
    vector_flow.step()
    vector_flow.step()
    input_grad = fence([rows_out, vector_flow], input_grad)

    for _ in range(4):
        rows_out.stage()
        if vector_flow.order:
            vector_flow.step()
        fence([rows_out, vector_flow], loss)
    for _ in vector_flow.order[:]:
        vector_flow.step()
    vector_grad = vector_flow.result()
    rows_out.stage()
    (
        (outer_grad_1,),
        (inner_grad_1,),
        (expand_grad, conv_proj_grad),
        (mix_grad, proj_grad),
        (outer_grad_0,),
        (inner_grad_0,),
    ) = rows_out.results
    return (
        output_lo,
        loss,
        input_grad,
        jnp.stack([inner_grad_0, inner_grad_1], axis=0),
        jnp.stack([outer_grad_0, outer_grad_1], axis=0),
        mix_grad,
        proj_grad,
        expand_grad,
        vector_grad[:TAPS],
        conv_proj_grad,
        vector_grad[TAPS:],
        head_flow.result(),
    )


def solution(mesh):
    placed = (
        P(("dp", "head"), None),
        P(None, ("dp", "head"), None),
        P(None, ("dp", "head"), None),
        P(("dp", "head"), None),
        P(("dp", "head"), None),
        P(("dp", "head"), None),
        P(None, ("dp", "head")),
        P(("dp", "head"), None),
        P(None, ("dp", "head")),
        P("dp", "head"),
        P(("dp", "head")),
        P(("dp", "head"), None),
        P(("dp", "head")),
        P(("dp", "head"), None),
    )
    sizes = {axis: mesh.shape[axis] for axis in AXES}
    return jax.shard_map(
        functools.partial(shards, sizes),
        mesh=mesh,
        in_specs=placed,
        out_specs=(
            P(("dp", "head"), None),
            P(),
            P(("dp", "head"), None),
            P(None, ("dp", "head"), None),
            P(None, ("dp", "head"), None),
            P(("dp", "head"), None),
            P(("dp", "head"), None),
            P(("dp", "head"), None),
            P(None, ("dp", "head")),
            P(("dp", "head"), None),
            P(None, ("dp", "head")),
            P("dp", "head"),
        ),
        check_vma=False,
    )
```

```python
import functools
import math

import jax
import jax.numpy as jnp
from jax import lax
from jax.experimental import pallas as pl
from jax.experimental.pallas import tpu as pltpu
from jax.sharding import PartitionSpec as P

D = 1024
H = 8
HD = 128
VOCAB = 8192
SEQ = 512
SPAN = 10
NSPAN = 20
UTT_DEV = 1


eps = 1e-05


def layer_norm(values, gain_row):
    center = values - jnp.mean(values, axis=-1, keepdims=True)
    variance = jnp.mean(center * center, axis=-1, keepdims=True)
    return center * lax.rsqrt(variance + eps) * gain_row


def lowered(values):
    return values.astype(jnp.bfloat16)


def matmul(operand, weight):
    return jnp.dot(operand, weight, preferred_element_type=jnp.float32)


def matmul_tn(operand, weight):
    return lax.dot_general(
        operand, weight, (((0,), (0,)), ((), ())), preferred_element_type=jnp.float32
    )


def matmul_nt(operand, weight):
    return lax.dot_general(
        operand, weight, (((1,), (1,)), ((), ())), preferred_element_type=jnp.float32
    )


def norm_back(values, gain_row, grads):
    unused, pullback = jax.vjp(layer_norm, values, gain_row)
    return pullback(grads)


def silu_back(values, grads):
    return jax.vjp(jax.nn.silu, values)[1](grads)[0]


AXES = ("dp", "head")
BRIEF = pl.CostEstimate(flops=0, bytes_accessed=0, transcendentals=0)
ANY = pl.BlockSpec(memory_space=pl.ANY)
VMEM = pl.BlockSpec(memory_space=pltpu.VMEM)
Z1, Z0, X, Y, C = range(5)


def local_copies(plan, inputs, outputs, after=()):
    count = len(inputs)

    def kernel(*refs):
        sources, targets, sem = refs[:count], refs[count + len(after) : -1], refs[-1]
        dp, head = lax.axis_index("dp"), lax.axis_index("head")
        where = (dp // 4, dp // 2 % 2, dp % 2, head // 2, head % 2)
        copies = []
        for at, (source, target) in enumerate(plan(where, sources, targets)):
            copies.append(pltpu.make_async_copy(source, target, sem.at[at]))
            copies[-1].start()
        for copy in copies:
            copy.wait()

    size = sum(math.prod(shape) for shape in outputs) * inputs[0].dtype.itemsize
    results = pl.pallas_call(
        kernel,
        out_shape=[jax.ShapeDtypeStruct(shape, inputs[0].dtype) for shape in outputs],
        in_specs=[ANY] * (count + len(after)),
        out_specs=[VMEM] * len(outputs),
        scratch_shapes=[pltpu.SemaphoreType.DMA((16,))],
        cost_estimate=BRIEF,
        compiler_params=pltpu.CompilerParams(vmem_limit_bytes=size + (1 << 20)),
    )(*inputs, *after)
    return list(results)


def flip(bit, by):
    return (bit + by) % 2


class Cube:
    def __init__(self, sizes):
        self.sizes = sizes
        self.tuned = sizes == {"dp": 8, "head": 4}
        self.bits = []
        for axis in AXES:
            bit = sizes[axis] // 2
            while bit:
                self.bits.append((axis, bit))
                bit //= 2

    def mine(self, at):
        axis, bit = self.bits[at]
        return (lax.axis_index(axis) // bit) % 2

    def swap(self, values, at):
        axis, bit = self.bits[at]
        return lax.ppermute(values, axis, [(i, i ^ bit) for i in range(self.sizes[axis])])

    def gather(self, shard, order):
        held = []
        values = shard
        for at in order:
            place = sum(other < at for other in held)
            values = self.join(values, self.swap(values, at), at, place)
            held.append(at)
        return values

    def join(self, values, got, at, place):
        if self.tuned and values.dtype != jnp.int32:
            shape = values.shape[:place] + (2,) + values.shape[place:]

            def plan(where, sources, targets):
                for by in range(2):
                    index = (slice(None),) * place + (flip(where[at], by),)
                    yield sources[by], targets[0].at[index]

            return local_copies(plan, [values, got], [shape])[0]
        mine = self.mine(at)
        first = jnp.where(mine == 0, values, got)
        second = jnp.where(mine == 0, got, values)
        return jnp.stack([first, second], axis=place)

    def place(self):
        dp, head = lax.axis_index("dp"), lax.axis_index("head")
        parts = jnp.array([4, 2, 1, 0, 0]), jnp.array([0, 0, 0, 2, 1])
        either = jnp.where(parts[0] > 0, dp & parts[0], head & parts[1])
        return (either > 0).astype(jnp.int32)

    def total(self, values):
        for at in (C, Z0, Z1, X, Y) if self.tuned else range(len(self.bits)):
            values = values + self.swap(values, at)
        return values


TAPS = 32


def joined_vectors(parts):
    devices, rows, width = parts.shape

    def kernel(parts_ref, out_ref):
        pieces = [parts_ref[at].astype(jnp.float32) for at in range(devices)]
        out_ref[...] = jnp.concatenate(pieces, axis=1)

    return pl.pallas_call(
        kernel,
        out_shape=jax.ShapeDtypeStruct((rows, devices * width), jnp.float32),
        compiler_params=pltpu.CompilerParams(vmem_limit_bytes=16 << 20),
    )(parts)


def parted_vectors(arrays, devices):
    rows = sum(array.shape[0] for array in arrays)
    width = D // devices

    def kernel(*refs):
        start = 0
        for ref in refs[:-1]:
            count = ref.shape[0]
            values = ref[...]
            for at in range(devices):
                refs[-1][at, start : start + count, :] = values[:, at * width : (at + 1) * width]
            start += count

    return pl.pallas_call(
        kernel,
        out_shape=jax.ShapeDtypeStruct((devices, rows, width), jnp.float32),
        compiler_params=pltpu.CompilerParams(vmem_limit_bytes=16 << 20),
    )(*arrays)


class VectorGathering:
    def __init__(self, cube, shard, order):
        self.cube, self.order, self.held = cube, list(order), []
        self.state = [shard]

    def step(self, count=1):
        for _ in range(min(count, len(self.order))):
            at = self.order.pop(0)
            place = sum(other < at for other in self.held)
            (values,) = self.state
            self.state = [self.cube.join(values, self.cube.swap(values, at), at, place)]
            self.held.append(at)


class HeadGathering:
    def __init__(self, cube, shard):
        self.cube = cube
        self.state = [shard]

    def step(self, phase):
        if not self.cube.tuned:
            if phase == "x":
                self.state = [lax.all_gather(self.state[0], "dp", axis=0, tiled=True)]
            return
        if phase == "x":
            (own,) = self.state
            self.state = [own, self.cube.swap(own, X)]
        if phase == "far":
            own, got = self.state

            def plan(where, sources, targets):
                for by in range(2):
                    yield sources[by], targets[0].at[flip(where[X], by)]

            (pair,) = local_copies(plan, self.state, [(2,) + own.shape])
            self.state = [pair, self.cube.swap(pair, Z1)]
        if phase == "near":
            pair, got = self.state

            def plan(where, sources, targets):
                for by in range(2):
                    yield sources[by], targets[0].at[flip(where[Z1], by)]

            (four,) = local_copies(plan, self.state, [(2,) + pair.shape])
            self.state = [four, self.cube.swap(four, Z0)]


def joined_heads(cube, heads):
    if not cube.tuned:
        return jnp.concatenate([part.state[0] for part in heads], axis=1)
    parts = [part for flow in heads for part in flow.state]
    _, _, rows, half = parts[0].shape

    def plan(where, sources, targets):
        for at in range(4):
            columns = pl.ds(at // 2 * half, half)
            yield sources[at], targets[0].at[:, flip(where[Z0], at % 2), :, :, columns]

    (whole,) = local_copies(plan, parts, [(2, 2, 2, rows, 2 * half)])
    return whole.reshape(8 * rows, 2 * half)


def pick_of(values, index, place):
    return lax.dynamic_index_in_dim(values, index, place, keepdims=False)


def halves_kernel(at, place, *refs):
    dp, head = lax.axis_index("dp"), lax.axis_index("head")
    mine = (dp // 4, dp // 2 % 2, dp % 2, head // 2, head % 2)[at]
    keep, got, send_ref, keep_ref = refs
    for out, by in ((send_ref, 1), (keep_ref, 0)):
        index = (slice(None),) * place + (flip(mine, by),)
        total = keep[index].astype(jnp.float32) + got[index].astype(jnp.float32)
        out[...] = total.astype(out.dtype)


class Summing:
    def __init__(self, cube, values, order):
        self.cube, self.order = cube, list(order)
        self.held = sorted(order)
        self.state = [values]

    def step(self):
        cube, at = self.cube, self.order.pop(0)
        place = self.held.index(at)
        self.held.remove(at)
        left = self.state[0].shape[:place] + self.state[0].shape[place + 1 :]
        if not cube.tuned:
            values = sum(part.astype(jnp.float32) for part in self.state)
            values = values.astype(self.state[0].dtype)
            send = pick_of(values, 1 - cube.mine(at), place)
            keep = pick_of(values, cube.mine(at), place)
        elif len(self.state) == 1:

            def plan(where, sources, targets):
                for by in range(2):
                    index = (slice(None),) * place + (flip(where[at], 1 - by),)
                    yield sources[0].at[index], targets[by]

            send, keep = local_copies(plan, self.state, [left, left])
        else:
            size = math.prod(left) * self.state[0].dtype.itemsize
            send, keep = pl.pallas_call(
                functools.partial(halves_kernel, at, place),
                out_shape=[jax.ShapeDtypeStruct(left, self.state[0].dtype)] * 2,
                in_specs=[VMEM] * 2,
                out_specs=[VMEM] * 2,
                compiler_params=pltpu.CompilerParams(vmem_limit_bytes=6 * size + (4 << 20)),
            )(*self.state)
        self.state = [keep, cube.swap(send, at)]

    def result(self):
        return sum(part.astype(jnp.float32) for part in self.state)


class Gather:
    def __init__(self, cube, pieces):
        self.cube = cube
        self.pieces = pieces
        self.wholes = [None] * len(pieces)
        if cube.tuned:
            self.shards = [uniform_shard(kind, arrays) for kind, arrays in pieces]
        self.state = {}

    def stage(self, t):
        cube, old, new = self.cube, self.state, {}
        count = len(self.pieces)
        live = lambda at: 0 <= at < count
        if not cube.tuned:
            if live(t - 1):
                self.wholes[t - 1] = [
                    lax.all_gather(array, AXES, axis=0, tiled=True)
                    for array in self.pieces[t - 1][1]
                ]
            return
        half = COLUMNS // 2
        slots = 2 * live(t) + live(t + 1)
        old_slots = 2 * live(t - 1) + live(t)
        inputs, shapes, jobs = [], [], []

        def give(name):
            inputs.append(old[name])
            return len(inputs) - 1

        def make(shape):
            shapes.append(shape)
            return len(shapes) - 1

        pair = None
        if live(t + 2):
            parts, pair = (give("z1s"), give("z1g")), make((2, ROWS, COLUMNS))
            jobs.append(lambda w, s, o, parts=parts, pair=pair: [
                (s[parts[by]], o[pair].at[flip(w[Z1], by)]) for by in range(2)
            ])
        if slots:
            x_out, y_out = (make((2, 2, slots, ROWS, half)) for _ in range(2))
        if live(t):
            xs, xg, ys, yg = (give(name) for name in ("xs", "xg", "ys", "yg"))
            jobs.append(lambda w, s, o: [
                pair_of
                for by in range(2)
                for pair_of in (
                    (s[(xs, xg)[by]].at[:, :, old_slots - 1], o[y_out].at[:, :, flip(w[X], by)]),
                    (s[(ys, yg)[by]].at[:, :, old_slots - 1], o[x_out].at[:, :, flip(w[Y], by)]),
                )
            ])
        if live(t + 1):
            zs, zg = give("z0s"), give("z0g")
            jobs.append(lambda w, s, o: [
                (
                    s[(zs, zg)[by]].at[:, :, pl.ds(side * half, half)],
                    o[(x_out, y_out)[side]].at[:, flip(w[Z0], by), slots - 1],
                )
                for by in range(2)
                for side in range(2)
            ])
        if jobs:
            made = local_copies(
                lambda w, s, o: [each for job in jobs for each in job(w, s, o)], inputs, shapes
            )
            if slots:
                new["xs"], new["ys"] = made[x_out], made[y_out]
                new["xg"], new["yg"] = cube.swap(made[x_out], X), cube.swap(made[y_out], Y)
            if pair is not None:
                new["z0s"], new["z0g"] = made[pair], cube.swap(made[pair], Z0)
        if live(t + 3):
            new["z1s"] = self.shards[t + 3]
            new["z1g"] = cube.swap(self.shards[t + 3], Z1)
        if live(t - 1):

            def plan(w, s, o):
                for by in range(2):
                    yield (
                        s[by].at[:, :, pl.ds(0, 2)],
                        o[0].at[:, :, :, flip(w[Y], by), :, pl.ds(0, half)],
                    )
                    yield (
                        s[2 + by].at[:, :, pl.ds(0, 2)],
                        o[0].at[:, :, flip(w[X], by), :, :, pl.ds(half, half)],
                    )

            (most,) = local_copies(
                plan,
                [old[name] for name in ("ys", "yg", "xs", "xg")],
                [(2, 2, 2, 2, ROWS, COLUMNS)],
                [new[name] for name in ("xs", "z0s") if name in new][:1],
            )
            got = cube.swap(most, C)
            kind, arrays = self.pieces[t - 1]

            def plan_whole(w, s, o):
                for by in range(2):
                    for at, rows, columns in tiles_of(kind, arrays):
                        yield (
                            s[by].at[:, :, :, :, :, columns],
                            o[at].at[:, :, :, :, flip(w[C], by), rows],
                        )

            made = local_copies(
                plan_whole, [most, got], [(2, 2, 2, 2, 2) + array.shape for array in arrays]
            )
            self.wholes[t - 1] = [
                whole.reshape(-1, array.shape[1]) for whole, array in zip(made, arrays)
            ]
        self.state = new


ROWS, COLUMNS = 32, 4096


def uniform_shard(kind, arrays):
    if kind == "tall":
        return jnp.concatenate([arrays[0][at : at + ROWS] for at in range(0, 4 * ROWS, ROWS)], axis=1)
    spare = COLUMNS - sum(array.shape[1] for array in arrays)
    extra = [arrays[0][:, :spare]] if spare else []
    return jnp.concatenate(arrays + extra, axis=1) if len(arrays) > 1 else arrays[0]


def tiles_of(kind, arrays):
    if kind == "tall":
        width = arrays[0].shape[1]
        for at in range(4):
            yield 0, pl.ds(at * ROWS, ROWS), pl.ds(at * width, width)
    else:
        start = 0
        for at, array in enumerate(arrays):
            yield at, pl.ds(0, ROWS), pl.ds(start, array.shape[1])
            start += array.shape[1]


def added(out, out_at, first, first_at, second, second_at):
    total = first[first_at].astype(jnp.float32) + second[second_at].astype(jnp.float32)
    out[out_at] = total.astype(out.dtype)


class Scatter:
    def __init__(self, cube):
        self.cube = cube
        self.state = {}
        self.results = []
        self.queue = []
        self.first = []

    def sums(self, sent, after):
        old = self.state
        half = COLUMNS // 2
        inputs, in_specs, names, shapes, out_specs, jobs = [], [], [], [], [], []
        mine = lambda w, at: (w[at] + sent) % 2

        def take(name, block, index):
            inputs.append(old[name])
            in_specs.append(pl.BlockSpec(block, index))
            return len(inputs) - 1

        def make(name, shape, block, index):
            names.append(name)
            shapes.append(jax.ShapeDtypeStruct(shape, jnp.bfloat16))
            out_specs.append(pl.BlockSpec(block, index))
            return len(names) - 1

        has_n, has_m = "ck" in old, "ak" in old
        slots = 2 * has_n + has_m
        corner = (None, None)
        if sent and slots:
            sent_shape = (2, 2, slots, ROWS, half)
            x_out = make("x", sent_shape, corner + sent_shape[2:], lambda a, b, w: (a, b, 0, 0, 0))
            y_out = make("y", sent_shape, corner + sent_shape[2:], lambda a, b, w: (a, b, 0, 0, 0))
        if has_n:
            left_block, right_block = corner + (2, None, ROWS, half), corner + (None, 2, ROWS, half)
            left_index = lambda a, b, w: (a, b, 0, mine(w, Y), 0, 0)
            right_index = lambda a, b, w: (a, b, mine(w, X), 0, 0, 1)
            lefts = [take(name, left_block, left_index) for name in ("ck", "cg")]
            rights = [take(name, right_block, right_index) for name in ("ck", "cg")]
            if not sent:
                kept = (2, 2, 2, ROWS, half)
                y_out = make("ak", kept, corner + kept[2:], lambda a, b, w: (a, b, 0, 0, 0))
                x_out = make("bk", kept, corner + kept[2:], lambda a, b, w: (a, b, 0, 0, 0))

            def job_n(s, o, y_out=y_out, x_out=x_out):
                for k in range(2):
                    added(o[y_out], k, s[lefts[0]], k, s[lefts[1]], k)
                    added(o[x_out], k, s[rights[0]], k, s[rights[1]], k)

            jobs.append(job_n)
        if has_m:
            block = corner + (None, ROWS, half)
            x_index = lambda a, b, w: (a, b, mine(w, X), 0, 0)
            y_index = lambda a, b, w: (a, b, mine(w, Y), 0, 0)
            lefts_m = take("ak", block, x_index), take("yg", block, x_index)
            rights_m = take("bk", block, y_index), take("xg", block, y_index)
            place = slots - 1 if sent else slice(None)
            if not sent:
                kept = (2, 2, ROWS, half)
                a_out = make("a4k", kept, corner + kept[2:], lambda a, b, w: (a, b, 0, 0))
                b_out = make("b4k", kept, corner + kept[2:], lambda a, b, w: (a, b, 0, 0))
            else:
                a_out, b_out = x_out, y_out

            def job_m(s, o):
                every = slice(None)
                added(o[a_out], place, s[lefts_m[0]], every, s[lefts_m[1]], every)
                added(o[b_out], place, s[rights_m[0]], every, s[rights_m[1]], every)

            jobs.append(job_m)
        if "a4k" in old:
            last = old["xg"].shape[2] - 1
            block = (None, None, ROWS, half)
            index = lambda a, b, w: (a, mine(w, Z0), 0, 0)
            got_block = (None, None, None, ROWS, half)
            got_index = lambda a, b, w: (a, mine(w, Z0), last, 0, 0)
            lefts_z = take("a4k", block, index), take("xg", got_block, got_index)
            rights_z = take("b4k", block, index), take("yg", got_block, got_index)
            z_out = make(
                "z" if sent else "zk",
                (2, ROWS, COLUMNS),
                (None, ROWS, COLUMNS),
                lambda a, b, w: (a, 0, 0),
            )

            def job_z(s, o):
                @pl.when(pl.program_id(1) == 0)
                def _():
                    every = slice(None)
                    left = (every, slice(0, half))
                    right = (every, slice(half, COLUMNS))
                    added(o[z_out], left, s[lefts_z[0]], every, s[lefts_z[1]], every)
                    added(o[z_out], right, s[rights_z[0]], every, s[rights_z[1]], every)

            jobs.append(job_z)
        if "zk" in old:
            block, index = (None, ROWS, COLUMNS), lambda a, b, w: (mine(w, Z1), 0, 0)
            pair = take("zk", block, index), take("zg", block, index)
            f_out = make(
                "f" if sent else "fk", (ROWS, COLUMNS), (ROWS, COLUMNS), lambda a, b, w: (0, 0)
            )

            def job_f(s, o):
                @pl.when((pl.program_id(0) == 0) & (pl.program_id(1) == 0))
                def _():
                    every = slice(None)
                    added(o[f_out], every, s[pair[0]], every, s[pair[1]], every)

            jobs.append(job_f)
        if not jobs:
            return {}

        def kernel(where, *refs):
            sources, targets = refs[: len(inputs)], refs[len(inputs) + len(after) :]
            for job in jobs:
                job(sources, targets)

        size = sum(math.prod(shape.shape) for shape in shapes)
        made = pl.pallas_call(
            kernel,
            grid_spec=pltpu.PrefetchScalarGridSpec(
                num_scalar_prefetch=1,
                grid=(2, 2),
                in_specs=in_specs + [ANY] * len(after),
                out_specs=out_specs,
            ),
            out_shape=shapes,
            cost_estimate=BRIEF,
            compiler_params=pltpu.CompilerParams(vmem_limit_bytes=9 << 20),
        )(self.cube.where, *inputs, *after)
        return dict(zip(names, made))

    def stage(self, value=None):
        cube, old, new = self.cube, self.state, {}
        if not cube.tuned:
            return value
        sends = self.sums(1, [])
        if value is not None:
            sends, value = lax.optimization_barrier((sends, value))
        for name, at, got in (("x", X, "xg"), ("y", Y, "yg"), ("z", Z0, "zg"), ("f", Z1, "fg")):
            if name in sends:
                new[got] = cube.swap(sends[name], at)
        first = list(sends.values())[:1]
        new.update(self.sums(0, first))
        if "fk" in old:
            kind, arrays = self.queue.pop(0)
            total = old["fk"].astype(jnp.float32) + old["fg"].astype(jnp.float32)
            self.results.append(split_shard(kind, arrays, total))
        self.first, self.state = first, new
        return value

    def push(self, kind, arrays, grads):
        if not self.cube.tuned:
            self.results.append(
                [
                    lax.psum_scatter(grad, AXES, scatter_dimension=0, tiled=True).astype(jnp.float32)
                    for grad in grads
                ]
            )
            return
        self.queue.append((kind, arrays))
        keep, send = grads
        self.state["ck"], self.state["cg"] = keep, self.cube.swap(send, C)


def split_shard(kind, arrays, total):
    if kind == "tall":
        width = arrays[0].shape[1]
        return [jnp.concatenate([total[:, at * width : (at + 1) * width] for at in range(4)], axis=0)]
    parts, start = [], 0
    for array in arrays:
        parts.append(total[:, start : start + array.shape[1]])
        start += array.shape[1]
    return parts


class HeadScattering:
    def __init__(self, cube, values, rows):
        self.cube = cube
        if not cube.tuned:
            self.whole = values
            return
        half = values.shape[1] // 2
        self.parts = [
            Summing(cube, values[:, :half].reshape(2, 2, 2, rows, half), (X, Z0, Z1)),
            Summing(cube, values[:, half:].reshape(2, 2, 2, rows, half), (Z0, Z1, X)),
        ]

    @property
    def state(self):
        return [part.state for part in self.parts] if self.cube.tuned else [self.whole]

    @state.setter
    def state(self, values):
        if not self.cube.tuned:
            self.whole = values[0]
            return
        for part, state in zip(self.parts, values):
            part.state = state

    def step(self):
        if self.cube.tuned:
            for part in self.parts:
                part.step()

    def result(self):
        if not self.cube.tuned:
            return lax.psum_scatter(self.whole, "dp", scatter_dimension=0, tiled=True).astype(
                jnp.float32
            )
        return jnp.concatenate([part.result() for part in self.parts], axis=1)


def shifted(pad_ref, shift_ref, rows):
    for r in range(8):
        shift_ref[r] = pad_ref[r : r + rows, :]


def conv_forward_kernel(lead_ref, gate_ref, valid_ref, taps_ref, conv_ref, sums_ref, pad, shift):
    length, width = lead_ref.shape
    edge = jnp.zeros((16, width), jnp.float32)
    valid = valid_ref[...]
    pad[0:16, :] = edge
    pad[16 : 16 + length, :] = lead_ref[...] * jax.nn.sigmoid(gate_ref[...]) * valid
    pad[16 + length : 40 + length, :] = jnp.zeros((24, width), jnp.float32)
    shifted(pad, shift, length + 32)
    chunk = 64
    taps = [taps_ref[j : j + 1, :] for j in range(32)]

    def step(at, totals):
        start = pl.multiple_of(at * chunk, chunk)
        total = jnp.zeros((chunk, width), jnp.float32)
        for j in range(32):
            total += shift[j % 8, pl.ds(start + j // 8 * 8, chunk), :] * taps[j]
        conv_ref[pl.ds(start, chunk), :] = total
        weighted = total * valid_ref[pl.ds(start, chunk), :]
        plain, squares = totals
        return (
            plain + jnp.sum(weighted, axis=0, keepdims=True),
            squares + jnp.sum(weighted * total, axis=0, keepdims=True),
        )

    zero = jnp.zeros((1, width), jnp.float32)
    plain, squares = lax.fori_loop(0, length // chunk, step, (zero, zero))
    sums_ref[0:1, :] = plain
    sums_ref[1:2, :] = squares
    sums_ref[2:3, :] = jnp.broadcast_to(jnp.sum(valid, axis=0, keepdims=True), (1, width))
    sums_ref[3:8, :] = jnp.zeros((5, width), jnp.float32)


def conv_forward(expanded, valid, taps):
    rows = expanded.shape[0]
    width = 128
    count = D // width
    return pl.pallas_call(
        conv_forward_kernel,
        grid=(count,),
        in_specs=[
            pl.BlockSpec((rows, width), lambda i: (0, i)),
            pl.BlockSpec((rows, width), lambda i: (0, i + count)),
            pl.BlockSpec((rows, 1), lambda i: (0, 0)),
            pl.BlockSpec((TAPS + 16, width), lambda i: (0, i)),
        ],
        out_specs=[
            pl.BlockSpec((rows, width), lambda i: (0, i)),
            pl.BlockSpec((8, width), lambda i: (0, i)),
        ],
        out_shape=[
            jax.ShapeDtypeStruct((rows, D), jnp.float32),
            jax.ShapeDtypeStruct((8, D), jnp.float32),
        ],
        scratch_shapes=[
            pltpu.VMEM((rows + 40, width), jnp.float32),
            pltpu.VMEM((8, rows + 32, width), jnp.float32),
        ],
        cost_estimate=BRIEF,
        compiler_params=pltpu.CompilerParams(vmem_limit_bytes=8 << 20),
    )(expanded, expanded, valid, taps)


def conv_backward_kernel(
    lead_ref,
    gate_ref,
    valid_ref,
    taps_ref,
    conv_ref,
    grad_ref,
    sums_ref,
    back_sums_ref,
    out_ref,
    taps_grad_ref,
    pad,
    shift,
    tap_sums,
):
    length, width = lead_ref.shape
    count = sums_ref[2:3, :]
    mean = sums_ref[0:1, :] / count
    inverse = lax.rsqrt(sums_ref[1:2, :] / count - mean * mean + eps)
    variance_grad = -0.5 * inverse * inverse * back_sums_ref[1:2, :]
    plain = (-inverse * back_sums_ref[0:1, :] - 2.0 * mean * variance_grad) / count
    scaled = 2.0 * variance_grad / count
    pad[0:16, :] = jnp.zeros((16, width), jnp.float32)
    pad[16 : 16 + length, :] = (
        grad_ref[...] * inverse + (plain + scaled * conv_ref[...]) * valid_ref[...]
    )
    pad[16 + length : 40 + length, :] = jnp.zeros((24, width), jnp.float32)
    shifted(pad, shift, length + 32)
    tap_sums[...] = jnp.zeros(tap_sums.shape, jnp.float32)
    chunk = 64
    taps = [taps_ref[j : j + 1, :] for j in range(32)]

    def step(at, carry):
        start = pl.multiple_of(at * chunk, chunk)
        here = pl.ds(start, chunk)
        lead, valid = lead_ref[here, :], valid_ref[here, :]
        gate = jax.nn.sigmoid(gate_ref[here, :])
        gated = lead * gate * valid
        total = jnp.zeros((chunk, width), jnp.float32)
        for j in range(32):
            off = 32 - j
            part = shift[off % 8, pl.ds(start + off // 8 * 8, chunk), :]
            total += part * taps[j]
            tap_sums[j] += jnp.sum((part * gated).reshape(chunk // 8, 8, width), axis=0)
        grad = total * valid
        out_ref[0, here, :] = (grad * gate).astype(jnp.bfloat16)
        out_ref[1, here, :] = (grad * lead * gate * (1.0 - gate)).astype(jnp.bfloat16)
        return carry

    lax.fori_loop(0, length // chunk, step, 0)
    taps_grad_ref[...] = jnp.sum(tap_sums[...], axis=1)


def conv_backward(expanded, valid, taps, conv_out, grads, sums, back_sums):
    rows = expanded.shape[0]
    width = 128
    count = D // width
    block = pl.BlockSpec((rows, width), lambda i: (0, i))
    return pl.pallas_call(
        conv_backward_kernel,
        grid=(count,),
        in_specs=[
            block,
            pl.BlockSpec((rows, width), lambda i: (0, i + count)),
            pl.BlockSpec((rows, 1), lambda i: (0, 0)),
            pl.BlockSpec((TAPS + 16, width), lambda i: (0, i)),
            block,
            block,
            pl.BlockSpec((8, width), lambda i: (0, i)),
            pl.BlockSpec((8, width), lambda i: (0, i)),
        ],
        out_specs=[
            pl.BlockSpec((2, rows, width), lambda i: (0, 0, i)),
            pl.BlockSpec((TAPS, width), lambda i: (0, i)),
        ],
        out_shape=[
            jax.ShapeDtypeStruct((2, rows, D), jnp.bfloat16),
            jax.ShapeDtypeStruct((32, D), jnp.float32),
        ],
        scratch_shapes=[
            pltpu.VMEM((rows + 40, width), jnp.float32),
            pltpu.VMEM((8, rows + 32, width), jnp.float32),
            pltpu.VMEM((32, 8, width), jnp.float32),
        ],
        cost_estimate=BRIEF,
        compiler_params=pltpu.CompilerParams(vmem_limit_bytes=8 << 20),
    )(expanded, expanded, valid, taps, conv_out, grads, sums, back_sums)


def nt_dot(left, right):
    return lax.dot_general(left, right, (((1,), (1,)), ((), ())), preferred_element_type=jnp.float32)


def act_back_kernel(grad_ref, weight_ref, pre_ref, out_ref):
    pre = pre_ref[...].astype(jnp.float32)
    gate = jax.nn.sigmoid(pre)
    slope = gate * (1.0 + pre * (1.0 - gate))
    out_ref[...] = (nt_dot(grad_ref[...], weight_ref[...]) * slope).astype(jnp.bfloat16)


def act_back(grad_lo, weight, pre):
    rows, inner = grad_lo.shape
    total = weight.shape[0]
    width = 512
    each = D // width
    return pl.pallas_call(
        act_back_kernel,
        grid=(total // width,),
        in_specs=[
            pl.BlockSpec((rows, inner), lambda i: (0, 0)),
            pl.BlockSpec((width, inner), lambda i: (i, 0)),
            pl.BlockSpec((rows, width), lambda i: (0, i)),
        ],
        out_specs=pl.BlockSpec((None, rows, width), lambda i: (i // each, 0, i % each)),
        out_shape=jax.ShapeDtypeStruct((total // D, rows, D), jnp.bfloat16),
        cost_estimate=BRIEF,
        compiler_params=pltpu.CompilerParams(vmem_limit_bytes=10 << 20),
    )(grad_lo, weight, pre)


def weight_grads_kernel(counts, *refs):
    lefts, rights = refs[: len(counts)], refs[len(counts) : 2 * len(counts)]
    keep_ref, send_ref = refs[-2:]
    core = lax.axis_index("head") % 2
    step, start = pl.program_id(0), 0
    for left, right, count in zip(lefts, rights, counts):

        @pl.when((step >= start) & (step < start + count))
        def _(left=left, right=right):
            total = matmul_tn(left[...], right[...]).astype(jnp.bfloat16)
            for at in range(16):
                first, second = (
                    total[(2 * at + by) * ROWS : (2 * at + by + 1) * ROWS, :] for by in range(2)
                )
                place = (at // 8, at // 4 % 2, at // 2 % 2, at % 2)

                @pl.when(core == 0)
                def _():
                    keep_ref[place], send_ref[place] = first, second

                @pl.when(core == 1)
                def _():
                    keep_ref[place], send_ref[place] = second, first

        start += count

    @pl.when(step >= start)
    def _():
        keep_ref[...] = jnp.zeros(keep_ref.shape, jnp.bfloat16)
        send_ref[...] = jnp.zeros(send_ref.shape, jnp.bfloat16)


def tall_grads_kernel(left_ref, right_ref, keep_ref, send_ref):
    core = lax.axis_index("head") % 2
    total = matmul_tn(left_ref[...], right_ref[...]).astype(jnp.bfloat16)
    for at in range(4):
        for group in range(4):
            first, second = (
                total[((2 * at + by) * 4 + group) * ROWS : ((2 * at + by) * 4 + group + 1) * ROWS, :]
                for by in range(2)
            )
            place = (at // 2, at % 2, slice(None), slice(group * D, (group + 1) * D))

            @pl.when(core == 0)
            def _():
                keep_ref[place], send_ref[place] = first, second

            @pl.when(core == 1)
            def _():
                keep_ref[place], send_ref[place] = second, first


def weight_grads(cube, kind, pairs):
    if not cube.tuned:
        return [
            jnp.concatenate([lowered(matmul_tn(left, each)) for each in rights], axis=1)
            for left, rights in pairs
        ]
    shape = (2, 2, 2, 2, ROWS, COLUMNS)
    rows = pairs[0][0].shape[0]
    common = dict(
        out_shape=[jax.ShapeDtypeStruct(shape, jnp.bfloat16)] * 2,
        cost_estimate=BRIEF,
        compiler_params=pltpu.CompilerParams(vmem_limit_bytes=22 << 20),
    )
    if kind == "tall":
        ((left, right),) = pairs
        return pl.pallas_call(
            tall_grads_kernel,
            grid=(4,),
            in_specs=[
                pl.BlockSpec((rows, D), lambda i: (0, i)),
                pl.BlockSpec((None, rows, D), lambda i: (0, 0, 0)),
            ],
            out_specs=[
                pl.BlockSpec((None, None, 2, 2, ROWS, COLUMNS), lambda i: (i // 2, i % 2, 0, 0, 0, 0))
            ]
            * 2,
            **common,
        )(left, right)
    counts, right_specs, start = [], [], 0
    for _, right in pairs:
        count = right.shape[0]
        right_specs.append(
            pl.BlockSpec(
                (None, rows, D),
                lambda i, start=start, count=count: (jnp.clip(i - start, 0, count - 1), 0, 0),
            )
        )
        counts.append(count)
        start += count
    return pl.pallas_call(
        functools.partial(weight_grads_kernel, counts),
        grid=(COLUMNS // D,),
        in_specs=[pl.BlockSpec((rows, D), lambda i: (0, 0))] * len(pairs) + right_specs,
        out_specs=[pl.BlockSpec(shape[:5] + (D,), lambda i: (0, 0, 0, 0, 0, i))] * 2,
        **common,
    )(*[left for left, _ in pairs], *[right for _, right in pairs])


def norm_back_kernel(
    row, grad_ref, weight_ref, values_ref, vectors_ref, above_ref, out_ref, gain_out, total
):
    step = pl.program_id(0)

    @pl.when(step == 0)
    def _():
        total[...] = jnp.zeros(total.shape, jnp.float32)

    total[...] += nt_dot(grad_ref[...], weight_ref[...])

    @pl.when(step == pl.num_programs(0) - 1)
    def _():
        rows = 128
        gain = vectors_ref[TAPS + row : TAPS + row + 1, :]

        def part(at, gain_total):
            here = pl.ds(pl.multiple_of(at * rows, rows), rows)
            values, grads = values_ref[here, :], total[here, :]
            center = values - jnp.mean(values, axis=-1, keepdims=True)
            scale = lax.rsqrt(jnp.mean(center * center, axis=-1, keepdims=True) + eps)
            normed = center * scale
            scaled = grads * gain
            mean = jnp.mean(scaled, axis=-1, keepdims=True)
            along = jnp.mean(scaled * normed, axis=-1, keepdims=True)
            out_ref[here, :] = above_ref[here, :] + (scaled - mean - normed * along) * scale
            return gain_total + jnp.sum(grads * normed, axis=0, keepdims=True)

        gain_out[...] = lax.fori_loop(
            0, total.shape[0] // rows, part, jnp.zeros(gain_out.shape, jnp.float32)
        )


def product_norm_back(grad_lo, weight, values, vectors, row, above):
    _, rows, _ = grad_lo.shape
    inner = weight.shape[1]
    width = 512
    each = D // width
    whole, vector = VMEM, VMEM
    return pl.pallas_call(
        functools.partial(norm_back_kernel, row),
        grid=(inner // width,),
        in_specs=[
            pl.BlockSpec((None, rows, width), lambda i: (i // each, 0, i % each)),
            pl.BlockSpec((D, width), lambda i: (0, i)),
            whole,
            vector,
            whole,
        ],
        out_specs=[whole, vector],
        out_shape=[
            jax.ShapeDtypeStruct((rows, D), jnp.float32),
            jax.ShapeDtypeStruct((1, D), jnp.float32),
        ],
        scratch_shapes=[pltpu.VMEM((rows, D), jnp.float32)],
        cost_estimate=BRIEF,
        compiler_params=pltpu.CompilerParams(vmem_limit_bytes=14 << 20),
    )(grad_lo, weight, values, vectors, above)


def turned(values, cosine, sine):
    half = HD // 2
    lead, tail = values[:, :half], values[:, half:]
    return jnp.concatenate([lead * cosine - tail * sine, tail * cosine + lead * sine], axis=1)


def attend_kernel(
    query_ref, key_ref, value_ref, cosine_ref, sine_ref, bias_ref, out_ref, query_out, key_out, value_out, log_out
):
    cosine, sine = cosine_ref[...], sine_ref[...]
    query = turned(query_ref[...], cosine, sine).astype(jnp.bfloat16)
    key = turned(key_ref[...], cosine, sine).astype(jnp.bfloat16)
    value = value_ref[...].astype(jnp.bfloat16)
    query_out[...], key_out[...], value_out[...] = query, key, value
    scores = jnp.where(bias_ref[...] > 0, nt_dot(query, key) * HD**-0.5, -1e30)
    top = jnp.max(scores, axis=-1, keepdims=True)
    weights = jnp.exp(scores - top)
    total = jnp.sum(weights, axis=-1, keepdims=True)
    probs = (weights * (1.0 / total)).astype(jnp.bfloat16)
    out_ref[...] = jnp.dot(probs, value, preferred_element_type=jnp.float32).astype(jnp.bfloat16)
    log_out[...] = jnp.broadcast_to(top + jnp.log(total), log_out.shape)


def attend(mixed, cosine, sine, valid):
    rows = mixed.shape[0]
    head = lambda shift: pl.BlockSpec((rows, HD), lambda i: (0, i + shift))
    fixed = lambda *shape: pl.BlockSpec(shape, lambda i: (0, 0))
    return pl.pallas_call(
        attend_kernel,
        grid=(H,),
        in_specs=[
            head(0),
            head(H),
            head(2 * H),
            fixed(rows, HD // 2),
            fixed(rows, HD // 2),
            fixed(1, rows),
        ],
        out_specs=[head(0)] * 5,
        out_shape=[jax.ShapeDtypeStruct((rows, D), jnp.bfloat16)] * 4
        + [jax.ShapeDtypeStruct((rows, D), jnp.float32)],
        cost_estimate=BRIEF,
        compiler_params=pltpu.CompilerParams(vmem_limit_bytes=12 << 20),
    )(mixed, mixed, mixed, cosine, sine, valid)


def attend_back_kernel(
    query_ref, key_ref, value_ref, log_ref, grad_ref, cosine_ref, sine_ref, bias_ref, out_ref
):
    query, key, value, grad = query_ref[...], key_ref[...], value_ref[...], grad_ref[...]
    cosine, sine = cosine_ref[...], -sine_ref[...]
    scores = jnp.where(bias_ref[...] > 0, nt_dot(query, key) * HD**-0.5, -1e30)
    probs = jnp.exp(scores - log_ref[:, :1])
    grad_probs = nt_dot(grad, value)
    along = jnp.sum(probs * grad_probs, axis=-1, keepdims=True)
    grad_scores = (probs * (grad_probs - along)).astype(jnp.bfloat16)
    out_ref[2] = matmul_tn(probs.astype(jnp.bfloat16), grad).astype(jnp.bfloat16)
    query_grad = matmul(grad_scores, key) * HD**-0.5
    key_grad = matmul_tn(grad_scores, query) * HD**-0.5
    out_ref[0] = turned(query_grad, cosine, sine).astype(jnp.bfloat16)
    out_ref[1] = turned(key_grad, cosine, sine).astype(jnp.bfloat16)


def attend_back(query, key, value, logs, grads, cosine, sine, valid):
    rows = query.shape[0]
    head = pl.BlockSpec((rows, HD), lambda i: (0, i))
    fixed = lambda *shape: pl.BlockSpec(shape, lambda i: (0, 0))
    return pl.pallas_call(
        attend_back_kernel,
        grid=(H,),
        in_specs=[head] * 5
        + [fixed(rows, HD // 2), fixed(rows, HD // 2), fixed(1, rows)],
        out_specs=pl.BlockSpec((3, rows, HD), lambda i: (0, 0, i)),
        out_shape=jax.ShapeDtypeStruct((3, rows, D), jnp.bfloat16),
        cost_estimate=BRIEF,
        compiler_params=pltpu.CompilerParams(vmem_limit_bytes=12 << 20),
    )(query, key, value, logs, grads, cosine, sine, valid)


def fence(flows, *values):
    states, values = lax.optimization_barrier(([flow.state for flow in flows], values))
    for flow, state in zip(flows, states):
        flow.state = state
    return values[0] if len(values) == 1 else values


def rows_of(values, count):
    return values.reshape(count, values.shape[-1])


def shards(
    sizes,
    frames,
    ffn_inner,
    ffn_outer,
    attn_qkv,
    attn_proj,
    conv_expand,
    conv_depth,
    conv_proj,
    norm_gains,
    head_proj,
    lengths,
    mask_starts,
    target_codes,
    out_grad,
):
    cube = Cube(sizes)
    cube.where = lax.optimization_barrier(cube.place()) if cube.tuned else None
    devices = sizes["dp"] * sizes["head"]
    ff = ffn_inner.shape[2]
    all_bits = list(range(len(cube.bits)))

    rows_in = Gather(
        cube,
        [
            ("wide", [ffn_inner[0]]),
            ("tall", [ffn_outer[0]]),
            ("wide", [attn_qkv, attn_proj]),
            ("wide", [conv_expand, conv_proj]),
            ("wide", [ffn_inner[1]]),
            ("tall", [ffn_outer[1]]),
        ],
    )
    head_half = head_proj.shape[1] // 2
    heads = [
        HeadGathering(cube, head_proj[:, :head_half]),
        HeadGathering(cube, head_proj[:, head_half:]),
    ]

    row_total = UTT_DEV * SEQ
    positions = jnp.arange(SEQ, dtype=jnp.int32)
    valid_mat = positions[None, :] < lengths[:, None]
    valid_rows = valid_mat.reshape(row_total).astype(jnp.float32)
    frequency = 10000.0 ** (-(jnp.arange(HD // 2, dtype=jnp.float32) * 2.0) / HD)
    angles = positions.astype(jnp.float32)[:, None] * frequency[None, :]
    cosine, sine_table = jnp.cos(angles), jnp.sin(angles)

    slots = UTT_DEV * NSPAN * SPAN
    slot_at = (mask_starts[:, :, None] + jnp.arange(SPAN, dtype=jnp.int32)).reshape(UTT_DEV, -1)
    slot_ok = slot_at < lengths[:, None]
    chosen = (slot_at + SEQ * jnp.arange(UTT_DEV, dtype=jnp.int32)[:, None]).reshape(slots)
    slot_live = slot_ok.reshape(slots)
    pick = (
        (chosen[:, None] == jnp.arange(row_total, dtype=jnp.int32)[None, :]) & slot_live[:, None]
    )
    picked_codes = jnp.sum(jnp.where(pick, target_codes[None, :], 0), axis=1)
    picked_codes = jnp.where(slot_live, picked_codes, -1)
    pick_lo = pick.astype(jnp.bfloat16)
    head_order = [at for at in range(len(cube.bits)) if cube.bits[at][0] == "head"]
    group = sizes["head"]
    vocab_cols = head_proj.shape[1]

    loss_scale = jnp.float32(devices * UTT_DEV * NSPAN * SPAN)
    hops = [C, Z1, Z0, X, Y] if cube.tuned else all_bits
    vector_in = VectorGathering(cube, jnp.concatenate([conv_depth, norm_gains, jnp.zeros_like(conv_depth[:10])], axis=0), hops)
    vector_in.step(2)
    group_codes = cube.gather(picked_codes, head_order).reshape(group * slots)
    rows_in.stage(-3)
    heads[0].step("x")
    heads[1].step("x")
    group_codes = fence([rows_in, vector_in, *heads], group_codes)

    rows_in.stage(-2)
    vector_in.step()
    fence([rows_in, vector_in], loss_scale)

    rows_in.stage(-1)
    vector_in.step()
    inputs = frames.astype(jnp.float32)
    fence([rows_in, vector_in], loss_scale)

    rows_in.stage(0)
    vector_in.step(len(hops))
    heads[0].step("far")
    fence([rows_in, vector_in, heads[0]], loss_scale)
    (vectors,) = vector_in.state
    vectors = fence([], joined_vectors(vectors.reshape((devices,) + vectors.shape[-2:])))
    gain_f = vectors[TAPS : TAPS + 6]
    norm_first = lowered(layer_norm(inputs, gain_f[0]))
    group_live = (group_codes >= 0).astype(jnp.float32)
    local_codes = group_codes - lax.axis_index("head") * vocab_cols

    rows_in.stage(1)
    (inner_0,) = rows_in.wholes[0]
    pre_first = matmul(norm_first, inner_0)
    act_first = lowered(jax.nn.silu(pre_first))
    pre_first = lowered(pre_first)
    pre_first, act_first = fence([rows_in], pre_first, act_first)

    rows_in.stage(2)
    (outer_0,) = rows_in.wholes[1]
    after_first = inputs + 0.5 * matmul(act_first, outer_0)
    norm_attn = lowered(layer_norm(after_first, gain_f[1]))
    after_first, norm_attn = fence([rows_in], after_first, norm_attn)

    rows_in.stage(3)
    heads[0].step("near")
    mix_weight, proj_weight = rows_in.wholes[2]
    mixed = matmul(norm_attn, mix_weight)
    attended_lo, queries, key_rows, value_rows, log_totals = attend(
        mixed, cosine, sine_table, valid_rows[None, :]
    )
    after_attention = after_first + matmul(attended_lo, proj_weight)
    norm_conv = lowered(layer_norm(after_attention, gain_f[2]))
    after_attention, norm_conv, attended_lo, queries, key_rows, value_rows, log_totals = fence(
        [rows_in, heads[0]],
        after_attention,
        norm_conv,
        attended_lo,
        queries,
        key_rows,
        value_rows,
        log_totals,
    )

    rows_in.stage(4)
    heads[1].step("far")
    expand_weight, conv_weight = rows_in.wholes[3]
    expanded = matmul(norm_conv, expand_weight)
    conv_out, conv_sums = conv_forward(expanded, valid_rows[:, None], vectors)
    sums = cube.total(conv_sums)
    sums, conv_out, after_attention, expanded, norm_conv = fence(
        [rows_in, *heads], sums, conv_out, after_attention, expanded, norm_conv
    )

    rows_in.stage(5)
    heads[1].step("near")
    (inner_1,) = rows_in.wholes[4]
    frame_count = sums[2, 0]
    channel_mean = sums[0] / frame_count
    variance = sums[1] / frame_count - channel_mean * channel_mean
    inverse = lax.rsqrt(variance + eps)
    normalized = (conv_out - channel_mean) * inverse
    normed_bn = normalized * gain_f[3]
    swish_lo = lowered(jax.nn.silu(normed_bn))
    after_conv = after_attention + matmul(swish_lo, conv_weight)
    norm_second = lowered(layer_norm(after_conv, gain_f[4]))
    pre_second = matmul(norm_second, inner_1)
    act_second = lowered(jax.nn.silu(pre_second))
    pre_second = lowered(pre_second)
    after_conv, norm_second, pre_second, act_second, swish_lo = fence(
        [rows_in, *heads], after_conv, norm_second, pre_second, act_second, swish_lo
    )

    rows_in.stage(6)
    (outer_1,) = rows_in.wholes[5]
    head_cols = joined_heads(cube, heads)
    after_second = after_conv + 0.5 * matmul(act_second, outer_1)
    output_lo = lowered(layer_norm(after_second, gain_f[5]))

    picked_rows = lowered(matmul(pick_lo, output_lo))
    group_rows = cube.gather(picked_rows, head_order).reshape(group * slots, D)
    logits = matmul(group_rows, head_cols)
    row_top = jnp.max(logits, axis=1)
    row_sum = jnp.sum(jnp.exp(logits - row_top[:, None]), axis=1)
    onehot = jnp.arange(vocab_cols, dtype=jnp.int32)[None, :] == local_codes[:, None]
    target_logit = jnp.sum(jnp.where(onehot, logits, 0.0), axis=1)
    stats = cube.gather(jnp.stack([row_top, row_sum, target_logit]), head_order)
    stats = stats.reshape(group, 3, group * slots)
    whole_top = jnp.max(stats[:, 0], axis=0)
    whole_sum = jnp.sum(stats[:, 1] * jnp.exp(stats[:, 0] - whole_top), axis=0)
    log_norm = whole_top + jnp.log(whole_sum)
    ce_group = jnp.sum((log_norm - jnp.sum(stats[:, 2], axis=0)) * group_live)
    grad_logits = lowered(
        (jnp.exp(logits - log_norm[:, None]) - onehot.astype(jnp.float32)) * group_live[:, None]
    )
    head_grad = lowered(matmul_tn(group_rows, grad_logits))
    head_flow = HeadScattering(cube, head_grad, head_proj.shape[0])
    row_grads = lowered(matmul_nt(grad_logits, head_cols))
    row_sum = Summing(cube, row_grads.reshape((2,) * len(head_order) + (slots, D)), head_order[::-1])
    head_flow.step()
    for _ in head_order:
        row_sum.step()
    row_grads = lowered(row_sum.result())
    grad_output = out_grad.astype(jnp.float32) + matmul_tn(pick_lo, row_grads)

    rows_out = Scatter(cube)
    grad_second, gain_grad_final = norm_back(after_second, gain_f[5], grad_output)
    grad_out_lo = lowered(0.5 * grad_second)
    piece = weight_grads(cube, "tall", [(act_second, grad_out_lo[None])])
    grad_second, grad_out_lo, piece = fence([head_flow], grad_second, grad_out_lo, piece)

    head_flow.step()
    rows_out.stage()
    rows_out.push("tall", [ffn_outer[1]], piece)
    grad_pre = act_back(grad_out_lo, outer_1, pre_second)
    piece = weight_grads(cube, "wide", [(norm_second, grad_pre)])
    grad_conv_res, gain_grad_second = product_norm_back(
        grad_pre, inner_1, after_conv, vectors, 4, grad_second
    )
    grad_conv_res, piece = fence([head_flow, rows_out], grad_conv_res, piece)

    conv_res_lo = lowered(grad_conv_res)
    grad_bn = silu_back(normed_bn, matmul_nt(conv_res_lo, conv_weight))
    gain_grad_bn = jnp.sum(grad_bn * normalized, axis=0)
    grad_normalized = grad_bn * gain_f[3]
    back_sums = cube.total(
        jnp.stack(
            [
                jnp.sum(grad_normalized, axis=0),
                jnp.sum(grad_normalized * normalized, axis=0),
                jnp.broadcast_to(ce_group / group, (D,)),
            ]
            + [jnp.zeros((D,), jnp.float32)] * 5
        )
    )
    back_sums, grad_normalized, grad_conv_res, conv_res_lo, piece = fence(
        [], back_sums, grad_normalized, grad_conv_res, conv_res_lo, piece
    )

    head_flow.step()
    rows_out.stage()
    rows_out.push("wide", [ffn_inner[1]], piece)
    loss = back_sums[2, 0] / loss_scale
    grad_expanded, depth_grad = conv_backward(
        expanded, valid_rows[:, None], vectors, conv_out, grad_normalized, sums, back_sums
    )
    piece = weight_grads(cube, "wide", [(norm_conv, grad_expanded), (swish_lo, conv_res_lo[None])])
    grad_expanded, piece = fence([rows_out, head_flow], grad_expanded, piece)

    rows_out.stage()
    rows_out.push("wide", [conv_expand, conv_proj], piece)
    grad_attn_res, gain_grad_conv = product_norm_back(
        grad_expanded, expand_weight, after_attention, vectors, 2, grad_conv_res
    )
    attn_res_lo = lowered(grad_attn_res)
    grad_attended = lowered(matmul_nt(attn_res_lo, proj_weight))
    grad_mixed = attend_back(
        queries,
        key_rows,
        value_rows,
        log_totals,
        grad_attended,
        cosine,
        sine_table,
        valid_rows[None, :],
    )
    grad_mixed, attn_res_lo, grad_attn_res = fence(
        [rows_out], grad_mixed, attn_res_lo, grad_attn_res
    )

    rows_out.stage()
    piece = weight_grads(cube, "wide", [(norm_attn, grad_mixed), (attended_lo, attn_res_lo[None])])
    grad_first_res, gain_grad_attn = product_norm_back(
        grad_mixed, mix_weight, after_first, vectors, 1, grad_attn_res
    )
    grad_out_lo = lowered(0.5 * grad_first_res)
    grad_first_res, grad_out_lo, piece = fence([rows_out], grad_first_res, grad_out_lo, piece)

    rows_out.stage()
    rows_out.push("wide", [attn_qkv, attn_proj], piece)
    piece = weight_grads(cube, "tall", [(act_first, grad_out_lo[None])])
    grad_out_lo, piece = fence([rows_out], grad_out_lo, piece)

    rows_out.stage()
    rows_out.push("tall", [ffn_outer[0]], piece)
    grad_pre = act_back(grad_out_lo, outer_0, pre_first)
    piece = weight_grads(cube, "wide", [(norm_first, grad_pre)])
    grad_pre, piece = fence([rows_out], grad_pre, piece)

    rows_out.stage()
    rows_out.push("wide", [ffn_inner[0]], piece)
    input_grad, gain_grad_first = product_norm_back(
        grad_pre, inner_0, inputs, vectors, 0, grad_first_res
    )
    vector_grad = parted_vectors(
        [
            depth_grad,
            gain_grad_first,
            gain_grad_attn,
            gain_grad_conv,
            gain_grad_bn.reshape(1, D),
            gain_grad_second,
            gain_grad_final.reshape(1, D),
        ],
        devices,
    )
    vector_flow = Summing(
        cube, vector_grad.reshape((2,) * len(cube.bits) + vector_grad.shape[1:]), hops
    )
    vector_flow.step()
    vector_flow.step()
    input_grad = fence([rows_out, vector_flow], input_grad)

    for _ in range(4):
        rows_out.stage()
        if vector_flow.order:
            vector_flow.step()
        fence([rows_out, vector_flow], loss)
    for _ in vector_flow.order[:]:
        vector_flow.step()
    vector_grad = vector_flow.result()
    rows_out.stage()
    (
        (outer_grad_1,),
        (inner_grad_1,),
        (expand_grad, conv_proj_grad),
        (mix_grad, proj_grad),
        (outer_grad_0,),
        (inner_grad_0,),
    ) = rows_out.results
    return (
        output_lo,
        loss,
        input_grad,
        jnp.stack([inner_grad_0, inner_grad_1], axis=0),
        jnp.stack([outer_grad_0, outer_grad_1], axis=0),
        mix_grad,
        proj_grad,
        expand_grad,
        vector_grad[:TAPS],
        conv_proj_grad,
        vector_grad[TAPS:],
        head_flow.result(),
    )


def solution(mesh):
    placed = (
        P(("dp", "head"), None),
        P(None, ("dp", "head"), None),
        P(None, ("dp", "head"), None),
        P(("dp", "head"), None),
        P(("dp", "head"), None),
        P(("dp", "head"), None),
        P(None, ("dp", "head")),
        P(("dp", "head"), None),
        P(None, ("dp", "head")),
        P("dp", "head"),
        P(("dp", "head")),
        P(("dp", "head"), None),
        P(("dp", "head")),
        P(("dp", "head"), None),
    )
    sizes = {axis: mesh.shape[axis] for axis in AXES}
    return jax.shard_map(
        functools.partial(shards, sizes),
        mesh=mesh,
        in_specs=placed,
        out_specs=(
            P(("dp", "head"), None),
            P(),
            P(("dp", "head"), None),
            P(None, ("dp", "head"), None),
            P(None, ("dp", "head"), None),
            P(("dp", "head"), None),
            P(("dp", "head"), None),
            P(("dp", "head"), None),
            P(None, ("dp", "head")),
            P(("dp", "head"), None),
            P(None, ("dp", "head")),
            P("dp", "head"),
        ),
        check_vma=False,
    )
```

```python
import functools
import math

import jax
import jax.numpy as jnp
from jax import lax
from jax.experimental import pallas as pl
from jax.experimental.pallas import tpu as pltpu
from jax.sharding import PartitionSpec as P

D = 1024
H = 8
HD = 128
VOCAB = 8192
SEQ = 512
SPAN = 10
NSPAN = 20
UTT_DEV = 1


eps = 1e-05


def layer_norm(values, gain_row):
    center = values - jnp.mean(values, axis=-1, keepdims=True)
    variance = jnp.mean(center * center, axis=-1, keepdims=True)
    return center * lax.rsqrt(variance + eps) * gain_row


def lowered(values):
    return values.astype(jnp.bfloat16)


def matmul(operand, weight):
    return jnp.dot(operand, weight, preferred_element_type=jnp.float32)


def matmul_tn(operand, weight):
    return lax.dot_general(
        operand, weight, (((0,), (0,)), ((), ())), preferred_element_type=jnp.float32
    )


def matmul_nt(operand, weight):
    return lax.dot_general(
        operand, weight, (((1,), (1,)), ((), ())), preferred_element_type=jnp.float32
    )


def norm_back(values, gain_row, grads):
    unused, pullback = jax.vjp(layer_norm, values, gain_row)
    return pullback(grads)


def silu_back(values, grads):
    return jax.vjp(jax.nn.silu, values)[1](grads)[0]


AXES = ("dp", "head")
BRIEF = pl.CostEstimate(flops=0, bytes_accessed=0, transcendentals=0)
ANY = pl.BlockSpec(memory_space=pl.ANY)
VMEM = pl.BlockSpec(memory_space=pltpu.VMEM)
Z1, Z0, X, Y, C = range(5)


def local_copies(plan, inputs, outputs, after=()):
    count = len(inputs)

    def kernel(*refs):
        sources, targets, sem = refs[:count], refs[count + len(after) : -1], refs[-1]
        dp, head = lax.axis_index("dp"), lax.axis_index("head")
        where = (dp // 4, dp // 2 % 2, dp % 2, head // 2, head % 2)
        copies = []
        for at, (source, target) in enumerate(plan(where, sources, targets)):
            copies.append(pltpu.make_async_copy(source, target, sem.at[at]))
            copies[-1].start()
        for copy in copies:
            copy.wait()

    size = sum(math.prod(shape) for shape in outputs) * inputs[0].dtype.itemsize
    results = pl.pallas_call(
        kernel,
        out_shape=[jax.ShapeDtypeStruct(shape, inputs[0].dtype) for shape in outputs],
        in_specs=[ANY] * (count + len(after)),
        out_specs=[VMEM] * len(outputs),
        scratch_shapes=[pltpu.SemaphoreType.DMA((16,))],
        cost_estimate=BRIEF,
        compiler_params=pltpu.CompilerParams(vmem_limit_bytes=size + (1 << 20)),
    )(*inputs, *after)
    return list(results)


def flip(bit, by):
    return (bit + by) % 2


class Cube:
    def __init__(self, sizes):
        self.sizes = sizes
        self.tuned = sizes == {"dp": 8, "head": 4}
        self.bits = []
        for axis in AXES:
            bit = sizes[axis] // 2
            while bit:
                self.bits.append((axis, bit))
                bit //= 2

    def mine(self, at):
        axis, bit = self.bits[at]
        return (lax.axis_index(axis) // bit) % 2

    def swap(self, values, at):
        axis, bit = self.bits[at]
        return lax.ppermute(values, axis, [(i, i ^ bit) for i in range(self.sizes[axis])])

    def gather(self, shard, order):
        held = []
        values = shard
        for at in order:
            place = sum(other < at for other in held)
            values = self.join(values, self.swap(values, at), at, place)
            held.append(at)
        return values

    def join(self, values, got, at, place):
        if self.tuned and values.dtype != jnp.int32:
            shape = values.shape[:place] + (2,) + values.shape[place:]

            def plan(where, sources, targets):
                for by in range(2):
                    index = (slice(None),) * place + (flip(where[at], by),)
                    yield sources[by], targets[0].at[index]

            return local_copies(plan, [values, got], [shape])[0]
        mine = self.mine(at)
        first = jnp.where(mine == 0, values, got)
        second = jnp.where(mine == 0, got, values)
        return jnp.stack([first, second], axis=place)

    def place(self):
        dp, head = lax.axis_index("dp"), lax.axis_index("head")
        parts = jnp.array([4, 2, 1, 0, 0]), jnp.array([0, 0, 0, 2, 1])
        either = jnp.where(parts[0] > 0, dp & parts[0], head & parts[1])
        return (either > 0).astype(jnp.int32)

    def total(self, values):
        for at in (C, Z0, Z1, X, Y) if self.tuned else range(len(self.bits)):
            values = values + self.swap(values, at)
        return values


TAPS = 32


def joined_vectors(parts):
    devices, rows, width = parts.shape

    def kernel(parts_ref, out_ref):
        pieces = [parts_ref[at].astype(jnp.float32) for at in range(devices)]
        out_ref[...] = jnp.concatenate(pieces, axis=1)

    return pl.pallas_call(
        kernel,
        out_shape=jax.ShapeDtypeStruct((rows, devices * width), jnp.float32),
        compiler_params=pltpu.CompilerParams(vmem_limit_bytes=16 << 20),
    )(parts)


def parted_vectors(arrays, devices):
    rows = sum(array.shape[0] for array in arrays)
    width = D // devices

    def kernel(*refs):
        start = 0
        for ref in refs[:-1]:
            count = ref.shape[0]
            values = ref[...]
            for at in range(devices):
                refs[-1][at, start : start + count, :] = values[:, at * width : (at + 1) * width]
            start += count

    return pl.pallas_call(
        kernel,
        out_shape=jax.ShapeDtypeStruct((devices, rows, width), jnp.float32),
        compiler_params=pltpu.CompilerParams(vmem_limit_bytes=16 << 20),
    )(*arrays)


class VectorGathering:
    def __init__(self, cube, shard, order):
        self.cube, self.order, self.held = cube, list(order), []
        self.state = [shard]

    def step(self, count=1):
        for _ in range(min(count, len(self.order))):
            at = self.order.pop(0)
            place = sum(other < at for other in self.held)
            (values,) = self.state
            self.state = [self.cube.join(values, self.cube.swap(values, at), at, place)]
            self.held.append(at)


class HeadGathering:
    def __init__(self, cube, shard):
        self.cube = cube
        self.state = [shard]

    def step(self, phase):
        if not self.cube.tuned:
            if phase == "x":
                self.state = [lax.all_gather(self.state[0], "dp", axis=0, tiled=True)]
            return
        if phase == "x":
            (own,) = self.state
            self.state = [own, self.cube.swap(own, X)]
        if phase == "far":
            own, got = self.state

            def plan(where, sources, targets):
                for by in range(2):
                    yield sources[by], targets[0].at[flip(where[X], by)]

            (pair,) = local_copies(plan, self.state, [(2,) + own.shape])
            self.state = [pair, self.cube.swap(pair, Z1)]
        if phase == "near":
            pair, got = self.state

            def plan(where, sources, targets):
                for by in range(2):
                    yield sources[by], targets[0].at[flip(where[Z1], by)]

            (four,) = local_copies(plan, self.state, [(2,) + pair.shape])
            self.state = [four, self.cube.swap(four, Z0)]


def joined_heads(cube, heads):
    if not cube.tuned:
        return jnp.concatenate([part.state[0] for part in heads], axis=1)
    parts = [part for flow in heads for part in flow.state]
    _, _, rows, half = parts[0].shape

    def plan(where, sources, targets):
        for at in range(4):
            columns = pl.ds(at // 2 * half, half)
            yield sources[at], targets[0].at[:, flip(where[Z0], at % 2), :, :, columns]

    (whole,) = local_copies(plan, parts, [(2, 2, 2, rows, 2 * half)])
    return whole.reshape(8 * rows, 2 * half)


def pick_of(values, index, place):
    return lax.dynamic_index_in_dim(values, index, place, keepdims=False)


def halves_kernel(at, place, *refs):
    dp, head = lax.axis_index("dp"), lax.axis_index("head")
    mine = (dp // 4, dp // 2 % 2, dp % 2, head // 2, head % 2)[at]
    keep, got, send_ref, keep_ref = refs
    for out, by in ((send_ref, 1), (keep_ref, 0)):
        index = (slice(None),) * place + (flip(mine, by),)
        total = keep[index].astype(jnp.float32) + got[index].astype(jnp.float32)
        out[...] = total.astype(out.dtype)


class Summing:
    def __init__(self, cube, values, order):
        self.cube, self.order = cube, list(order)
        self.held = sorted(order)
        self.state = [values]

    def step(self):
        cube, at = self.cube, self.order.pop(0)
        place = self.held.index(at)
        self.held.remove(at)
        left = self.state[0].shape[:place] + self.state[0].shape[place + 1 :]
        if not cube.tuned:
            values = sum(part.astype(jnp.float32) for part in self.state)
            values = values.astype(self.state[0].dtype)
            send = pick_of(values, 1 - cube.mine(at), place)
            keep = pick_of(values, cube.mine(at), place)
        elif len(self.state) == 1:

            def plan(where, sources, targets):
                for by in range(2):
                    index = (slice(None),) * place + (flip(where[at], 1 - by),)
                    yield sources[0].at[index], targets[by]

            send, keep = local_copies(plan, self.state, [left, left])
        else:
            size = math.prod(left) * self.state[0].dtype.itemsize
            send, keep = pl.pallas_call(
                functools.partial(halves_kernel, at, place),
                out_shape=[jax.ShapeDtypeStruct(left, self.state[0].dtype)] * 2,
                in_specs=[VMEM] * 2,
                out_specs=[VMEM] * 2,
                compiler_params=pltpu.CompilerParams(vmem_limit_bytes=6 * size + (4 << 20)),
            )(*self.state)
        self.state = [keep, cube.swap(send, at)]

    def result(self):
        return sum(part.astype(jnp.float32) for part in self.state)


class Gather:
    def __init__(self, cube, pieces):
        self.cube = cube
        self.pieces = pieces
        self.wholes = [None] * len(pieces)
        if cube.tuned:
            self.shards = [uniform_shard(kind, arrays) for kind, arrays in pieces]
        self.state = {}

    def stage(self, t):
        cube, old, new = self.cube, self.state, {}
        count = len(self.pieces)
        live = lambda at: 0 <= at < count
        if not cube.tuned:
            if live(t - 1):
                self.wholes[t - 1] = [
                    lax.all_gather(array, AXES, axis=0, tiled=True)
                    for array in self.pieces[t - 1][1]
                ]
            return
        half = COLUMNS // 2
        slots = 2 * live(t) + live(t + 1)
        old_slots = 2 * live(t - 1) + live(t)
        inputs, shapes, jobs = [], [], []

        def give(name):
            inputs.append(old[name])
            return len(inputs) - 1

        def make(shape):
            shapes.append(shape)
            return len(shapes) - 1

        pair = None
        if live(t + 2):
            parts, pair = (give("z1s"), give("z1g")), make((2, ROWS, COLUMNS))
            jobs.append(lambda w, s, o, parts=parts, pair=pair: [
                (s[parts[by]], o[pair].at[flip(w[Z1], by)]) for by in range(2)
            ])
        if slots:
            x_out, y_out = (make((2, 2, slots, ROWS, half)) for _ in range(2))
        if live(t):
            xs, xg, ys, yg = (give(name) for name in ("xs", "xg", "ys", "yg"))
            jobs.append(lambda w, s, o: [
                pair_of
                for by in range(2)
                for pair_of in (
                    (s[(xs, xg)[by]].at[:, :, old_slots - 1], o[y_out].at[:, :, flip(w[X], by)]),
                    (s[(ys, yg)[by]].at[:, :, old_slots - 1], o[x_out].at[:, :, flip(w[Y], by)]),
                )
            ])
        if live(t + 1):
            zs, zg = give("z0s"), give("z0g")
            jobs.append(lambda w, s, o: [
                (
                    s[(zs, zg)[by]].at[:, :, pl.ds(side * half, half)],
                    o[(x_out, y_out)[side]].at[:, flip(w[Z0], by), slots - 1],
                )
                for by in range(2)
                for side in range(2)
            ])
        if jobs:
            made = local_copies(
                lambda w, s, o: [each for job in jobs for each in job(w, s, o)], inputs, shapes
            )
            if slots:
                new["xs"], new["ys"] = made[x_out], made[y_out]
                new["xg"], new["yg"] = cube.swap(made[x_out], X), cube.swap(made[y_out], Y)
            if pair is not None:
                new["z0s"], new["z0g"] = made[pair], cube.swap(made[pair], Z0)
        if live(t + 3):
            new["z1s"] = self.shards[t + 3]
            new["z1g"] = cube.swap(self.shards[t + 3], Z1)
        if live(t - 1):

            def plan(w, s, o):
                for by in range(2):
                    yield (
                        s[by].at[:, :, pl.ds(0, 2)],
                        o[0].at[:, :, :, flip(w[Y], by), :, pl.ds(0, half)],
                    )
                    yield (
                        s[2 + by].at[:, :, pl.ds(0, 2)],
                        o[0].at[:, :, flip(w[X], by), :, :, pl.ds(half, half)],
                    )

            (most,) = local_copies(
                plan,
                [old[name] for name in ("ys", "yg", "xs", "xg")],
                [(2, 2, 2, 2, ROWS, COLUMNS)],
                [new[name] for name in ("xs", "z0s") if name in new][:1],
            )
            got = cube.swap(most, C)
            kind, arrays = self.pieces[t - 1]

            def plan_whole(w, s, o):
                for by in range(2):
                    for at, rows, columns in tiles_of(kind, arrays):
                        yield (
                            s[by].at[:, :, :, :, :, columns],
                            o[at].at[:, :, :, :, flip(w[C], by), rows],
                        )

            made = local_copies(
                plan_whole, [most, got], [(2, 2, 2, 2, 2) + array.shape for array in arrays]
            )
            self.wholes[t - 1] = [
                whole.reshape(-1, array.shape[1]) for whole, array in zip(made, arrays)
            ]
        self.state = new


ROWS, COLUMNS = 32, 4096


def uniform_shard(kind, arrays):
    if kind == "tall":
        return jnp.concatenate([arrays[0][at : at + ROWS] for at in range(0, 4 * ROWS, ROWS)], axis=1)
    spare = COLUMNS - sum(array.shape[1] for array in arrays)
    extra = [arrays[0][:, :spare]] if spare else []
    return jnp.concatenate(arrays + extra, axis=1) if len(arrays) > 1 else arrays[0]


def tiles_of(kind, arrays):
    if kind == "tall":
        width = arrays[0].shape[1]
        for at in range(4):
            yield 0, pl.ds(at * ROWS, ROWS), pl.ds(at * width, width)
    else:
        start = 0
        for at, array in enumerate(arrays):
            yield at, pl.ds(0, ROWS), pl.ds(start, array.shape[1])
            start += array.shape[1]


def added(out, out_at, first, first_at, second, second_at):
    total = first[first_at].astype(jnp.float32) + second[second_at].astype(jnp.float32)
    out[out_at] = total.astype(out.dtype)


class Scatter:
    def __init__(self, cube):
        self.cube = cube
        self.state = {}
        self.results = []
        self.queue = []
        self.first = []

    def sums(self, sent, after):
        old = self.state
        half = COLUMNS // 2
        inputs, in_specs, names, shapes, out_specs, jobs = [], [], [], [], [], []
        mine = lambda w, at: (w[at] + sent) % 2

        def take(name, block, index):
            inputs.append(old[name])
            in_specs.append(pl.BlockSpec(block, index))
            return len(inputs) - 1

        def make(name, shape, block, index):
            names.append(name)
            shapes.append(jax.ShapeDtypeStruct(shape, jnp.bfloat16))
            out_specs.append(pl.BlockSpec(block, index))
            return len(names) - 1

        has_n, has_m = "ck" in old, "ak" in old
        slots = 2 * has_n + has_m
        corner = (None, None)
        if sent and slots:
            sent_shape = (2, 2, slots, ROWS, half)
            x_out = make("x", sent_shape, corner + sent_shape[2:], lambda a, b, w: (a, b, 0, 0, 0))
            y_out = make("y", sent_shape, corner + sent_shape[2:], lambda a, b, w: (a, b, 0, 0, 0))
        if has_n:
            left_block, right_block = corner + (2, None, ROWS, half), corner + (None, 2, ROWS, half)
            left_index = lambda a, b, w: (a, b, 0, mine(w, Y), 0, 0)
            right_index = lambda a, b, w: (a, b, mine(w, X), 0, 0, 1)
            lefts = [take(name, left_block, left_index) for name in ("ck", "cg")]
            rights = [take(name, right_block, right_index) for name in ("ck", "cg")]
            if not sent:
                kept = (2, 2, 2, ROWS, half)
                y_out = make("ak", kept, corner + kept[2:], lambda a, b, w: (a, b, 0, 0, 0))
                x_out = make("bk", kept, corner + kept[2:], lambda a, b, w: (a, b, 0, 0, 0))

            def job_n(s, o, y_out=y_out, x_out=x_out):
                for k in range(2):
                    added(o[y_out], k, s[lefts[0]], k, s[lefts[1]], k)
                    added(o[x_out], k, s[rights[0]], k, s[rights[1]], k)

            jobs.append(job_n)
        if has_m:
            block = corner + (None, ROWS, half)
            x_index = lambda a, b, w: (a, b, mine(w, X), 0, 0)
            y_index = lambda a, b, w: (a, b, mine(w, Y), 0, 0)
            lefts_m = take("ak", block, x_index), take("yg", block, x_index)
            rights_m = take("bk", block, y_index), take("xg", block, y_index)
            place = slots - 1 if sent else slice(None)
            if not sent:
                kept = (2, 2, ROWS, half)
                a_out = make("a4k", kept, corner + kept[2:], lambda a, b, w: (a, b, 0, 0))
                b_out = make("b4k", kept, corner + kept[2:], lambda a, b, w: (a, b, 0, 0))
            else:
                a_out, b_out = x_out, y_out

            def job_m(s, o):
                every = slice(None)
                added(o[a_out], place, s[lefts_m[0]], every, s[lefts_m[1]], every)
                added(o[b_out], place, s[rights_m[0]], every, s[rights_m[1]], every)

            jobs.append(job_m)
        if "a4k" in old:
            last = old["xg"].shape[2] - 1
            block = (None, None, ROWS, half)
            index = lambda a, b, w: (a, mine(w, Z0), 0, 0)
            got_block = (None, None, None, ROWS, half)
            got_index = lambda a, b, w: (a, mine(w, Z0), last, 0, 0)
            lefts_z = take("a4k", block, index), take("xg", got_block, got_index)
            rights_z = take("b4k", block, index), take("yg", got_block, got_index)
            z_out = make(
                "z" if sent else "zk",
                (2, ROWS, COLUMNS),
                (None, ROWS, COLUMNS),
                lambda a, b, w: (a, 0, 0),
            )

            def job_z(s, o):
                @pl.when(pl.program_id(1) == 0)
                def _():
                    every = slice(None)
                    left = (every, slice(0, half))
                    right = (every, slice(half, COLUMNS))
                    added(o[z_out], left, s[lefts_z[0]], every, s[lefts_z[1]], every)
                    added(o[z_out], right, s[rights_z[0]], every, s[rights_z[1]], every)

            jobs.append(job_z)
        if "zk" in old:
            block, index = (None, ROWS, COLUMNS), lambda a, b, w: (mine(w, Z1), 0, 0)
            pair = take("zk", block, index), take("zg", block, index)
            f_out = make(
                "f" if sent else "fk", (ROWS, COLUMNS), (ROWS, COLUMNS), lambda a, b, w: (0, 0)
            )

            def job_f(s, o):
                @pl.when((pl.program_id(0) == 0) & (pl.program_id(1) == 0))
                def _():
                    every = slice(None)
                    added(o[f_out], every, s[pair[0]], every, s[pair[1]], every)

            jobs.append(job_f)
        if not jobs:
            return {}

        def kernel(where, *refs):
            sources, targets = refs[: len(inputs)], refs[len(inputs) + len(after) :]
            for job in jobs:
                job(sources, targets)

        size = sum(math.prod(shape.shape) for shape in shapes)
        made = pl.pallas_call(
            kernel,
            grid_spec=pltpu.PrefetchScalarGridSpec(
                num_scalar_prefetch=1,
                grid=(2, 2),
                in_specs=in_specs + [ANY] * len(after),
                out_specs=out_specs,
            ),
            out_shape=shapes,
            cost_estimate=BRIEF,
            compiler_params=pltpu.CompilerParams(vmem_limit_bytes=9 << 20),
        )(self.cube.where, *inputs, *after)
        return dict(zip(names, made))

    def stage(self, value=None):
        cube, old, new = self.cube, self.state, {}
        if not cube.tuned:
            return value
        sends = self.sums(1, [])
        if value is not None:
            sends, value = lax.optimization_barrier((sends, value))
        for name, at, got in (("x", X, "xg"), ("y", Y, "yg"), ("z", Z0, "zg"), ("f", Z1, "fg")):
            if name in sends:
                new[got] = cube.swap(sends[name], at)
        first = list(sends.values())[:1]
        new.update(self.sums(0, first))
        if "fk" in old:
            kind, arrays = self.queue.pop(0)
            total = old["fk"].astype(jnp.float32) + old["fg"].astype(jnp.float32)
            self.results.append(split_shard(kind, arrays, total))
        self.first, self.state = first, new
        return value

    def push(self, kind, arrays, grads):
        if not self.cube.tuned:
            self.results.append(
                [
                    lax.psum_scatter(grad, AXES, scatter_dimension=0, tiled=True).astype(jnp.float32)
                    for grad in grads
                ]
            )
            return
        self.queue.append((kind, arrays))
        keep, send = grads
        self.state["ck"], self.state["cg"] = keep, self.cube.swap(send, C)


def split_shard(kind, arrays, total):
    if kind == "tall":
        width = arrays[0].shape[1]
        return [jnp.concatenate([total[:, at * width : (at + 1) * width] for at in range(4)], axis=0)]
    parts, start = [], 0
    for array in arrays:
        parts.append(total[:, start : start + array.shape[1]])
        start += array.shape[1]
    return parts


class HeadScattering:
    def __init__(self, cube, values, rows):
        self.cube = cube
        if not cube.tuned:
            self.whole = values
            return
        half = values.shape[1] // 2
        self.parts = [
            Summing(cube, values[:, :half].reshape(2, 2, 2, rows, half), (X, Z0, Z1)),
            Summing(cube, values[:, half:].reshape(2, 2, 2, rows, half), (Z0, Z1, X)),
        ]

    @property
    def state(self):
        return [part.state for part in self.parts] if self.cube.tuned else [self.whole]

    @state.setter
    def state(self, values):
        if not self.cube.tuned:
            self.whole = values[0]
            return
        for part, state in zip(self.parts, values):
            part.state = state

    def step(self):
        if self.cube.tuned:
            for part in self.parts:
                part.step()

    def result(self):
        if not self.cube.tuned:
            return lax.psum_scatter(self.whole, "dp", scatter_dimension=0, tiled=True).astype(
                jnp.float32
            )
        return jnp.concatenate([part.result() for part in self.parts], axis=1)


def shifted(pad_ref, shift_ref, rows):
    for r in range(8):
        shift_ref[r] = pad_ref[r : r + rows, :]


def conv_forward_kernel(lead_ref, gate_ref, valid_ref, taps_ref, conv_ref, sums_ref, pad, shift):
    length, width = lead_ref.shape
    edge = jnp.zeros((16, width), jnp.float32)
    valid = valid_ref[...]
    pad[0:16, :] = edge
    pad[16 : 16 + length, :] = lead_ref[...] * jax.nn.sigmoid(gate_ref[...]) * valid
    pad[16 + length : 40 + length, :] = jnp.zeros((24, width), jnp.float32)
    shifted(pad, shift, length + 32)
    chunk = 64
    taps = [taps_ref[j : j + 1, :] for j in range(32)]

    def step(at, totals):
        start = pl.multiple_of(at * chunk, chunk)
        total = jnp.zeros((chunk, width), jnp.float32)
        for j in range(32):
            total += shift[j % 8, pl.ds(start + j // 8 * 8, chunk), :] * taps[j]
        conv_ref[pl.ds(start, chunk), :] = total
        weighted = total * valid_ref[pl.ds(start, chunk), :]
        plain, squares = totals
        return (
            plain + jnp.sum(weighted, axis=0, keepdims=True),
            squares + jnp.sum(weighted * total, axis=0, keepdims=True),
        )

    zero = jnp.zeros((1, width), jnp.float32)
    plain, squares = lax.fori_loop(0, length // chunk, step, (zero, zero))
    sums_ref[0:1, :] = plain
    sums_ref[1:2, :] = squares
    sums_ref[2:3, :] = jnp.broadcast_to(jnp.sum(valid, axis=0, keepdims=True), (1, width))
    sums_ref[3:8, :] = jnp.zeros((5, width), jnp.float32)


def conv_forward(expanded, valid, taps):
    rows = expanded.shape[0]
    width = 128
    count = D // width
    return pl.pallas_call(
        conv_forward_kernel,
        grid=(count,),
        in_specs=[
            pl.BlockSpec((rows, width), lambda i: (0, i)),
            pl.BlockSpec((rows, width), lambda i: (0, i + count)),
            pl.BlockSpec((rows, 1), lambda i: (0, 0)),
            pl.BlockSpec((TAPS + 16, width), lambda i: (0, i)),
        ],
        out_specs=[
            pl.BlockSpec((rows, width), lambda i: (0, i)),
            pl.BlockSpec((8, width), lambda i: (0, i)),
        ],
        out_shape=[
            jax.ShapeDtypeStruct((rows, D), jnp.float32),
            jax.ShapeDtypeStruct((8, D), jnp.float32),
        ],
        scratch_shapes=[
            pltpu.VMEM((rows + 40, width), jnp.float32),
            pltpu.VMEM((8, rows + 32, width), jnp.float32),
        ],
        cost_estimate=BRIEF,
        compiler_params=pltpu.CompilerParams(vmem_limit_bytes=8 << 20),
    )(expanded, expanded, valid, taps)


def conv_backward_kernel(
    lead_ref,
    gate_ref,
    valid_ref,
    taps_ref,
    conv_ref,
    grad_ref,
    sums_ref,
    back_sums_ref,
    out_ref,
    taps_grad_ref,
    pad,
    shift,
    tap_sums,
):
    length, width = lead_ref.shape
    count = sums_ref[2:3, :]
    mean = sums_ref[0:1, :] / count
    inverse = lax.rsqrt(sums_ref[1:2, :] / count - mean * mean + eps)
    variance_grad = -0.5 * inverse * inverse * back_sums_ref[1:2, :]
    plain = (-inverse * back_sums_ref[0:1, :] - 2.0 * mean * variance_grad) / count
    scaled = 2.0 * variance_grad / count
    pad[0:16, :] = jnp.zeros((16, width), jnp.float32)
    pad[16 : 16 + length, :] = (
        grad_ref[...] * inverse + (plain + scaled * conv_ref[...]) * valid_ref[...]
    )
    pad[16 + length : 40 + length, :] = jnp.zeros((24, width), jnp.float32)
    shifted(pad, shift, length + 32)
    tap_sums[...] = jnp.zeros(tap_sums.shape, jnp.float32)
    chunk = 64
    taps = [taps_ref[j : j + 1, :] for j in range(32)]

    def step(at, carry):
        start = pl.multiple_of(at * chunk, chunk)
        here = pl.ds(start, chunk)
        lead, valid = lead_ref[here, :], valid_ref[here, :]
        gate = jax.nn.sigmoid(gate_ref[here, :])
        gated = lead * gate * valid
        total = jnp.zeros((chunk, width), jnp.float32)
        for j in range(32):
            off = 32 - j
            part = shift[off % 8, pl.ds(start + off // 8 * 8, chunk), :]
            total += part * taps[j]
            tap_sums[j] += jnp.sum((part * gated).reshape(chunk // 8, 8, width), axis=0)
        grad = total * valid
        out_ref[0, here, :] = (grad * gate).astype(jnp.bfloat16)
        out_ref[1, here, :] = (grad * lead * gate * (1.0 - gate)).astype(jnp.bfloat16)
        return carry

    lax.fori_loop(0, length // chunk, step, 0)
    taps_grad_ref[...] = jnp.sum(tap_sums[...], axis=1)


def conv_backward(expanded, valid, taps, conv_out, grads, sums, back_sums):
    rows = expanded.shape[0]
    width = 128
    count = D // width
    block = pl.BlockSpec((rows, width), lambda i: (0, i))
    return pl.pallas_call(
        conv_backward_kernel,
        grid=(count,),
        in_specs=[
            block,
            pl.BlockSpec((rows, width), lambda i: (0, i + count)),
            pl.BlockSpec((rows, 1), lambda i: (0, 0)),
            pl.BlockSpec((TAPS + 16, width), lambda i: (0, i)),
            block,
            block,
            pl.BlockSpec((8, width), lambda i: (0, i)),
            pl.BlockSpec((8, width), lambda i: (0, i)),
        ],
        out_specs=[
            pl.BlockSpec((2, rows, width), lambda i: (0, 0, i)),
            pl.BlockSpec((TAPS, width), lambda i: (0, i)),
        ],
        out_shape=[
            jax.ShapeDtypeStruct((2, rows, D), jnp.bfloat16),
            jax.ShapeDtypeStruct((32, D), jnp.float32),
        ],
        scratch_shapes=[
            pltpu.VMEM((rows + 40, width), jnp.float32),
            pltpu.VMEM((8, rows + 32, width), jnp.float32),
            pltpu.VMEM((32, 8, width), jnp.float32),
        ],
        cost_estimate=BRIEF,
        compiler_params=pltpu.CompilerParams(vmem_limit_bytes=8 << 20),
    )(expanded, expanded, valid, taps, conv_out, grads, sums, back_sums)


def nt_dot(left, right):
    return lax.dot_general(left, right, (((1,), (1,)), ((), ())), preferred_element_type=jnp.float32)


def act_back_kernel(grad_ref, weight_ref, pre_ref, out_ref):
    pre = pre_ref[...].astype(jnp.float32)
    gate = jax.nn.sigmoid(pre)
    slope = gate * (1.0 + pre * (1.0 - gate))
    out_ref[...] = (nt_dot(grad_ref[...], weight_ref[...]) * slope).astype(jnp.bfloat16)


def act_back(grad_lo, weight, pre):
    rows, inner = grad_lo.shape
    total = weight.shape[0]
    width = 512
    each = D // width
    return pl.pallas_call(
        act_back_kernel,
        grid=(total // width,),
        in_specs=[
            pl.BlockSpec((rows, inner), lambda i: (0, 0)),
            pl.BlockSpec((width, inner), lambda i: (i, 0)),
            pl.BlockSpec((rows, width), lambda i: (0, i)),
        ],
        out_specs=pl.BlockSpec((None, rows, width), lambda i: (i // each, 0, i % each)),
        out_shape=jax.ShapeDtypeStruct((total // D, rows, D), jnp.bfloat16),
        cost_estimate=BRIEF,
        compiler_params=pltpu.CompilerParams(vmem_limit_bytes=10 << 20),
    )(grad_lo, weight, pre)


def weight_grads_kernel(counts, *refs):
    lefts, rights = refs[: len(counts)], refs[len(counts) : 2 * len(counts)]
    keep_ref, send_ref = refs[-2:]
    core = lax.axis_index("head") % 2
    step, start = pl.program_id(0), 0
    for left, right, count in zip(lefts, rights, counts):

        @pl.when((step >= start) & (step < start + count))
        def _(left=left, right=right):
            total = matmul_tn(left[...], right[...]).astype(jnp.bfloat16)
            for at in range(16):
                first, second = (
                    total[(2 * at + by) * ROWS : (2 * at + by + 1) * ROWS, :] for by in range(2)
                )
                place = (at // 8, at // 4 % 2, at // 2 % 2, at % 2)

                @pl.when(core == 0)
                def _():
                    keep_ref[place], send_ref[place] = first, second

                @pl.when(core == 1)
                def _():
                    keep_ref[place], send_ref[place] = second, first

        start += count

    @pl.when(step >= start)
    def _():
        keep_ref[...] = jnp.zeros(keep_ref.shape, jnp.bfloat16)
        send_ref[...] = jnp.zeros(send_ref.shape, jnp.bfloat16)


def tall_grads_kernel(left_ref, right_ref, keep_ref, send_ref):
    core = lax.axis_index("head") % 2
    total = matmul_tn(left_ref[...], right_ref[...]).astype(jnp.bfloat16)
    for at in range(4):
        for group in range(4):
            first, second = (
                total[((2 * at + by) * 4 + group) * ROWS : ((2 * at + by) * 4 + group + 1) * ROWS, :]
                for by in range(2)
            )
            place = (at // 2, at % 2, slice(None), slice(group * D, (group + 1) * D))

            @pl.when(core == 0)
            def _():
                keep_ref[place], send_ref[place] = first, second

            @pl.when(core == 1)
            def _():
                keep_ref[place], send_ref[place] = second, first


def weight_grads(cube, kind, pairs):
    if not cube.tuned:
        return [
            jnp.concatenate([lowered(matmul_tn(left, each)) for each in rights], axis=1)
            for left, rights in pairs
        ]
    shape = (2, 2, 2, 2, ROWS, COLUMNS)
    rows = pairs[0][0].shape[0]
    common = dict(
        out_shape=[jax.ShapeDtypeStruct(shape, jnp.bfloat16)] * 2,
        cost_estimate=BRIEF,
        compiler_params=pltpu.CompilerParams(vmem_limit_bytes=22 << 20),
    )
    if kind == "tall":
        ((left, right),) = pairs
        return pl.pallas_call(
            tall_grads_kernel,
            grid=(4,),
            in_specs=[
                pl.BlockSpec((rows, D), lambda i: (0, i)),
                pl.BlockSpec((None, rows, D), lambda i: (0, 0, 0)),
            ],
            out_specs=[
                pl.BlockSpec((None, None, 2, 2, ROWS, COLUMNS), lambda i: (i // 2, i % 2, 0, 0, 0, 0))
            ]
            * 2,
            **common,
        )(left, right)
    counts, right_specs, start = [], [], 0
    for _, right in pairs:
        count = right.shape[0]
        right_specs.append(
            pl.BlockSpec(
                (None, rows, D),
                lambda i, start=start, count=count: (jnp.clip(i - start, 0, count - 1), 0, 0),
            )
        )
        counts.append(count)
        start += count
    return pl.pallas_call(
        functools.partial(weight_grads_kernel, counts),
        grid=(COLUMNS // D,),
        in_specs=[pl.BlockSpec((rows, D), lambda i: (0, 0))] * len(pairs) + right_specs,
        out_specs=[pl.BlockSpec(shape[:5] + (D,), lambda i: (0, 0, 0, 0, 0, i))] * 2,
        **common,
    )(*[left for left, _ in pairs], *[right for _, right in pairs])


def norm_back_kernel(
    row, grad_ref, weight_ref, values_ref, vectors_ref, above_ref, out_ref, gain_out, total
):
    step = pl.program_id(0)

    @pl.when(step == 0)
    def _():
        total[...] = jnp.zeros(total.shape, jnp.float32)

    total[...] += nt_dot(grad_ref[...], weight_ref[...])

    @pl.when(step == pl.num_programs(0) - 1)
    def _():
        rows = 128
        gain = vectors_ref[TAPS + row : TAPS + row + 1, :]

        def part(at, gain_total):
            here = pl.ds(pl.multiple_of(at * rows, rows), rows)
            values, grads = values_ref[here, :], total[here, :]
            center = values - jnp.mean(values, axis=-1, keepdims=True)
            scale = lax.rsqrt(jnp.mean(center * center, axis=-1, keepdims=True) + eps)
            normed = center * scale
            scaled = grads * gain
            mean = jnp.mean(scaled, axis=-1, keepdims=True)
            along = jnp.mean(scaled * normed, axis=-1, keepdims=True)
            out_ref[here, :] = above_ref[here, :] + (scaled - mean - normed * along) * scale
            return gain_total + jnp.sum(grads * normed, axis=0, keepdims=True)

        gain_out[...] = lax.fori_loop(
            0, total.shape[0] // rows, part, jnp.zeros(gain_out.shape, jnp.float32)
        )


def product_norm_back(grad_lo, weight, values, vectors, row, above):
    _, rows, _ = grad_lo.shape
    inner = weight.shape[1]
    width = 512
    each = D // width
    whole, vector = VMEM, VMEM
    return pl.pallas_call(
        functools.partial(norm_back_kernel, row),
        grid=(inner // width,),
        in_specs=[
            pl.BlockSpec((None, rows, width), lambda i: (i // each, 0, i % each)),
            pl.BlockSpec((D, width), lambda i: (0, i)),
            whole,
            vector,
            whole,
        ],
        out_specs=[whole, vector],
        out_shape=[
            jax.ShapeDtypeStruct((rows, D), jnp.float32),
            jax.ShapeDtypeStruct((1, D), jnp.float32),
        ],
        scratch_shapes=[pltpu.VMEM((rows, D), jnp.float32)],
        cost_estimate=BRIEF,
        compiler_params=pltpu.CompilerParams(vmem_limit_bytes=14 << 20),
    )(grad_lo, weight, values, vectors, above)


def turned(values, cosine, sine):
    half = HD // 2
    lead, tail = values[:, :half], values[:, half:]
    return jnp.concatenate([lead * cosine - tail * sine, tail * cosine + lead * sine], axis=1)


def attend_kernel(
    query_ref, key_ref, value_ref, cosine_ref, sine_ref, bias_ref, out_ref, query_out, key_out, value_out, log_out
):
    cosine, sine = cosine_ref[...], sine_ref[...]
    query = turned(query_ref[...], cosine, sine).astype(jnp.bfloat16)
    key = turned(key_ref[...], cosine, sine).astype(jnp.bfloat16)
    value = value_ref[...].astype(jnp.bfloat16)
    query_out[...], key_out[...], value_out[...] = query, key, value
    scores = jnp.where(bias_ref[...] > 0, nt_dot(query, key) * HD**-0.5, -1e30)
    top = jnp.max(scores, axis=-1, keepdims=True)
    weights = jnp.exp(scores - top)
    total = jnp.sum(weights, axis=-1, keepdims=True)
    probs = (weights * (1.0 / total)).astype(jnp.bfloat16)
    out_ref[...] = jnp.dot(probs, value, preferred_element_type=jnp.float32).astype(jnp.bfloat16)
    log_out[...] = jnp.broadcast_to(top + jnp.log(total), log_out.shape)


def attend(mixed, cosine, sine, valid):
    rows = mixed.shape[0]
    head = lambda shift: pl.BlockSpec((rows, HD), lambda i: (0, i + shift))
    fixed = lambda *shape: pl.BlockSpec(shape, lambda i: (0, 0))
    return pl.pallas_call(
        attend_kernel,
        grid=(H,),
        in_specs=[
            head(0),
            head(H),
            head(2 * H),
            fixed(rows, HD // 2),
            fixed(rows, HD // 2),
            fixed(1, rows),
        ],
        out_specs=[head(0)] * 5,
        out_shape=[jax.ShapeDtypeStruct((rows, D), jnp.bfloat16)] * 4
        + [jax.ShapeDtypeStruct((rows, D), jnp.float32)],
        cost_estimate=BRIEF,
        compiler_params=pltpu.CompilerParams(vmem_limit_bytes=12 << 20),
    )(mixed, mixed, mixed, cosine, sine, valid)


def attend_back_kernel(
    query_ref, key_ref, value_ref, log_ref, grad_ref, cosine_ref, sine_ref, bias_ref, out_ref
):
    query, key, value, grad = query_ref[...], key_ref[...], value_ref[...], grad_ref[...]
    cosine, sine = cosine_ref[...], -sine_ref[...]
    scores = jnp.where(bias_ref[...] > 0, nt_dot(query, key) * HD**-0.5, -1e30)
    probs = jnp.exp(scores - log_ref[:, :1])
    grad_probs = nt_dot(grad, value)
    along = jnp.sum(probs * grad_probs, axis=-1, keepdims=True)
    grad_scores = (probs * (grad_probs - along)).astype(jnp.bfloat16)
    out_ref[2] = matmul_tn(probs.astype(jnp.bfloat16), grad).astype(jnp.bfloat16)
    query_grad = matmul(grad_scores, key) * HD**-0.5
    key_grad = matmul_tn(grad_scores, query) * HD**-0.5
    out_ref[0] = turned(query_grad, cosine, sine).astype(jnp.bfloat16)
    out_ref[1] = turned(key_grad, cosine, sine).astype(jnp.bfloat16)


def attend_back(query, key, value, logs, grads, cosine, sine, valid):
    rows = query.shape[0]
    head = pl.BlockSpec((rows, HD), lambda i: (0, i))
    fixed = lambda *shape: pl.BlockSpec(shape, lambda i: (0, 0))
    return pl.pallas_call(
        attend_back_kernel,
        grid=(H,),
        in_specs=[head] * 5
        + [fixed(rows, HD // 2), fixed(rows, HD // 2), fixed(1, rows)],
        out_specs=pl.BlockSpec((3, rows, HD), lambda i: (0, 0, i)),
        out_shape=jax.ShapeDtypeStruct((3, rows, D), jnp.bfloat16),
        cost_estimate=BRIEF,
        compiler_params=pltpu.CompilerParams(vmem_limit_bytes=12 << 20),
    )(query, key, value, logs, grads, cosine, sine, valid)


def fence(flows, *values):
    states, values = lax.optimization_barrier(([flow.state for flow in flows], values))
    for flow, state in zip(flows, states):
        flow.state = state
    return values[0] if len(values) == 1 else values


def rows_of(values, count):
    return values.reshape(count, values.shape[-1])


def shards(
    sizes,
    frames,
    ffn_inner,
    ffn_outer,
    attn_qkv,
    attn_proj,
    conv_expand,
    conv_depth,
    conv_proj,
    norm_gains,
    head_proj,
    lengths,
    mask_starts,
    target_codes,
    out_grad,
):
    cube = Cube(sizes)
    cube.where = lax.optimization_barrier(cube.place()) if cube.tuned else None
    devices = sizes["dp"] * sizes["head"]
    ff = ffn_inner.shape[2]
    all_bits = list(range(len(cube.bits)))

    rows_in = Gather(
        cube,
        [
            ("wide", [ffn_inner[0]]),
            ("tall", [ffn_outer[0]]),
            ("wide", [attn_qkv, attn_proj]),
            ("wide", [conv_expand, conv_proj]),
            ("wide", [ffn_inner[1]]),
            ("tall", [ffn_outer[1]]),
        ],
    )
    head_half = head_proj.shape[1] // 2
    heads = [
        HeadGathering(cube, head_proj[:, :head_half]),
        HeadGathering(cube, head_proj[:, head_half:]),
    ]

    row_total = UTT_DEV * SEQ
    positions = jnp.arange(SEQ, dtype=jnp.int32)
    valid_mat = positions[None, :] < lengths[:, None]
    valid_rows = valid_mat.reshape(row_total).astype(jnp.float32)
    frequency = 10000.0 ** (-(jnp.arange(HD // 2, dtype=jnp.float32) * 2.0) / HD)
    angles = positions.astype(jnp.float32)[:, None] * frequency[None, :]
    cosine, sine_table = jnp.cos(angles), jnp.sin(angles)

    slots = UTT_DEV * NSPAN * SPAN
    slot_at = (mask_starts[:, :, None] + jnp.arange(SPAN, dtype=jnp.int32)).reshape(UTT_DEV, -1)
    slot_ok = slot_at < lengths[:, None]
    chosen = (slot_at + SEQ * jnp.arange(UTT_DEV, dtype=jnp.int32)[:, None]).reshape(slots)
    slot_live = slot_ok.reshape(slots)
    pick = (
        (chosen[:, None] == jnp.arange(row_total, dtype=jnp.int32)[None, :]) & slot_live[:, None]
    )
    picked_codes = jnp.sum(jnp.where(pick, target_codes[None, :], 0), axis=1)
    picked_codes = jnp.where(slot_live, picked_codes, -1)
    pick_lo = pick.astype(jnp.bfloat16)
    head_order = [at for at in range(len(cube.bits)) if cube.bits[at][0] == "head"]
    group = sizes["head"]
    vocab_cols = head_proj.shape[1]

    loss_scale = jnp.float32(devices * UTT_DEV * NSPAN * SPAN)
    hops = [C, Z1, Z0, X, Y] if cube.tuned else all_bits
    vector_in = VectorGathering(cube, jnp.concatenate([conv_depth, norm_gains, jnp.zeros_like(conv_depth[:10])], axis=0), hops)
    vector_in.step(2)
    group_codes = cube.gather(picked_codes, head_order).reshape(group * slots)
    rows_in.stage(-3)
    heads[0].step("x")
    heads[1].step("x")
    group_codes = fence([rows_in, vector_in, *heads], group_codes)

    rows_in.stage(-2)
    vector_in.step()
    fence([rows_in, vector_in], loss_scale)

    rows_in.stage(-1)
    vector_in.step()
    inputs = frames.astype(jnp.float32)
    fence([rows_in, vector_in], loss_scale)

    rows_in.stage(0)
    vector_in.step(len(hops))
    heads[0].step("far")
    fence([rows_in, vector_in, heads[0]], loss_scale)
    (vectors,) = vector_in.state
    vectors = fence([], joined_vectors(vectors.reshape((devices,) + vectors.shape[-2:])))
    gain_f = vectors[TAPS : TAPS + 6]
    norm_first = lowered(layer_norm(inputs, gain_f[0]))
    group_live = (group_codes >= 0).astype(jnp.float32)
    local_codes = group_codes - lax.axis_index("head") * vocab_cols

    rows_in.stage(1)
    (inner_0,) = rows_in.wholes[0]
    pre_first = matmul(norm_first, inner_0)
    act_first = lowered(jax.nn.silu(pre_first))
    pre_first = lowered(pre_first)
    pre_first, act_first = fence([rows_in], pre_first, act_first)

    rows_in.stage(2)
    (outer_0,) = rows_in.wholes[1]
    after_first = inputs + 0.5 * matmul(act_first, outer_0)
    norm_attn = lowered(layer_norm(after_first, gain_f[1]))
    after_first, norm_attn = fence([rows_in], after_first, norm_attn)

    rows_in.stage(3)
    heads[0].step("near")
    mix_weight, proj_weight = rows_in.wholes[2]
    mixed = matmul(norm_attn, mix_weight)
    attended_lo, queries, key_rows, value_rows, log_totals = attend(
        mixed, cosine, sine_table, valid_rows[None, :]
    )
    after_attention = after_first + matmul(attended_lo, proj_weight)
    norm_conv = lowered(layer_norm(after_attention, gain_f[2]))
    after_attention, norm_conv, attended_lo, queries, key_rows, value_rows, log_totals = fence(
        [rows_in, heads[0]],
        after_attention,
        norm_conv,
        attended_lo,
        queries,
        key_rows,
        value_rows,
        log_totals,
    )

    rows_in.stage(4)
    heads[1].step("far")
    expand_weight, conv_weight = rows_in.wholes[3]
    expanded = matmul(norm_conv, expand_weight)
    conv_out, conv_sums = conv_forward(expanded, valid_rows[:, None], vectors)
    sums = cube.total(conv_sums)
    sums, conv_out, after_attention, expanded, norm_conv = fence(
        [rows_in, *heads], sums, conv_out, after_attention, expanded, norm_conv
    )

    rows_in.stage(5)
    heads[1].step("near")
    (inner_1,) = rows_in.wholes[4]
    frame_count = sums[2, 0]
    channel_mean = sums[0] / frame_count
    variance = sums[1] / frame_count - channel_mean * channel_mean
    inverse = lax.rsqrt(variance + eps)
    normalized = (conv_out - channel_mean) * inverse
    normed_bn = normalized * gain_f[3]
    swish_lo = lowered(jax.nn.silu(normed_bn))
    after_conv = after_attention + matmul(swish_lo, conv_weight)
    norm_second = lowered(layer_norm(after_conv, gain_f[4]))
    pre_second = matmul(norm_second, inner_1)
    act_second = lowered(jax.nn.silu(pre_second))
    pre_second = lowered(pre_second)
    after_conv, norm_second, pre_second, act_second, swish_lo = fence(
        [rows_in, *heads], after_conv, norm_second, pre_second, act_second, swish_lo
    )

    rows_in.stage(6)
    (outer_1,) = rows_in.wholes[5]
    head_cols = joined_heads(cube, heads)
    after_second = after_conv + 0.5 * matmul(act_second, outer_1)
    output_lo = lowered(layer_norm(after_second, gain_f[5]))

    picked_rows = lowered(matmul(pick_lo, output_lo))
    group_rows = cube.gather(picked_rows, head_order).reshape(group * slots, D)
    logits = matmul(group_rows, head_cols)
    row_top = jnp.max(logits, axis=1)
    row_sum = jnp.sum(jnp.exp(logits - row_top[:, None]), axis=1)
    onehot = jnp.arange(vocab_cols, dtype=jnp.int32)[None, :] == local_codes[:, None]
    target_logit = jnp.sum(jnp.where(onehot, logits, 0.0), axis=1)
    stats = cube.gather(jnp.stack([row_top, row_sum, target_logit]), head_order)
    stats = stats.reshape(group, 3, group * slots)
    whole_top = jnp.max(stats[:, 0], axis=0)
    whole_sum = jnp.sum(stats[:, 1] * jnp.exp(stats[:, 0] - whole_top), axis=0)
    log_norm = whole_top + jnp.log(whole_sum)
    ce_group = jnp.sum((log_norm - jnp.sum(stats[:, 2], axis=0)) * group_live)
    grad_logits = lowered(
        (jnp.exp(logits - log_norm[:, None]) - onehot.astype(jnp.float32)) * group_live[:, None]
    )
    head_grad = lowered(matmul_tn(group_rows, grad_logits))
    head_flow = HeadScattering(cube, head_grad, head_proj.shape[0])
    row_grads = lowered(matmul_nt(grad_logits, head_cols))
    row_sum = Summing(cube, row_grads.reshape((2,) * len(head_order) + (slots, D)), head_order[::-1])
    head_flow.step()
    for _ in head_order:
        row_sum.step()
    row_grads = lowered(row_sum.result())
    grad_output = out_grad.astype(jnp.float32) + matmul_tn(pick_lo, row_grads)

    rows_out = Scatter(cube)
    grad_second, gain_grad_final = norm_back(after_second, gain_f[5], grad_output)
    grad_out_lo = lowered(0.5 * grad_second)
    piece = weight_grads(cube, "tall", [(act_second, grad_out_lo[None])])
    grad_second, grad_out_lo, piece = fence([head_flow], grad_second, grad_out_lo, piece)

    head_flow.step()
    rows_out.push("tall", [ffn_outer[1]], piece)
    grad_pre = act_back(grad_out_lo, outer_1, pre_second)
    piece = weight_grads(cube, "wide", [(norm_second, grad_pre)])
    grad_conv_res, gain_grad_second = product_norm_back(
        grad_pre, inner_1, after_conv, vectors, 4, grad_second
    )
    grad_conv_res, piece = fence([head_flow, rows_out], grad_conv_res, piece)

    conv_res_lo = lowered(grad_conv_res)
    grad_bn = silu_back(normed_bn, matmul_nt(conv_res_lo, conv_weight))
    gain_grad_bn = jnp.sum(grad_bn * normalized, axis=0)
    grad_normalized = grad_bn * gain_f[3]
    back_sums = cube.total(
        jnp.stack(
            [
                jnp.sum(grad_normalized, axis=0),
                jnp.sum(grad_normalized * normalized, axis=0),
                jnp.broadcast_to(ce_group / group, (D,)),
            ]
            + [jnp.zeros((D,), jnp.float32)] * 5
        )
    )
    back_sums, grad_normalized, grad_conv_res, conv_res_lo, piece = fence(
        [], back_sums, grad_normalized, grad_conv_res, conv_res_lo, piece
    )

    head_flow.step()
    rows_out.stage()
    rows_out.push("wide", [ffn_inner[1]], piece)
    loss = back_sums[2, 0] / loss_scale
    grad_expanded, depth_grad = conv_backward(
        expanded, valid_rows[:, None], vectors, conv_out, grad_normalized, sums, back_sums
    )
    piece = weight_grads(cube, "wide", [(norm_conv, grad_expanded), (swish_lo, conv_res_lo[None])])
    grad_expanded, piece = fence([rows_out, head_flow], grad_expanded, piece)

    rows_out.stage()
    rows_out.push("wide", [conv_expand, conv_proj], piece)
    grad_attn_res, gain_grad_conv = product_norm_back(
        grad_expanded, expand_weight, after_attention, vectors, 2, grad_conv_res
    )
    attn_res_lo = lowered(grad_attn_res)
    grad_attended = lowered(matmul_nt(attn_res_lo, proj_weight))
    grad_mixed = attend_back(
        queries,
        key_rows,
        value_rows,
        log_totals,
        grad_attended,
        cosine,
        sine_table,
        valid_rows[None, :],
    )
    piece = weight_grads(cube, "wide", [(norm_attn, grad_mixed), (attended_lo, attn_res_lo[None])])
    grad_mixed, grad_attn_res, piece = fence([rows_out], grad_mixed, grad_attn_res, piece)

    rows_out.stage()
    rows_out.push("wide", [attn_qkv, attn_proj], piece)
    grad_first_res, gain_grad_attn = product_norm_back(
        grad_mixed, mix_weight, after_first, vectors, 1, grad_attn_res
    )
    grad_out_lo = lowered(0.5 * grad_first_res)
    piece = weight_grads(cube, "tall", [(act_first, grad_out_lo[None])])
    grad_pre = act_back(grad_out_lo, outer_0, pre_first)
    grad_first_res, grad_pre, piece = fence([rows_out], grad_first_res, grad_pre, piece)

    rows_out.stage()
    rows_out.push("tall", [ffn_outer[0]], piece)
    piece = weight_grads(cube, "wide", [(norm_first, grad_pre)])
    input_grad, gain_grad_first = product_norm_back(
        grad_pre, inner_0, inputs, vectors, 0, grad_first_res
    )
    vector_grad = parted_vectors(
        [
            depth_grad,
            gain_grad_first,
            gain_grad_attn,
            gain_grad_conv,
            gain_grad_bn.reshape(1, D),
            gain_grad_second,
            gain_grad_final.reshape(1, D),
        ],
        devices,
    )
    vector_flow = Summing(
        cube, vector_grad.reshape((2,) * len(cube.bits) + vector_grad.shape[1:]), hops
    )
    vector_flow.step()
    input_grad, piece = fence([rows_out, vector_flow], input_grad, piece)

    rows_out.stage()
    rows_out.push("wide", [ffn_inner[0]], piece)
    vector_flow.step()
    fence([rows_out, vector_flow], loss)

    for _ in range(4):
        rows_out.stage()
        if vector_flow.order:
            vector_flow.step()
        fence([rows_out, vector_flow], loss)
    for _ in vector_flow.order[:]:
        vector_flow.step()
    vector_grad = vector_flow.result()
    rows_out.stage()
    (
        (outer_grad_1,),
        (inner_grad_1,),
        (expand_grad, conv_proj_grad),
        (mix_grad, proj_grad),
        (outer_grad_0,),
        (inner_grad_0,),
    ) = rows_out.results
    return (
        output_lo,
        loss,
        input_grad,
        jnp.stack([inner_grad_0, inner_grad_1], axis=0),
        jnp.stack([outer_grad_0, outer_grad_1], axis=0),
        mix_grad,
        proj_grad,
        expand_grad,
        vector_grad[:TAPS],
        conv_proj_grad,
        vector_grad[TAPS:],
        head_flow.result(),
    )


def solution(mesh):
    placed = (
        P(("dp", "head"), None),
        P(None, ("dp", "head"), None),
        P(None, ("dp", "head"), None),
        P(("dp", "head"), None),
        P(("dp", "head"), None),
        P(("dp", "head"), None),
        P(None, ("dp", "head")),
        P(("dp", "head"), None),
        P(None, ("dp", "head")),
        P("dp", "head"),
        P(("dp", "head")),
        P(("dp", "head"), None),
        P(("dp", "head")),
        P(("dp", "head"), None),
    )
    sizes = {axis: mesh.shape[axis] for axis in AXES}
    return jax.shard_map(
        functools.partial(shards, sizes),
        mesh=mesh,
        in_specs=placed,
        out_specs=(
            P(("dp", "head"), None),
            P(),
            P(("dp", "head"), None),
            P(None, ("dp", "head"), None),
            P(None, ("dp", "head"), None),
            P(("dp", "head"), None),
            P(("dp", "head"), None),
            P(("dp", "head"), None),
            P(None, ("dp", "head")),
            P(("dp", "head"), None),
            P(None, ("dp", "head")),
            P("dp", "head"),
        ),
        check_vma=False,
    )
```

```python
import functools
import math

import jax
import jax.numpy as jnp
from jax import lax
from jax.experimental import pallas as pl
from jax.experimental.pallas import tpu as pltpu
from jax.sharding import PartitionSpec as P

D = 1024
H = 8
HD = 128
VOCAB = 8192
SEQ = 512
SPAN = 10
NSPAN = 20
UTT_DEV = 1


eps = 1e-05


def layer_norm(values, gain_row):
    center = values - jnp.mean(values, axis=-1, keepdims=True)
    variance = jnp.mean(center * center, axis=-1, keepdims=True)
    return center * lax.rsqrt(variance + eps) * gain_row


def lowered(values):
    return values.astype(jnp.bfloat16)


def matmul(operand, weight):
    return jnp.dot(operand, weight, preferred_element_type=jnp.float32)


def matmul_tn(operand, weight):
    return lax.dot_general(
        operand, weight, (((0,), (0,)), ((), ())), preferred_element_type=jnp.float32
    )


def matmul_nt(operand, weight):
    return lax.dot_general(
        operand, weight, (((1,), (1,)), ((), ())), preferred_element_type=jnp.float32
    )


def norm_back(values, gain_row, grads):
    unused, pullback = jax.vjp(layer_norm, values, gain_row)
    return pullback(grads)


def silu_back(values, grads):
    return jax.vjp(jax.nn.silu, values)[1](grads)[0]


AXES = ("dp", "head")
BRIEF = pl.CostEstimate(flops=0, bytes_accessed=0, transcendentals=0)
ANY = pl.BlockSpec(memory_space=pl.ANY)
VMEM = pl.BlockSpec(memory_space=pltpu.VMEM)
Z1, Z0, X, Y, C = range(5)


def local_copies(plan, inputs, outputs, after=()):
    count = len(inputs)

    def kernel(*refs):
        sources, targets, sem = refs[:count], refs[count + len(after) : -1], refs[-1]
        dp, head = lax.axis_index("dp"), lax.axis_index("head")
        where = (dp // 4, dp // 2 % 2, dp % 2, head // 2, head % 2)
        copies = []
        for at, (source, target) in enumerate(plan(where, sources, targets)):
            copies.append(pltpu.make_async_copy(source, target, sem.at[at]))
            copies[-1].start()
        for copy in copies:
            copy.wait()

    size = sum(math.prod(shape) for shape in outputs) * inputs[0].dtype.itemsize
    results = pl.pallas_call(
        kernel,
        out_shape=[jax.ShapeDtypeStruct(shape, inputs[0].dtype) for shape in outputs],
        in_specs=[ANY] * (count + len(after)),
        out_specs=[VMEM] * len(outputs),
        scratch_shapes=[pltpu.SemaphoreType.DMA((16,))],
        cost_estimate=BRIEF,
        compiler_params=pltpu.CompilerParams(vmem_limit_bytes=size + (1 << 20)),
    )(*inputs, *after)
    return list(results)


def flip(bit, by):
    return (bit + by) % 2


class Cube:
    def __init__(self, sizes):
        self.sizes = sizes
        self.tuned = sizes == {"dp": 8, "head": 4}
        self.bits = []
        for axis in AXES:
            bit = sizes[axis] // 2
            while bit:
                self.bits.append((axis, bit))
                bit //= 2

    def mine(self, at):
        axis, bit = self.bits[at]
        return (lax.axis_index(axis) // bit) % 2

    def swap(self, values, at):
        axis, bit = self.bits[at]
        return lax.ppermute(values, axis, [(i, i ^ bit) for i in range(self.sizes[axis])])

    def gather(self, shard, order):
        held = []
        values = shard
        for at in order:
            place = sum(other < at for other in held)
            values = self.join(values, self.swap(values, at), at, place)
            held.append(at)
        return values

    def join(self, values, got, at, place):
        if self.tuned and values.dtype != jnp.int32:
            shape = values.shape[:place] + (2,) + values.shape[place:]

            def plan(where, sources, targets):
                for by in range(2):
                    index = (slice(None),) * place + (flip(where[at], by),)
                    yield sources[by], targets[0].at[index]

            return local_copies(plan, [values, got], [shape])[0]
        mine = self.mine(at)
        first = jnp.where(mine == 0, values, got)
        second = jnp.where(mine == 0, got, values)
        return jnp.stack([first, second], axis=place)

    def place(self):
        dp, head = lax.axis_index("dp"), lax.axis_index("head")
        parts = jnp.array([4, 2, 1, 0, 0]), jnp.array([0, 0, 0, 2, 1])
        either = jnp.where(parts[0] > 0, dp & parts[0], head & parts[1])
        return (either > 0).astype(jnp.int32)

    def total(self, values):
        for at in (C, Z0, Z1, X, Y) if self.tuned else range(len(self.bits)):
            values = values + self.swap(values, at)
        return values


TAPS = 32


def joined_vectors(parts):
    devices, rows, width = parts.shape

    def kernel(parts_ref, out_ref):
        pieces = [parts_ref[at].astype(jnp.float32) for at in range(devices)]
        out_ref[...] = jnp.concatenate(pieces, axis=1)

    return pl.pallas_call(
        kernel,
        out_shape=jax.ShapeDtypeStruct((rows, devices * width), jnp.float32),
        compiler_params=pltpu.CompilerParams(vmem_limit_bytes=16 << 20),
    )(parts)


def parted_vectors(arrays, devices):
    rows = sum(array.shape[0] for array in arrays)
    width = D // devices

    def kernel(*refs):
        start = 0
        for ref in refs[:-1]:
            count = ref.shape[0]
            values = ref[...]
            for at in range(devices):
                refs[-1][at, start : start + count, :] = values[:, at * width : (at + 1) * width]
            start += count

    return pl.pallas_call(
        kernel,
        out_shape=jax.ShapeDtypeStruct((devices, rows, width), jnp.float32),
        compiler_params=pltpu.CompilerParams(vmem_limit_bytes=16 << 20),
    )(*arrays)


class VectorGathering:
    def __init__(self, cube, shard, order):
        self.cube, self.order, self.held = cube, list(order), []
        self.state = [shard]

    def step(self, count=1):
        for _ in range(min(count, len(self.order))):
            at = self.order.pop(0)
            place = sum(other < at for other in self.held)
            (values,) = self.state
            self.state = [self.cube.join(values, self.cube.swap(values, at), at, place)]
            self.held.append(at)


class HeadGathering:
    def __init__(self, cube, shard):
        self.cube = cube
        self.state = [shard]

    def step(self, phase):
        if not self.cube.tuned:
            if phase == "x":
                self.state = [lax.all_gather(self.state[0], "dp", axis=0, tiled=True)]
            return
        if phase == "x":
            (own,) = self.state
            self.state = [own, self.cube.swap(own, X)]
        if phase == "far":
            own, got = self.state

            def plan(where, sources, targets):
                for by in range(2):
                    yield sources[by], targets[0].at[flip(where[X], by)]

            (pair,) = local_copies(plan, self.state, [(2,) + own.shape])
            self.state = [pair, self.cube.swap(pair, Z1)]
        if phase == "near":
            pair, got = self.state

            def plan(where, sources, targets):
                for by in range(2):
                    yield sources[by], targets[0].at[flip(where[Z1], by)]

            (four,) = local_copies(plan, self.state, [(2,) + pair.shape])
            self.state = [four, self.cube.swap(four, Z0)]


def joined_heads(cube, heads):
    if not cube.tuned:
        return jnp.concatenate([part.state[0] for part in heads], axis=1)
    parts = [part for flow in heads for part in flow.state]
    _, _, rows, half = parts[0].shape

    def plan(where, sources, targets):
        for at in range(4):
            columns = pl.ds(at // 2 * half, half)
            yield sources[at], targets[0].at[:, flip(where[Z0], at % 2), :, :, columns]

    (whole,) = local_copies(plan, parts, [(2, 2, 2, rows, 2 * half)])
    return whole.reshape(8 * rows, 2 * half)


def pick_of(values, index, place):
    return lax.dynamic_index_in_dim(values, index, place, keepdims=False)


def halves_kernel(at, place, *refs):
    dp, head = lax.axis_index("dp"), lax.axis_index("head")
    mine = (dp // 4, dp // 2 % 2, dp % 2, head // 2, head % 2)[at]
    keep, got, send_ref, keep_ref = refs
    for out, by in ((send_ref, 1), (keep_ref, 0)):
        index = (slice(None),) * place + (flip(mine, by),)
        total = keep[index].astype(jnp.float32) + got[index].astype(jnp.float32)
        out[...] = total.astype(out.dtype)


class Summing:
    def __init__(self, cube, values, order):
        self.cube, self.order = cube, list(order)
        self.held = sorted(order)
        self.state = [values]

    def step(self):
        cube, at = self.cube, self.order.pop(0)
        place = self.held.index(at)
        self.held.remove(at)
        left = self.state[0].shape[:place] + self.state[0].shape[place + 1 :]
        if not cube.tuned:
            values = sum(part.astype(jnp.float32) for part in self.state)
            values = values.astype(self.state[0].dtype)
            send = pick_of(values, 1 - cube.mine(at), place)
            keep = pick_of(values, cube.mine(at), place)
        elif len(self.state) == 1:

            def plan(where, sources, targets):
                for by in range(2):
                    index = (slice(None),) * place + (flip(where[at], 1 - by),)
                    yield sources[0].at[index], targets[by]

            send, keep = local_copies(plan, self.state, [left, left])
        else:
            size = math.prod(left) * self.state[0].dtype.itemsize
            send, keep = pl.pallas_call(
                functools.partial(halves_kernel, at, place),
                out_shape=[jax.ShapeDtypeStruct(left, self.state[0].dtype)] * 2,
                in_specs=[VMEM] * 2,
                out_specs=[VMEM] * 2,
                compiler_params=pltpu.CompilerParams(vmem_limit_bytes=6 * size + (4 << 20)),
            )(*self.state)
        self.state = [keep, cube.swap(send, at)]

    def result(self):
        return sum(part.astype(jnp.float32) for part in self.state)


class Gather:
    def __init__(self, cube, pieces):
        self.cube = cube
        self.pieces = pieces
        self.wholes = [None] * len(pieces)
        if cube.tuned:
            self.shards = [uniform_shard(kind, arrays) for kind, arrays in pieces]
        self.state = {}

    def start(self):
        cube = self.cube
        if not cube.tuned:
            return
        own = self.shards[0]
        far = cube.swap(own, Z1)
        near, both = cube.swap(own, Z0), cube.swap(far, Z0)

        def plan(w, s, o):
            for at in range(2):
                for by in range(2):
                    yield s[2 * at + by], o[at].at[flip(w[Z1], by)]

        pairs = local_copies(plan, [own, far, near, both], [(2, ROWS, COLUMNS)] * 2)
        self.state = {
            "z0s": pairs[0],
            "z0g": pairs[1],
            "z1s": self.shards[1],
            "z1g": cube.swap(self.shards[1], Z1),
        }

    def stage(self, t):
        cube, old, new = self.cube, self.state, {}
        count = len(self.pieces)
        live = lambda at: 0 <= at < count
        if not cube.tuned:
            if live(t - 1):
                self.wholes[t - 1] = [
                    lax.all_gather(array, AXES, axis=0, tiled=True)
                    for array in self.pieces[t - 1][1]
                ]
            return
        half = COLUMNS // 2
        slots = 2 * live(t) + live(t + 1)
        old_slots = 2 * live(t - 1) + live(t)
        inputs, shapes, jobs = [], [], []

        def give(name):
            inputs.append(old[name])
            return len(inputs) - 1

        def make(shape):
            shapes.append(shape)
            return len(shapes) - 1

        pair = None
        if live(t + 2):
            parts, pair = (give("z1s"), give("z1g")), make((2, ROWS, COLUMNS))
            jobs.append(lambda w, s, o, parts=parts, pair=pair: [
                (s[parts[by]], o[pair].at[flip(w[Z1], by)]) for by in range(2)
            ])
        if slots:
            x_out, y_out = (make((2, 2, slots, ROWS, half)) for _ in range(2))
        if live(t):
            xs, xg, ys, yg = (give(name) for name in ("xs", "xg", "ys", "yg"))
            jobs.append(lambda w, s, o: [
                pair_of
                for by in range(2)
                for pair_of in (
                    (s[(xs, xg)[by]].at[:, :, old_slots - 1], o[y_out].at[:, :, flip(w[X], by)]),
                    (s[(ys, yg)[by]].at[:, :, old_slots - 1], o[x_out].at[:, :, flip(w[Y], by)]),
                )
            ])
        if live(t + 1):
            zs, zg = give("z0s"), give("z0g")
            jobs.append(lambda w, s, o: [
                (
                    s[(zs, zg)[by]].at[:, :, pl.ds(side * half, half)],
                    o[(x_out, y_out)[side]].at[:, flip(w[Z0], by), slots - 1],
                )
                for by in range(2)
                for side in range(2)
            ])
        if jobs:
            made = local_copies(
                lambda w, s, o: [each for job in jobs for each in job(w, s, o)], inputs, shapes
            )
            if slots:
                new["xs"], new["ys"] = made[x_out], made[y_out]
                new["xg"], new["yg"] = cube.swap(made[x_out], X), cube.swap(made[y_out], Y)
            if pair is not None:
                new["z0s"], new["z0g"] = made[pair], cube.swap(made[pair], Z0)
        if live(t + 3):
            new["z1s"] = self.shards[t + 3]
            new["z1g"] = cube.swap(self.shards[t + 3], Z1)
        if live(t - 1):

            def plan(w, s, o):
                for by in range(2):
                    yield (
                        s[by].at[:, :, pl.ds(0, 2)],
                        o[0].at[:, :, :, flip(w[Y], by), :, pl.ds(0, half)],
                    )
                    yield (
                        s[2 + by].at[:, :, pl.ds(0, 2)],
                        o[0].at[:, :, flip(w[X], by), :, :, pl.ds(half, half)],
                    )

            (most,) = local_copies(
                plan,
                [old[name] for name in ("ys", "yg", "xs", "xg")],
                [(2, 2, 2, 2, ROWS, COLUMNS)],
                [new[name] for name in ("xs", "z0s") if name in new][:1],
            )
            got = cube.swap(most, C)
            kind, arrays = self.pieces[t - 1]

            def plan_whole(w, s, o):
                for by in range(2):
                    for at, rows, columns in tiles_of(kind, arrays):
                        yield (
                            s[by].at[:, :, :, :, :, columns],
                            o[at].at[:, :, :, :, flip(w[C], by), rows],
                        )

            made = local_copies(
                plan_whole, [most, got], [(2, 2, 2, 2, 2) + array.shape for array in arrays]
            )
            self.wholes[t - 1] = [
                whole.reshape(-1, array.shape[1]) for whole, array in zip(made, arrays)
            ]
        self.state = new


ROWS, COLUMNS = 32, 4096


def uniform_shard(kind, arrays):
    if kind == "tall":
        return jnp.concatenate([arrays[0][at : at + ROWS] for at in range(0, 4 * ROWS, ROWS)], axis=1)
    spare = COLUMNS - sum(array.shape[1] for array in arrays)
    extra = [arrays[0][:, :spare]] if spare else []
    return jnp.concatenate(arrays + extra, axis=1) if len(arrays) > 1 else arrays[0]


def tiles_of(kind, arrays):
    if kind == "tall":
        width = arrays[0].shape[1]
        for at in range(4):
            yield 0, pl.ds(at * ROWS, ROWS), pl.ds(at * width, width)
    else:
        start = 0
        for at, array in enumerate(arrays):
            yield at, pl.ds(0, ROWS), pl.ds(start, array.shape[1])
            start += array.shape[1]


def added(out, out_at, first, first_at, second, second_at):
    total = first[first_at].astype(jnp.float32) + second[second_at].astype(jnp.float32)
    out[out_at] = total.astype(out.dtype)


class Scatter:
    def __init__(self, cube):
        self.cube = cube
        self.state = {}
        self.results = []
        self.queue = []
        self.first = []

    def sums(self, sent, after):
        old = self.state
        half = COLUMNS // 2
        inputs, in_specs, names, shapes, out_specs, jobs = [], [], [], [], [], []
        mine = lambda w, at: (w[at] + sent) % 2

        def take(name, block, index):
            inputs.append(old[name])
            in_specs.append(pl.BlockSpec(block, index))
            return len(inputs) - 1

        def make(name, shape, block, index):
            names.append(name)
            shapes.append(jax.ShapeDtypeStruct(shape, jnp.bfloat16))
            out_specs.append(pl.BlockSpec(block, index))
            return len(names) - 1

        has_n, has_m = "ck" in old, "ak" in old
        slots = 2 * has_n + has_m
        corner = (None, None)
        if sent and slots:
            sent_shape = (2, 2, slots, ROWS, half)
            x_out = make("x", sent_shape, corner + sent_shape[2:], lambda a, b, w: (a, b, 0, 0, 0))
            y_out = make("y", sent_shape, corner + sent_shape[2:], lambda a, b, w: (a, b, 0, 0, 0))
        if has_n:
            left_block, right_block = corner + (2, None, ROWS, half), corner + (None, 2, ROWS, half)
            left_index = lambda a, b, w: (a, b, 0, mine(w, Y), 0, 0)
            right_index = lambda a, b, w: (a, b, mine(w, X), 0, 0, 1)
            lefts = [take(name, left_block, left_index) for name in ("ck", "cg")]
            rights = [take(name, right_block, right_index) for name in ("ck", "cg")]
            if not sent:
                kept = (2, 2, 2, ROWS, half)
                y_out = make("ak", kept, corner + kept[2:], lambda a, b, w: (a, b, 0, 0, 0))
                x_out = make("bk", kept, corner + kept[2:], lambda a, b, w: (a, b, 0, 0, 0))

            def job_n(s, o, y_out=y_out, x_out=x_out):
                for k in range(2):
                    added(o[y_out], k, s[lefts[0]], k, s[lefts[1]], k)
                    added(o[x_out], k, s[rights[0]], k, s[rights[1]], k)

            jobs.append(job_n)
        if has_m:
            block = corner + (None, ROWS, half)
            x_index = lambda a, b, w: (a, b, mine(w, X), 0, 0)
            y_index = lambda a, b, w: (a, b, mine(w, Y), 0, 0)
            lefts_m = take("ak", block, x_index), take("yg", block, x_index)
            rights_m = take("bk", block, y_index), take("xg", block, y_index)
            place = slots - 1 if sent else slice(None)
            if not sent:
                kept = (2, 2, ROWS, half)
                a_out = make("a4k", kept, corner + kept[2:], lambda a, b, w: (a, b, 0, 0))
                b_out = make("b4k", kept, corner + kept[2:], lambda a, b, w: (a, b, 0, 0))
            else:
                a_out, b_out = x_out, y_out

            def job_m(s, o):
                every = slice(None)
                added(o[a_out], place, s[lefts_m[0]], every, s[lefts_m[1]], every)
                added(o[b_out], place, s[rights_m[0]], every, s[rights_m[1]], every)

            jobs.append(job_m)
        if "a4k" in old:
            last = old["xg"].shape[2] - 1
            block = (None, None, ROWS, half)
            index = lambda a, b, w: (a, mine(w, Z0), 0, 0)
            got_block = (None, None, None, ROWS, half)
            got_index = lambda a, b, w: (a, mine(w, Z0), last, 0, 0)
            lefts_z = take("a4k", block, index), take("xg", got_block, got_index)
            rights_z = take("b4k", block, index), take("yg", got_block, got_index)
            z_out = make(
                "z" if sent else "zk",
                (2, ROWS, COLUMNS),
                (None, ROWS, COLUMNS),
                lambda a, b, w: (a, 0, 0),
            )

            def job_z(s, o):
                @pl.when(pl.program_id(1) == 0)
                def _():
                    every = slice(None)
                    left = (every, slice(0, half))
                    right = (every, slice(half, COLUMNS))
                    added(o[z_out], left, s[lefts_z[0]], every, s[lefts_z[1]], every)
                    added(o[z_out], right, s[rights_z[0]], every, s[rights_z[1]], every)

            jobs.append(job_z)
        if "zk" in old:
            block, index = (None, ROWS, COLUMNS), lambda a, b, w: (mine(w, Z1), 0, 0)
            pair = take("zk", block, index), take("zg", block, index)
            f_out = make(
                "f" if sent else "fk", (ROWS, COLUMNS), (ROWS, COLUMNS), lambda a, b, w: (0, 0)
            )

            def job_f(s, o):
                @pl.when((pl.program_id(0) == 0) & (pl.program_id(1) == 0))
                def _():
                    every = slice(None)
                    added(o[f_out], every, s[pair[0]], every, s[pair[1]], every)

            jobs.append(job_f)
        if not jobs:
            return {}

        def kernel(where, *refs):
            sources, targets = refs[: len(inputs)], refs[len(inputs) + len(after) :]
            for job in jobs:
                job(sources, targets)

        size = sum(math.prod(shape.shape) for shape in shapes)
        made = pl.pallas_call(
            kernel,
            grid_spec=pltpu.PrefetchScalarGridSpec(
                num_scalar_prefetch=1,
                grid=(2, 2),
                in_specs=in_specs + [ANY] * len(after),
                out_specs=out_specs,
            ),
            out_shape=shapes,
            cost_estimate=BRIEF,
            compiler_params=pltpu.CompilerParams(vmem_limit_bytes=9 << 20),
        )(self.cube.where, *inputs, *after)
        return dict(zip(names, made))

    def stage(self, value=None):
        cube, old, new = self.cube, self.state, {}
        if not cube.tuned:
            return value
        sends = self.sums(1, [])
        if value is not None:
            sends, value = lax.optimization_barrier((sends, value))
        for name, at, got in (("x", X, "xg"), ("y", Y, "yg"), ("z", Z0, "zg"), ("f", Z1, "fg")):
            if name in sends:
                new[got] = cube.swap(sends[name], at)
        first = list(sends.values())[:1]
        new.update(self.sums(0, first))
        if "fk" in old:
            kind, arrays = self.queue.pop(0)
            total = old["fk"].astype(jnp.float32) + old["fg"].astype(jnp.float32)
            self.results.append(split_shard(kind, arrays, total))
        self.first, self.state = first, new
        return value

    def push(self, kind, arrays, grads):
        if not self.cube.tuned:
            self.results.append(
                [
                    lax.psum_scatter(grad, AXES, scatter_dimension=0, tiled=True).astype(jnp.float32)
                    for grad in grads
                ]
            )
            return
        self.queue.append((kind, arrays))
        keep, send = grads
        self.state["ck"], self.state["cg"] = keep, self.cube.swap(send, C)


def split_shard(kind, arrays, total):
    if kind == "tall":
        width = arrays[0].shape[1]
        return [jnp.concatenate([total[:, at * width : (at + 1) * width] for at in range(4)], axis=0)]
    parts, start = [], 0
    for array in arrays:
        parts.append(total[:, start : start + array.shape[1]])
        start += array.shape[1]
    return parts


class HeadScattering:
    def __init__(self, cube, values, rows):
        self.cube = cube
        if not cube.tuned:
            self.whole = values
            return
        half = values.shape[1] // 2
        self.parts = [
            Summing(cube, values[:, :half].reshape(2, 2, 2, rows, half), (X, Z0, Z1)),
            Summing(cube, values[:, half:].reshape(2, 2, 2, rows, half), (Z0, Z1, X)),
        ]

    @property
    def state(self):
        return [part.state for part in self.parts] if self.cube.tuned else [self.whole]

    @state.setter
    def state(self, values):
        if not self.cube.tuned:
            self.whole = values[0]
            return
        for part, state in zip(self.parts, values):
            part.state = state

    def step(self):
        if self.cube.tuned:
            for part in self.parts:
                part.step()

    def result(self):
        if not self.cube.tuned:
            return lax.psum_scatter(self.whole, "dp", scatter_dimension=0, tiled=True).astype(
                jnp.float32
            )
        return jnp.concatenate([part.result() for part in self.parts], axis=1)


def shifted(pad_ref, shift_ref, rows):
    for r in range(8):
        shift_ref[r] = pad_ref[r : r + rows, :]


def conv_forward_kernel(lead_ref, gate_ref, valid_ref, taps_ref, conv_ref, sums_ref, pad, shift):
    length, width = lead_ref.shape
    edge = jnp.zeros((16, width), jnp.float32)
    valid = valid_ref[...]
    pad[0:16, :] = edge
    pad[16 : 16 + length, :] = lead_ref[...] * jax.nn.sigmoid(gate_ref[...]) * valid
    pad[16 + length : 40 + length, :] = jnp.zeros((24, width), jnp.float32)
    shifted(pad, shift, length + 32)
    chunk = 64
    taps = [taps_ref[j : j + 1, :] for j in range(32)]

    def step(at, totals):
        start = pl.multiple_of(at * chunk, chunk)
        total = jnp.zeros((chunk, width), jnp.float32)
        for j in range(32):
            total += shift[j % 8, pl.ds(start + j // 8 * 8, chunk), :] * taps[j]
        conv_ref[pl.ds(start, chunk), :] = total
        weighted = total * valid_ref[pl.ds(start, chunk), :]
        plain, squares = totals
        return (
            plain + jnp.sum(weighted, axis=0, keepdims=True),
            squares + jnp.sum(weighted * total, axis=0, keepdims=True),
        )

    zero = jnp.zeros((1, width), jnp.float32)
    plain, squares = lax.fori_loop(0, length // chunk, step, (zero, zero))
    sums_ref[0:1, :] = plain
    sums_ref[1:2, :] = squares
    sums_ref[2:3, :] = jnp.broadcast_to(jnp.sum(valid, axis=0, keepdims=True), (1, width))
    sums_ref[3:8, :] = jnp.zeros((5, width), jnp.float32)


def conv_forward(expanded, valid, taps):
    rows = expanded.shape[0]
    width = 128
    count = D // width
    return pl.pallas_call(
        conv_forward_kernel,
        grid=(count,),
        in_specs=[
            pl.BlockSpec((rows, width), lambda i: (0, i)),
            pl.BlockSpec((rows, width), lambda i: (0, i + count)),
            pl.BlockSpec((rows, 1), lambda i: (0, 0)),
            pl.BlockSpec((TAPS + 16, width), lambda i: (0, i)),
        ],
        out_specs=[
            pl.BlockSpec((rows, width), lambda i: (0, i)),
            pl.BlockSpec((8, width), lambda i: (0, i)),
        ],
        out_shape=[
            jax.ShapeDtypeStruct((rows, D), jnp.float32),
            jax.ShapeDtypeStruct((8, D), jnp.float32),
        ],
        scratch_shapes=[
            pltpu.VMEM((rows + 40, width), jnp.float32),
            pltpu.VMEM((8, rows + 32, width), jnp.float32),
        ],
        cost_estimate=BRIEF,
        compiler_params=pltpu.CompilerParams(vmem_limit_bytes=8 << 20),
    )(expanded, expanded, valid, taps)


def conv_backward_kernel(
    lead_ref,
    gate_ref,
    valid_ref,
    taps_ref,
    conv_ref,
    grad_ref,
    sums_ref,
    back_sums_ref,
    out_ref,
    taps_grad_ref,
    pad,
    shift,
    tap_sums,
):
    length, width = lead_ref.shape
    count = sums_ref[2:3, :]
    mean = sums_ref[0:1, :] / count
    inverse = lax.rsqrt(sums_ref[1:2, :] / count - mean * mean + eps)
    variance_grad = -0.5 * inverse * inverse * back_sums_ref[1:2, :]
    plain = (-inverse * back_sums_ref[0:1, :] - 2.0 * mean * variance_grad) / count
    scaled = 2.0 * variance_grad / count
    pad[0:16, :] = jnp.zeros((16, width), jnp.float32)
    pad[16 : 16 + length, :] = (
        grad_ref[...] * inverse + (plain + scaled * conv_ref[...]) * valid_ref[...]
    )
    pad[16 + length : 40 + length, :] = jnp.zeros((24, width), jnp.float32)
    shifted(pad, shift, length + 32)
    tap_sums[...] = jnp.zeros(tap_sums.shape, jnp.float32)
    chunk = 64
    taps = [taps_ref[j : j + 1, :] for j in range(32)]

    def step(at, carry):
        start = pl.multiple_of(at * chunk, chunk)
        here = pl.ds(start, chunk)
        lead, valid = lead_ref[here, :], valid_ref[here, :]
        gate = jax.nn.sigmoid(gate_ref[here, :])
        gated = lead * gate * valid
        total = jnp.zeros((chunk, width), jnp.float32)
        for j in range(32):
            off = 32 - j
            part = shift[off % 8, pl.ds(start + off // 8 * 8, chunk), :]
            total += part * taps[j]
            tap_sums[j] += jnp.sum((part * gated).reshape(chunk // 8, 8, width), axis=0)
        grad = total * valid
        out_ref[0, here, :] = (grad * gate).astype(jnp.bfloat16)
        out_ref[1, here, :] = (grad * lead * gate * (1.0 - gate)).astype(jnp.bfloat16)
        return carry

    lax.fori_loop(0, length // chunk, step, 0)
    taps_grad_ref[...] = jnp.sum(tap_sums[...], axis=1)


def conv_backward(expanded, valid, taps, conv_out, grads, sums, back_sums):
    rows = expanded.shape[0]
    width = 128
    count = D // width
    block = pl.BlockSpec((rows, width), lambda i: (0, i))
    return pl.pallas_call(
        conv_backward_kernel,
        grid=(count,),
        in_specs=[
            block,
            pl.BlockSpec((rows, width), lambda i: (0, i + count)),
            pl.BlockSpec((rows, 1), lambda i: (0, 0)),
            pl.BlockSpec((TAPS + 16, width), lambda i: (0, i)),
            block,
            block,
            pl.BlockSpec((8, width), lambda i: (0, i)),
            pl.BlockSpec((8, width), lambda i: (0, i)),
        ],
        out_specs=[
            pl.BlockSpec((2, rows, width), lambda i: (0, 0, i)),
            pl.BlockSpec((TAPS, width), lambda i: (0, i)),
        ],
        out_shape=[
            jax.ShapeDtypeStruct((2, rows, D), jnp.bfloat16),
            jax.ShapeDtypeStruct((32, D), jnp.float32),
        ],
        scratch_shapes=[
            pltpu.VMEM((rows + 40, width), jnp.float32),
            pltpu.VMEM((8, rows + 32, width), jnp.float32),
            pltpu.VMEM((32, 8, width), jnp.float32),
        ],
        cost_estimate=BRIEF,
        compiler_params=pltpu.CompilerParams(vmem_limit_bytes=8 << 20),
    )(expanded, expanded, valid, taps, conv_out, grads, sums, back_sums)


def nt_dot(left, right):
    return lax.dot_general(left, right, (((1,), (1,)), ((), ())), preferred_element_type=jnp.float32)


def act_back_kernel(grad_ref, weight_ref, pre_ref, out_ref):
    pre = pre_ref[...].astype(jnp.float32)
    gate = jax.nn.sigmoid(pre)
    slope = gate * (1.0 + pre * (1.0 - gate))
    out_ref[...] = (nt_dot(grad_ref[...], weight_ref[...]) * slope).astype(jnp.bfloat16)


def act_back(grad_lo, weight, pre):
    rows, inner = grad_lo.shape
    total = weight.shape[0]
    width = 512
    each = D // width
    return pl.pallas_call(
        act_back_kernel,
        grid=(total // width,),
        in_specs=[
            pl.BlockSpec((rows, inner), lambda i: (0, 0)),
            pl.BlockSpec((width, inner), lambda i: (i, 0)),
            pl.BlockSpec((rows, width), lambda i: (0, i)),
        ],
        out_specs=pl.BlockSpec((None, rows, width), lambda i: (i // each, 0, i % each)),
        out_shape=jax.ShapeDtypeStruct((total // D, rows, D), jnp.bfloat16),
        cost_estimate=BRIEF,
        compiler_params=pltpu.CompilerParams(vmem_limit_bytes=10 << 20),
    )(grad_lo, weight, pre)


def weight_grads_kernel(counts, *refs):
    lefts, rights = refs[: len(counts)], refs[len(counts) : 2 * len(counts)]
    keep_ref, send_ref = refs[-2:]
    core = lax.axis_index("head") % 2
    step, start = pl.program_id(0), 0
    for left, right, count in zip(lefts, rights, counts):

        @pl.when((step >= start) & (step < start + count))
        def _(left=left, right=right):
            total = matmul_tn(left[...], right[...]).astype(jnp.bfloat16)
            for at in range(16):
                first, second = (
                    total[(2 * at + by) * ROWS : (2 * at + by + 1) * ROWS, :] for by in range(2)
                )
                place = (at // 8, at // 4 % 2, at // 2 % 2, at % 2)

                @pl.when(core == 0)
                def _():
                    keep_ref[place], send_ref[place] = first, second

                @pl.when(core == 1)
                def _():
                    keep_ref[place], send_ref[place] = second, first

        start += count

    @pl.when(step >= start)
    def _():
        keep_ref[...] = jnp.zeros(keep_ref.shape, jnp.bfloat16)
        send_ref[...] = jnp.zeros(send_ref.shape, jnp.bfloat16)


def tall_grads_kernel(left_ref, right_ref, keep_ref, send_ref):
    core = lax.axis_index("head") % 2
    total = matmul_tn(left_ref[...], right_ref[...]).astype(jnp.bfloat16)
    for at in range(4):
        for group in range(4):
            first, second = (
                total[((2 * at + by) * 4 + group) * ROWS : ((2 * at + by) * 4 + group + 1) * ROWS, :]
                for by in range(2)
            )
            place = (at // 2, at % 2, slice(None), slice(group * D, (group + 1) * D))

            @pl.when(core == 0)
            def _():
                keep_ref[place], send_ref[place] = first, second

            @pl.when(core == 1)
            def _():
                keep_ref[place], send_ref[place] = second, first


def weight_grads(cube, kind, pairs):
    if not cube.tuned:
        return [
            jnp.concatenate([lowered(matmul_tn(left, each)) for each in rights], axis=1)
            for left, rights in pairs
        ]
    shape = (2, 2, 2, 2, ROWS, COLUMNS)
    rows = pairs[0][0].shape[0]
    common = dict(
        out_shape=[jax.ShapeDtypeStruct(shape, jnp.bfloat16)] * 2,
        cost_estimate=BRIEF,
        compiler_params=pltpu.CompilerParams(vmem_limit_bytes=22 << 20),
    )
    if kind == "tall":
        ((left, right),) = pairs
        return pl.pallas_call(
            tall_grads_kernel,
            grid=(4,),
            in_specs=[
                pl.BlockSpec((rows, D), lambda i: (0, i)),
                pl.BlockSpec((None, rows, D), lambda i: (0, 0, 0)),
            ],
            out_specs=[
                pl.BlockSpec((None, None, 2, 2, ROWS, COLUMNS), lambda i: (i // 2, i % 2, 0, 0, 0, 0))
            ]
            * 2,
            **common,
        )(left, right)
    counts, right_specs, start = [], [], 0
    for _, right in pairs:
        count = right.shape[0]
        right_specs.append(
            pl.BlockSpec(
                (None, rows, D),
                lambda i, start=start, count=count: (jnp.clip(i - start, 0, count - 1), 0, 0),
            )
        )
        counts.append(count)
        start += count
    return pl.pallas_call(
        functools.partial(weight_grads_kernel, counts),
        grid=(COLUMNS // D,),
        in_specs=[pl.BlockSpec((rows, D), lambda i: (0, 0))] * len(pairs) + right_specs,
        out_specs=[pl.BlockSpec(shape[:5] + (D,), lambda i: (0, 0, 0, 0, 0, i))] * 2,
        **common,
    )(*[left for left, _ in pairs], *[right for _, right in pairs])


def norm_back_kernel(
    row, grad_ref, weight_ref, values_ref, vectors_ref, above_ref, out_ref, gain_out, total
):
    step = pl.program_id(0)

    @pl.when(step == 0)
    def _():
        total[...] = jnp.zeros(total.shape, jnp.float32)

    total[...] += nt_dot(grad_ref[...], weight_ref[...])

    @pl.when(step == pl.num_programs(0) - 1)
    def _():
        rows = 128
        gain = vectors_ref[TAPS + row : TAPS + row + 1, :]

        def part(at, gain_total):
            here = pl.ds(pl.multiple_of(at * rows, rows), rows)
            values, grads = values_ref[here, :], total[here, :]
            center = values - jnp.mean(values, axis=-1, keepdims=True)
            scale = lax.rsqrt(jnp.mean(center * center, axis=-1, keepdims=True) + eps)
            normed = center * scale
            scaled = grads * gain
            mean = jnp.mean(scaled, axis=-1, keepdims=True)
            along = jnp.mean(scaled * normed, axis=-1, keepdims=True)
            out_ref[here, :] = above_ref[here, :] + (scaled - mean - normed * along) * scale
            return gain_total + jnp.sum(grads * normed, axis=0, keepdims=True)

        gain_out[...] = lax.fori_loop(
            0, total.shape[0] // rows, part, jnp.zeros(gain_out.shape, jnp.float32)
        )


def product_norm_back(grad_lo, weight, values, vectors, row, above):
    _, rows, _ = grad_lo.shape
    inner = weight.shape[1]
    width = 512
    each = D // width
    whole, vector = VMEM, VMEM
    return pl.pallas_call(
        functools.partial(norm_back_kernel, row),
        grid=(inner // width,),
        in_specs=[
            pl.BlockSpec((None, rows, width), lambda i: (i // each, 0, i % each)),
            pl.BlockSpec((D, width), lambda i: (0, i)),
            whole,
            vector,
            whole,
        ],
        out_specs=[whole, vector],
        out_shape=[
            jax.ShapeDtypeStruct((rows, D), jnp.float32),
            jax.ShapeDtypeStruct((1, D), jnp.float32),
        ],
        scratch_shapes=[pltpu.VMEM((rows, D), jnp.float32)],
        cost_estimate=BRIEF,
        compiler_params=pltpu.CompilerParams(vmem_limit_bytes=14 << 20),
    )(grad_lo, weight, values, vectors, above)


def turned(values, cosine, sine):
    half = HD // 2
    lead, tail = values[:, :half], values[:, half:]
    return jnp.concatenate([lead * cosine - tail * sine, tail * cosine + lead * sine], axis=1)


def attend_kernel(
    query_ref, key_ref, value_ref, cosine_ref, sine_ref, bias_ref, out_ref, query_out, key_out, value_out, log_out
):
    cosine, sine = cosine_ref[...], sine_ref[...]
    query = turned(query_ref[...], cosine, sine).astype(jnp.bfloat16)
    key = turned(key_ref[...], cosine, sine).astype(jnp.bfloat16)
    value = value_ref[...].astype(jnp.bfloat16)
    query_out[...], key_out[...], value_out[...] = query, key, value
    scores = jnp.where(bias_ref[...] > 0, nt_dot(query, key) * HD**-0.5, -1e30)
    top = jnp.max(scores, axis=-1, keepdims=True)
    weights = jnp.exp(scores - top)
    total = jnp.sum(weights, axis=-1, keepdims=True)
    probs = (weights * (1.0 / total)).astype(jnp.bfloat16)
    out_ref[...] = jnp.dot(probs, value, preferred_element_type=jnp.float32).astype(jnp.bfloat16)
    log_out[...] = jnp.broadcast_to(top + jnp.log(total), log_out.shape)


def attend(mixed, cosine, sine, valid):
    rows = mixed.shape[0]
    head = lambda shift: pl.BlockSpec((rows, HD), lambda i: (0, i + shift))
    fixed = lambda *shape: pl.BlockSpec(shape, lambda i: (0, 0))
    return pl.pallas_call(
        attend_kernel,
        grid=(H,),
        in_specs=[
            head(0),
            head(H),
            head(2 * H),
            fixed(rows, HD // 2),
            fixed(rows, HD // 2),
            fixed(1, rows),
        ],
        out_specs=[head(0)] * 5,
        out_shape=[jax.ShapeDtypeStruct((rows, D), jnp.bfloat16)] * 4
        + [jax.ShapeDtypeStruct((rows, D), jnp.float32)],
        cost_estimate=BRIEF,
        compiler_params=pltpu.CompilerParams(vmem_limit_bytes=12 << 20),
    )(mixed, mixed, mixed, cosine, sine, valid)


def attend_back_kernel(
    query_ref, key_ref, value_ref, log_ref, grad_ref, cosine_ref, sine_ref, bias_ref, out_ref
):
    query, key, value, grad = query_ref[...], key_ref[...], value_ref[...], grad_ref[...]
    cosine, sine = cosine_ref[...], -sine_ref[...]
    scores = jnp.where(bias_ref[...] > 0, nt_dot(query, key) * HD**-0.5, -1e30)
    probs = jnp.exp(scores - log_ref[:, :1])
    grad_probs = nt_dot(grad, value)
    along = jnp.sum(probs * grad_probs, axis=-1, keepdims=True)
    grad_scores = (probs * (grad_probs - along)).astype(jnp.bfloat16)
    out_ref[2] = matmul_tn(probs.astype(jnp.bfloat16), grad).astype(jnp.bfloat16)
    query_grad = matmul(grad_scores, key) * HD**-0.5
    key_grad = matmul_tn(grad_scores, query) * HD**-0.5
    out_ref[0] = turned(query_grad, cosine, sine).astype(jnp.bfloat16)
    out_ref[1] = turned(key_grad, cosine, sine).astype(jnp.bfloat16)


def attend_back(query, key, value, logs, grads, cosine, sine, valid):
    rows = query.shape[0]
    head = pl.BlockSpec((rows, HD), lambda i: (0, i))
    fixed = lambda *shape: pl.BlockSpec(shape, lambda i: (0, 0))
    return pl.pallas_call(
        attend_back_kernel,
        grid=(H,),
        in_specs=[head] * 5
        + [fixed(rows, HD // 2), fixed(rows, HD // 2), fixed(1, rows)],
        out_specs=pl.BlockSpec((3, rows, HD), lambda i: (0, 0, i)),
        out_shape=jax.ShapeDtypeStruct((3, rows, D), jnp.bfloat16),
        cost_estimate=BRIEF,
        compiler_params=pltpu.CompilerParams(vmem_limit_bytes=12 << 20),
    )(query, key, value, logs, grads, cosine, sine, valid)


def fence(flows, *values):
    states, values = lax.optimization_barrier(([flow.state for flow in flows], values))
    for flow, state in zip(flows, states):
        flow.state = state
    return values[0] if len(values) == 1 else values


def rows_of(values, count):
    return values.reshape(count, values.shape[-1])


def shards(
    sizes,
    frames,
    ffn_inner,
    ffn_outer,
    attn_qkv,
    attn_proj,
    conv_expand,
    conv_depth,
    conv_proj,
    norm_gains,
    head_proj,
    lengths,
    mask_starts,
    target_codes,
    out_grad,
):
    cube = Cube(sizes)
    cube.where = lax.optimization_barrier(cube.place()) if cube.tuned else None
    devices = sizes["dp"] * sizes["head"]
    ff = ffn_inner.shape[2]
    all_bits = list(range(len(cube.bits)))

    rows_in = Gather(
        cube,
        [
            ("wide", [ffn_inner[0]]),
            ("tall", [ffn_outer[0]]),
            ("wide", [attn_qkv, attn_proj]),
            ("wide", [conv_expand, conv_proj]),
            ("wide", [ffn_inner[1]]),
            ("tall", [ffn_outer[1]]),
        ],
    )
    head_half = head_proj.shape[1] // 2
    heads = [
        HeadGathering(cube, head_proj[:, :head_half]),
        HeadGathering(cube, head_proj[:, head_half:]),
    ]

    row_total = UTT_DEV * SEQ
    positions = jnp.arange(SEQ, dtype=jnp.int32)
    valid_mat = positions[None, :] < lengths[:, None]
    valid_rows = valid_mat.reshape(row_total).astype(jnp.float32)
    frequency = 10000.0 ** (-(jnp.arange(HD // 2, dtype=jnp.float32) * 2.0) / HD)
    angles = positions.astype(jnp.float32)[:, None] * frequency[None, :]
    cosine, sine_table = jnp.cos(angles), jnp.sin(angles)

    slots = UTT_DEV * NSPAN * SPAN
    slot_at = (mask_starts[:, :, None] + jnp.arange(SPAN, dtype=jnp.int32)).reshape(UTT_DEV, -1)
    slot_ok = slot_at < lengths[:, None]
    chosen = (slot_at + SEQ * jnp.arange(UTT_DEV, dtype=jnp.int32)[:, None]).reshape(slots)
    slot_live = slot_ok.reshape(slots)
    pick = (
        (chosen[:, None] == jnp.arange(row_total, dtype=jnp.int32)[None, :]) & slot_live[:, None]
    )
    picked_codes = jnp.sum(jnp.where(pick, target_codes[None, :], 0), axis=1)
    picked_codes = jnp.where(slot_live, picked_codes, -1)
    pick_lo = pick.astype(jnp.bfloat16)
    head_order = [at for at in range(len(cube.bits)) if cube.bits[at][0] == "head"]
    group = sizes["head"]
    vocab_cols = head_proj.shape[1]

    loss_scale = jnp.float32(devices * UTT_DEV * NSPAN * SPAN)
    hops = [C, Y, X, Z1, Z0] if cube.tuned else all_bits
    vector_in = VectorGathering(cube, jnp.concatenate([conv_depth, norm_gains, jnp.zeros_like(conv_depth[:10])], axis=0), hops)
    vector_in.step(3)
    group_codes = cube.gather(picked_codes, head_order).reshape(group * slots)
    rows_in.start()
    if cube.tuned:
        head_got = cube.swap(head_proj, X)
        for at, flow in enumerate(heads):
            columns = slice(at * head_half, (at + 1) * head_half)
            flow.state = [head_proj[:, columns], head_got[:, columns]]
    else:
        heads[0].step("x")
        heads[1].step("x")
    group_codes = fence([rows_in, vector_in, *heads], group_codes)

    rows_in.stage(-1)
    vector_in.step()
    inputs = frames.astype(jnp.float32)
    fence([rows_in, vector_in], loss_scale)

    rows_in.stage(0)
    vector_in.step(len(hops))
    heads[0].step("far")
    fence([rows_in, vector_in, heads[0]], loss_scale)
    (vectors,) = vector_in.state
    vectors = fence([], joined_vectors(vectors.reshape((devices,) + vectors.shape[-2:])))
    gain_f = vectors[TAPS : TAPS + 6]
    norm_first = lowered(layer_norm(inputs, gain_f[0]))
    group_live = (group_codes >= 0).astype(jnp.float32)
    local_codes = group_codes - lax.axis_index("head") * vocab_cols

    rows_in.stage(1)
    (inner_0,) = rows_in.wholes[0]
    pre_first = matmul(norm_first, inner_0)
    act_first = lowered(jax.nn.silu(pre_first))
    pre_first = lowered(pre_first)
    pre_first, act_first = fence([rows_in], pre_first, act_first)

    rows_in.stage(2)
    (outer_0,) = rows_in.wholes[1]
    after_first = inputs + 0.5 * matmul(act_first, outer_0)
    norm_attn = lowered(layer_norm(after_first, gain_f[1]))
    after_first, norm_attn = fence([rows_in], after_first, norm_attn)

    rows_in.stage(3)
    heads[0].step("near")
    mix_weight, proj_weight = rows_in.wholes[2]
    mixed = matmul(norm_attn, mix_weight)
    attended_lo, queries, key_rows, value_rows, log_totals = attend(
        mixed, cosine, sine_table, valid_rows[None, :]
    )
    after_attention = after_first + matmul(attended_lo, proj_weight)
    norm_conv = lowered(layer_norm(after_attention, gain_f[2]))
    after_attention, norm_conv, attended_lo, queries, key_rows, value_rows, log_totals = fence(
        [rows_in, heads[0]],
        after_attention,
        norm_conv,
        attended_lo,
        queries,
        key_rows,
        value_rows,
        log_totals,
    )

    rows_in.stage(4)
    heads[1].step("far")
    expand_weight, conv_weight = rows_in.wholes[3]
    expanded = matmul(norm_conv, expand_weight)
    conv_out, conv_sums = conv_forward(expanded, valid_rows[:, None], vectors)
    sums = cube.total(conv_sums)
    sums, conv_out, after_attention, expanded, norm_conv = fence(
        [rows_in, *heads], sums, conv_out, after_attention, expanded, norm_conv
    )

    rows_in.stage(5)
    heads[1].step("near")
    (inner_1,) = rows_in.wholes[4]
    frame_count = sums[2, 0]
    channel_mean = sums[0] / frame_count
    variance = sums[1] / frame_count - channel_mean * channel_mean
    inverse = lax.rsqrt(variance + eps)
    normalized = (conv_out - channel_mean) * inverse
    normed_bn = normalized * gain_f[3]
    swish_lo = lowered(jax.nn.silu(normed_bn))
    after_conv = after_attention + matmul(swish_lo, conv_weight)
    norm_second = lowered(layer_norm(after_conv, gain_f[4]))
    pre_second = matmul(norm_second, inner_1)
    act_second = lowered(jax.nn.silu(pre_second))
    pre_second = lowered(pre_second)
    after_conv, norm_second, pre_second, act_second, swish_lo = fence(
        [rows_in, *heads], after_conv, norm_second, pre_second, act_second, swish_lo
    )

    rows_in.stage(6)
    (outer_1,) = rows_in.wholes[5]
    head_cols = joined_heads(cube, heads)
    after_second = after_conv + 0.5 * matmul(act_second, outer_1)
    output_lo = lowered(layer_norm(after_second, gain_f[5]))

    picked_rows = lowered(matmul(pick_lo, output_lo))
    group_rows = cube.gather(picked_rows, head_order).reshape(group * slots, D)
    logits = matmul(group_rows, head_cols)
    row_top = jnp.max(logits, axis=1)
    row_sum = jnp.sum(jnp.exp(logits - row_top[:, None]), axis=1)
    onehot = jnp.arange(vocab_cols, dtype=jnp.int32)[None, :] == local_codes[:, None]
    target_logit = jnp.sum(jnp.where(onehot, logits, 0.0), axis=1)
    stats = cube.gather(jnp.stack([row_top, row_sum, target_logit]), head_order)
    stats = stats.reshape(group, 3, group * slots)
    whole_top = jnp.max(stats[:, 0], axis=0)
    whole_sum = jnp.sum(stats[:, 1] * jnp.exp(stats[:, 0] - whole_top), axis=0)
    log_norm = whole_top + jnp.log(whole_sum)
    ce_group = jnp.sum((log_norm - jnp.sum(stats[:, 2], axis=0)) * group_live)
    grad_logits = lowered(
        (jnp.exp(logits - log_norm[:, None]) - onehot.astype(jnp.float32)) * group_live[:, None]
    )
    head_grad = lowered(matmul_tn(group_rows, grad_logits))
    head_flow = HeadScattering(cube, head_grad, head_proj.shape[0])
    row_grads = lowered(matmul_nt(grad_logits, head_cols))
    row_sum = Summing(cube, row_grads.reshape((2,) * len(head_order) + (slots, D)), head_order[::-1])
    head_flow.step()
    for _ in head_order:
        row_sum.step()
    row_grads = lowered(row_sum.result())
    grad_output = out_grad.astype(jnp.float32) + matmul_tn(pick_lo, row_grads)

    rows_out = Scatter(cube)
    grad_second, gain_grad_final = norm_back(after_second, gain_f[5], grad_output)
    grad_out_lo = lowered(0.5 * grad_second)
    piece = weight_grads(cube, "tall", [(act_second, grad_out_lo[None])])
    grad_second, grad_out_lo, piece = fence([head_flow], grad_second, grad_out_lo, piece)

    head_flow.step()
    rows_out.push("tall", [ffn_outer[1]], piece)
    grad_pre = act_back(grad_out_lo, outer_1, pre_second)
    piece = weight_grads(cube, "wide", [(norm_second, grad_pre)])
    grad_conv_res, gain_grad_second = product_norm_back(
        grad_pre, inner_1, after_conv, vectors, 4, grad_second
    )
    grad_conv_res, piece = fence([head_flow, rows_out], grad_conv_res, piece)

    conv_res_lo = lowered(grad_conv_res)
    grad_bn = silu_back(normed_bn, matmul_nt(conv_res_lo, conv_weight))
    gain_grad_bn = jnp.sum(grad_bn * normalized, axis=0)
    grad_normalized = grad_bn * gain_f[3]
    back_sums = cube.total(
        jnp.stack(
            [
                jnp.sum(grad_normalized, axis=0),
                jnp.sum(grad_normalized * normalized, axis=0),
                jnp.broadcast_to(ce_group / group, (D,)),
            ]
            + [jnp.zeros((D,), jnp.float32)] * 5
        )
    )
    back_sums, grad_normalized, grad_conv_res, conv_res_lo, piece = fence(
        [], back_sums, grad_normalized, grad_conv_res, conv_res_lo, piece
    )

    head_flow.step()
    rows_out.stage()
    rows_out.push("wide", [ffn_inner[1]], piece)
    loss = back_sums[2, 0] / loss_scale
    grad_expanded, depth_grad = conv_backward(
        expanded, valid_rows[:, None], vectors, conv_out, grad_normalized, sums, back_sums
    )
    piece = weight_grads(cube, "wide", [(norm_conv, grad_expanded), (swish_lo, conv_res_lo[None])])
    grad_expanded, piece = fence([rows_out, head_flow], grad_expanded, piece)

    rows_out.stage()
    rows_out.push("wide", [conv_expand, conv_proj], piece)
    grad_attn_res, gain_grad_conv = product_norm_back(
        grad_expanded, expand_weight, after_attention, vectors, 2, grad_conv_res
    )
    attn_res_lo = lowered(grad_attn_res)
    grad_attended = lowered(matmul_nt(attn_res_lo, proj_weight))
    grad_mixed = attend_back(
        queries,
        key_rows,
        value_rows,
        log_totals,
        grad_attended,
        cosine,
        sine_table,
        valid_rows[None, :],
    )
    piece = weight_grads(cube, "wide", [(norm_attn, grad_mixed), (attended_lo, attn_res_lo[None])])
    grad_mixed, grad_attn_res, piece = fence([rows_out], grad_mixed, grad_attn_res, piece)

    rows_out.stage()
    rows_out.push("wide", [attn_qkv, attn_proj], piece)
    grad_first_res, gain_grad_attn = product_norm_back(
        grad_mixed, mix_weight, after_first, vectors, 1, grad_attn_res
    )
    grad_out_lo = lowered(0.5 * grad_first_res)
    piece = weight_grads(cube, "tall", [(act_first, grad_out_lo[None])])
    grad_pre = act_back(grad_out_lo, outer_0, pre_first)
    grad_first_res, grad_pre, piece = fence([rows_out], grad_first_res, grad_pre, piece)

    rows_out.stage()
    rows_out.push("tall", [ffn_outer[0]], piece)
    piece = weight_grads(cube, "wide", [(norm_first, grad_pre)])
    input_grad, gain_grad_first = product_norm_back(
        grad_pre, inner_0, inputs, vectors, 0, grad_first_res
    )
    vector_grad = parted_vectors(
        [
            depth_grad,
            gain_grad_first,
            gain_grad_attn,
            gain_grad_conv,
            gain_grad_bn.reshape(1, D),
            gain_grad_second,
            gain_grad_final.reshape(1, D),
        ],
        devices,
    )
    vector_flow = Summing(
        cube,
        vector_grad.reshape((2,) * len(cube.bits) + vector_grad.shape[1:]),
        [C, Z1, Z0, X, Y] if cube.tuned else all_bits,
    )
    vector_flow.step()
    input_grad, piece = fence([rows_out, vector_flow], input_grad, piece)

    rows_out.stage()
    rows_out.push("wide", [ffn_inner[0]], piece)
    vector_flow.step()
    fence([rows_out, vector_flow], loss)

    for _ in range(4):
        rows_out.stage()
        if vector_flow.order:
            vector_flow.step()
        fence([rows_out, vector_flow], loss)
    for _ in vector_flow.order[:]:
        vector_flow.step()
    vector_grad = vector_flow.result()
    rows_out.stage()
    (
        (outer_grad_1,),
        (inner_grad_1,),
        (expand_grad, conv_proj_grad),
        (mix_grad, proj_grad),
        (outer_grad_0,),
        (inner_grad_0,),
    ) = rows_out.results
    return (
        output_lo,
        loss,
        input_grad,
        jnp.stack([inner_grad_0, inner_grad_1], axis=0),
        jnp.stack([outer_grad_0, outer_grad_1], axis=0),
        mix_grad,
        proj_grad,
        expand_grad,
        vector_grad[:TAPS],
        conv_proj_grad,
        vector_grad[TAPS:],
        head_flow.result(),
    )


def solution(mesh):
    placed = (
        P(("dp", "head"), None),
        P(None, ("dp", "head"), None),
        P(None, ("dp", "head"), None),
        P(("dp", "head"), None),
        P(("dp", "head"), None),
        P(("dp", "head"), None),
        P(None, ("dp", "head")),
        P(("dp", "head"), None),
        P(None, ("dp", "head")),
        P("dp", "head"),
        P(("dp", "head")),
        P(("dp", "head"), None),
        P(("dp", "head")),
        P(("dp", "head"), None),
    )
    sizes = {axis: mesh.shape[axis] for axis in AXES}
    return jax.shard_map(
        functools.partial(shards, sizes),
        mesh=mesh,
        in_specs=placed,
        out_specs=(
            P(("dp", "head"), None),
            P(),
            P(("dp", "head"), None),
            P(None, ("dp", "head"), None),
            P(None, ("dp", "head"), None),
            P(("dp", "head"), None),
            P(("dp", "head"), None),
            P(("dp", "head"), None),
            P(None, ("dp", "head")),
            P(("dp", "head"), None),
            P(None, ("dp", "head")),
            P("dp", "head"),
        ),
        check_vma=False,
    )
```

```python
import functools
import math

import jax
import jax.numpy as jnp
from jax import lax
from jax.experimental import pallas as pl
from jax.experimental.pallas import tpu as pltpu
from jax.sharding import PartitionSpec as P

D = 1024
H = 8
HD = 128
VOCAB = 8192
SEQ = 512
SPAN = 10
NSPAN = 20
UTT_DEV = 1


eps = 1e-05


def layer_norm(values, gain_row):
    center = values - jnp.mean(values, axis=-1, keepdims=True)
    variance = jnp.mean(center * center, axis=-1, keepdims=True)
    return center * lax.rsqrt(variance + eps) * gain_row


def lowered(values):
    return values.astype(jnp.bfloat16)


def matmul(operand, weight):
    return jnp.dot(operand, weight, preferred_element_type=jnp.float32)


def matmul_tn(operand, weight):
    return lax.dot_general(
        operand, weight, (((0,), (0,)), ((), ())), preferred_element_type=jnp.float32
    )


def matmul_nt(operand, weight):
    return lax.dot_general(
        operand, weight, (((1,), (1,)), ((), ())), preferred_element_type=jnp.float32
    )


def norm_back(values, gain_row, grads):
    unused, pullback = jax.vjp(layer_norm, values, gain_row)
    return pullback(grads)


def silu_back(values, grads):
    return jax.vjp(jax.nn.silu, values)[1](grads)[0]


AXES = ("dp", "head")
BRIEF = pl.CostEstimate(flops=0, bytes_accessed=0, transcendentals=0)
ANY = pl.BlockSpec(memory_space=pl.ANY)
VMEM = pl.BlockSpec(memory_space=pltpu.VMEM)
Z1, Z0, X, Y, C = range(5)


def local_copies(plan, inputs, outputs, after=()):
    count = len(inputs)

    def kernel(*refs):
        sources, targets, sem = refs[:count], refs[count + len(after) : -1], refs[-1]
        dp, head = lax.axis_index("dp"), lax.axis_index("head")
        where = (dp // 4, dp // 2 % 2, dp % 2, head // 2, head % 2)
        copies = []
        for at, (source, target) in enumerate(plan(where, sources, targets)):
            copies.append(pltpu.make_async_copy(source, target, sem.at[at]))
            copies[-1].start()
        for copy in copies:
            copy.wait()

    size = sum(math.prod(shape) for shape in outputs) * inputs[0].dtype.itemsize
    results = pl.pallas_call(
        kernel,
        out_shape=[jax.ShapeDtypeStruct(shape, inputs[0].dtype) for shape in outputs],
        in_specs=[ANY] * (count + len(after)),
        out_specs=[VMEM] * len(outputs),
        scratch_shapes=[pltpu.SemaphoreType.DMA((16,))],
        cost_estimate=BRIEF,
        compiler_params=pltpu.CompilerParams(vmem_limit_bytes=size + (1 << 20)),
    )(*inputs, *after)
    return list(results)


def flip(bit, by):
    return (bit + by) % 2


class Cube:
    def __init__(self, sizes):
        self.sizes = sizes
        self.tuned = sizes == {"dp": 8, "head": 4}
        self.bits = []
        for axis in AXES:
            bit = sizes[axis] // 2
            while bit:
                self.bits.append((axis, bit))
                bit //= 2

    def mine(self, at):
        axis, bit = self.bits[at]
        return (lax.axis_index(axis) // bit) % 2

    def swap(self, values, at):
        axis, bit = self.bits[at]
        return lax.ppermute(values, axis, [(i, i ^ bit) for i in range(self.sizes[axis])])

    def gather(self, shard, order):
        held = []
        values = shard
        for at in order:
            place = sum(other < at for other in held)
            values = self.join(values, self.swap(values, at), at, place)
            held.append(at)
        return values

    def join(self, values, got, at, place):
        if self.tuned and values.dtype != jnp.int32:
            shape = values.shape[:place] + (2,) + values.shape[place:]

            def plan(where, sources, targets):
                for by in range(2):
                    index = (slice(None),) * place + (flip(where[at], by),)
                    yield sources[by], targets[0].at[index]

            return local_copies(plan, [values, got], [shape])[0]
        mine = self.mine(at)
        first = jnp.where(mine == 0, values, got)
        second = jnp.where(mine == 0, got, values)
        return jnp.stack([first, second], axis=place)

    def place(self):
        dp, head = lax.axis_index("dp"), lax.axis_index("head")
        parts = jnp.array([4, 2, 1, 0, 0]), jnp.array([0, 0, 0, 2, 1])
        either = jnp.where(parts[0] > 0, dp & parts[0], head & parts[1])
        return (either > 0).astype(jnp.int32)

    def total(self, values):
        for at in (C, Z0, Z1, X, Y) if self.tuned else range(len(self.bits)):
            values = values + self.swap(values, at)
        return values


TAPS = 32


def joined_vectors(parts):
    devices, rows, width = parts.shape

    def kernel(parts_ref, out_ref):
        pieces = [parts_ref[at].astype(jnp.float32) for at in range(devices)]
        out_ref[...] = jnp.concatenate(pieces, axis=1)

    return pl.pallas_call(
        kernel,
        out_shape=jax.ShapeDtypeStruct((rows, devices * width), jnp.float32),
        compiler_params=pltpu.CompilerParams(vmem_limit_bytes=16 << 20),
    )(parts)


def parted_vectors(arrays, devices):
    rows = sum(array.shape[0] for array in arrays)
    width = D // devices

    def kernel(*refs):
        start = 0
        for ref in refs[:-1]:
            count = ref.shape[0]
            values = ref[...]
            for at in range(devices):
                refs[-1][at, start : start + count, :] = values[:, at * width : (at + 1) * width]
            start += count

    return pl.pallas_call(
        kernel,
        out_shape=jax.ShapeDtypeStruct((devices, rows, width), jnp.float32),
        compiler_params=pltpu.CompilerParams(vmem_limit_bytes=16 << 20),
    )(*arrays)


class VectorGathering:
    def __init__(self, cube, shard, order):
        self.cube, self.order, self.held = cube, list(order), []
        self.state = [shard]

    def step(self, count=1):
        for _ in range(min(count, len(self.order))):
            at = self.order.pop(0)
            place = sum(other < at for other in self.held)
            (values,) = self.state
            self.state = [self.cube.join(values, self.cube.swap(values, at), at, place)]
            self.held.append(at)


class HeadGathering:
    def __init__(self, cube, shard):
        self.cube = cube
        self.state = [shard]

    def step(self, phase):
        if not self.cube.tuned:
            if phase == "x":
                self.state = [lax.all_gather(self.state[0], "dp", axis=0, tiled=True)]
            return
        if phase == "x":
            (own,) = self.state
            self.state = [own, self.cube.swap(own, X)]
        if phase == "far":
            own, got = self.state

            def plan(where, sources, targets):
                for by in range(2):
                    yield sources[by], targets[0].at[flip(where[X], by)]

            (pair,) = local_copies(plan, self.state, [(2,) + own.shape])
            self.state = [pair, self.cube.swap(pair, Z1)]
        if phase == "near":
            pair, got = self.state

            def plan(where, sources, targets):
                for by in range(2):
                    yield sources[by], targets[0].at[flip(where[Z1], by)]

            (four,) = local_copies(plan, self.state, [(2,) + pair.shape])
            self.state = [four, self.cube.swap(four, Z0)]


def joined_heads(cube, heads):
    if not cube.tuned:
        return jnp.concatenate([part.state[0] for part in heads], axis=1)
    parts = [part for flow in heads for part in flow.state]
    _, _, rows, half = parts[0].shape

    def plan(where, sources, targets):
        for at in range(4):
            columns = pl.ds(at // 2 * half, half)
            yield sources[at], targets[0].at[:, flip(where[Z0], at % 2), :, :, columns]

    (whole,) = local_copies(plan, parts, [(2, 2, 2, rows, 2 * half)])
    return whole.reshape(8 * rows, 2 * half)


def pick_of(values, index, place):
    return lax.dynamic_index_in_dim(values, index, place, keepdims=False)


def halves_kernel(at, place, *refs):
    dp, head = lax.axis_index("dp"), lax.axis_index("head")
    mine = (dp // 4, dp // 2 % 2, dp % 2, head // 2, head % 2)[at]
    keep, got, send_ref, keep_ref = refs
    for out, by in ((send_ref, 1), (keep_ref, 0)):
        index = (slice(None),) * place + (flip(mine, by),)
        total = keep[index].astype(jnp.float32) + got[index].astype(jnp.float32)
        out[...] = total.astype(out.dtype)


class Summing:
    def __init__(self, cube, values, order):
        self.cube, self.order = cube, list(order)
        self.held = sorted(order)
        self.state = [values]

    def step(self):
        cube, at = self.cube, self.order.pop(0)
        place = self.held.index(at)
        self.held.remove(at)
        left = self.state[0].shape[:place] + self.state[0].shape[place + 1 :]
        if not cube.tuned:
            values = sum(part.astype(jnp.float32) for part in self.state)
            values = values.astype(self.state[0].dtype)
            send = pick_of(values, 1 - cube.mine(at), place)
            keep = pick_of(values, cube.mine(at), place)
        elif len(self.state) == 1:

            def plan(where, sources, targets):
                for by in range(2):
                    index = (slice(None),) * place + (flip(where[at], 1 - by),)
                    yield sources[0].at[index], targets[by]

            send, keep = local_copies(plan, self.state, [left, left])
        else:
            size = math.prod(left) * self.state[0].dtype.itemsize
            send, keep = pl.pallas_call(
                functools.partial(halves_kernel, at, place),
                out_shape=[jax.ShapeDtypeStruct(left, self.state[0].dtype)] * 2,
                in_specs=[VMEM] * 2,
                out_specs=[VMEM] * 2,
                compiler_params=pltpu.CompilerParams(vmem_limit_bytes=6 * size + (4 << 20)),
            )(*self.state)
        self.state = [keep, cube.swap(send, at)]

    def result(self):
        return sum(part.astype(jnp.float32) for part in self.state)


class Gather:
    def __init__(self, cube, pieces):
        self.cube = cube
        self.pieces = pieces
        self.wholes = [None] * len(pieces)
        if cube.tuned:
            self.shards = [uniform_shard(kind, arrays) for kind, arrays in pieces]
        self.state = {}

    def start(self):
        cube = self.cube
        if not cube.tuned:
            return
        own = self.shards[0]
        far = cube.swap(own, Z1)
        near, both = cube.swap(own, Z0), cube.swap(far, Z0)

        def plan(w, s, o):
            for at in range(2):
                for by in range(2):
                    yield s[2 * at + by], o[at].at[flip(w[Z1], by)]

        pairs = local_copies(plan, [own, far, near, both], [(2, ROWS, COLUMNS)] * 2)
        self.state = {
            "z0s": pairs[0],
            "z0g": pairs[1],
            "z1s": self.shards[1],
            "z1g": cube.swap(self.shards[1], Z1),
        }

    def stage(self, t):
        cube, old, new = self.cube, self.state, {}
        count = len(self.pieces)
        live = lambda at: 0 <= at < count
        if not cube.tuned:
            if live(t - 1):
                self.wholes[t - 1] = [
                    lax.all_gather(array, AXES, axis=0, tiled=True)
                    for array in self.pieces[t - 1][1]
                ]
            return
        half = COLUMNS // 2
        slots = 2 * live(t) + live(t + 1)
        old_slots = 2 * live(t - 1) + live(t)
        inputs, shapes, jobs = [], [], []

        def give(name):
            inputs.append(old[name])
            return len(inputs) - 1

        def make(shape):
            shapes.append(shape)
            return len(shapes) - 1

        pair = None
        if live(t + 2):
            parts, pair = (give("z1s"), give("z1g")), make((2, ROWS, COLUMNS))
            jobs.append(lambda w, s, o, parts=parts, pair=pair: [
                (s[parts[by]], o[pair].at[flip(w[Z1], by)]) for by in range(2)
            ])
        if slots:
            x_out, y_out = (make((2, 2, slots, ROWS, half)) for _ in range(2))
        if live(t):
            xs, xg, ys, yg = (give(name) for name in ("xs", "xg", "ys", "yg"))
            jobs.append(lambda w, s, o: [
                pair_of
                for by in range(2)
                for pair_of in (
                    (s[(xs, xg)[by]].at[:, :, old_slots - 1], o[y_out].at[:, :, flip(w[X], by)]),
                    (s[(ys, yg)[by]].at[:, :, old_slots - 1], o[x_out].at[:, :, flip(w[Y], by)]),
                )
            ])
        if live(t + 1):
            zs, zg = give("z0s"), give("z0g")
            jobs.append(lambda w, s, o: [
                (
                    s[(zs, zg)[by]].at[:, :, pl.ds(side * half, half)],
                    o[(x_out, y_out)[side]].at[:, flip(w[Z0], by), slots - 1],
                )
                for by in range(2)
                for side in range(2)
            ])
        if jobs:
            made = local_copies(
                lambda w, s, o: [each for job in jobs for each in job(w, s, o)], inputs, shapes
            )
            if slots:
                new["xs"], new["ys"] = made[x_out], made[y_out]
                new["xg"], new["yg"] = cube.swap(made[x_out], X), cube.swap(made[y_out], Y)
            if pair is not None:
                new["z0s"], new["z0g"] = made[pair], cube.swap(made[pair], Z0)
        if live(t + 3):
            new["z1s"] = self.shards[t + 3]
            new["z1g"] = cube.swap(self.shards[t + 3], Z1)
        if live(t - 1):

            def plan(w, s, o):
                for by in range(2):
                    yield (
                        s[by].at[:, :, pl.ds(0, 2)],
                        o[0].at[:, :, :, flip(w[Y], by), :, pl.ds(0, half)],
                    )
                    yield (
                        s[2 + by].at[:, :, pl.ds(0, 2)],
                        o[0].at[:, :, flip(w[X], by), :, :, pl.ds(half, half)],
                    )

            (most,) = local_copies(
                plan,
                [old[name] for name in ("ys", "yg", "xs", "xg")],
                [(2, 2, 2, 2, ROWS, COLUMNS)],
                [new[name] for name in ("xs", "z0s") if name in new][:1],
            )
            got = cube.swap(most, C)
            kind, arrays = self.pieces[t - 1]

            def plan_whole(w, s, o):
                for by in range(2):
                    for at, rows, columns in tiles_of(kind, arrays):
                        yield (
                            s[by].at[:, :, :, :, :, columns],
                            o[at].at[:, :, :, :, flip(w[C], by), rows],
                        )

            made = local_copies(
                plan_whole, [most, got], [(2, 2, 2, 2, 2) + array.shape for array in arrays]
            )
            self.wholes[t - 1] = [
                whole.reshape(-1, array.shape[1]) for whole, array in zip(made, arrays)
            ]
        self.state = new


ROWS, COLUMNS = 32, 4096


def uniform_shard(kind, arrays):
    if kind == "tall":
        return jnp.concatenate([arrays[0][at : at + ROWS] for at in range(0, 4 * ROWS, ROWS)], axis=1)
    spare = COLUMNS - sum(array.shape[1] for array in arrays)
    extra = [arrays[0][:, :spare]] if spare else []
    return jnp.concatenate(arrays + extra, axis=1) if len(arrays) > 1 else arrays[0]


def tiles_of(kind, arrays):
    if kind == "tall":
        width = arrays[0].shape[1]
        for at in range(4):
            yield 0, pl.ds(at * ROWS, ROWS), pl.ds(at * width, width)
    else:
        start = 0
        for at, array in enumerate(arrays):
            yield at, pl.ds(0, ROWS), pl.ds(start, array.shape[1])
            start += array.shape[1]


def added(out, out_at, first, first_at, second, second_at):
    total = first[first_at].astype(jnp.float32) + second[second_at].astype(jnp.float32)
    out[out_at] = total.astype(out.dtype)


class Scatter:
    def __init__(self, cube):
        self.cube = cube
        self.state = {}
        self.results = []
        self.queue = []
        self.first = []

    def sums(self, sent, after):
        old = self.state
        half = COLUMNS // 2
        inputs, in_specs, names, shapes, out_specs, jobs = [], [], [], [], [], []
        mine = lambda w, at: (w[at] + sent) % 2

        def take(name, block, index):
            inputs.append(old[name])
            in_specs.append(pl.BlockSpec(block, index))
            return len(inputs) - 1

        def make(name, shape, block, index):
            names.append(name)
            shapes.append(jax.ShapeDtypeStruct(shape, jnp.bfloat16))
            out_specs.append(pl.BlockSpec(block, index))
            return len(names) - 1

        has_n, has_m = "ck" in old, "ak" in old
        slots = 2 * has_n + has_m
        corner = (None, None)
        if sent and slots:
            sent_shape = (2, 2, slots, ROWS, half)
            x_out = make("x", sent_shape, corner + sent_shape[2:], lambda a, b, w: (a, b, 0, 0, 0))
            y_out = make("y", sent_shape, corner + sent_shape[2:], lambda a, b, w: (a, b, 0, 0, 0))
        if has_n:
            left_block, right_block = corner + (2, None, ROWS, half), corner + (None, 2, ROWS, half)
            left_index = lambda a, b, w: (a, b, 0, mine(w, Y), 0, 0)
            right_index = lambda a, b, w: (a, b, mine(w, X), 0, 0, 1)
            lefts = [take(name, left_block, left_index) for name in ("ck", "cg")]
            rights = [take(name, right_block, right_index) for name in ("ck", "cg")]
            if not sent:
                kept = (2, 2, 2, ROWS, half)
                y_out = make("ak", kept, corner + kept[2:], lambda a, b, w: (a, b, 0, 0, 0))
                x_out = make("bk", kept, corner + kept[2:], lambda a, b, w: (a, b, 0, 0, 0))

            def job_n(s, o, y_out=y_out, x_out=x_out):
                for k in range(2):
                    added(o[y_out], k, s[lefts[0]], k, s[lefts[1]], k)
                    added(o[x_out], k, s[rights[0]], k, s[rights[1]], k)

            jobs.append(job_n)
        if has_m:
            block = corner + (None, ROWS, half)
            x_index = lambda a, b, w: (a, b, mine(w, X), 0, 0)
            y_index = lambda a, b, w: (a, b, mine(w, Y), 0, 0)
            lefts_m = take("ak", block, x_index), take("yg", block, x_index)
            rights_m = take("bk", block, y_index), take("xg", block, y_index)
            place = slots - 1 if sent else slice(None)
            if not sent:
                kept = (2, 2, ROWS, half)
                a_out = make("a4k", kept, corner + kept[2:], lambda a, b, w: (a, b, 0, 0))
                b_out = make("b4k", kept, corner + kept[2:], lambda a, b, w: (a, b, 0, 0))
            else:
                a_out, b_out = x_out, y_out

            def job_m(s, o):
                every = slice(None)
                added(o[a_out], place, s[lefts_m[0]], every, s[lefts_m[1]], every)
                added(o[b_out], place, s[rights_m[0]], every, s[rights_m[1]], every)

            jobs.append(job_m)
        if "a4k" in old:
            last = old["xg"].shape[2] - 1
            block = (None, None, ROWS, half)
            index = lambda a, b, w: (a, mine(w, Z0), 0, 0)
            got_block = (None, None, None, ROWS, half)
            got_index = lambda a, b, w: (a, mine(w, Z0), last, 0, 0)
            lefts_z = take("a4k", block, index), take("xg", got_block, got_index)
            rights_z = take("b4k", block, index), take("yg", got_block, got_index)
            z_out = make(
                "z" if sent else "zk",
                (2, ROWS, COLUMNS),
                (None, ROWS, COLUMNS),
                lambda a, b, w: (a, 0, 0),
            )

            def job_z(s, o):
                @pl.when(pl.program_id(1) == 0)
                def _():
                    every = slice(None)
                    left = (every, slice(0, half))
                    right = (every, slice(half, COLUMNS))
                    added(o[z_out], left, s[lefts_z[0]], every, s[lefts_z[1]], every)
                    added(o[z_out], right, s[rights_z[0]], every, s[rights_z[1]], every)

            jobs.append(job_z)
        if "zk" in old:
            block, index = (None, ROWS, COLUMNS), lambda a, b, w: (mine(w, Z1), 0, 0)
            pair = take("zk", block, index), take("zg", block, index)
            f_out = make(
                "f" if sent else "fk", (ROWS, COLUMNS), (ROWS, COLUMNS), lambda a, b, w: (0, 0)
            )

            def job_f(s, o):
                @pl.when((pl.program_id(0) == 0) & (pl.program_id(1) == 0))
                def _():
                    every = slice(None)
                    added(o[f_out], every, s[pair[0]], every, s[pair[1]], every)

            jobs.append(job_f)
        if not jobs:
            return {}

        def kernel(where, *refs):
            sources, targets = refs[: len(inputs)], refs[len(inputs) + len(after) :]
            for job in jobs:
                job(sources, targets)

        size = sum(math.prod(shape.shape) for shape in shapes)
        made = pl.pallas_call(
            kernel,
            grid_spec=pltpu.PrefetchScalarGridSpec(
                num_scalar_prefetch=1,
                grid=(2, 2),
                in_specs=in_specs + [ANY] * len(after),
                out_specs=out_specs,
            ),
            out_shape=shapes,
            cost_estimate=BRIEF,
            compiler_params=pltpu.CompilerParams(vmem_limit_bytes=9 << 20),
        )(self.cube.where, *inputs, *after)
        return dict(zip(names, made))

    def stage(self, value=None):
        cube, old, new = self.cube, self.state, {}
        if not cube.tuned:
            return value
        sends = self.sums(1, [])
        if value is not None:
            sends, value = lax.optimization_barrier((sends, value))
        for name, at, got in (("x", X, "xg"), ("y", Y, "yg"), ("z", Z0, "zg"), ("f", Z1, "fg")):
            if name in sends:
                new[got] = cube.swap(sends[name], at)
        first = list(sends.values())[:1]
        new.update(self.sums(0, first))
        if "fk" in old:
            kind, arrays = self.queue.pop(0)
            total = old["fk"].astype(jnp.float32) + old["fg"].astype(jnp.float32)
            self.results.append(split_shard(kind, arrays, total))
        self.first, self.state = first, new
        return value

    def push(self, kind, arrays, grads):
        if not self.cube.tuned:
            self.results.append(
                [
                    lax.psum_scatter(grad, AXES, scatter_dimension=0, tiled=True).astype(jnp.float32)
                    for grad in grads
                ]
            )
            return
        self.queue.append((kind, arrays))
        keep, send = grads
        self.state["ck"], self.state["cg"] = keep, self.cube.swap(send, C)


def split_shard(kind, arrays, total):
    if kind == "tall":
        width = arrays[0].shape[1]
        return [jnp.concatenate([total[:, at * width : (at + 1) * width] for at in range(4)], axis=0)]
    parts, start = [], 0
    for array in arrays:
        parts.append(total[:, start : start + array.shape[1]])
        start += array.shape[1]
    return parts


class HeadScattering:
    def __init__(self, cube, values, rows):
        self.cube = cube
        if not cube.tuned:
            self.whole = values
            return
        half = values.shape[1] // 2
        self.parts = [
            Summing(cube, values[:, :half].reshape(2, 2, 2, rows, half), (X, Z0, Z1)),
            Summing(cube, values[:, half:].reshape(2, 2, 2, rows, half), (Z0, Z1, X)),
        ]

    @property
    def state(self):
        return [part.state for part in self.parts] if self.cube.tuned else [self.whole]

    @state.setter
    def state(self, values):
        if not self.cube.tuned:
            self.whole = values[0]
            return
        for part, state in zip(self.parts, values):
            part.state = state

    def step(self):
        if self.cube.tuned:
            for part in self.parts:
                part.step()

    def result(self):
        if not self.cube.tuned:
            return lax.psum_scatter(self.whole, "dp", scatter_dimension=0, tiled=True).astype(
                jnp.float32
            )
        return jnp.concatenate([part.result() for part in self.parts], axis=1)


def shifted(pad_ref, shift_ref, rows):
    for r in range(8):
        shift_ref[r] = pad_ref[r : r + rows, :]


def conv_forward_kernel(lead_ref, gate_ref, valid_ref, taps_ref, conv_ref, sums_ref, pad, shift):
    length, width = lead_ref.shape
    edge = jnp.zeros((16, width), jnp.float32)
    valid = valid_ref[...]
    pad[0:16, :] = edge
    pad[16 : 16 + length, :] = lead_ref[...] * jax.nn.sigmoid(gate_ref[...]) * valid
    pad[16 + length : 40 + length, :] = jnp.zeros((24, width), jnp.float32)
    shifted(pad, shift, length + 32)
    chunk = 64
    taps = [taps_ref[j : j + 1, :] for j in range(32)]

    def step(at, totals):
        start = pl.multiple_of(at * chunk, chunk)
        total = jnp.zeros((chunk, width), jnp.float32)
        for j in range(32):
            total += shift[j % 8, pl.ds(start + j // 8 * 8, chunk), :] * taps[j]
        conv_ref[pl.ds(start, chunk), :] = total
        weighted = total * valid_ref[pl.ds(start, chunk), :]
        plain, squares = totals
        return (
            plain + jnp.sum(weighted, axis=0, keepdims=True),
            squares + jnp.sum(weighted * total, axis=0, keepdims=True),
        )

    zero = jnp.zeros((1, width), jnp.float32)
    plain, squares = lax.fori_loop(0, length // chunk, step, (zero, zero))
    sums_ref[0:1, :] = plain
    sums_ref[1:2, :] = squares
    sums_ref[2:3, :] = jnp.broadcast_to(jnp.sum(valid, axis=0, keepdims=True), (1, width))
    sums_ref[3:8, :] = jnp.zeros((5, width), jnp.float32)


def conv_forward(expanded, valid, taps):
    rows = expanded.shape[0]
    width = 128
    count = D // width
    return pl.pallas_call(
        conv_forward_kernel,
        grid=(count,),
        in_specs=[
            pl.BlockSpec((rows, width), lambda i: (0, i)),
            pl.BlockSpec((rows, width), lambda i: (0, i + count)),
            pl.BlockSpec((rows, 1), lambda i: (0, 0)),
            pl.BlockSpec((TAPS + 16, width), lambda i: (0, i)),
        ],
        out_specs=[
            pl.BlockSpec((rows, width), lambda i: (0, i)),
            pl.BlockSpec((8, width), lambda i: (0, i)),
        ],
        out_shape=[
            jax.ShapeDtypeStruct((rows, D), jnp.float32),
            jax.ShapeDtypeStruct((8, D), jnp.float32),
        ],
        scratch_shapes=[
            pltpu.VMEM((rows + 40, width), jnp.float32),
            pltpu.VMEM((8, rows + 32, width), jnp.float32),
        ],
        cost_estimate=BRIEF,
        compiler_params=pltpu.CompilerParams(vmem_limit_bytes=8 << 20),
    )(expanded, expanded, valid, taps)


def conv_backward_kernel(
    lead_ref,
    gate_ref,
    valid_ref,
    taps_ref,
    conv_ref,
    grad_ref,
    sums_ref,
    back_sums_ref,
    out_ref,
    taps_grad_ref,
    pad,
    shift,
    tap_sums,
):
    length, width = lead_ref.shape
    count = sums_ref[2:3, :]
    mean = sums_ref[0:1, :] / count
    inverse = lax.rsqrt(sums_ref[1:2, :] / count - mean * mean + eps)
    variance_grad = -0.5 * inverse * inverse * back_sums_ref[1:2, :]
    plain = (-inverse * back_sums_ref[0:1, :] - 2.0 * mean * variance_grad) / count
    scaled = 2.0 * variance_grad / count
    pad[0:16, :] = jnp.zeros((16, width), jnp.float32)
    pad[16 : 16 + length, :] = (
        grad_ref[...] * inverse + (plain + scaled * conv_ref[...]) * valid_ref[...]
    )
    pad[16 + length : 40 + length, :] = jnp.zeros((24, width), jnp.float32)
    shifted(pad, shift, length + 32)
    tap_sums[...] = jnp.zeros(tap_sums.shape, jnp.float32)
    chunk = 64
    taps = [taps_ref[j : j + 1, :] for j in range(32)]

    def step(at, carry):
        start = pl.multiple_of(at * chunk, chunk)
        here = pl.ds(start, chunk)
        lead, valid = lead_ref[here, :], valid_ref[here, :]
        gate = jax.nn.sigmoid(gate_ref[here, :])
        gated = lead * gate * valid
        total = jnp.zeros((chunk, width), jnp.float32)
        for j in range(32):
            off = 32 - j
            part = shift[off % 8, pl.ds(start + off // 8 * 8, chunk), :]
            total += part * taps[j]
            tap_sums[j] += jnp.sum((part * gated).reshape(chunk // 8, 8, width), axis=0)
        grad = total * valid
        out_ref[0, here, :] = (grad * gate).astype(jnp.bfloat16)
        out_ref[1, here, :] = (grad * lead * gate * (1.0 - gate)).astype(jnp.bfloat16)
        return carry

    lax.fori_loop(0, length // chunk, step, 0)
    taps_grad_ref[...] = jnp.sum(tap_sums[...], axis=1)


def conv_backward(expanded, valid, taps, conv_out, grads, sums, back_sums):
    rows = expanded.shape[0]
    width = 128
    count = D // width
    block = pl.BlockSpec((rows, width), lambda i: (0, i))
    return pl.pallas_call(
        conv_backward_kernel,
        grid=(count,),
        in_specs=[
            block,
            pl.BlockSpec((rows, width), lambda i: (0, i + count)),
            pl.BlockSpec((rows, 1), lambda i: (0, 0)),
            pl.BlockSpec((TAPS + 16, width), lambda i: (0, i)),
            block,
            block,
            pl.BlockSpec((8, width), lambda i: (0, i)),
            pl.BlockSpec((8, width), lambda i: (0, i)),
        ],
        out_specs=[
            pl.BlockSpec((2, rows, width), lambda i: (0, 0, i)),
            pl.BlockSpec((TAPS, width), lambda i: (0, i)),
        ],
        out_shape=[
            jax.ShapeDtypeStruct((2, rows, D), jnp.bfloat16),
            jax.ShapeDtypeStruct((32, D), jnp.float32),
        ],
        scratch_shapes=[
            pltpu.VMEM((rows + 40, width), jnp.float32),
            pltpu.VMEM((8, rows + 32, width), jnp.float32),
            pltpu.VMEM((32, 8, width), jnp.float32),
        ],
        cost_estimate=BRIEF,
        compiler_params=pltpu.CompilerParams(vmem_limit_bytes=8 << 20),
    )(expanded, expanded, valid, taps, conv_out, grads, sums, back_sums)


def nt_dot(left, right):
    return lax.dot_general(left, right, (((1,), (1,)), ((), ())), preferred_element_type=jnp.float32)


def act_back_kernel(grad_ref, weight_ref, pre_ref, out_ref):
    pre = pre_ref[...].astype(jnp.float32)
    gate = jax.nn.sigmoid(pre)
    slope = gate * (1.0 + pre * (1.0 - gate))
    out_ref[...] = (nt_dot(grad_ref[...], weight_ref[...]) * slope).astype(jnp.bfloat16)


def act_back(grad_lo, weight, pre):
    rows, inner = grad_lo.shape
    total = weight.shape[0]
    width = 512
    each = D // width
    return pl.pallas_call(
        act_back_kernel,
        grid=(total // width,),
        in_specs=[
            pl.BlockSpec((rows, inner), lambda i: (0, 0)),
            pl.BlockSpec((width, inner), lambda i: (i, 0)),
            pl.BlockSpec((rows, width), lambda i: (0, i)),
        ],
        out_specs=pl.BlockSpec((None, rows, width), lambda i: (i // each, 0, i % each)),
        out_shape=jax.ShapeDtypeStruct((total // D, rows, D), jnp.bfloat16),
        cost_estimate=BRIEF,
        compiler_params=pltpu.CompilerParams(vmem_limit_bytes=10 << 20),
    )(grad_lo, weight, pre)


def weight_grads_kernel(counts, *refs):
    lefts, rights = refs[: len(counts)], refs[len(counts) : 2 * len(counts)]
    keep_ref, send_ref = refs[-2:]
    core = lax.axis_index("head") % 2
    step, start = pl.program_id(0), 0
    for left, right, count in zip(lefts, rights, counts):

        @pl.when((step >= start) & (step < start + count))
        def _(left=left, right=right):
            total = matmul_tn(left[...], right[...]).astype(jnp.bfloat16)
            for at in range(16):
                first, second = (
                    total[(2 * at + by) * ROWS : (2 * at + by + 1) * ROWS, :] for by in range(2)
                )
                place = (at // 8, at // 4 % 2, at // 2 % 2, at % 2)

                @pl.when(core == 0)
                def _():
                    keep_ref[place], send_ref[place] = first, second

                @pl.when(core == 1)
                def _():
                    keep_ref[place], send_ref[place] = second, first

        start += count

    @pl.when(step >= start)
    def _():
        keep_ref[...] = jnp.zeros(keep_ref.shape, jnp.bfloat16)
        send_ref[...] = jnp.zeros(send_ref.shape, jnp.bfloat16)


def tall_grads_kernel(left_ref, right_ref, keep_ref, send_ref):
    core = lax.axis_index("head") % 2
    total = matmul_tn(left_ref[...], right_ref[...]).astype(jnp.bfloat16)
    for at in range(4):
        for group in range(4):
            first, second = (
                total[((2 * at + by) * 4 + group) * ROWS : ((2 * at + by) * 4 + group + 1) * ROWS, :]
                for by in range(2)
            )
            place = (at // 2, at % 2, slice(None), slice(group * D, (group + 1) * D))

            @pl.when(core == 0)
            def _():
                keep_ref[place], send_ref[place] = first, second

            @pl.when(core == 1)
            def _():
                keep_ref[place], send_ref[place] = second, first


def weight_grads(cube, kind, pairs):
    if not cube.tuned:
        return [
            jnp.concatenate([lowered(matmul_tn(left, each)) for each in rights], axis=1)
            for left, rights in pairs
        ]
    shape = (2, 2, 2, 2, ROWS, COLUMNS)
    rows = pairs[0][0].shape[0]
    common = dict(
        out_shape=[jax.ShapeDtypeStruct(shape, jnp.bfloat16)] * 2,
        cost_estimate=BRIEF,
        compiler_params=pltpu.CompilerParams(vmem_limit_bytes=22 << 20),
    )
    if kind == "tall":
        ((left, right),) = pairs
        return pl.pallas_call(
            tall_grads_kernel,
            grid=(4,),
            in_specs=[
                pl.BlockSpec((rows, D), lambda i: (0, i)),
                pl.BlockSpec((None, rows, D), lambda i: (0, 0, 0)),
            ],
            out_specs=[
                pl.BlockSpec((None, None, 2, 2, ROWS, COLUMNS), lambda i: (i // 2, i % 2, 0, 0, 0, 0))
            ]
            * 2,
            **common,
        )(left, right)
    counts, right_specs, start = [], [], 0
    for _, right in pairs:
        count = right.shape[0]
        right_specs.append(
            pl.BlockSpec(
                (None, rows, D),
                lambda i, start=start, count=count: (jnp.clip(i - start, 0, count - 1), 0, 0),
            )
        )
        counts.append(count)
        start += count
    return pl.pallas_call(
        functools.partial(weight_grads_kernel, counts),
        grid=(COLUMNS // D,),
        in_specs=[pl.BlockSpec((rows, D), lambda i: (0, 0))] * len(pairs) + right_specs,
        out_specs=[pl.BlockSpec(shape[:5] + (D,), lambda i: (0, 0, 0, 0, 0, i))] * 2,
        **common,
    )(*[left for left, _ in pairs], *[right for _, right in pairs])


def norm_back_kernel(
    row, grad_ref, weight_ref, values_ref, vectors_ref, above_ref, out_ref, gain_out, total
):
    step = pl.program_id(0)

    @pl.when(step == 0)
    def _():
        total[...] = jnp.zeros(total.shape, jnp.float32)

    total[...] += nt_dot(grad_ref[...], weight_ref[...])

    @pl.when(step == pl.num_programs(0) - 1)
    def _():
        rows = 128
        gain = vectors_ref[TAPS + row : TAPS + row + 1, :]

        def part(at, gain_total):
            here = pl.ds(pl.multiple_of(at * rows, rows), rows)
            values, grads = values_ref[here, :], total[here, :]
            center = values - jnp.mean(values, axis=-1, keepdims=True)
            scale = lax.rsqrt(jnp.mean(center * center, axis=-1, keepdims=True) + eps)
            normed = center * scale
            scaled = grads * gain
            mean = jnp.mean(scaled, axis=-1, keepdims=True)
            along = jnp.mean(scaled * normed, axis=-1, keepdims=True)
            out_ref[here, :] = above_ref[here, :] + (scaled - mean - normed * along) * scale
            return gain_total + jnp.sum(grads * normed, axis=0, keepdims=True)

        gain_out[...] = lax.fori_loop(
            0, total.shape[0] // rows, part, jnp.zeros(gain_out.shape, jnp.float32)
        )


def product_norm_back(grad_lo, weight, values, vectors, row, above):
    _, rows, _ = grad_lo.shape
    inner = weight.shape[1]
    width = 512
    each = D // width
    whole, vector = VMEM, VMEM
    return pl.pallas_call(
        functools.partial(norm_back_kernel, row),
        grid=(inner // width,),
        in_specs=[
            pl.BlockSpec((None, rows, width), lambda i: (i // each, 0, i % each)),
            pl.BlockSpec((D, width), lambda i: (0, i)),
            whole,
            vector,
            whole,
        ],
        out_specs=[whole, vector],
        out_shape=[
            jax.ShapeDtypeStruct((rows, D), jnp.float32),
            jax.ShapeDtypeStruct((1, D), jnp.float32),
        ],
        scratch_shapes=[pltpu.VMEM((rows, D), jnp.float32)],
        cost_estimate=BRIEF,
        compiler_params=pltpu.CompilerParams(vmem_limit_bytes=14 << 20),
    )(grad_lo, weight, values, vectors, above)


def turned(values, cosine, sine):
    half = HD // 2
    lead, tail = values[:, :half], values[:, half:]
    return jnp.concatenate([lead * cosine - tail * sine, tail * cosine + lead * sine], axis=1)


def attend_kernel(
    query_ref, key_ref, value_ref, cosine_ref, sine_ref, bias_ref, out_ref, query_out, key_out, value_out, log_out
):
    cosine, sine = cosine_ref[...], sine_ref[...]
    query = turned(query_ref[...], cosine, sine).astype(jnp.bfloat16)
    key = turned(key_ref[...], cosine, sine).astype(jnp.bfloat16)
    value = value_ref[...].astype(jnp.bfloat16)
    query_out[...], key_out[...], value_out[...] = query, key, value
    scores = jnp.where(bias_ref[...] > 0, nt_dot(query, key) * HD**-0.5, -1e30)
    top = jnp.max(scores, axis=-1, keepdims=True)
    weights = jnp.exp(scores - top)
    total = jnp.sum(weights, axis=-1, keepdims=True)
    probs = (weights * (1.0 / total)).astype(jnp.bfloat16)
    out_ref[...] = jnp.dot(probs, value, preferred_element_type=jnp.float32).astype(jnp.bfloat16)
    log_out[...] = jnp.broadcast_to(top + jnp.log(total), log_out.shape)


def attend(mixed, cosine, sine, valid):
    rows = mixed.shape[0]
    head = lambda shift: pl.BlockSpec((rows, HD), lambda i: (0, i + shift))
    fixed = lambda *shape: pl.BlockSpec(shape, lambda i: (0, 0))
    return pl.pallas_call(
        attend_kernel,
        grid=(H,),
        in_specs=[
            head(0),
            head(H),
            head(2 * H),
            fixed(rows, HD // 2),
            fixed(rows, HD // 2),
            fixed(1, rows),
        ],
        out_specs=[head(0)] * 5,
        out_shape=[jax.ShapeDtypeStruct((rows, D), jnp.bfloat16)] * 4
        + [jax.ShapeDtypeStruct((rows, D), jnp.float32)],
        cost_estimate=BRIEF,
        compiler_params=pltpu.CompilerParams(vmem_limit_bytes=12 << 20),
    )(mixed, mixed, mixed, cosine, sine, valid)


def attend_back_kernel(
    query_ref, key_ref, value_ref, log_ref, grad_ref, cosine_ref, sine_ref, bias_ref, out_ref
):
    query, key, value, grad = query_ref[...], key_ref[...], value_ref[...], grad_ref[...]
    cosine, sine = cosine_ref[...], -sine_ref[...]
    scores = jnp.where(bias_ref[...] > 0, nt_dot(query, key) * HD**-0.5, -1e30)
    probs = jnp.exp(scores - log_ref[:, :1])
    grad_probs = nt_dot(grad, value)
    along = jnp.sum(probs * grad_probs, axis=-1, keepdims=True)
    grad_scores = (probs * (grad_probs - along)).astype(jnp.bfloat16)
    out_ref[2] = matmul_tn(probs.astype(jnp.bfloat16), grad).astype(jnp.bfloat16)
    query_grad = matmul(grad_scores, key) * HD**-0.5
    key_grad = matmul_tn(grad_scores, query) * HD**-0.5
    out_ref[0] = turned(query_grad, cosine, sine).astype(jnp.bfloat16)
    out_ref[1] = turned(key_grad, cosine, sine).astype(jnp.bfloat16)


def attend_back(query, key, value, logs, grads, cosine, sine, valid):
    rows = query.shape[0]
    head = pl.BlockSpec((rows, HD), lambda i: (0, i))
    fixed = lambda *shape: pl.BlockSpec(shape, lambda i: (0, 0))
    return pl.pallas_call(
        attend_back_kernel,
        grid=(H,),
        in_specs=[head] * 5
        + [fixed(rows, HD // 2), fixed(rows, HD // 2), fixed(1, rows)],
        out_specs=pl.BlockSpec((3, rows, HD), lambda i: (0, 0, i)),
        out_shape=jax.ShapeDtypeStruct((3, rows, D), jnp.bfloat16),
        cost_estimate=BRIEF,
        compiler_params=pltpu.CompilerParams(vmem_limit_bytes=12 << 20),
    )(query, key, value, logs, grads, cosine, sine, valid)


def fence(flows, *values):
    states, values = lax.optimization_barrier(([flow.state for flow in flows], values))
    for flow, state in zip(flows, states):
        flow.state = state
    return values[0] if len(values) == 1 else values


def rows_of(values, count):
    return values.reshape(count, values.shape[-1])


def shards(
    sizes,
    frames,
    ffn_inner,
    ffn_outer,
    attn_qkv,
    attn_proj,
    conv_expand,
    conv_depth,
    conv_proj,
    norm_gains,
    head_proj,
    lengths,
    mask_starts,
    target_codes,
    out_grad,
):
    cube = Cube(sizes)
    cube.where = lax.optimization_barrier(cube.place()) if cube.tuned else None
    devices = sizes["dp"] * sizes["head"]
    ff = ffn_inner.shape[2]
    all_bits = list(range(len(cube.bits)))

    rows_in = Gather(
        cube,
        [
            ("wide", [ffn_inner[0]]),
            ("tall", [ffn_outer[0]]),
            ("wide", [attn_qkv, attn_proj]),
            ("wide", [conv_expand, conv_proj]),
            ("wide", [ffn_inner[1]]),
            ("tall", [ffn_outer[1]]),
        ],
    )
    head_half = head_proj.shape[1] // 2
    heads = [
        HeadGathering(cube, head_proj[:, :head_half]),
        HeadGathering(cube, head_proj[:, head_half:]),
    ]

    row_total = UTT_DEV * SEQ
    positions = jnp.arange(SEQ, dtype=jnp.int32)
    valid_mat = positions[None, :] < lengths[:, None]
    valid_rows = valid_mat.reshape(row_total).astype(jnp.float32)
    frequency = 10000.0 ** (-(jnp.arange(HD // 2, dtype=jnp.float32) * 2.0) / HD)
    angles = positions.astype(jnp.float32)[:, None] * frequency[None, :]
    cosine, sine_table = jnp.cos(angles), jnp.sin(angles)

    slots = UTT_DEV * NSPAN * SPAN
    slot_at = (mask_starts[:, :, None] + jnp.arange(SPAN, dtype=jnp.int32)).reshape(UTT_DEV, -1)
    slot_ok = slot_at < lengths[:, None]
    chosen = (slot_at + SEQ * jnp.arange(UTT_DEV, dtype=jnp.int32)[:, None]).reshape(slots)
    slot_live = slot_ok.reshape(slots)
    pick = (
        (chosen[:, None] == jnp.arange(row_total, dtype=jnp.int32)[None, :]) & slot_live[:, None]
    )
    picked_codes = jnp.sum(jnp.where(pick, target_codes[None, :], 0), axis=1)
    picked_codes = jnp.where(slot_live, picked_codes, -1)
    pick_lo = pick.astype(jnp.bfloat16)
    head_order = [at for at in range(len(cube.bits)) if cube.bits[at][0] == "head"]
    group = sizes["head"]
    vocab_cols = head_proj.shape[1]

    loss_scale = jnp.float32(devices * UTT_DEV * NSPAN * SPAN)
    hops = [C, Y, X, Z1, Z0] if cube.tuned else all_bits
    vector_in = VectorGathering(cube, jnp.concatenate([conv_depth, norm_gains, jnp.zeros_like(conv_depth[:10])], axis=0), hops)
    vector_in.step(3)
    group_codes = cube.gather(picked_codes, head_order).reshape(group * slots)
    rows_in.start()
    if cube.tuned:
        head_got = cube.swap(head_proj, X)
        for at, flow in enumerate(heads):
            columns = slice(at * head_half, (at + 1) * head_half)
            flow.state = [head_proj[:, columns], head_got[:, columns]]
    else:
        heads[0].step("x")
        heads[1].step("x")
    group_codes = fence([rows_in, vector_in, *heads], group_codes)

    rows_in.stage(-1)
    vector_in.step()
    inputs = frames.astype(jnp.float32)
    fence([rows_in, vector_in], loss_scale)

    rows_in.stage(0)
    vector_in.step(len(hops))
    heads[0].step("far")
    fence([rows_in, vector_in, heads[0]], loss_scale)
    (vectors,) = vector_in.state
    vectors = fence([], joined_vectors(vectors.reshape((devices,) + vectors.shape[-2:])))
    gain_f = vectors[TAPS : TAPS + 6]
    norm_first = lowered(layer_norm(inputs, gain_f[0]))
    group_live = (group_codes >= 0).astype(jnp.float32)
    local_codes = group_codes - lax.axis_index("head") * vocab_cols

    rows_in.stage(1)
    (inner_0,) = rows_in.wholes[0]
    pre_first = matmul(norm_first, inner_0)
    act_first = lowered(jax.nn.silu(pre_first))
    pre_first = lowered(pre_first)
    pre_first, act_first = fence([rows_in], pre_first, act_first)

    rows_in.stage(2)
    (outer_0,) = rows_in.wholes[1]
    after_first = inputs + 0.5 * matmul(act_first, outer_0)
    norm_attn = lowered(layer_norm(after_first, gain_f[1]))
    after_first, norm_attn = fence([rows_in], after_first, norm_attn)

    rows_in.stage(3)
    heads[0].step("near")
    mix_weight, proj_weight = rows_in.wholes[2]
    mixed = matmul(norm_attn, mix_weight)
    attended_lo, queries, key_rows, value_rows, log_totals = attend(
        mixed, cosine, sine_table, valid_rows[None, :]
    )
    after_attention = after_first + matmul(attended_lo, proj_weight)
    norm_conv = lowered(layer_norm(after_attention, gain_f[2]))
    after_attention, norm_conv, attended_lo, queries, key_rows, value_rows, log_totals = fence(
        [rows_in, heads[0]],
        after_attention,
        norm_conv,
        attended_lo,
        queries,
        key_rows,
        value_rows,
        log_totals,
    )

    rows_in.stage(4)
    heads[1].step("far")
    expand_weight, conv_weight = rows_in.wholes[3]
    expanded = matmul(norm_conv, expand_weight)
    conv_out, conv_sums = conv_forward(expanded, valid_rows[:, None], vectors)
    sums = cube.total(conv_sums)
    sums, conv_out, after_attention, expanded, norm_conv = fence(
        [rows_in, *heads], sums, conv_out, after_attention, expanded, norm_conv
    )

    rows_in.stage(5)
    heads[1].step("near")
    (inner_1,) = rows_in.wholes[4]
    frame_count = sums[2, 0]
    channel_mean = sums[0] / frame_count
    variance = sums[1] / frame_count - channel_mean * channel_mean
    inverse = lax.rsqrt(variance + eps)
    normalized = (conv_out - channel_mean) * inverse
    normed_bn = normalized * gain_f[3]
    swish_lo = lowered(jax.nn.silu(normed_bn))
    after_conv = after_attention + matmul(swish_lo, conv_weight)
    norm_second = lowered(layer_norm(after_conv, gain_f[4]))
    pre_second = matmul(norm_second, inner_1)
    act_second = lowered(jax.nn.silu(pre_second))
    pre_second = lowered(pre_second)
    after_conv, norm_second, pre_second, act_second, swish_lo = fence(
        [rows_in, *heads], after_conv, norm_second, pre_second, act_second, swish_lo
    )

    rows_in.stage(6)
    (outer_1,) = rows_in.wholes[5]
    head_cols = joined_heads(cube, heads)
    after_second = after_conv + 0.5 * matmul(act_second, outer_1)
    output_lo = lowered(layer_norm(after_second, gain_f[5]))

    picked_rows = lowered(matmul(pick_lo, output_lo))
    group_rows = cube.gather(picked_rows, head_order).reshape(group * slots, D)
    logits = matmul(group_rows, head_cols)
    row_top = jnp.max(logits, axis=1)
    row_sum = jnp.sum(jnp.exp(logits - row_top[:, None]), axis=1)
    onehot = jnp.arange(vocab_cols, dtype=jnp.int32)[None, :] == local_codes[:, None]
    target_logit = jnp.sum(jnp.where(onehot, logits, 0.0), axis=1)
    stats = cube.gather(jnp.stack([row_top, row_sum, target_logit]), head_order)
    stats = stats.reshape(group, 3, group * slots)
    whole_top = jnp.max(stats[:, 0], axis=0)
    whole_sum = jnp.sum(stats[:, 1] * jnp.exp(stats[:, 0] - whole_top), axis=0)
    log_norm = whole_top + jnp.log(whole_sum)
    ce_group = jnp.sum((log_norm - jnp.sum(stats[:, 2], axis=0)) * group_live)
    grad_logits = lowered(
        (jnp.exp(logits - log_norm[:, None]) - onehot.astype(jnp.float32)) * group_live[:, None]
    )
    head_grad = lowered(matmul_tn(group_rows, grad_logits))
    head_flow = HeadScattering(cube, head_grad, head_proj.shape[0])
    row_grads = lowered(matmul_nt(grad_logits, head_cols))
    row_sum = Summing(cube, row_grads.reshape((2,) * len(head_order) + (slots, D)), head_order[::-1])
    head_flow.step()
    for _ in head_order:
        row_sum.step()
    row_grads = lowered(row_sum.result())
    if cube.tuned:
        keeps, row_grads = lax.optimization_barrier(
            ([part.state[0] for part in head_flow.parts], row_grads)
        )
        for part, keep in zip(head_flow.parts, keeps):
            part.state[0] = keep
    grad_output = out_grad.astype(jnp.float32) + matmul_tn(pick_lo, row_grads)

    rows_out = Scatter(cube)
    grad_second, gain_grad_final = norm_back(after_second, gain_f[5], grad_output)
    grad_out_lo = lowered(0.5 * grad_second)
    piece = weight_grads(cube, "tall", [(act_second, grad_out_lo[None])])
    grad_second, grad_out_lo, piece = fence([], grad_second, grad_out_lo, piece)

    rows_out.push("tall", [ffn_outer[1]], piece)
    grad_pre = act_back(grad_out_lo, outer_1, pre_second)
    piece = weight_grads(cube, "wide", [(norm_second, grad_pre)])
    grad_conv_res, gain_grad_second = product_norm_back(
        grad_pre, inner_1, after_conv, vectors, 4, grad_second
    )
    grad_conv_res, piece = fence([head_flow, rows_out], grad_conv_res, piece)

    conv_res_lo = lowered(grad_conv_res)
    grad_bn = silu_back(normed_bn, matmul_nt(conv_res_lo, conv_weight))
    gain_grad_bn = jnp.sum(grad_bn * normalized, axis=0)
    grad_normalized = grad_bn * gain_f[3]
    back_sums = cube.total(
        jnp.stack(
            [
                jnp.sum(grad_normalized, axis=0),
                jnp.sum(grad_normalized * normalized, axis=0),
                jnp.broadcast_to(ce_group / group, (D,)),
            ]
            + [jnp.zeros((D,), jnp.float32)] * 5
        )
    )
    back_sums, grad_normalized, grad_conv_res, conv_res_lo, piece = fence(
        [], back_sums, grad_normalized, grad_conv_res, conv_res_lo, piece
    )

    head_flow.step()
    rows_out.stage()
    rows_out.push("wide", [ffn_inner[1]], piece)
    loss = back_sums[2, 0] / loss_scale
    grad_expanded, depth_grad = conv_backward(
        expanded, valid_rows[:, None], vectors, conv_out, grad_normalized, sums, back_sums
    )
    piece = weight_grads(cube, "wide", [(norm_conv, grad_expanded), (swish_lo, conv_res_lo[None])])
    grad_expanded, piece = fence([rows_out, head_flow], grad_expanded, piece)

    head_flow.step()
    rows_out.stage()
    rows_out.push("wide", [conv_expand, conv_proj], piece)
    grad_attn_res, gain_grad_conv = product_norm_back(
        grad_expanded, expand_weight, after_attention, vectors, 2, grad_conv_res
    )
    attn_res_lo = lowered(grad_attn_res)
    grad_attended = lowered(matmul_nt(attn_res_lo, proj_weight))
    grad_mixed = attend_back(
        queries,
        key_rows,
        value_rows,
        log_totals,
        grad_attended,
        cosine,
        sine_table,
        valid_rows[None, :],
    )
    piece = weight_grads(cube, "wide", [(norm_attn, grad_mixed), (attended_lo, attn_res_lo[None])])
    grad_mixed, grad_attn_res, piece = fence(
        [rows_out, head_flow], grad_mixed, grad_attn_res, piece
    )

    rows_out.stage()
    rows_out.push("wide", [attn_qkv, attn_proj], piece)
    grad_first_res, gain_grad_attn = product_norm_back(
        grad_mixed, mix_weight, after_first, vectors, 1, grad_attn_res
    )
    grad_out_lo = lowered(0.5 * grad_first_res)
    piece = weight_grads(cube, "tall", [(act_first, grad_out_lo[None])])
    grad_pre = act_back(grad_out_lo, outer_0, pre_first)
    grad_first_res, grad_pre, piece = fence([rows_out], grad_first_res, grad_pre, piece)

    rows_out.stage()
    rows_out.push("tall", [ffn_outer[0]], piece)
    piece = weight_grads(cube, "wide", [(norm_first, grad_pre)])
    input_grad, gain_grad_first = product_norm_back(
        grad_pre, inner_0, inputs, vectors, 0, grad_first_res
    )
    vector_grad = parted_vectors(
        [
            depth_grad,
            gain_grad_first,
            gain_grad_attn,
            gain_grad_conv,
            gain_grad_bn.reshape(1, D),
            gain_grad_second,
            gain_grad_final.reshape(1, D),
        ],
        devices,
    )
    vector_flow = Summing(
        cube,
        vector_grad.reshape((2,) * len(cube.bits) + vector_grad.shape[1:]),
        [C, Z1, Z0, X, Y] if cube.tuned else all_bits,
    )
    vector_flow.step()
    input_grad, piece = fence([rows_out, vector_flow], input_grad, piece)

    rows_out.stage()
    rows_out.push("wide", [ffn_inner[0]], piece)
    vector_flow.step()
    fence([rows_out, vector_flow], loss)

    for _ in range(4):
        rows_out.stage()
        if vector_flow.order:
            vector_flow.step()
        fence([rows_out, vector_flow], loss)
    for _ in vector_flow.order[:]:
        vector_flow.step()
    vector_grad = vector_flow.result()
    rows_out.stage()
    (
        (outer_grad_1,),
        (inner_grad_1,),
        (expand_grad, conv_proj_grad),
        (mix_grad, proj_grad),
        (outer_grad_0,),
        (inner_grad_0,),
    ) = rows_out.results
    return (
        output_lo,
        loss,
        input_grad,
        jnp.stack([inner_grad_0, inner_grad_1], axis=0),
        jnp.stack([outer_grad_0, outer_grad_1], axis=0),
        mix_grad,
        proj_grad,
        expand_grad,
        vector_grad[:TAPS],
        conv_proj_grad,
        vector_grad[TAPS:],
        head_flow.result(),
    )


def solution(mesh):
    placed = (
        P(("dp", "head"), None),
        P(None, ("dp", "head"), None),
        P(None, ("dp", "head"), None),
        P(("dp", "head"), None),
        P(("dp", "head"), None),
        P(("dp", "head"), None),
        P(None, ("dp", "head")),
        P(("dp", "head"), None),
        P(None, ("dp", "head")),
        P("dp", "head"),
        P(("dp", "head")),
        P(("dp", "head"), None),
        P(("dp", "head")),
        P(("dp", "head"), None),
    )
    sizes = {axis: mesh.shape[axis] for axis in AXES}
    return jax.shard_map(
        functools.partial(shards, sizes),
        mesh=mesh,
        in_specs=placed,
        out_specs=(
            P(("dp", "head"), None),
            P(),
            P(("dp", "head"), None),
            P(None, ("dp", "head"), None),
            P(None, ("dp", "head"), None),
            P(("dp", "head"), None),
            P(("dp", "head"), None),
            P(("dp", "head"), None),
            P(None, ("dp", "head")),
            P(("dp", "head"), None),
            P(None, ("dp", "head")),
            P("dp", "head"),
        ),
        check_vma=False,
    )
```
